32 devices in a mesh: dp: 4 (over y, x), ctx: 8 (over z, core).
Axes of the slice: x: 2, y: 2, z: 4, core: 2. Of those that a mesh axis runs over, the one named last changes fastest.
Arguments:
- layer_input: bfloat16 [2, 4, 1024, 2048], P(None, 'dp', 'ctx'), may hold values from -6 to 6
- out_grad: bfloat16 [2, 4, 1024, 2048], P(None, 'dp', 'ctx'), may hold values from -6 to 6
- prefix_len: int32 [2, 4], P(None, 'dp'), may hold values from 102 to 512
- qkv_weight: bfloat16 [2048, 6144], P(('dp', 'ctx')), may hold values from -0.125 to 0.125
- qkv_bias: bfloat16 [6144], P(('dp', 'ctx')), may hold values from -3 to 3
- dense_weight: bfloat16 [2048, 2048], P(('dp', 'ctx')), may hold values from -1.5 to 1.5
- dense_bias: bfloat16 [2048], P(('dp', 'ctx')), may hold values from -3 to 3
- expand_weight: bfloat16 [2048, 8192], P(('dp', 'ctx')), may hold values from -0.125 to 0.125
- expand_bias: bfloat16 [8192], P(('dp', 'ctx')), may hold values from -3 to 3
- shrink_weight: bfloat16 [8192, 2048], P(('dp', 'ctx')), may hold values from -0.0625 to 0.0625
- shrink_bias: bfloat16 [2048], P(('dp', 'ctx')), may hold values from -3 to 3
- attn_gain: bfloat16 [2048], P(('dp', 'ctx')), may hold values from 0.099609375 to 1.8984375
- attn_shift: bfloat16 [2048], P(('dp', 'ctx')), may hold values from -2 to 2
- mlp_gain: bfloat16 [2048], P(('dp', 'ctx')), may hold values from 0.099609375 to 1.8984375
- mlp_shift: bfloat16 [2048], P(('dp', 'ctx')), may hold values from -2 to 2
Outputs:
- layer_output: bfloat16 [2, 4, 1024, 2048], P(None, 'dp', 'ctx')
- input_grad: bfloat16 [2, 4, 1024, 2048], P(None, 'dp', 'ctx')
- qkv_weight_grad: float32 [2048, 6144], P(('dp', 'ctx'))
- qkv_bias_grad: float32 [4096], P(('dp', 'ctx'))
- value_bias_grad: float32 [2048], P(('dp', 'ctx'))
- dense_weight_grad: float32 [2048, 2048], P(('dp', 'ctx'))
- dense_bias_grad: float32 [2048], P(('dp', 'ctx'))
- expand_weight_grad: float32 [2048, 8192], P(('dp', 'ctx'))
- expand_bias_grad: float32 [8192], P(('dp', 'ctx'))
- shrink_weight_grad: float32 [8192, 2048], P(('dp', 'ctx'))
- shrink_bias_grad: float32 [2048], P(('dp', 'ctx'))
- attn_gain_grad: float32 [2048], P(('dp', 'ctx'))
- attn_shift_grad: float32 [2048], P(('dp', 'ctx'))
- mlp_gain_grad: float32 [2048], P(('dp', 'ctx'))
- mlp_shift_grad: float32 [2048], P(('dp', 'ctx'))
The draws below stay inside these ranges and needn't reach their ends.
All inputs are finite; a program needn't handle non-finite values.
Results may differ from the reference program's by a relative error of at most 0.011.
Values may be sent and summed in bfloat16 or wider, within the bound.
A program may use at most 704 MiB of HBM per device.

```python
import math
import jax
import jax.numpy as jnp
from jax import lax

D = 2048
HEADS = 8
HEAD = 256
ROT = 64
FF = 8192
SEQ = 1024
MICRO = 2
SEQUENCES = 4


def plant(array, key, low, high):
    spot = [jax.random.randint(jax.random.fold_in(key, axis), (), 0, length) for axis, length in enumerate(array.shape)]
    widest = array.shape.index(max(array.shape))
    next_to = spot[:widest] + [(spot[widest] + 1) % array.shape[widest]] + spot[widest + 1:]
    return array.at[tuple(spot)].set(low).at[tuple(next_to)].set(high)


def levels(key, shape, shards, low, high):
    def one(dim, blocks):
        draws = jax.random.uniform(jax.random.fold_in(jax.random.fold_in(key, 6), dim), (blocks,), jnp.float32, low / len(shards), high / len(shards))
        return jnp.repeat(jnp.exp(draws), shape[dim] // blocks).reshape((-1,) + (1,) * (len(shape) - dim - 1))

    factor_of = one(*shards[0])
    for cut in shards[1:]:
        factor_of = factor_of * one(*cut)
    return factor_of


def normal_values(key, extent, deviation, reach, pieces=(), kind=jnp.bfloat16):
    array = deviation * jax.random.normal(key, extent, jnp.float32)
    if pieces:
        array = array * levels(key, extent, pieces, -0.22, 0.18)
    return jnp.clip(array, -reach, reach).astype(kind)


def setup_inputs(seed: int = 0) -> dict:
    streams_of = jax.random.split(jax.random.key(seed), 16)
    layer_input = normal_values(streams_of[0], (MICRO, SEQUENCES, SEQ, D), 1.0, 6.0, ((1, 4), (2, 8)))
    out_grad = normal_values(streams_of[1], (MICRO, SEQUENCES, SEQ, D), 1.0, 6.0, ((1, 4), (2, 8)))
    prefix_len = plant(jax.random.randint(streams_of[2], (MICRO, SEQUENCES), SEQ // 10, SEQ // 2 + 1), jax.random.fold_in(streams_of[2], 1), SEQ // 10, (SEQ // 2 + 1) - 1).astype(jnp.int32)
    qkv_weight = normal_values(streams_of[3], (D, 3 * D), D ** -0.5, 0.125, ((0, 32),))
    qkv_bias = normal_values(streams_of[4], (3 * D,), 0.5, 3.0, ((0, 32),))
    dense_weight = normal_values(streams_of[5], (D, D), (max(D // 128, 1)) ** -0.5, 1.5, ((0, 32),))
    dense_bias = normal_values(streams_of[6], (D,), 0.5, 3.0, ((0, 32),))
    expand_weight = normal_values(streams_of[7], (D, FF), D ** -0.5, 0.125, ((0, 32),))
    expand_bias = normal_values(streams_of[8], (FF,), 0.5, 3.0, ((0, 32),))
    shrink_weight = normal_values(streams_of[9], (FF, D), FF ** -0.5, 0.0625, ((0, 32),))
    shrink_bias = normal_values(streams_of[10], (D,), 0.5, 3.0, ((0, 32),))
    attn_gain = jnp.clip(1.0 + 0.18 * jax.random.normal(streams_of[11], (D,), jnp.float32), 0.099609375, 1.8984375).astype(jnp.bfloat16)
    attn_shift = normal_values(streams_of[12], (D,), 0.3, 2.0, ((0, 32),))
    mlp_gain = jnp.clip(1.0 + 0.18 * jax.random.normal(streams_of[13], (D,), jnp.float32), 0.099609375, 1.8984375).astype(jnp.bfloat16)
    mlp_shift = normal_values(streams_of[14], (D,), 0.3, 2.0, ((0, 32),))
    return {"layer_input": layer_input, "out_grad": out_grad, "prefix_len": prefix_len, "qkv_weight": qkv_weight, "qkv_bias": qkv_bias, "dense_weight": dense_weight, "dense_bias": dense_bias, "expand_weight": expand_weight, "expand_bias": expand_bias, "shrink_weight": shrink_weight, "shrink_bias": shrink_bias, "attn_gain": attn_gain, "attn_shift": attn_shift, "mlp_gain": mlp_gain, "mlp_shift": mlp_shift}


HIGHEST = lax.Precision.HIGHEST

@jax.custom_vjp
def low(v):
    return lax.optimization_barrier(v.astype(jnp.bfloat16)).astype(jnp.float32)

@jax.custom_vjp
def low_back(v):
    return v

def low_keep(v):
    return (low(v), None)

def low_pass(kept, grad):
    return (grad,)

def back_keep(v):
    return (v, None)

def back_low(kept, grad):
    return (low(grad),)
low.defvjp(low_keep, low_pass)
low_back.defvjp(back_keep, back_low)

def norm_rows(inputs, norm_gain, norm_bias):
    row_mean = lax.optimization_barrier(jnp.mean(inputs, axis=-1, keepdims=True))
    centered = inputs - row_mean
    variance = lax.optimization_barrier(jnp.mean(centered * centered, axis=-1, keepdims=True))
    return centered * lax.rsqrt(variance + 1e-05) * norm_gain + norm_bias

def rope_tables(positions):
    freqs = jnp.exp(jnp.arange(ROT // 2, dtype=jnp.float32) * (-2.0 * math.log(10000.0) / ROT))
    angles = positions[:, None] * freqs[None, :]
    return (jnp.cos(angles), jnp.sin(angles))

def rotate(heads, cos_table, sin_table):
    half_rot = ROT // 2
    lower = heads[..., :half_rot]
    upper = heads[..., half_rot:ROT]
    cos_wide = cos_table[:, None, :]
    sin_wide = sin_table[:, None, :]
    return jnp.concatenate([lower * cos_wide - upper * sin_wide, upper * cos_wide + lower * sin_wide, heads[..., ROT:]], axis=-1)

def forward(inputs, prefix, qkv_weight, qkv_bias, dense_weight, dense_bias, expand_weight, expand_bias, shrink_weight, shrink_bias, attn_gain, attn_shift, mlp_gain, mlp_shift):
    group = inputs.shape[0]
    heads_shape = (group, SEQ, HEADS, HEAD)
    hidden_attn = low(norm_rows(inputs, attn_gain, attn_shift))
    hidden_mlp = low(norm_rows(inputs, mlp_gain, mlp_shift))
    joined = low_back(jnp.einsum('gsd,de->gse', hidden_attn, qkv_weight, precision=HIGHEST) + qkv_bias)
    cos_table, sin_table = rope_tables(jnp.arange(SEQ, dtype=jnp.float32))
    queries = low(rotate(joined[..., :D].reshape(heads_shape), cos_table, sin_table))
    key_rows = low(rotate(joined[..., D:2 * D].reshape(heads_shape), cos_table, sin_table))
    value_rows = low(joined[..., 2 * D:].reshape(heads_shape))
    scores = low_back(jnp.einsum('gqhe,gkhe->ghqk', queries, key_rows, precision=HIGHEST) * (1.0 / math.sqrt(HEAD)))
    positions = jnp.arange(SEQ, dtype=jnp.int32)
    allowed = (positions[None, :] <= positions[:, None])[None] | (positions[None, None, :] < prefix[:, None, None])
    scores = jnp.where(allowed[:, None], scores, -1e+30)
    attn_probs = low(jax.nn.softmax(scores, axis=-1))
    mixed = jnp.einsum('ghqk,gkhe->gqhe', attn_probs, value_rows, precision=HIGHEST).reshape(group, SEQ, D)
    mixed = low_back(low(mixed))
    attn_out = jnp.einsum('gsd,de->gse', mixed, dense_weight, precision=HIGHEST) + dense_bias
    expanded = low_back(jnp.einsum('gsd,df->gsf', hidden_mlp, expand_weight, precision=HIGHEST) + expand_bias)
    activated = low(jax.nn.gelu(expanded, approximate=False))
    mlp_out = jnp.einsum('gsf,fd->gsd', activated, shrink_weight, precision=HIGHEST) + shrink_bias
    return inputs + attn_out + mlp_out

def reference(layer_input, out_grad, prefix_len, qkv_weight, qkv_bias, dense_weight, dense_bias, expand_weight, expand_bias, shrink_weight, shrink_bias, attn_gain, attn_shift, mlp_gain, mlp_shift):
    params = tuple((member.astype(jnp.float32) for member in (qkv_weight, qkv_bias, dense_weight, dense_bias, expand_weight, expand_bias, shrink_weight, shrink_bias, attn_gain, attn_shift, mlp_gain, mlp_shift)))
    group = math.gcd(4, MICRO * SEQUENCES)
    steps = MICRO * SEQUENCES // group
    inputs = layer_input.astype(jnp.float32).reshape(steps, group, SEQ, D)
    cotangent = out_grad.astype(jnp.float32).reshape(steps, group, SEQ, D)
    prefixes = prefix_len.reshape(steps, group).astype(jnp.int32)

    def one_step(totals, block):
        input_block, cot_block, prefix_block = block

        def run(inp, *weights):
            return forward(inp, prefix_block, *weights)
        outputs, pullback = jax.vjp(run, input_block, *params)
        grads = pullback(cot_block)
        totals = tuple((total_sum + member for total_sum, member in zip(totals, grads[1:])))
        return (totals, (outputs, grads[0]))
    zeros = tuple((jnp.zeros_like(member) for member in params))
    totals, (outputs, input_grads) = lax.scan(one_step, zeros, (inputs, cotangent, prefixes))
    whole = (MICRO, SEQUENCES, SEQ, D)
    return (outputs.reshape(whole).astype(jnp.bfloat16), input_grads.reshape(whole).astype(jnp.bfloat16), totals[0], totals[1][:2 * D], totals[1][2 * D:], totals[2], totals[3], totals[4], totals[5], totals[6], totals[7], totals[8], totals[9], totals[10], totals[11])
```

```python
import math

import jax
import jax.numpy as jnp
from jax import lax
from jax.sharding import PartitionSpec as P

HEADS = 8
HEAD = 256
ROT = 64
SEQ = 1024


def norm_rows(inputs, norm_gain, norm_bias):
    row_mean = jnp.mean(inputs, axis=-1, keepdims=True)
    centered = inputs - row_mean
    variance = jnp.mean(centered * centered, axis=-1, keepdims=True)
    return centered * lax.rsqrt(variance + 1e-05) * norm_gain + norm_bias


def gelu_exact(values):
    return jax.nn.gelu(values, approximate=False)


def rope_tables(positions):
    freqs = jnp.exp(jnp.arange(ROT // 2, dtype=jnp.float32) * (-2.0 * math.log(10000.0) / ROT))
    angles = positions[:, None] * freqs[None, :]
    return (jnp.cos(angles), jnp.sin(angles))


def rotate(heads, cos_table, sin_table):
    half_rot = ROT // 2
    lower = heads[..., :half_rot]
    upper = heads[..., half_rot:ROT]
    cos_wide = cos_table[:, None, :]
    sin_wide = sin_table[:, None, :]
    return jnp.concatenate(
        [
            lower * cos_wide - upper * sin_wide,
            upper * cos_wide + lower * sin_wide,
            heads[..., ROT:],
        ],
        axis=-1,
    )


def unpack_small(packed, lengths, devices):
    table_rows = packed.reshape(devices, -1)
    members = []
    offset = 0
    for length in lengths:
        members.append(table_rows[:, offset : offset + length].reshape(-1).astype(jnp.float32))
        offset = offset + length
    return members


def contract_rows(left_mat, right_mat):
    return lax.dot_general(
        left_mat, right_mat, (((0,), (0,)), ((), ())), preferred_element_type=jnp.float32
    )


def contract_cols(left_mat, right_mat):
    return lax.dot_general(
        left_mat, right_mat, (((1,), (1,)), ((), ())), preferred_element_type=jnp.float32
    )


def shards(
    layer_input,
    out_grad,
    prefix_len,
    qkv_weight,
    qkv_bias,
    dense_weight,
    dense_bias,
    expand_weight,
    expand_bias,
    shrink_weight,
    shrink_bias,
    attn_gain,
    attn_shift,
    mlp_gain,
    mlp_shift,
):
    devices = lax.axis_size("dp") * lax.axis_size("ctx")
    ctx_index = lax.axis_index("ctx")
    micro, seq_count, span, width = layer_input.shape
    sequences = micro * seq_count
    rows = sequences * span
    heads_shape = (sequences, span, HEADS, HEAD)
    scale = 1.0 / math.sqrt(HEAD)
    attn_lengths = (attn_gain.shape[0], attn_shift.shape[0], qkv_bias.shape[0], dense_bias.shape[0])
    mlp_lengths = (
        mlp_gain.shape[0],
        mlp_shift.shape[0],
        expand_bias.shape[0],
        shrink_bias.shape[0],
    )
    attn_packed = jnp.concatenate([attn_gain, attn_shift, qkv_bias, dense_bias])
    mlp_packed = jnp.concatenate([mlp_gain, mlp_shift, expand_bias, shrink_bias])

    def fetch_attn():
        return (
            lax.all_gather(qkv_weight, ("dp", "ctx"), axis=0, tiled=True),
            lax.all_gather(dense_weight, ("dp", "ctx"), axis=0, tiled=True),
            lax.all_gather(attn_packed, ("dp", "ctx"), axis=0, tiled=True),
        )

    def fetch_mlp():
        return (
            lax.all_gather(expand_weight, ("dp", "ctx"), axis=0, tiled=True),
            lax.all_gather(shrink_weight, ("dp", "ctx"), axis=0, tiled=True),
            lax.all_gather(mlp_packed, ("dp", "ctx"), axis=0, tiled=True),
        )

    local_pos = ctx_index * span + jnp.arange(span, dtype=jnp.int32)
    cos_table, sin_table = rope_tables(local_pos.astype(jnp.float32))
    key_pos = jnp.arange(SEQ, dtype=jnp.int32)
    causal = key_pos[None, :] <= local_pos[:, None]
    inputs = layer_input.astype(jnp.float32).reshape(rows, width)
    cot_rows = out_grad.reshape(rows, width)
    cot_float = cot_rows.astype(jnp.float32)
    prefix = prefix_len.reshape(sequences)
    allowed = (causal[None] | (key_pos[None, None, :] < prefix[:, None, None]))[:, None]
    attn_set = fetch_attn()
    qkv_full, dense_full, attn_small = attn_set
    gain_attn, shift_attn, joined_shift, dense_shift = unpack_small(
        attn_small, attn_lengths, devices
    )
    hidden_attn = norm_rows(inputs, gain_attn, shift_attn).astype(jnp.bfloat16)
    joined = jnp.dot(hidden_attn, qkv_full, preferred_element_type=jnp.float32) + joined_shift
    queries = rotate(joined[:, :width].reshape(heads_shape), cos_table, sin_table).astype(
        jnp.bfloat16
    )
    key_rows = rotate(
        joined[:, width : 2 * width].reshape(heads_shape), cos_table, sin_table
    ).astype(jnp.bfloat16)
    value_rows = joined[:, 2 * width :].reshape(heads_shape).astype(jnp.bfloat16)
    all_keys, all_values = (
        lax.all_gather(key_rows, "ctx", axis=1, tiled=True),
        lax.all_gather(value_rows, "ctx", axis=1, tiled=True),
    )
    scores = (
        jnp.einsum("sqhe,skhe->shqk", queries, all_keys, preferred_element_type=jnp.float32) * scale
    )
    scores = jnp.where(allowed, scores, -1e30)
    row_max = jnp.max(scores, axis=-1, keepdims=True)
    expo = jnp.exp(scores - row_max)
    row_total = jnp.sum(expo, axis=-1, keepdims=True)
    log_total = row_max + jnp.log(row_total)
    probs_low = (expo / row_total).astype(jnp.bfloat16)
    mixed = jnp.einsum("shqk,skhe->sqhe", probs_low, all_values, preferred_element_type=jnp.float32)
    mixed = mixed.reshape(rows, width).astype(jnp.bfloat16)
    attn_out = jnp.dot(mixed, dense_full, preferred_element_type=jnp.float32) + dense_shift
    mlp_set = fetch_mlp()
    expand_full, shrink_full, mlp_small = mlp_set
    gain_mlp, shift_mlp, expand_shift, shrink_shift = unpack_small(mlp_small, mlp_lengths, devices)
    hidden_mlp = norm_rows(inputs, gain_mlp, shift_mlp).astype(jnp.bfloat16)
    expanded = jnp.dot(hidden_mlp, expand_full, preferred_element_type=jnp.float32) + expand_shift
    activated = gelu_exact(expanded).astype(jnp.bfloat16)
    mlp_out = jnp.dot(activated, shrink_full, preferred_element_type=jnp.float32) + shrink_shift
    layer_output = (
        (inputs + attn_out + mlp_out).astype(jnp.bfloat16).reshape(micro, seq_count, span, width)
    )
    attn_back_set = fetch_attn()
    qkv_back, dense_back, attn_small_back = attn_back_set
    gain_attn, shift_attn, joined_shift, dense_shift = unpack_small(
        attn_small_back, attn_lengths, devices
    )
    grad_out_shift = jnp.sum(cot_float, axis=0)
    grad_mixed = contract_cols(cot_rows, dense_back).astype(jnp.bfloat16).reshape(heads_shape)
    again = (
        jnp.einsum("sqhe,skhe->shqk", queries, all_keys, preferred_element_type=jnp.float32) * scale
    )
    again = jnp.where(allowed, again, -1e30)
    probs = jnp.exp(again - log_total)
    grad_probs = jnp.einsum(
        "sqhe,skhe->shqk", grad_mixed, all_values, preferred_element_type=jnp.float32
    )
    delta = jnp.sum(probs * grad_probs, axis=-1, keepdims=True)
    grad_scores = (probs * (grad_probs - delta)).astype(jnp.bfloat16)
    grad_queries = (
        jnp.einsum("shqk,skhe->sqhe", grad_scores, all_keys, preferred_element_type=jnp.float32)
        * scale
    )
    all_queries, all_grad_mixed = (
        lax.all_gather(queries, "ctx", axis=1, tiled=True),
        lax.all_gather(grad_mixed, "ctx", axis=1, tiled=True),
    )
    stat_lse = jnp.transpose(log_total[..., 0], (0, 2, 1))
    stat_delta = jnp.transpose(delta[..., 0], (0, 2, 1))
    lse_all, delta_all = (
        lax.all_gather(stat_lse, "ctx", axis=1, tiled=True),
        lax.all_gather(stat_delta, "ctx", axis=1, tiled=True),
    )
    lse_all = jnp.transpose(lse_all, (0, 2, 1))[..., None]
    delta_all = jnp.transpose(delta_all, (0, 2, 1))[..., None]
    key_allowed = (local_pos[None, :] <= key_pos[:, None])[None] | (
        local_pos[None, None, :] < prefix[:, None, None]
    )
    block_scores = (
        jnp.einsum("sqhe,skhe->shqk", all_queries, key_rows, preferred_element_type=jnp.float32)
        * scale
    )
    block_scores = jnp.where(key_allowed[:, None], block_scores, -1e30)
    block_probs = jnp.exp(block_scores - lse_all)
    block_grad_probs = jnp.einsum(
        "sqhe,skhe->shqk", all_grad_mixed, value_rows, preferred_element_type=jnp.float32
    )
    block_grad_scores = (block_probs * (block_grad_probs - delta_all)).astype(jnp.bfloat16)
    own_keys = (
        jnp.einsum(
            "shqk,sqhe->skhe", block_grad_scores, all_queries, preferred_element_type=jnp.float32
        )
        * scale
    )
    own_values = jnp.einsum(
        "shqk,sqhe->skhe",
        block_probs.astype(jnp.bfloat16),
        all_grad_mixed,
        preferred_element_type=jnp.float32,
    )
    grad_joined = jnp.concatenate(
        [
            rotate(grad_queries, cos_table, -sin_table).reshape(rows, width),
            rotate(own_keys, cos_table, -sin_table).reshape(rows, width),
            own_values.reshape(rows, width),
        ],
        axis=1,
    ).astype(jnp.bfloat16)
    grad_joined_shift = jnp.sum(grad_joined.astype(jnp.float32), axis=0)
    grad_hidden_attn = contract_cols(grad_joined, qkv_back)
    unused_attn, attn_back = jax.vjp(norm_rows, inputs, gain_attn, shift_attn)
    grad_in_attn, grad_gain_attn, grad_shift_attn = attn_back(grad_hidden_attn)
    attn_columns = jnp.concatenate(
        [
            grad_gain_attn[:, None],
            grad_shift_attn[:, None],
            grad_joined_shift[: 2 * width].reshape(width, 2),
            grad_joined_shift[2 * width :][:, None],
            grad_out_shift[:, None],
        ],
        axis=1,
    )
    hidden_part = hidden_attn
    small_part = attn_columns
    attn_grads = lax.psum_scatter(
        jnp.concatenate(
            [contract_rows(hidden_part, grad_joined), contract_rows(mixed, cot_rows), small_part],
            axis=1,
        ),
        ("dp", "ctx"),
        scatter_dimension=0,
        tiled=True,
    )
    qkv_grad = attn_grads[:, : 3 * width]
    dense_grad = attn_grads[:, 3 * width : 4 * width]
    attn_tail = attn_grads[:, 4 * width :]
    mlp_back_set = fetch_mlp()
    expand_back, shrink_back, mlp_small_back = mlp_back_set
    gain_mlp, shift_mlp, expand_shift, shrink_shift = unpack_small(
        mlp_small_back, mlp_lengths, devices
    )
    unused_gelu, gelu_back = jax.vjp(gelu_exact, expanded)
    grad_act = contract_cols(cot_rows, shrink_back)
    grad_expanded = gelu_back(grad_act)[0].astype(jnp.bfloat16)
    grad_expand_shift = jnp.sum(grad_expanded.astype(jnp.float32), axis=0)
    grad_hidden_mlp = contract_cols(grad_expanded, expand_back)
    unused_mlp, mlp_back = jax.vjp(norm_rows, inputs, gain_mlp, shift_mlp)
    grad_in_mlp, grad_gain_mlp, grad_shift_mlp = mlp_back(grad_hidden_mlp)
    ratio = expand_shift.shape[0] // width
    mlp_columns = jnp.concatenate(
        [
            grad_gain_mlp[:, None],
            grad_shift_mlp[:, None],
            grad_expand_shift.reshape(width, ratio),
            grad_out_shift[:, None],
        ],
        axis=1,
    )
    ff_width = expand_back.shape[1]
    hidden_part = hidden_mlp
    small_part = mlp_columns
    expand_grads = lax.psum_scatter(
        jnp.concatenate([contract_rows(hidden_part, grad_expanded), small_part], axis=1),
        ("dp", "ctx"),
        scatter_dimension=0,
        tiled=True,
    )
    shrink_grad = lax.psum_scatter(
        contract_rows(activated, cot_rows), ("dp", "ctx"), scatter_dimension=0, tiled=True
    )
    expand_grad = expand_grads[:, :ff_width]
    mlp_tail = expand_grads[:, ff_width:]
    input_grad = (
        (cot_float + grad_in_attn + grad_in_mlp)
        .astype(jnp.bfloat16)
        .reshape(micro, seq_count, span, width)
    )
    return (
        layer_output,
        input_grad,
        qkv_grad,
        attn_tail[:, 2:4].reshape(-1),
        attn_tail[:, 4],
        dense_grad,
        attn_tail[:, 5],
        expand_grad,
        mlp_tail[:, 2 : 2 + ratio].reshape(-1),
        shrink_grad,
        mlp_tail[:, 2 + ratio],
        attn_tail[:, 0],
        attn_tail[:, 1],
        mlp_tail[:, 0],
        mlp_tail[:, 1],
    )


def low(values):
    return values.astype(jnp.bfloat16)


def small_params(packed_row):
    return lax.all_gather(packed_row, ("dp", "ctx"), axis=0, tiled=True)


def tensor_shards(
    layer_input,
    out_grad,
    prefix_len,
    qkv_weight,
    qkv_bias,
    dense_weight,
    dense_bias,
    expand_weight,
    expand_bias,
    shrink_weight,
    shrink_bias,
    attn_gain,
    attn_shift,
    mlp_gain,
    mlp_shift,
):
    dp_size = lax.axis_size("dp")
    ctx_size = lax.axis_size("ctx")
    devices = dp_size * ctx_size
    me = lax.axis_index("ctx")
    group = lax.axis_index("dp")
    micro, seq_count, span, width = layer_input.shape
    sequences = micro * seq_count
    tokens = sequences * SEQ
    row_share = qkv_weight.shape[0]
    scale = 1.0 / math.sqrt(HEAD)
    ff = expand_weight.shape[1]
    unit = shrink_weight.shape[0]
    lengths = tuple(
        member.shape[0]
        for member in (attn_gain, attn_shift, mlp_gain, mlp_shift, qkv_bias, dense_bias, expand_bias, shrink_bias)
    )
    packed = jnp.concatenate(
        [attn_gain, attn_shift, mlp_gain, mlp_shift, qkv_bias, dense_bias, expand_bias, shrink_bias]
    )
    own_x = layer_input.reshape(sequences, span, width)
    own_g = out_grad.reshape(sequences, span, width)
    x_all = lax.all_gather(own_x, "ctx", axis=1, tiled=True).reshape(tokens, width)
    g_all = lax.all_gather(own_g, "ctx", axis=1, tiled=True).reshape(tokens, width)
    columns = jnp.concatenate(
        [
            qkv_weight.reshape(row_share, 3, ctx_size, HEAD),
            expand_weight.reshape(row_share, dp_size, ctx_size, unit),
        ],
        axis=1,
    )
    columns = jnp.transpose(columns, (2, 0, 1, 3)).reshape(ctx_size * row_share, -1)
    columns = lax.all_to_all(columns, "ctx", split_axis=0, concat_axis=0, tiled=True)
    columns = lax.all_gather(columns, "dp", axis=0, tiled=True)
    qkv_part = columns[:, : 3 * HEAD]
    expand_part = columns[:, 3 * HEAD :]
    shrink_part = lax.all_gather(shrink_weight, "dp", axis=0, tiled=True)
    dense_full = lax.all_gather(dense_weight, ("dp", "ctx"), axis=0, tiled=True)
    dense_part = lax.dynamic_slice_in_dim(dense_full, me * HEAD, HEAD, 0)
    small = unpack_small(small_params(packed), lengths, devices)
    gain_attn, shift_attn, gain_mlp, shift_mlp, qkv_shift, dense_shift, expand_shift, shrink_shift = small
    qkv_shift = lax.dynamic_slice_in_dim(qkv_shift.reshape(3, ctx_size, HEAD), me, 1, 1).reshape(-1)
    expand_shift = lax.dynamic_slice_in_dim(
        expand_shift.reshape(dp_size, ctx_size, unit), me, 1, 1
    ).reshape(-1)

    inputs = x_all.astype(jnp.float32)
    row_mean = jnp.mean(inputs, axis=-1, keepdims=True)
    centered = inputs - row_mean
    spread = lax.rsqrt(jnp.mean(centered * centered, axis=-1, keepdims=True) + 1e-05)
    normal = centered * spread
    hidden_attn = low(normal * gain_attn + shift_attn)
    hidden_mlp = low(normal * gain_mlp + shift_mlp)

    cos_table, sin_table = rope_tables(jnp.arange(SEQ, dtype=jnp.float32))
    joined = jnp.dot(hidden_attn, qkv_part, preferred_element_type=jnp.float32) + qkv_shift
    joined = joined.reshape(sequences, SEQ, 3, HEAD)

    def turn(heads, sin_values):
        return rotate(heads[:, :, None, :], cos_table, sin_values)[:, :, 0]

    queries = low(turn(joined[:, :, 0], sin_table))
    key_rows = low(turn(joined[:, :, 1], sin_table))
    value_rows = low(joined[:, :, 2])
    positions = jnp.arange(SEQ, dtype=jnp.int32)
    prefix = prefix_len.reshape(sequences)
    allowed = (positions[None, :] <= positions[:, None])[None] | (
        positions[None, None, :] < prefix[:, None, None]
    )
    scores = jnp.einsum("sqe,ske->sqk", queries, key_rows, preferred_element_type=jnp.float32) * scale
    scores = jnp.where(allowed, scores, -1e30)
    expo = jnp.exp(scores - jnp.max(scores, axis=-1, keepdims=True))
    probs = expo / jnp.sum(expo, axis=-1, keepdims=True)
    probs_low = low(probs)
    mixed = low(
        jnp.einsum("sqk,ske->sqe", probs_low, value_rows, preferred_element_type=jnp.float32)
    ).reshape(tokens, HEAD)
    expanded = jnp.dot(hidden_mlp, expand_part, preferred_element_type=jnp.float32) + expand_shift
    activated = low(gelu_exact(expanded))
    features = jnp.concatenate([mixed, activated], axis=1)
    out_part = jnp.concatenate([dense_part, shrink_part], axis=0)
    partial = low(jnp.dot(features, out_part, preferred_element_type=jnp.float32))
    reduced = lax.psum_scatter(
        partial.reshape(sequences, SEQ, width), "ctx", scatter_dimension=1, tiled=True
    )
    layer_output = low(
        own_x.astype(jnp.float32) + reduced.astype(jnp.float32) + (dense_shift + shrink_shift)
    ).reshape(layer_input.shape)

    out_grads = low(contract_rows(features, g_all))
    grad_features = contract_cols(g_all, out_part)
    unused, gelu_back = jax.vjp(gelu_exact, expanded)
    grad_expanded = low(gelu_back(grad_features[:, HEAD:])[0])
    grad_mixed = low(grad_features[:, :HEAD]).reshape(sequences, SEQ, HEAD)
    shrink_grad = lax.psum_scatter(out_grads[HEAD:], "dp", scatter_dimension=0, tiled=True)
    dense_own = jnp.zeros((ctx_size, HEAD, width), jnp.bfloat16)
    dense_own = lax.dynamic_update_slice(dense_own, out_grads[:HEAD][None], (me, 0, 0))
    dense_grad = lax.psum_scatter(
        dense_own.reshape(ctx_size * HEAD, width), ("dp", "ctx"), scatter_dimension=0, tiled=True
    )
    expand_grads = low(contract_rows(hidden_mlp, grad_expanded))
    back_mlp = contract_cols(grad_expanded, expand_part)

    grad_probs = jnp.einsum("sqe,ske->sqk", grad_mixed, value_rows, preferred_element_type=jnp.float32)
    delta = jnp.sum(probs * grad_probs, axis=-1, keepdims=True)
    grad_scores = low(probs * (grad_probs - delta))
    grad_queries = (
        jnp.einsum("sqk,ske->sqe", grad_scores, key_rows, preferred_element_type=jnp.float32) * scale
    )
    grad_keys = (
        jnp.einsum("sqk,sqe->ske", grad_scores, queries, preferred_element_type=jnp.float32) * scale
    )
    grad_values = jnp.einsum("sqk,sqe->ske", probs_low, grad_mixed, preferred_element_type=jnp.float32)
    grad_joined = low(
        jnp.concatenate([turn(grad_queries, -sin_table), turn(grad_keys, -sin_table), grad_values], axis=-1)
    ).reshape(tokens, 3 * HEAD)
    qkv_grads = low(contract_rows(hidden_attn, grad_joined))
    back_attn = contract_cols(grad_joined, qkv_part)
    column_grads = jnp.concatenate([qkv_grads, expand_grads], axis=1)
    column_grads = lax.psum_scatter(column_grads, "dp", scatter_dimension=0, tiled=True)
    column_grads = lax.all_to_all(column_grads, "ctx", split_axis=0, concat_axis=0, tiled=True)
    column_grads = column_grads.reshape(ctx_size, row_share, 3 + dp_size, HEAD)
    column_grads = jnp.transpose(column_grads, (1, 2, 0, 3)).astype(jnp.float32)
    qkv_grad = column_grads[:, :3].reshape(row_share, 3 * width)
    expand_grad = column_grads[:, 3:].reshape(row_share, ff)

    combined = low(back_attn * gain_attn + back_mlp * gain_mlp)
    combined = lax.psum_scatter(
        combined.reshape(sequences, SEQ, width), "ctx", scatter_dimension=1, tiled=True
    ).astype(jnp.float32)
    own = own_x.astype(jnp.float32)
    own_center = own - jnp.mean(own, axis=-1, keepdims=True)
    own_spread = lax.rsqrt(jnp.mean(own_center * own_center, axis=-1, keepdims=True) + 1e-05)
    own_normal = own_center * own_spread
    share = own_spread * (
        combined
        - jnp.mean(combined, axis=-1, keepdims=True)
        - own_normal * jnp.mean(combined * own_normal, axis=-1, keepdims=True)
    )
    input_grad = low(own_g.astype(jnp.float32) + share).reshape(layer_input.shape)

    def place(values, parts):
        board = jnp.zeros((parts, ctx_size, values.shape[0] // parts), jnp.float32)
        board = lax.dynamic_update_slice(board, values.reshape(parts, 1, -1), (0, me, 0))
        return board.reshape(devices, -1)

    joined_sum = jnp.sum(grad_joined.astype(jnp.float32), axis=0)
    expand_sum = jnp.sum(grad_expanded.astype(jnp.float32), axis=0)
    out_sum = jnp.sum(own_g.astype(jnp.float32), axis=(0, 1))
    board = jnp.concatenate(
        [
            place(joined_sum[: 2 * HEAD], 2),
            place(joined_sum[2 * HEAD :], 1),
            out_sum.reshape(devices, -1),
            place(expand_sum, dp_size),
            jnp.sum(back_attn * normal, axis=0).reshape(devices, -1),
            jnp.sum(back_attn, axis=0).reshape(devices, -1),
            jnp.sum(back_mlp * normal, axis=0).reshape(devices, -1),
            jnp.sum(back_mlp, axis=0).reshape(devices, -1),
        ],
        axis=1,
    )
    tail = lax.psum_scatter(board, ("dp", "ctx"), scatter_dimension=0, tiled=True).reshape(-1)
    share_len = width // devices
    at = 0
    pieces = []
    for length in (2 * share_len, share_len, share_len, ff // devices, share_len, share_len, share_len, share_len):
        pieces.append(tail[at : at + length])
        at += length
    return (
        layer_output,
        input_grad,
        qkv_grad,
        pieces[0],
        pieces[1],
        dense_grad.astype(jnp.float32),
        pieces[2],
        expand_grad,
        pieces[3],
        shrink_grad.astype(jnp.float32),
        pieces[2],
        pieces[4],
        pieces[5],
        pieces[6],
        pieces[7],
    )


def solution(mesh):
    placed = (
        P(None, "dp", "ctx", None),
        P(None, "dp", "ctx", None),
        P(None, "dp"),
        P(("dp", "ctx"), None),
        P(("dp", "ctx")),
        P(("dp", "ctx"), None),
        P(("dp", "ctx")),
        P(("dp", "ctx"), None),
        P(("dp", "ctx")),
        P(("dp", "ctx"), None),
        P(("dp", "ctx")),
        P(("dp", "ctx")),
        P(("dp", "ctx")),
        P(("dp", "ctx")),
        P(("dp", "ctx")),
    )
    return jax.shard_map(
        tensor_shards if mesh.shape["ctx"] == HEADS else shards,
        mesh=mesh,
        in_specs=placed,
        out_specs=(
            P(None, "dp", "ctx", None),
            P(None, "dp", "ctx", None),
            P(("dp", "ctx"), None),
            P(("dp", "ctx")),
            P(("dp", "ctx")),
            P(("dp", "ctx"), None),
            P(("dp", "ctx")),
            P(("dp", "ctx"), None),
            P(("dp", "ctx")),
            P(("dp", "ctx"), None),
            P(("dp", "ctx")),
            P(("dp", "ctx")),
            P(("dp", "ctx")),
            P(("dp", "ctx")),
            P(("dp", "ctx")),
        ),
        check_vma=False,
    )
```

```python
import functools
import math

import jax
import jax.numpy as jnp
from jax import lax
from jax.experimental import pallas as pl
from jax.experimental.pallas import tpu as pltpu
from jax.sharding import PartitionSpec as P

HEADS = 8
HEAD = 256
ROT = 64
SEQ = 1024


def norm_rows(inputs, norm_gain, norm_bias):
    row_mean = jnp.mean(inputs, axis=-1, keepdims=True)
    centered = inputs - row_mean
    variance = jnp.mean(centered * centered, axis=-1, keepdims=True)
    return centered * lax.rsqrt(variance + 1e-05) * norm_gain + norm_bias


def gelu_exact(values):
    return jax.nn.gelu(values, approximate=False)


def rope_tables(positions):
    freqs = jnp.exp(jnp.arange(ROT // 2, dtype=jnp.float32) * (-2.0 * math.log(10000.0) / ROT))
    angles = positions[:, None] * freqs[None, :]
    return (jnp.cos(angles), jnp.sin(angles))


def rotate(heads, cos_table, sin_table):
    half_rot = ROT // 2
    lower = heads[..., :half_rot]
    upper = heads[..., half_rot:ROT]
    cos_wide = cos_table[:, None, :]
    sin_wide = sin_table[:, None, :]
    return jnp.concatenate(
        [
            lower * cos_wide - upper * sin_wide,
            upper * cos_wide + lower * sin_wide,
            heads[..., ROT:],
        ],
        axis=-1,
    )


def unpack_small(packed, lengths, devices):
    table_rows = packed.reshape(devices, -1)
    members = []
    offset = 0
    for length in lengths:
        members.append(table_rows[:, offset : offset + length].reshape(-1).astype(jnp.float32))
        offset = offset + length
    return members


def contract_rows(left_mat, right_mat):
    return lax.dot_general(
        left_mat, right_mat, (((0,), (0,)), ((), ())), preferred_element_type=jnp.float32
    )


def contract_cols(left_mat, right_mat):
    return lax.dot_general(
        left_mat, right_mat, (((1,), (1,)), ((), ())), preferred_element_type=jnp.float32
    )


def shards(
    layer_input,
    out_grad,
    prefix_len,
    qkv_weight,
    qkv_bias,
    dense_weight,
    dense_bias,
    expand_weight,
    expand_bias,
    shrink_weight,
    shrink_bias,
    attn_gain,
    attn_shift,
    mlp_gain,
    mlp_shift,
):
    devices = lax.axis_size("dp") * lax.axis_size("ctx")
    ctx_index = lax.axis_index("ctx")
    micro, seq_count, span, width = layer_input.shape
    sequences = micro * seq_count
    rows = sequences * span
    heads_shape = (sequences, span, HEADS, HEAD)
    scale = 1.0 / math.sqrt(HEAD)
    attn_lengths = (attn_gain.shape[0], attn_shift.shape[0], qkv_bias.shape[0], dense_bias.shape[0])
    mlp_lengths = (
        mlp_gain.shape[0],
        mlp_shift.shape[0],
        expand_bias.shape[0],
        shrink_bias.shape[0],
    )
    attn_packed = jnp.concatenate([attn_gain, attn_shift, qkv_bias, dense_bias])
    mlp_packed = jnp.concatenate([mlp_gain, mlp_shift, expand_bias, shrink_bias])

    def fetch_attn():
        return (
            lax.all_gather(qkv_weight, ("dp", "ctx"), axis=0, tiled=True),
            lax.all_gather(dense_weight, ("dp", "ctx"), axis=0, tiled=True),
            lax.all_gather(attn_packed, ("dp", "ctx"), axis=0, tiled=True),
        )

    def fetch_mlp():
        return (
            lax.all_gather(expand_weight, ("dp", "ctx"), axis=0, tiled=True),
            lax.all_gather(shrink_weight, ("dp", "ctx"), axis=0, tiled=True),
            lax.all_gather(mlp_packed, ("dp", "ctx"), axis=0, tiled=True),
        )

    local_pos = ctx_index * span + jnp.arange(span, dtype=jnp.int32)
    cos_table, sin_table = rope_tables(local_pos.astype(jnp.float32))
    key_pos = jnp.arange(SEQ, dtype=jnp.int32)
    causal = key_pos[None, :] <= local_pos[:, None]
    inputs = layer_input.astype(jnp.float32).reshape(rows, width)
    cot_rows = out_grad.reshape(rows, width)
    cot_float = cot_rows.astype(jnp.float32)
    prefix = prefix_len.reshape(sequences)
    allowed = (causal[None] | (key_pos[None, None, :] < prefix[:, None, None]))[:, None]
    attn_set = fetch_attn()
    qkv_full, dense_full, attn_small = attn_set
    gain_attn, shift_attn, joined_shift, dense_shift = unpack_small(
        attn_small, attn_lengths, devices
    )
    hidden_attn = norm_rows(inputs, gain_attn, shift_attn).astype(jnp.bfloat16)
    joined = jnp.dot(hidden_attn, qkv_full, preferred_element_type=jnp.float32) + joined_shift
    queries = rotate(joined[:, :width].reshape(heads_shape), cos_table, sin_table).astype(
        jnp.bfloat16
    )
    key_rows = rotate(
        joined[:, width : 2 * width].reshape(heads_shape), cos_table, sin_table
    ).astype(jnp.bfloat16)
    value_rows = joined[:, 2 * width :].reshape(heads_shape).astype(jnp.bfloat16)
    all_keys, all_values = (
        lax.all_gather(key_rows, "ctx", axis=1, tiled=True),
        lax.all_gather(value_rows, "ctx", axis=1, tiled=True),
    )
    scores = (
        jnp.einsum("sqhe,skhe->shqk", queries, all_keys, preferred_element_type=jnp.float32) * scale
    )
    scores = jnp.where(allowed, scores, -1e30)
    row_max = jnp.max(scores, axis=-1, keepdims=True)
    expo = jnp.exp(scores - row_max)
    row_total = jnp.sum(expo, axis=-1, keepdims=True)
    log_total = row_max + jnp.log(row_total)
    probs_low = (expo / row_total).astype(jnp.bfloat16)
    mixed = jnp.einsum("shqk,skhe->sqhe", probs_low, all_values, preferred_element_type=jnp.float32)
    mixed = mixed.reshape(rows, width).astype(jnp.bfloat16)
    attn_out = jnp.dot(mixed, dense_full, preferred_element_type=jnp.float32) + dense_shift
    mlp_set = fetch_mlp()
    expand_full, shrink_full, mlp_small = mlp_set
    gain_mlp, shift_mlp, expand_shift, shrink_shift = unpack_small(mlp_small, mlp_lengths, devices)
    hidden_mlp = norm_rows(inputs, gain_mlp, shift_mlp).astype(jnp.bfloat16)
    expanded = jnp.dot(hidden_mlp, expand_full, preferred_element_type=jnp.float32) + expand_shift
    activated = gelu_exact(expanded).astype(jnp.bfloat16)
    mlp_out = jnp.dot(activated, shrink_full, preferred_element_type=jnp.float32) + shrink_shift
    layer_output = (
        (inputs + attn_out + mlp_out).astype(jnp.bfloat16).reshape(micro, seq_count, span, width)
    )
    attn_back_set = fetch_attn()
    qkv_back, dense_back, attn_small_back = attn_back_set
    gain_attn, shift_attn, joined_shift, dense_shift = unpack_small(
        attn_small_back, attn_lengths, devices
    )
    grad_out_shift = jnp.sum(cot_float, axis=0)
    grad_mixed = contract_cols(cot_rows, dense_back).astype(jnp.bfloat16).reshape(heads_shape)
    again = (
        jnp.einsum("sqhe,skhe->shqk", queries, all_keys, preferred_element_type=jnp.float32) * scale
    )
    again = jnp.where(allowed, again, -1e30)
    probs = jnp.exp(again - log_total)
    grad_probs = jnp.einsum(
        "sqhe,skhe->shqk", grad_mixed, all_values, preferred_element_type=jnp.float32
    )
    delta = jnp.sum(probs * grad_probs, axis=-1, keepdims=True)
    grad_scores = (probs * (grad_probs - delta)).astype(jnp.bfloat16)
    grad_queries = (
        jnp.einsum("shqk,skhe->sqhe", grad_scores, all_keys, preferred_element_type=jnp.float32)
        * scale
    )
    all_queries, all_grad_mixed = (
        lax.all_gather(queries, "ctx", axis=1, tiled=True),
        lax.all_gather(grad_mixed, "ctx", axis=1, tiled=True),
    )
    stat_lse = jnp.transpose(log_total[..., 0], (0, 2, 1))
    stat_delta = jnp.transpose(delta[..., 0], (0, 2, 1))
    lse_all, delta_all = (
        lax.all_gather(stat_lse, "ctx", axis=1, tiled=True),
        lax.all_gather(stat_delta, "ctx", axis=1, tiled=True),
    )
    lse_all = jnp.transpose(lse_all, (0, 2, 1))[..., None]
    delta_all = jnp.transpose(delta_all, (0, 2, 1))[..., None]
    key_allowed = (local_pos[None, :] <= key_pos[:, None])[None] | (
        local_pos[None, None, :] < prefix[:, None, None]
    )
    block_scores = (
        jnp.einsum("sqhe,skhe->shqk", all_queries, key_rows, preferred_element_type=jnp.float32)
        * scale
    )
    block_scores = jnp.where(key_allowed[:, None], block_scores, -1e30)
    block_probs = jnp.exp(block_scores - lse_all)
    block_grad_probs = jnp.einsum(
        "sqhe,skhe->shqk", all_grad_mixed, value_rows, preferred_element_type=jnp.float32
    )
    block_grad_scores = (block_probs * (block_grad_probs - delta_all)).astype(jnp.bfloat16)
    own_keys = (
        jnp.einsum(
            "shqk,sqhe->skhe", block_grad_scores, all_queries, preferred_element_type=jnp.float32
        )
        * scale
    )
    own_values = jnp.einsum(
        "shqk,sqhe->skhe",
        block_probs.astype(jnp.bfloat16),
        all_grad_mixed,
        preferred_element_type=jnp.float32,
    )
    grad_joined = jnp.concatenate(
        [
            rotate(grad_queries, cos_table, -sin_table).reshape(rows, width),
            rotate(own_keys, cos_table, -sin_table).reshape(rows, width),
            own_values.reshape(rows, width),
        ],
        axis=1,
    ).astype(jnp.bfloat16)
    grad_joined_shift = jnp.sum(grad_joined.astype(jnp.float32), axis=0)
    grad_hidden_attn = contract_cols(grad_joined, qkv_back)
    unused_attn, attn_back = jax.vjp(norm_rows, inputs, gain_attn, shift_attn)
    grad_in_attn, grad_gain_attn, grad_shift_attn = attn_back(grad_hidden_attn)
    attn_columns = jnp.concatenate(
        [
            grad_gain_attn[:, None],
            grad_shift_attn[:, None],
            grad_joined_shift[: 2 * width].reshape(width, 2),
            grad_joined_shift[2 * width :][:, None],
            grad_out_shift[:, None],
        ],
        axis=1,
    )
    hidden_part = hidden_attn
    small_part = attn_columns
    attn_grads = lax.psum_scatter(
        jnp.concatenate(
            [contract_rows(hidden_part, grad_joined), contract_rows(mixed, cot_rows), small_part],
            axis=1,
        ),
        ("dp", "ctx"),
        scatter_dimension=0,
        tiled=True,
    )
    qkv_grad = attn_grads[:, : 3 * width]
    dense_grad = attn_grads[:, 3 * width : 4 * width]
    attn_tail = attn_grads[:, 4 * width :]
    mlp_back_set = fetch_mlp()
    expand_back, shrink_back, mlp_small_back = mlp_back_set
    gain_mlp, shift_mlp, expand_shift, shrink_shift = unpack_small(
        mlp_small_back, mlp_lengths, devices
    )
    unused_gelu, gelu_back = jax.vjp(gelu_exact, expanded)
    grad_act = contract_cols(cot_rows, shrink_back)
    grad_expanded = gelu_back(grad_act)[0].astype(jnp.bfloat16)
    grad_expand_shift = jnp.sum(grad_expanded.astype(jnp.float32), axis=0)
    grad_hidden_mlp = contract_cols(grad_expanded, expand_back)
    unused_mlp, mlp_back = jax.vjp(norm_rows, inputs, gain_mlp, shift_mlp)
    grad_in_mlp, grad_gain_mlp, grad_shift_mlp = mlp_back(grad_hidden_mlp)
    ratio = expand_shift.shape[0] // width
    mlp_columns = jnp.concatenate(
        [
            grad_gain_mlp[:, None],
            grad_shift_mlp[:, None],
            grad_expand_shift.reshape(width, ratio),
            grad_out_shift[:, None],
        ],
        axis=1,
    )
    ff_width = expand_back.shape[1]
    hidden_part = hidden_mlp
    small_part = mlp_columns
    expand_grads = lax.psum_scatter(
        jnp.concatenate([contract_rows(hidden_part, grad_expanded), small_part], axis=1),
        ("dp", "ctx"),
        scatter_dimension=0,
        tiled=True,
    )
    shrink_grad = lax.psum_scatter(
        contract_rows(activated, cot_rows), ("dp", "ctx"), scatter_dimension=0, tiled=True
    )
    expand_grad = expand_grads[:, :ff_width]
    mlp_tail = expand_grads[:, ff_width:]
    input_grad = (
        (cot_float + grad_in_attn + grad_in_mlp)
        .astype(jnp.bfloat16)
        .reshape(micro, seq_count, span, width)
    )
    return (
        layer_output,
        input_grad,
        qkv_grad,
        attn_tail[:, 2:4].reshape(-1),
        attn_tail[:, 4],
        dense_grad,
        attn_tail[:, 5],
        expand_grad,
        mlp_tail[:, 2 : 2 + ratio].reshape(-1),
        shrink_grad,
        mlp_tail[:, 2 + ratio],
        attn_tail[:, 0],
        attn_tail[:, 1],
        mlp_tail[:, 0],
        mlp_tail[:, 1],
    )


def low(values):
    return values.astype(jnp.bfloat16)


MESH_ID = pl.DeviceIdType.MESH


def remote(src, dst, send_sem, recv_sem, dp, ctx):
    return pltpu.make_async_remote_copy(
        src_ref=src,
        dst_ref=dst,
        send_sem=send_sem,
        recv_sem=recv_sem,
        device_id=(dp, ctx),
        device_id_type=MESH_ID,
    )


def greet_all(dp, ctx, dp_size, ctx_size):
    barrier = pltpu.get_barrier_semaphore()
    devices = dp_size * ctx_size
    me = dp * ctx_size + ctx

    def greet(step, carry):
        other = lax.rem(me + step, devices)
        pl.semaphore_signal(
            barrier, inc=1, device_id=(other // ctx_size, lax.rem(other, ctx_size)), device_id_type=MESH_ID
        )
        return carry

    lax.fori_loop(1, devices, greet, 0)
    pl.semaphore_wait(barrier, devices - 1)


def gather_kernel(
    dp_size,
    ctx_size,
    x,
    qkv,
    expand,
    dense,
    shrink,
    packed,
    x_all,
    panels,
    out_w,
    small,
    local_sem,
    small_sem,
    block_send,
    block_recv,
    core_send,
    core_recv,
    panel_send,
    panel_recv,
    share_send,
    share_recv,
    pass_send,
    pass_recv,
):
    d = lax.axis_index("dp")
    c = lax.axis_index("ctx")
    z = c // 2
    sibling = c + 1 - 2 * lax.rem(c, 2)
    x_mate = d + 1 - 2 * lax.rem(d, 2)
    y_mate = lax.rem(d + 2, 4)
    micro, span = x.shape[0], x.shape[1]
    devices = dp_size * ctx_size
    me = d * ctx_size + c
    rows = qkv.shape[0]
    unit = shrink.shape[0]
    levels = ctx_size // 2
    panel_rows = ctx_size * rows
    n_panels = 3 + dp_size

    greet_all(d, c, dp_size, ctx_size)

    def column_block(panel, target):
        if panel < 3:
            start = panel * (qkv.shape[1] // 3) + target * HEAD
            return qkv.at[:, pl.ds(pl.multiple_of(start, HEAD), HEAD)]
        start = (panel - 3) * ctx_size * unit + target * unit
        return expand.at[:, pl.ds(pl.multiple_of(start, HEAD), HEAD)]

    own_rows = pl.ds(pl.multiple_of((d * ctx_size + c) * rows, rows), rows)

    for panel in range(n_panels):
        pltpu.make_async_copy(
            column_block(panel, c), panels.at[panel, own_rows], local_sem.at[panel]
        ).start()

        def push(step, carry, panel=panel):
            target = lax.rem(c + step, ctx_size)
            remote(
                column_block(panel, target),
                panels.at[panel, own_rows],
                panel_send.at[panel],
                panel_recv.at[panel],
                d,
                target,
            ).start()
            return carry

        lax.fori_loop(1, ctx_size, push, 0)

    def shrink_rows(owner, offset, count):
        return out_w.at[pl.ds(pl.multiple_of(HEAD + owner * unit + offset, 16), count)]

    shrink_local = pltpu.make_async_copy(shrink, shrink_rows(d, 0, unit), local_sem.at[n_panels])
    shrink_local.start()
    for way, mate in ((0, x_mate), (1, y_mate)):
        remote(
            shrink, shrink_rows(d, 0, unit), share_send.at[n_panels, way], share_recv.at[n_panels, way], mate, c
        ).start()

    per_head = HEAD // rows
    head_of = (d * ctx_size + c) // per_head
    dense_rows = pl.ds(pl.multiple_of(lax.rem(c, per_head) * rows, rows), rows)
    dense_out = remote(dense, out_w.at[dense_rows], panel_send.at[n_panels], panel_recv.at[n_panels], d, head_of)
    dense_own = pltpu.make_async_copy(dense, out_w.at[dense_rows], local_sem.at[n_panels + 1])
    stays = head_of == c

    @pl.when(stays)
    def _():
        dense_own.start()

    @pl.when(jnp.logical_not(stays))
    def _():
        dense_out.start()

    def block(origin, m):
        return x_all.at[m, pl.ds(pl.multiple_of(origin * span, span), span)]

    x_local = []
    for m in range(micro):
        copy = pltpu.make_async_copy(x.at[m], block(c, m), local_sem.at[n_panels + 2 + m])
        copy.start()
        x_local.append(copy)

    def chain(way, hop, m):
        step = 2 if way == 0 else -2
        origin = c - step * hop
        src = x.at[m] if hop == 0 else block(origin, m)
        exists = jnp.logical_and(z >= hop, z <= levels - 2) if way == 0 else jnp.logical_and(
            z + hop <= levels - 1, z >= 1
        )
        copy = remote(src, block(origin, m), block_send.at[way, hop, m], block_recv.at[way, hop, m], d, c + step)
        return exists, copy

    def arrives(way, hop):
        return z >= hop + 1 if way == 0 else z + hop + 1 <= levels - 1

    def core_copy(slot, origin, m):
        src = x.at[m] if slot == 0 else block(origin, m)
        return remote(src, block(origin, m), core_send.at[slot, m], core_recv.at[slot, m], d, sibling)

    for m in range(micro):
        core_copy(0, c, m).start()
        for way in range(2):
            exists, copy = chain(way, 0, m)

            @pl.when(exists)
            def _(copy=copy):
                copy.start()

    small_copy = pltpu.make_async_copy(packed, small.at[me], local_sem.at[n_panels + 2 + micro])
    small_copy.start()

    def push_small(step, carry):
        other = lax.rem(me + step, devices)
        remote(
            packed,
            small.at[me],
            small_sem.at[0],
            small_sem.at[1],
            other // ctx_size,
            lax.rem(other, ctx_size),
        ).start()
        return carry

    lax.fori_loop(1, devices, push_small, 0)

    def slot_of(way, hop):
        return 1 + way * (levels - 1) + hop

    def hop_step(hop):
        for m in range(micro):
            for way in range(2):
                step = 2 if way == 0 else -2

                @pl.when(arrives(way, hop))
                def _(way=way, m=m, step=step):
                    origin = c - step * (hop + 1)
                    remote(
                        block(origin, m), block(origin, m), block_send.at[way, hop, m], block_recv.at[way, hop, m], d, c - step
                    ).wait_recv()
                    core_copy(slot_of(way, hop), origin, m).start()

                if hop + 1 <= levels - 2:
                    exists, copy = chain(way, hop + 1, m)

                    @pl.when(exists)
                    def _(copy=copy):
                        copy.start()

    def group_rows(owner, offset, count):
        return pl.ds(pl.multiple_of(owner * panel_rows + offset, 16), count)

    def panel_share(panel, way, mate):
        view = panels.at[panel, group_rows(d, 0, panel_rows)]
        return remote(view, view, share_send.at[panel, way], share_recv.at[panel, way], mate, c)

    def panel_step(panel):
        pltpu.make_async_copy(column_block(panel, c), panels.at[panel, own_rows], local_sem.at[panel]).wait()
        whole = panels.at[panel, group_rows(d, 0, (ctx_size - 1) * rows)]
        remote(whole, whole, panel_send.at[panel], panel_recv.at[panel], d, sibling).wait_recv()
        panel_share(panel, 0, x_mate).start()
        panel_share(panel, 1, y_mate).start()

    half = panel_rows // 2

    def panel_pass(panel, way):
        owner, mate = ((x_mate, y_mate), (y_mate, x_mate))[way]
        view = panels.at[panel, group_rows(owner, way * half, half)]
        return remote(view, view, pass_send.at[panel, way], pass_recv.at[panel, way], mate, c)

    def panel_forward(panel):
        for way, owner in ((0, x_mate), (1, y_mate)):
            view = panels.at[panel, group_rows(owner, 0, panel_rows)]
            remote(view, view, share_send.at[panel, way], share_recv.at[panel, way], owner, c).wait_recv()
            panel_pass(panel, way).start()

    def shrink_share_wait(way, owner):
        view = shrink_rows(owner, 0, unit)
        remote(view, view, share_send.at[n_panels, way], share_recv.at[n_panels, way], owner, c).wait_recv()

    def shrink_pass(way):
        owner, mate = ((x_mate, y_mate), (y_mate, x_mate))[way]
        view = shrink_rows(owner, way * (unit // 2), unit // 2)
        return remote(view, view, pass_send.at[n_panels, way], pass_recv.at[n_panels, way], mate, c)

    source = c // (ctx_size // dp_size)
    at_source = d == source
    from_x = x_mate == source
    from_y = y_mate == source
    head_rows = out_w.at[pl.ds(0, HEAD)]
    half_head = HEAD // 2

    def dense_share(way, mate):
        return remote(head_rows, head_rows, share_send.at[n_panels + 1, way], share_recv.at[n_panels + 1, way], mate, c)

    def dense_pass(way, mate):
        view = out_w.at[pl.ds(way * half_head, half_head)]
        return remote(view, view, pass_send.at[n_panels + 1, way], pass_recv.at[n_panels + 1, way], mate, c)

    owns_share = jnp.logical_and(at_source, stays)

    def dense_gather_step():
        @pl.when(owns_share)
        def _():
            dense_own.wait()
            view = out_w.at[pl.ds(0, (per_head - 1) * rows)]
            remote(view, view, panel_send.at[n_panels], panel_recv.at[n_panels], d, sibling).wait_recv()

        @pl.when(jnp.logical_and(at_source, jnp.logical_not(stays)))
        def _():
            remote(head_rows, head_rows, panel_send.at[n_panels], panel_recv.at[n_panels], d, sibling).wait_recv()

        @pl.when(at_source)
        def _():
            dense_share(0, x_mate).start()
            dense_share(1, y_mate).start()

    def dense_forward_step():
        @pl.when(from_x)
        def _():
            dense_share(0, x_mate).wait_recv()
            dense_pass(0, y_mate).start()

        @pl.when(from_y)
        def _():
            dense_share(1, y_mate).wait_recv()
            dense_pass(1, x_mate).start()

    across = jnp.logical_not(jnp.logical_or(at_source, jnp.logical_or(from_x, from_y)))

    for panel in range(3):
        panel_step(panel)
    shrink_share_wait(0, x_mate)
    shrink_pass(0).start()
    shrink_share_wait(1, y_mate)
    shrink_pass(1).start()
    dense_gather_step()
    hop_step(0)
    for panel in range(3, n_panels):
        panel_step(panel)
        panel_forward(panel - 3)
    hop_step(1)
    dense_forward_step()
    for panel in range(n_panels - 3, n_panels):
        panel_forward(panel)
    for hop in range(2, levels - 1):
        hop_step(hop)

    for panel in range(n_panels):
        for way, mate in ((0, x_mate), (1, y_mate)):
            panel_share(panel, way, mate).wait_send()
            panel_pass(panel, way).wait_send()
        for way in range(2):
            diagonal = 3 - d
            view = panels.at[panel, group_rows(diagonal, way * half, half)]
            remote(view, view, pass_send.at[panel, way], pass_recv.at[panel, way], x_mate, c).wait_recv()
        whole = panels.at[panel, group_rows(d, 0, (ctx_size - 1) * rows)]
        remote(whole, whole, panel_send.at[panel], panel_recv.at[panel], x_mate, c).wait_send()
    shrink_local.wait()
    for way in range(2):
        mate = (x_mate, y_mate)[way]
        remote(
            shrink, shrink_rows(d, 0, unit), share_send.at[n_panels, way], share_recv.at[n_panels, way], mate, c
        ).wait_send()
        shrink_pass(way).wait_send()
        view = shrink_rows(3 - d, way * (unit // 2), unit // 2)
        remote(view, view, pass_send.at[n_panels, way], pass_recv.at[n_panels, way], mate, c).wait_recv()

    @pl.when(jnp.logical_not(stays))
    def _():
        dense_out.wait_send()

    @pl.when(at_source)
    def _():
        dense_share(0, x_mate).wait_send()
        dense_share(1, y_mate).wait_send()

    @pl.when(from_x)
    def _():
        dense_pass(0, y_mate).wait_send()

    @pl.when(from_y)
    def _():
        dense_pass(1, x_mate).wait_send()

    @pl.when(across)
    def _():
        dense_pass(0, y_mate).wait_recv()
        dense_pass(1, x_mate).wait_recv()

    for m in range(micro):
        x_local[m].wait()
        core_copy(0, c, m).wait_send()
        core_copy(0, sibling, m).wait_recv()
        for way in range(2):
            step = 2 if way == 0 else -2
            for hop in range(levels - 1):
                exists, copy = chain(way, hop, m)

                @pl.when(exists)
                def _(copy=copy):
                    copy.wait_send()

                @pl.when(arrives(way, hop))
                def _(way=way, hop=hop, m=m, step=step):
                    slot = slot_of(way, hop)
                    core_copy(slot, c - step * (hop + 1), m).wait_send()
                    core_copy(slot, sibling - step * (hop + 1), m).wait_recv()

    small_copy.wait()
    rest = small.at[pl.ds(0, devices - 1)]
    remote(rest, rest, small_sem.at[0], small_sem.at[1], d, sibling).wait()


def gather_call(dp_size, ctx_size, x, qkv, expand, dense, shrink, packed):
    micro, span, width = x.shape
    rows = qkv.shape[0]
    n_panels = 3 + dp_size
    levels = ctx_size // 2
    devices = dp_size * ctx_size
    dma = pltpu.SemaphoreType.DMA
    out_shape = (
        jax.ShapeDtypeStruct((micro, ctx_size * span, width), x.dtype),
        jax.ShapeDtypeStruct((n_panels, devices * rows, HEAD), x.dtype),
        jax.ShapeDtypeStruct((HEAD + dp_size * shrink.shape[0], width), x.dtype),
        jax.ShapeDtypeStruct((devices,) + packed.shape, x.dtype),
    )
    anywhere = pl.BlockSpec(memory_space=pl.ANY)
    return pl.pallas_call(
        functools.partial(gather_kernel, dp_size, ctx_size),
        out_shape=out_shape,
        in_specs=[anywhere] * 6,
        out_specs=(anywhere,) * 4,
        scratch_shapes=[
            dma((n_panels + 3 + micro,)),
            dma((2,)),
            dma((2, levels - 1, micro)),
            dma((2, levels - 1, micro)),
            dma((2 * levels - 1, micro)),
            dma((2 * levels - 1, micro)),
            dma((n_panels + 1,)),
            dma((n_panels + 1,)),
            dma((n_panels + 2, 2)),
            dma((n_panels + 2, 2)),
            dma((n_panels + 2, 2)),
            dma((n_panels + 2, 2)),
        ],
        compiler_params=pltpu.CompilerParams(collective_id=1, has_side_effects=True),
        name="gather_all",
    )(x, qkv, expand, dense, shrink, packed)


def tensor_shards(
    layer_input,
    out_grad,
    prefix_len,
    qkv_weight,
    qkv_bias,
    dense_weight,
    dense_bias,
    expand_weight,
    expand_bias,
    shrink_weight,
    shrink_bias,
    attn_gain,
    attn_shift,
    mlp_gain,
    mlp_shift,
):
    dp_size = lax.axis_size("dp")
    ctx_size = lax.axis_size("ctx")
    devices = dp_size * ctx_size
    me = lax.axis_index("ctx")
    group = lax.axis_index("dp")
    micro, seq_count, span, width = layer_input.shape
    sequences = micro * seq_count
    tokens = sequences * SEQ
    row_share = qkv_weight.shape[0]
    scale = 1.0 / math.sqrt(HEAD)
    ff = expand_weight.shape[1]
    unit = shrink_weight.shape[0]
    lengths = tuple(
        member.shape[0]
        for member in (attn_gain, attn_shift, mlp_gain, mlp_shift, qkv_bias, dense_bias, expand_bias, shrink_bias)
    )
    packed = jnp.concatenate(
        [attn_gain, attn_shift, mlp_gain, mlp_shift, qkv_bias, dense_bias, expand_bias, shrink_bias]
    )
    own_x = layer_input.reshape(sequences, span, width)
    own_g = out_grad.reshape(sequences, span, width)
    g_all = lax.all_gather(own_g, "ctx", axis=1, tiled=True).reshape(tokens, width)
    count = packed.shape[0]
    packed = jnp.pad(packed, (0, -count % 2048)).reshape(-1, 128)
    x_all, panels, out_part, small = gather_call(
        dp_size, ctx_size, own_x, qkv_weight, expand_weight, dense_weight, shrink_weight, packed
    )
    x_all = x_all.reshape(tokens, width)
    qkv_part = panels[:3]
    expand_part = panels[3:]
    small = unpack_small(small.reshape(devices, -1)[:, :count], lengths, devices)
    gain_attn, shift_attn, gain_mlp, shift_mlp, qkv_shift, dense_shift, expand_shift, shrink_shift = small
    qkv_shift = lax.dynamic_slice_in_dim(qkv_shift.reshape(3, ctx_size, HEAD), me, 1, 1).reshape(-1)
    expand_shift = lax.dynamic_slice_in_dim(
        expand_shift.reshape(dp_size, ctx_size, unit), me, 1, 1
    ).reshape(-1)

    inputs = x_all.astype(jnp.float32)
    row_mean = jnp.mean(inputs, axis=-1, keepdims=True)
    centered = inputs - row_mean
    spread = lax.rsqrt(jnp.mean(centered * centered, axis=-1, keepdims=True) + 1e-05)
    normal = centered * spread
    hidden_attn = low(normal * gain_attn + shift_attn)
    hidden_mlp = low(normal * gain_mlp + shift_mlp)

    cos_table, sin_table = rope_tables(jnp.arange(SEQ, dtype=jnp.float32))
    joined = jnp.einsum("td,pde->tpe", hidden_attn, qkv_part, preferred_element_type=jnp.float32)
    joined = joined.reshape(tokens, -1) + qkv_shift
    joined = joined.reshape(sequences, SEQ, 3, HEAD)

    def turn(heads, sin_values):
        return rotate(heads[:, :, None, :], cos_table, sin_values)[:, :, 0]

    queries = low(turn(joined[:, :, 0], sin_table))
    key_rows = low(turn(joined[:, :, 1], sin_table))
    value_rows = low(joined[:, :, 2])
    positions = jnp.arange(SEQ, dtype=jnp.int32)
    prefix = prefix_len.reshape(sequences)
    allowed = (positions[None, :] <= positions[:, None])[None] | (
        positions[None, None, :] < prefix[:, None, None]
    )
    scores = jnp.einsum("sqe,ske->sqk", queries, key_rows, preferred_element_type=jnp.float32) * scale
    scores = jnp.where(allowed, scores, -1e30)
    expo = jnp.exp(scores - jnp.max(scores, axis=-1, keepdims=True))
    probs = expo / jnp.sum(expo, axis=-1, keepdims=True)
    probs_low = low(probs)
    mixed = low(
        jnp.einsum("sqk,ske->sqe", probs_low, value_rows, preferred_element_type=jnp.float32)
    ).reshape(tokens, HEAD)
    expanded = jnp.einsum("td,pde->tpe", hidden_mlp, expand_part, preferred_element_type=jnp.float32)
    expanded = expanded.reshape(tokens, -1) + expand_shift
    activated = low(gelu_exact(expanded))
    features = jnp.concatenate([mixed, activated], axis=1)
    partial = low(jnp.dot(features, out_part, preferred_element_type=jnp.float32))
    reduced = lax.psum_scatter(
        partial.reshape(sequences, SEQ, width), "ctx", scatter_dimension=1, tiled=True
    )
    layer_output = low(
        own_x.astype(jnp.float32) + reduced.astype(jnp.float32) + (dense_shift + shrink_shift)
    ).reshape(layer_input.shape)

    out_grads = low(contract_rows(features, g_all))
    grad_features = contract_cols(g_all, out_part)
    unused, gelu_back = jax.vjp(gelu_exact, expanded)
    grad_expanded = low(gelu_back(grad_features[:, HEAD:])[0])
    grad_mixed = low(grad_features[:, :HEAD]).reshape(sequences, SEQ, HEAD)
    shrink_grad = lax.psum_scatter(out_grads[HEAD:], "dp", scatter_dimension=0, tiled=True)
    dense_own = jnp.zeros((ctx_size, HEAD, width), jnp.bfloat16)
    dense_own = lax.dynamic_update_slice(dense_own, out_grads[:HEAD][None], (me, 0, 0))
    dense_grad = lax.psum_scatter(
        dense_own.reshape(ctx_size * HEAD, width), ("dp", "ctx"), scatter_dimension=0, tiled=True
    )
    expand_grads = low(contract_rows(hidden_mlp, grad_expanded))
    back_mlp = jnp.einsum(
        "tpe,pde->td",
        grad_expanded.reshape(tokens, -1, HEAD),
        expand_part,
        preferred_element_type=jnp.float32,
    )

    grad_probs = jnp.einsum("sqe,ske->sqk", grad_mixed, value_rows, preferred_element_type=jnp.float32)
    delta = jnp.sum(probs * grad_probs, axis=-1, keepdims=True)
    grad_scores = low(probs * (grad_probs - delta))
    grad_queries = (
        jnp.einsum("sqk,ske->sqe", grad_scores, key_rows, preferred_element_type=jnp.float32) * scale
    )
    grad_keys = (
        jnp.einsum("sqk,sqe->ske", grad_scores, queries, preferred_element_type=jnp.float32) * scale
    )
    grad_values = jnp.einsum("sqk,sqe->ske", probs_low, grad_mixed, preferred_element_type=jnp.float32)
    grad_joined = low(
        jnp.concatenate([turn(grad_queries, -sin_table), turn(grad_keys, -sin_table), grad_values], axis=-1)
    ).reshape(tokens, 3 * HEAD)
    qkv_grads = low(contract_rows(hidden_attn, grad_joined))
    back_attn = jnp.einsum(
        "tpe,pde->td",
        grad_joined.reshape(tokens, -1, HEAD),
        qkv_part,
        preferred_element_type=jnp.float32,
    )
    column_grads = jnp.concatenate([qkv_grads, expand_grads], axis=1)
    column_grads = lax.psum_scatter(column_grads, "dp", scatter_dimension=0, tiled=True)
    column_grads = lax.all_to_all(column_grads, "ctx", split_axis=0, concat_axis=0, tiled=True)
    column_grads = column_grads.reshape(ctx_size, row_share, 3 + dp_size, HEAD)
    column_grads = jnp.transpose(column_grads, (1, 2, 0, 3)).astype(jnp.float32)
    qkv_grad = column_grads[:, :3].reshape(row_share, 3 * width)
    expand_grad = column_grads[:, 3:].reshape(row_share, ff)

    combined = low(back_attn * gain_attn + back_mlp * gain_mlp)
    combined = lax.psum_scatter(
        combined.reshape(sequences, SEQ, width), "ctx", scatter_dimension=1, tiled=True
    ).astype(jnp.float32)
    own = own_x.astype(jnp.float32)
    own_center = own - jnp.mean(own, axis=-1, keepdims=True)
    own_spread = lax.rsqrt(jnp.mean(own_center * own_center, axis=-1, keepdims=True) + 1e-05)
    own_normal = own_center * own_spread
    share = own_spread * (
        combined
        - jnp.mean(combined, axis=-1, keepdims=True)
        - own_normal * jnp.mean(combined * own_normal, axis=-1, keepdims=True)
    )
    input_grad = low(own_g.astype(jnp.float32) + share).reshape(layer_input.shape)

    def place(values, parts):
        board = jnp.zeros((parts, ctx_size, values.shape[0] // parts), jnp.float32)
        board = lax.dynamic_update_slice(board, values.reshape(parts, 1, -1), (0, me, 0))
        return board.reshape(devices, -1)

    joined_sum = jnp.sum(grad_joined.astype(jnp.float32), axis=0)
    expand_sum = jnp.sum(grad_expanded.astype(jnp.float32), axis=0)
    out_sum = jnp.sum(own_g.astype(jnp.float32), axis=(0, 1))
    board = jnp.concatenate(
        [
            place(joined_sum[: 2 * HEAD], 2),
            place(joined_sum[2 * HEAD :], 1),
            out_sum.reshape(devices, -1),
            place(expand_sum, dp_size),
            jnp.sum(back_attn * normal, axis=0).reshape(devices, -1),
            jnp.sum(back_attn, axis=0).reshape(devices, -1),
            jnp.sum(back_mlp * normal, axis=0).reshape(devices, -1),
            jnp.sum(back_mlp, axis=0).reshape(devices, -1),
        ],
        axis=1,
    )
    tail = lax.psum_scatter(board, ("dp", "ctx"), scatter_dimension=0, tiled=True).reshape(-1)
    share_len = width // devices
    at = 0
    pieces = []
    for length in (2 * share_len, share_len, share_len, ff // devices, share_len, share_len, share_len, share_len):
        pieces.append(tail[at : at + length])
        at += length
    return (
        layer_output,
        input_grad,
        qkv_grad,
        pieces[0],
        pieces[1],
        dense_grad.astype(jnp.float32),
        pieces[2],
        expand_grad,
        pieces[3],
        shrink_grad.astype(jnp.float32),
        pieces[2],
        pieces[4],
        pieces[5],
        pieces[6],
        pieces[7],
    )


def solution(mesh):
    placed = (
        P(None, "dp", "ctx", None),
        P(None, "dp", "ctx", None),
        P(None, "dp"),
        P(("dp", "ctx"), None),
        P(("dp", "ctx")),
        P(("dp", "ctx"), None),
        P(("dp", "ctx")),
        P(("dp", "ctx"), None),
        P(("dp", "ctx")),
        P(("dp", "ctx"), None),
        P(("dp", "ctx")),
        P(("dp", "ctx")),
        P(("dp", "ctx")),
        P(("dp", "ctx")),
        P(("dp", "ctx")),
    )
    return jax.shard_map(
        tensor_shards if (mesh.shape["dp"], mesh.shape["ctx"]) == (4, HEADS) else shards,
        mesh=mesh,
        in_specs=placed,
        out_specs=(
            P(None, "dp", "ctx", None),
            P(None, "dp", "ctx", None),
            P(("dp", "ctx"), None),
            P(("dp", "ctx")),
            P(("dp", "ctx")),
            P(("dp", "ctx"), None),
            P(("dp", "ctx")),
            P(("dp", "ctx"), None),
            P(("dp", "ctx")),
            P(("dp", "ctx"), None),
            P(("dp", "ctx")),
            P(("dp", "ctx")),
            P(("dp", "ctx")),
            P(("dp", "ctx")),
            P(("dp", "ctx")),
        ),
        check_vma=False,
    )
```

```python
import functools
import math

import jax
import jax.numpy as jnp
from jax import lax
from jax.experimental import pallas as pl
from jax.experimental.pallas import tpu as pltpu
from jax.sharding import PartitionSpec as P

HEADS = 8
HEAD = 256
ROT = 64
SEQ = 1024


def norm_rows(inputs, norm_gain, norm_bias):
    row_mean = jnp.mean(inputs, axis=-1, keepdims=True)
    centered = inputs - row_mean
    variance = jnp.mean(centered * centered, axis=-1, keepdims=True)
    return centered * lax.rsqrt(variance + 1e-05) * norm_gain + norm_bias


def gelu_exact(values):
    return jax.nn.gelu(values, approximate=False)


def rope_tables(positions):
    freqs = jnp.exp(jnp.arange(ROT // 2, dtype=jnp.float32) * (-2.0 * math.log(10000.0) / ROT))
    angles = positions[:, None] * freqs[None, :]
    return (jnp.cos(angles), jnp.sin(angles))


def rotate(heads, cos_table, sin_table):
    half_rot = ROT // 2
    lower = heads[..., :half_rot]
    upper = heads[..., half_rot:ROT]
    cos_wide = cos_table[:, None, :]
    sin_wide = sin_table[:, None, :]
    return jnp.concatenate(
        [
            lower * cos_wide - upper * sin_wide,
            upper * cos_wide + lower * sin_wide,
            heads[..., ROT:],
        ],
        axis=-1,
    )


def unpack_small(packed, lengths, devices):
    table_rows = packed.reshape(devices, -1)
    members = []
    offset = 0
    for length in lengths:
        members.append(table_rows[:, offset : offset + length].reshape(-1).astype(jnp.float32))
        offset = offset + length
    return members


def contract_rows(left_mat, right_mat):
    return lax.dot_general(
        left_mat, right_mat, (((0,), (0,)), ((), ())), preferred_element_type=jnp.float32
    )


def contract_cols(left_mat, right_mat):
    return lax.dot_general(
        left_mat, right_mat, (((1,), (1,)), ((), ())), preferred_element_type=jnp.float32
    )


def shards(
    layer_input,
    out_grad,
    prefix_len,
    qkv_weight,
    qkv_bias,
    dense_weight,
    dense_bias,
    expand_weight,
    expand_bias,
    shrink_weight,
    shrink_bias,
    attn_gain,
    attn_shift,
    mlp_gain,
    mlp_shift,
):
    devices = lax.axis_size("dp") * lax.axis_size("ctx")
    ctx_index = lax.axis_index("ctx")
    micro, seq_count, span, width = layer_input.shape
    sequences = micro * seq_count
    rows = sequences * span
    heads_shape = (sequences, span, HEADS, HEAD)
    scale = 1.0 / math.sqrt(HEAD)
    attn_lengths = (attn_gain.shape[0], attn_shift.shape[0], qkv_bias.shape[0], dense_bias.shape[0])
    mlp_lengths = (
        mlp_gain.shape[0],
        mlp_shift.shape[0],
        expand_bias.shape[0],
        shrink_bias.shape[0],
    )
    attn_packed = jnp.concatenate([attn_gain, attn_shift, qkv_bias, dense_bias])
    mlp_packed = jnp.concatenate([mlp_gain, mlp_shift, expand_bias, shrink_bias])

    def fetch_attn():
        return (
            lax.all_gather(qkv_weight, ("dp", "ctx"), axis=0, tiled=True),
            lax.all_gather(dense_weight, ("dp", "ctx"), axis=0, tiled=True),
            lax.all_gather(attn_packed, ("dp", "ctx"), axis=0, tiled=True),
        )

    def fetch_mlp():
        return (
            lax.all_gather(expand_weight, ("dp", "ctx"), axis=0, tiled=True),
            lax.all_gather(shrink_weight, ("dp", "ctx"), axis=0, tiled=True),
            lax.all_gather(mlp_packed, ("dp", "ctx"), axis=0, tiled=True),
        )

    local_pos = ctx_index * span + jnp.arange(span, dtype=jnp.int32)
    cos_table, sin_table = rope_tables(local_pos.astype(jnp.float32))
    key_pos = jnp.arange(SEQ, dtype=jnp.int32)
    causal = key_pos[None, :] <= local_pos[:, None]
    inputs = layer_input.astype(jnp.float32).reshape(rows, width)
    cot_rows = out_grad.reshape(rows, width)
    cot_float = cot_rows.astype(jnp.float32)
    prefix = prefix_len.reshape(sequences)
    allowed = (causal[None] | (key_pos[None, None, :] < prefix[:, None, None]))[:, None]
    attn_set = fetch_attn()
    qkv_full, dense_full, attn_small = attn_set
    gain_attn, shift_attn, joined_shift, dense_shift = unpack_small(
        attn_small, attn_lengths, devices
    )
    hidden_attn = norm_rows(inputs, gain_attn, shift_attn).astype(jnp.bfloat16)
    joined = jnp.dot(hidden_attn, qkv_full, preferred_element_type=jnp.float32) + joined_shift
    queries = rotate(joined[:, :width].reshape(heads_shape), cos_table, sin_table).astype(
        jnp.bfloat16
    )
    key_rows = rotate(
        joined[:, width : 2 * width].reshape(heads_shape), cos_table, sin_table
    ).astype(jnp.bfloat16)
    value_rows = joined[:, 2 * width :].reshape(heads_shape).astype(jnp.bfloat16)
    all_keys, all_values = (
        lax.all_gather(key_rows, "ctx", axis=1, tiled=True),
        lax.all_gather(value_rows, "ctx", axis=1, tiled=True),
    )
    scores = (
        jnp.einsum("sqhe,skhe->shqk", queries, all_keys, preferred_element_type=jnp.float32) * scale
    )
    scores = jnp.where(allowed, scores, -1e30)
    row_max = jnp.max(scores, axis=-1, keepdims=True)
    expo = jnp.exp(scores - row_max)
    row_total = jnp.sum(expo, axis=-1, keepdims=True)
    log_total = row_max + jnp.log(row_total)
    probs_low = (expo / row_total).astype(jnp.bfloat16)
    mixed = jnp.einsum("shqk,skhe->sqhe", probs_low, all_values, preferred_element_type=jnp.float32)
    mixed = mixed.reshape(rows, width).astype(jnp.bfloat16)
    attn_out = jnp.dot(mixed, dense_full, preferred_element_type=jnp.float32) + dense_shift
    mlp_set = fetch_mlp()
    expand_full, shrink_full, mlp_small = mlp_set
    gain_mlp, shift_mlp, expand_shift, shrink_shift = unpack_small(mlp_small, mlp_lengths, devices)
    hidden_mlp = norm_rows(inputs, gain_mlp, shift_mlp).astype(jnp.bfloat16)
    expanded = jnp.dot(hidden_mlp, expand_full, preferred_element_type=jnp.float32) + expand_shift
    activated = gelu_exact(expanded).astype(jnp.bfloat16)
    mlp_out = jnp.dot(activated, shrink_full, preferred_element_type=jnp.float32) + shrink_shift
    layer_output = (
        (inputs + attn_out + mlp_out).astype(jnp.bfloat16).reshape(micro, seq_count, span, width)
    )
    attn_back_set = fetch_attn()
    qkv_back, dense_back, attn_small_back = attn_back_set
    gain_attn, shift_attn, joined_shift, dense_shift = unpack_small(
        attn_small_back, attn_lengths, devices
    )
    grad_out_shift = jnp.sum(cot_float, axis=0)
    grad_mixed = contract_cols(cot_rows, dense_back).astype(jnp.bfloat16).reshape(heads_shape)
    again = (
        jnp.einsum("sqhe,skhe->shqk", queries, all_keys, preferred_element_type=jnp.float32) * scale
    )
    again = jnp.where(allowed, again, -1e30)
    probs = jnp.exp(again - log_total)
    grad_probs = jnp.einsum(
        "sqhe,skhe->shqk", grad_mixed, all_values, preferred_element_type=jnp.float32
    )
    delta = jnp.sum(probs * grad_probs, axis=-1, keepdims=True)
    grad_scores = (probs * (grad_probs - delta)).astype(jnp.bfloat16)
    grad_queries = (
        jnp.einsum("shqk,skhe->sqhe", grad_scores, all_keys, preferred_element_type=jnp.float32)
        * scale
    )
    all_queries, all_grad_mixed = (
        lax.all_gather(queries, "ctx", axis=1, tiled=True),
        lax.all_gather(grad_mixed, "ctx", axis=1, tiled=True),
    )
    stat_lse = jnp.transpose(log_total[..., 0], (0, 2, 1))
    stat_delta = jnp.transpose(delta[..., 0], (0, 2, 1))
    lse_all, delta_all = (
        lax.all_gather(stat_lse, "ctx", axis=1, tiled=True),
        lax.all_gather(stat_delta, "ctx", axis=1, tiled=True),
    )
    lse_all = jnp.transpose(lse_all, (0, 2, 1))[..., None]
    delta_all = jnp.transpose(delta_all, (0, 2, 1))[..., None]
    key_allowed = (local_pos[None, :] <= key_pos[:, None])[None] | (
        local_pos[None, None, :] < prefix[:, None, None]
    )
    block_scores = (
        jnp.einsum("sqhe,skhe->shqk", all_queries, key_rows, preferred_element_type=jnp.float32)
        * scale
    )
    block_scores = jnp.where(key_allowed[:, None], block_scores, -1e30)
    block_probs = jnp.exp(block_scores - lse_all)
    block_grad_probs = jnp.einsum(
        "sqhe,skhe->shqk", all_grad_mixed, value_rows, preferred_element_type=jnp.float32
    )
    block_grad_scores = (block_probs * (block_grad_probs - delta_all)).astype(jnp.bfloat16)
    own_keys = (
        jnp.einsum(
            "shqk,sqhe->skhe", block_grad_scores, all_queries, preferred_element_type=jnp.float32
        )
        * scale
    )
    own_values = jnp.einsum(
        "shqk,sqhe->skhe",
        block_probs.astype(jnp.bfloat16),
        all_grad_mixed,
        preferred_element_type=jnp.float32,
    )
    grad_joined = jnp.concatenate(
        [
            rotate(grad_queries, cos_table, -sin_table).reshape(rows, width),
            rotate(own_keys, cos_table, -sin_table).reshape(rows, width),
            own_values.reshape(rows, width),
        ],
        axis=1,
    ).astype(jnp.bfloat16)
    grad_joined_shift = jnp.sum(grad_joined.astype(jnp.float32), axis=0)
    grad_hidden_attn = contract_cols(grad_joined, qkv_back)
    unused_attn, attn_back = jax.vjp(norm_rows, inputs, gain_attn, shift_attn)
    grad_in_attn, grad_gain_attn, grad_shift_attn = attn_back(grad_hidden_attn)
    attn_columns = jnp.concatenate(
        [
            grad_gain_attn[:, None],
            grad_shift_attn[:, None],
            grad_joined_shift[: 2 * width].reshape(width, 2),
            grad_joined_shift[2 * width :][:, None],
            grad_out_shift[:, None],
        ],
        axis=1,
    )
    hidden_part = hidden_attn
    small_part = attn_columns
    attn_grads = lax.psum_scatter(
        jnp.concatenate(
            [contract_rows(hidden_part, grad_joined), contract_rows(mixed, cot_rows), small_part],
            axis=1,
        ),
        ("dp", "ctx"),
        scatter_dimension=0,
        tiled=True,
    )
    qkv_grad = attn_grads[:, : 3 * width]
    dense_grad = attn_grads[:, 3 * width : 4 * width]
    attn_tail = attn_grads[:, 4 * width :]
    mlp_back_set = fetch_mlp()
    expand_back, shrink_back, mlp_small_back = mlp_back_set
    gain_mlp, shift_mlp, expand_shift, shrink_shift = unpack_small(
        mlp_small_back, mlp_lengths, devices
    )
    unused_gelu, gelu_back = jax.vjp(gelu_exact, expanded)
    grad_act = contract_cols(cot_rows, shrink_back)
    grad_expanded = gelu_back(grad_act)[0].astype(jnp.bfloat16)
    grad_expand_shift = jnp.sum(grad_expanded.astype(jnp.float32), axis=0)
    grad_hidden_mlp = contract_cols(grad_expanded, expand_back)
    unused_mlp, mlp_back = jax.vjp(norm_rows, inputs, gain_mlp, shift_mlp)
    grad_in_mlp, grad_gain_mlp, grad_shift_mlp = mlp_back(grad_hidden_mlp)
    ratio = expand_shift.shape[0] // width
    mlp_columns = jnp.concatenate(
        [
            grad_gain_mlp[:, None],
            grad_shift_mlp[:, None],
            grad_expand_shift.reshape(width, ratio),
            grad_out_shift[:, None],
        ],
        axis=1,
    )
    ff_width = expand_back.shape[1]
    hidden_part = hidden_mlp
    small_part = mlp_columns
    expand_grads = lax.psum_scatter(
        jnp.concatenate([contract_rows(hidden_part, grad_expanded), small_part], axis=1),
        ("dp", "ctx"),
        scatter_dimension=0,
        tiled=True,
    )
    shrink_grad = lax.psum_scatter(
        contract_rows(activated, cot_rows), ("dp", "ctx"), scatter_dimension=0, tiled=True
    )
    expand_grad = expand_grads[:, :ff_width]
    mlp_tail = expand_grads[:, ff_width:]
    input_grad = (
        (cot_float + grad_in_attn + grad_in_mlp)
        .astype(jnp.bfloat16)
        .reshape(micro, seq_count, span, width)
    )
    return (
        layer_output,
        input_grad,
        qkv_grad,
        attn_tail[:, 2:4].reshape(-1),
        attn_tail[:, 4],
        dense_grad,
        attn_tail[:, 5],
        expand_grad,
        mlp_tail[:, 2 : 2 + ratio].reshape(-1),
        shrink_grad,
        mlp_tail[:, 2 + ratio],
        attn_tail[:, 0],
        attn_tail[:, 1],
        mlp_tail[:, 0],
        mlp_tail[:, 1],
    )


def low(values):
    return values.astype(jnp.bfloat16)


MESH_ID = pl.DeviceIdType.MESH


def remote(src, dst, send_sem, recv_sem, dp, ctx):
    return pltpu.make_async_remote_copy(
        src_ref=src,
        dst_ref=dst,
        send_sem=send_sem,
        recv_sem=recv_sem,
        device_id=(dp, ctx),
        device_id_type=MESH_ID,
    )


def greet_all(dp, ctx, dp_size, ctx_size):
    barrier = pltpu.get_barrier_semaphore()
    devices = dp_size * ctx_size
    me = dp * ctx_size + ctx

    def greet(step, carry):
        other = lax.rem(me + step, devices)
        pl.semaphore_signal(
            barrier, inc=1, device_id=(other // ctx_size, lax.rem(other, ctx_size)), device_id_type=MESH_ID
        )
        return carry

    lax.fori_loop(1, devices, greet, 0)
    pl.semaphore_wait(barrier, devices - 1)


def gather_kernel(
    dp_size,
    ctx_size,
    x,
    qkv,
    expand,
    dense,
    shrink,
    packed,
    x_all,
    panels,
    out_w,
    small,
    local_sem,
    small_sem,
    block_send,
    block_recv,
    core_send,
    core_recv,
    panel_send,
    panel_recv,
    share_send,
    share_recv,
    pass_send,
    pass_recv,
):
    d = lax.axis_index("dp")
    c = lax.axis_index("ctx")
    z = c // 2
    sibling = c + 1 - 2 * lax.rem(c, 2)
    x_mate = d + 1 - 2 * lax.rem(d, 2)
    y_mate = lax.rem(d + 2, 4)
    micro, span = x.shape[0], x.shape[1]
    devices = dp_size * ctx_size
    me = d * ctx_size + c
    rows = qkv.shape[0]
    unit = shrink.shape[0]
    levels = ctx_size // 2
    panel_rows = ctx_size * rows
    n_panels = 3 + dp_size

    greet_all(d, c, dp_size, ctx_size)

    def column_block(panel, target):
        if panel < 3:
            start = panel * (qkv.shape[1] // 3) + target * HEAD
            return qkv.at[:, pl.ds(pl.multiple_of(start, HEAD), HEAD)]
        start = (panel - 3) * ctx_size * unit + target * unit
        return expand.at[:, pl.ds(pl.multiple_of(start, HEAD), HEAD)]

    own_rows = pl.ds(pl.multiple_of((d * ctx_size + c) * rows, rows), rows)

    for panel in range(n_panels):
        pltpu.make_async_copy(
            column_block(panel, c), panels.at[panel, own_rows], local_sem.at[panel]
        ).start()

        def push(step, carry, panel=panel):
            target = lax.rem(c + step, ctx_size)
            remote(
                column_block(panel, target),
                panels.at[panel, own_rows],
                panel_send.at[panel],
                panel_recv.at[panel],
                d,
                target,
            ).start()
            return carry

        lax.fori_loop(1, ctx_size, push, 0)

    def shrink_rows(owner, offset, count):
        return out_w.at[pl.ds(pl.multiple_of(HEAD + owner * unit + offset, 16), count)]

    shrink_local = pltpu.make_async_copy(shrink, shrink_rows(d, 0, unit), local_sem.at[n_panels])
    shrink_local.start()
    for way, mate in ((0, x_mate), (1, y_mate)):
        remote(
            shrink, shrink_rows(d, 0, unit), share_send.at[n_panels, way], share_recv.at[n_panels, way], mate, c
        ).start()

    per_head = HEAD // rows
    head_of = (d * ctx_size + c) // per_head
    dense_rows = pl.ds(pl.multiple_of(lax.rem(c, per_head) * rows, rows), rows)
    dense_out = remote(dense, out_w.at[dense_rows], panel_send.at[n_panels], panel_recv.at[n_panels], d, head_of)
    dense_own = pltpu.make_async_copy(dense, out_w.at[dense_rows], local_sem.at[n_panels + 1])
    stays = head_of == c

    @pl.when(stays)
    def _():
        dense_own.start()

    @pl.when(jnp.logical_not(stays))
    def _():
        dense_out.start()

    def block(origin, m):
        return x_all.at[m, pl.ds(pl.multiple_of(origin * span, span), span)]

    x_local = []
    for m in range(micro):
        copy = pltpu.make_async_copy(x.at[m], block(c, m), local_sem.at[n_panels + 2 + m])
        copy.start()
        x_local.append(copy)

    def chain(way, hop, m):
        step = 2 if way == 0 else -2
        origin = c - step * hop
        src = x.at[m] if hop == 0 else block(origin, m)
        exists = jnp.logical_and(z >= hop, z <= levels - 2) if way == 0 else jnp.logical_and(
            z + hop <= levels - 1, z >= 1
        )
        copy = remote(src, block(origin, m), block_send.at[way, hop, m], block_recv.at[way, hop, m], d, c + step)
        return exists, copy

    def arrives(way, hop):
        return z >= hop + 1 if way == 0 else z + hop + 1 <= levels - 1

    def core_copy(slot, origin, m):
        src = x.at[m] if slot == 0 else block(origin, m)
        return remote(src, block(origin, m), core_send.at[slot, m], core_recv.at[slot, m], d, sibling)

    for m in range(micro):
        core_copy(0, c, m).start()
        for way in range(2):
            exists, copy = chain(way, 0, m)

            @pl.when(exists)
            def _(copy=copy):
                copy.start()

    small_copy = pltpu.make_async_copy(packed, small.at[me], local_sem.at[n_panels + 2 + micro])
    small_copy.start()

    def push_small(step, carry):
        other = lax.rem(me + step, devices)
        remote(
            packed,
            small.at[me],
            small_sem.at[0],
            small_sem.at[1],
            other // ctx_size,
            lax.rem(other, ctx_size),
        ).start()
        return carry

    lax.fori_loop(1, devices, push_small, 0)

    def slot_of(way, hop):
        return 1 + way * (levels - 1) + hop

    def hop_step(hop):
        for m in range(micro):
            for way in range(2):
                step = 2 if way == 0 else -2

                @pl.when(arrives(way, hop))
                def _(way=way, m=m, step=step):
                    origin = c - step * (hop + 1)
                    remote(
                        block(origin, m), block(origin, m), block_send.at[way, hop, m], block_recv.at[way, hop, m], d, c - step
                    ).wait_recv()
                    core_copy(slot_of(way, hop), origin, m).start()

                if hop + 1 <= levels - 2:
                    exists, copy = chain(way, hop + 1, m)

                    @pl.when(exists)
                    def _(copy=copy):
                        copy.start()

    def group_rows(owner, offset, count):
        return pl.ds(pl.multiple_of(owner * panel_rows + offset, 16), count)

    def panel_share(panel, way, mate):
        view = panels.at[panel, group_rows(d, 0, panel_rows)]
        return remote(view, view, share_send.at[panel, way], share_recv.at[panel, way], mate, c)

    def panel_step(panel):
        pltpu.make_async_copy(column_block(panel, c), panels.at[panel, own_rows], local_sem.at[panel]).wait()
        whole = panels.at[panel, group_rows(d, 0, (ctx_size - 1) * rows)]
        remote(whole, whole, panel_send.at[panel], panel_recv.at[panel], d, sibling).wait_recv()
        panel_share(panel, 0, x_mate).start()
        panel_share(panel, 1, y_mate).start()

    half = panel_rows // 2

    def panel_pass(panel, way):
        owner, mate = ((x_mate, y_mate), (y_mate, x_mate))[way]
        view = panels.at[panel, group_rows(owner, way * half, half)]
        return remote(view, view, pass_send.at[panel, way], pass_recv.at[panel, way], mate, c)

    def panel_forward(panel):
        for way, owner in ((0, x_mate), (1, y_mate)):
            view = panels.at[panel, group_rows(owner, 0, panel_rows)]
            remote(view, view, share_send.at[panel, way], share_recv.at[panel, way], owner, c).wait_recv()
            panel_pass(panel, way).start()

    def shrink_share_wait(way, owner):
        view = shrink_rows(owner, 0, unit)
        remote(view, view, share_send.at[n_panels, way], share_recv.at[n_panels, way], owner, c).wait_recv()

    def shrink_pass(way):
        owner, mate = ((x_mate, y_mate), (y_mate, x_mate))[way]
        view = shrink_rows(owner, way * (unit // 2), unit // 2)
        return remote(view, view, pass_send.at[n_panels, way], pass_recv.at[n_panels, way], mate, c)

    source = c // (ctx_size // dp_size)
    at_source = d == source
    from_x = x_mate == source
    from_y = y_mate == source
    head_rows = out_w.at[pl.ds(0, HEAD)]
    half_head = HEAD // 2

    def dense_share(way, mate):
        return remote(head_rows, head_rows, share_send.at[n_panels + 1, way], share_recv.at[n_panels + 1, way], mate, c)

    def dense_pass(way, mate):
        view = out_w.at[pl.ds(way * half_head, half_head)]
        return remote(view, view, pass_send.at[n_panels + 1, way], pass_recv.at[n_panels + 1, way], mate, c)

    owns_share = jnp.logical_and(at_source, stays)

    def dense_gather_step():
        @pl.when(owns_share)
        def _():
            dense_own.wait()
            view = out_w.at[pl.ds(0, (per_head - 1) * rows)]
            remote(view, view, panel_send.at[n_panels], panel_recv.at[n_panels], d, sibling).wait_recv()

        @pl.when(jnp.logical_and(at_source, jnp.logical_not(stays)))
        def _():
            remote(head_rows, head_rows, panel_send.at[n_panels], panel_recv.at[n_panels], d, sibling).wait_recv()

        @pl.when(at_source)
        def _():
            dense_share(0, x_mate).start()
            dense_share(1, y_mate).start()

    def dense_forward_step():
        @pl.when(from_x)
        def _():
            dense_share(0, x_mate).wait_recv()
            dense_pass(0, y_mate).start()

        @pl.when(from_y)
        def _():
            dense_share(1, y_mate).wait_recv()
            dense_pass(1, x_mate).start()

    across = jnp.logical_not(jnp.logical_or(at_source, jnp.logical_or(from_x, from_y)))

    for panel in range(3):
        panel_step(panel)
    shrink_share_wait(0, x_mate)
    shrink_pass(0).start()
    shrink_share_wait(1, y_mate)
    shrink_pass(1).start()
    dense_gather_step()
    hop_step(0)
    for panel in range(3, n_panels):
        panel_step(panel)
        panel_forward(panel - 3)
    hop_step(1)
    dense_forward_step()
    for panel in range(n_panels - 3, n_panels):
        panel_forward(panel)
    for hop in range(2, levels - 1):
        hop_step(hop)

    for panel in range(n_panels):
        for way, mate in ((0, x_mate), (1, y_mate)):
            panel_share(panel, way, mate).wait_send()
            panel_pass(panel, way).wait_send()
        for way in range(2):
            diagonal = 3 - d
            view = panels.at[panel, group_rows(diagonal, way * half, half)]
            remote(view, view, pass_send.at[panel, way], pass_recv.at[panel, way], x_mate, c).wait_recv()
        whole = panels.at[panel, group_rows(d, 0, (ctx_size - 1) * rows)]
        remote(whole, whole, panel_send.at[panel], panel_recv.at[panel], x_mate, c).wait_send()
    shrink_local.wait()
    for way in range(2):
        mate = (x_mate, y_mate)[way]
        remote(
            shrink, shrink_rows(d, 0, unit), share_send.at[n_panels, way], share_recv.at[n_panels, way], mate, c
        ).wait_send()
        shrink_pass(way).wait_send()
        view = shrink_rows(3 - d, way * (unit // 2), unit // 2)
        remote(view, view, pass_send.at[n_panels, way], pass_recv.at[n_panels, way], mate, c).wait_recv()

    @pl.when(jnp.logical_not(stays))
    def _():
        dense_out.wait_send()

    @pl.when(at_source)
    def _():
        dense_share(0, x_mate).wait_send()
        dense_share(1, y_mate).wait_send()

    @pl.when(from_x)
    def _():
        dense_pass(0, y_mate).wait_send()

    @pl.when(from_y)
    def _():
        dense_pass(1, x_mate).wait_send()

    @pl.when(across)
    def _():
        dense_pass(0, y_mate).wait_recv()
        dense_pass(1, x_mate).wait_recv()

    for m in range(micro):
        x_local[m].wait()
        core_copy(0, c, m).wait_send()
        core_copy(0, sibling, m).wait_recv()
        for way in range(2):
            step = 2 if way == 0 else -2
            for hop in range(levels - 1):
                exists, copy = chain(way, hop, m)

                @pl.when(exists)
                def _(copy=copy):
                    copy.wait_send()

                @pl.when(arrives(way, hop))
                def _(way=way, hop=hop, m=m, step=step):
                    slot = slot_of(way, hop)
                    core_copy(slot, c - step * (hop + 1), m).wait_send()
                    core_copy(slot, sibling - step * (hop + 1), m).wait_recv()

    small_copy.wait()
    rest = small.at[pl.ds(0, devices - 1)]
    remote(rest, rest, small_sem.at[0], small_sem.at[1], d, sibling).wait()


def gather_call(dp_size, ctx_size, x, qkv, expand, dense, shrink, packed):
    micro, span, width = x.shape
    rows = qkv.shape[0]
    n_panels = 3 + dp_size
    levels = ctx_size // 2
    devices = dp_size * ctx_size
    dma = pltpu.SemaphoreType.DMA
    out_shape = (
        jax.ShapeDtypeStruct((micro, ctx_size * span, width), x.dtype),
        jax.ShapeDtypeStruct((n_panels, devices * rows, HEAD), x.dtype),
        jax.ShapeDtypeStruct((HEAD + dp_size * shrink.shape[0], width), x.dtype),
        jax.ShapeDtypeStruct((devices,) + packed.shape, x.dtype),
    )
    anywhere = pl.BlockSpec(memory_space=pl.ANY)
    return pl.pallas_call(
        functools.partial(gather_kernel, dp_size, ctx_size),
        out_shape=out_shape,
        in_specs=[anywhere] * 6,
        out_specs=(anywhere,) * 4,
        scratch_shapes=[
            dma((n_panels + 3 + micro,)),
            dma((2,)),
            dma((2, levels - 1, micro)),
            dma((2, levels - 1, micro)),
            dma((2 * levels - 1, micro)),
            dma((2 * levels - 1, micro)),
            dma((n_panels + 1,)),
            dma((n_panels + 1,)),
            dma((n_panels + 2, 2)),
            dma((n_panels + 2, 2)),
            dma((n_panels + 2, 2)),
            dma((n_panels + 2, 2)),
        ],
        compiler_params=pltpu.CompilerParams(collective_id=1, has_side_effects=True),
        name="gather_all",
    )(x, qkv, expand, dense, shrink, packed)


def add_into(dst, srcs, rows):
    chunk = 16 if dst.shape[-1] > 1024 else 64

    def step(index, carry):
        at = pl.ds(pl.multiple_of(index * chunk, 16), chunk)
        total = srcs[0][at, :].astype(jnp.float32)
        for src in srcs[1:]:
            total = total + src[at, :].astype(jnp.float32)
        dst[at, :] = total.astype(dst.dtype)
        return carry

    lax.fori_loop(0, rows // chunk, step, 0)


def reduce_kernel(
    dp_size,
    ctx_size,
    back,
    qkv_grads,
    expand_grads,
    out_grads,
    board,
    back_out,
    panel_out,
    shrink_out,
    dense_out,
    tail_out,
    back_own,
    back_core,
    back_chain,
    panel_own,
    panel_recv,
    panel_last,
    shrink_own,
    shrink_recv,
    shrink_last,
    dense_own,
    dense_recv,
    board_recv,
    load_sem,
    core_send,
    core_recv,
    chain_send,
    chain_recv,
    first_send,
    first_recv,
    last_send,
    last_recv,
    out_send,
    out_recv,
    dense_send,
    dense_sem,
    board_sem,
    store_sem,
):
    d = lax.axis_index("dp")
    c = lax.axis_index("ctx")
    z = c // 2
    core = lax.rem(c, 2)
    sibling = c + 1 - 2 * core
    x_mate = d + 1 - 2 * lax.rem(d, 2)
    y_mate = lax.rem(d + 2, 4)
    diagonal = 3 - d
    micro = back.shape[0]
    span = back.shape[1] // ctx_size
    levels = ctx_size // 2
    devices = dp_size * ctx_size
    me = d * ctx_size + c
    n_panels = 3 + dp_size
    group_rows = qkv_grads.shape[0] // dp_size
    half = group_rows // 2
    rows = group_rows // ctx_size
    unit = (out_grads.shape[0] - HEAD) // dp_size
    shrink_half = unit // 2
    head_half = HEAD // 2

    greet_all(d, c, dp_size, ctx_size)

    def back_view(parity, level, m):
        start = (2 * level + parity) * span
        return back.at[m, pl.ds(pl.multiple_of(start, span), span)]

    def back_load(level, m):
        return pltpu.make_async_copy(back_view(core, level, m), back_own.at[level, m], load_sem.at[0, level * micro + m])

    def core_copy(level, m):
        return remote(
            back_view(1 - core, level, m),
            back_core.at[level, m],
            core_send.at[level, m],
            core_recv.at[level, m],
            d,
            sibling,
        )

    order = []
    for pair in range((levels + 1) // 2):
        for level in (levels - 1 - pair, pair):
            if level not in order:
                order.append(level)
    for level in order:
        for m in range(micro):
            core_copy(level, m).start()
            back_load(level, m).start()

    mates = ((x_mate, y_mate), (y_mate, x_mate))

    def panel_view(panel, owner, way):
        at = pl.ds(pl.multiple_of(owner * group_rows + way * half, 16), half)
        if panel < 3:
            return qkv_grads.at[at, pl.ds(panel * HEAD, HEAD)]
        return expand_grads.at[at, pl.ds((panel - 3) * HEAD, HEAD)]

    def shrink_view(owner, way):
        return out_grads.at[pl.ds(pl.multiple_of(HEAD + owner * unit + way * shrink_half, 16), shrink_half)]

    def first_copies(index, view, recv):
        copies = []
        for way in range(2):
            mate = mates[way][0]
            for slot, owner in ((0, mate), (1, diagonal)):
                copies.append(
                    remote(
                        view(owner, way),
                        recv.at[way, slot],
                        first_send.at[index, way, slot],
                        first_recv.at[index, way, slot],
                        mate,
                        c,
                    )
                )
        return copies

    def own_loads(index, view, own):
        copies = []
        for way in range(2):
            for slot, owner in ((0, d), (1, mates[way][1])):
                copies.append(
                    pltpu.make_async_copy(view(owner, way), own.at[way, slot], load_sem.at[1 + index, way * 2 + slot])
                )
        return copies

    def last_copies(index, own, last):
        return [
            remote(
                own.at[way, 1], last.at[way], last_send.at[index, way], last_recv.at[index, way], mates[way][1], c
            )
            for way in range(2)
        ]

    def unit_parts(index):
        if index < n_panels:
            return (
                functools.partial(panel_view, index),
                panel_own.at[index],
                panel_recv.at[index],
                panel_last.at[index],
                half,
            )
        return shrink_view, shrink_own, shrink_recv, shrink_last, shrink_half

    def open_unit(index):
        view, own, recv, last, count = unit_parts(index)
        for copy in first_copies(index, view, recv) + own_loads(index, view, own):
            copy.start()

    def first_step(index):
        view, own, recv, last, count = unit_parts(index)
        arrivals = first_copies(index, view, recv)
        loads = own_loads(index, view, own)
        sends = last_copies(index, own, last)
        for way in range(2):
            arrivals[way * 2 + 1].wait_recv()
            loads[way * 2 + 1].wait()
            add_into(own.at[way, 1], (own.at[way, 1], recv.at[way, 1]), count)
            sends[way].start()

    def last_step(index):
        view, own, recv, last, count = unit_parts(index)
        arrivals = first_copies(index, view, recv)
        loads = own_loads(index, view, own)
        ends = last_copies(index, own, last)
        for way in range(2):
            arrivals[way * 2].wait_recv()
            loads[way * 2].wait()
            ends[way].wait_recv()
            add_into(own.at[way, 0], (own.at[way, 0], recv.at[way, 0], last.at[way]), count)

    def close_unit(index):
        view, own, recv, last, count = unit_parts(index)
        for copy in first_copies(index, view, recv) + last_copies(index, own, last):
            copy.wait_send()

    per_half = half // rows

    def panel_chunk(panel, target):
        start = pl.multiple_of(lax.rem(target, per_half) * rows, rows)
        return panel_own.at[panel, target // per_half, 0, pl.ds(start, rows)]

    def panel_local(panel):
        return pltpu.make_async_copy(panel_chunk(panel, c), panel_out.at[panel, c], store_sem.at[panel])

    def send_panel(panel):
        def push(step, carry):
            target = lax.rem(c + step, ctx_size)
            remote(
                panel_chunk(panel, target), panel_out.at[panel, c], out_send.at[panel], out_recv.at[panel], d, target
            ).start()
            return carry

        lax.fori_loop(1, ctx_size, push, 0)
        panel_local(panel).start()

    def end_panel(panel):
        rest = panel_out.at[panel, pl.ds(0, ctx_size - 1)]
        remote(rest, rest, out_send.at[panel], out_recv.at[panel], d, sibling).wait()
        panel_local(panel).wait()

    source = c // (ctx_size // dp_size)
    at_source = d == source
    from_x = x_mate == source
    from_y = y_mate == source
    across = diagonal == source
    per_head = HEAD // rows

    def dense_half(way):
        return out_grads.at[pl.ds(way * head_half, head_half)]

    def dense_copy(way, src, slot, mate):
        return remote(src, dense_recv.at[slot], dense_send.at[way], dense_sem.at[slot], mate, c)

    dense_load = pltpu.make_async_copy(out_grads.at[pl.ds(0, HEAD)], dense_own, load_sem.at[0, levels * micro])
    dense_load.start()

    @pl.when(across)
    def _():
        dense_copy(0, dense_half(0), 0, y_mate).start()
        dense_copy(1, dense_half(1), 0, x_mate).start()

    def middle(mate, mine, axis):
        own = dense_own.at[pl.ds(mine * head_half, head_half)]
        dense_copy(1 - mine, dense_half(1 - mine), 1 + 2 * axis + 1 - mine, mate).start()
        dense_copy(mine, own, 0, mate).wait_recv()
        add_into(own, (own, dense_recv.at[0]), head_half)
        dense_copy(mine, own, 1 + 2 * axis + mine, mate).start()

    def dense_chunk(piece):
        return dense_own.at[pl.ds(piece * rows, rows)]

    first_owner = lax.rem(c, ctx_size // per_head) * per_head

    def dense_send_out(piece):
        return remote(
            dense_chunk(piece), dense_out, dense_send.at[2 + piece], dense_sem.at[5], d, first_owner + piece
        )

    def dense_store(piece):
        return pltpu.make_async_copy(dense_chunk(piece), dense_out, store_sem.at[n_panels])

    board_load = pltpu.make_async_copy(board.at[me], board_recv.at[me], load_sem.at[0, levels * micro + 1])
    board_load.start()

    def push_board(step, carry):
        other = lax.rem(me + step, devices)
        remote(
            board.at[other],
            board_recv.at[me],
            board_sem.at[0],
            board_sem.at[1],
            other // ctx_size,
            lax.rem(other, ctx_size),
        ).start()
        return carry

    lax.fori_loop(1, devices, push_board, 0)

    for index in range(n_panels):
        open_unit(index)

    for level in order:
        for m in range(micro):
            back_load(level, m).wait()
            core_copy(level, m).wait_recv()
            add_into(back_own.at[level, m], (back_own.at[level, m], back_core.at[level, m]), span)

    def chain_copy(way, level, m):
        return remote(
            back_own.at[level, m],
            back_chain.at[way, level, m],
            chain_send.at[way, level, m],
            chain_recv.at[way, level, m],
            d,
            c + (2 if way == 0 else -2),
        )

    def sends(way, level):
        return z < level if way == 0 else z > level

    def hears(way, level):
        if way == 0:
            return jnp.logical_and(z >= 1, z <= level)
        return jnp.logical_and(z <= levels - 2, z >= level)

    def chain_step(way, level):
        for m in range(micro):
            @pl.when(jnp.logical_and(sends(way, level), hears(way, level)))
            def _(m=m):
                chain_copy(way, level, m).wait_recv()
                add_into(back_own.at[level, m], (back_own.at[level, m], back_chain.at[way, level, m]), span)

            @pl.when(sends(way, level))
            def _(m=m):
                chain_copy(way, level, m).start()

    def chain_end():
        for level in range(levels):
            for m in range(micro):
                for way in range(2):
                    @pl.when(jnp.logical_and(z == level, hears(way, level)))
                    def _(way=way, level=level, m=m):
                        chain_copy(way, level, m).wait_recv()
                        add_into(back_own.at[level, m], (back_own.at[level, m], back_chain.at[way, level, m]), span)

                @pl.when(z == level)
                def _(level=level, m=m):
                    pltpu.make_async_copy(back_own.at[level, m], back_out.at[m], store_sem.at[n_panels + 2 + m]).start()

    chain_step(0, levels - 1)
    chain_step(1, 0)
    first_step(0)
    first_step(1)
    dense_load.wait()

    @pl.when(from_x)
    def _():
        middle(x_mate, 0, 0)

    @pl.when(from_y)
    def _():
        middle(y_mate, 1, 1)

    first_step(2)
    last_step(0)
    send_panel(0)
    chain_step(0, levels - 2)
    chain_step(1, 1)
    first_step(3)
    last_step(1)
    send_panel(1)
    open_unit(n_panels)
    first_step(4)
    last_step(2)
    send_panel(2)

    @pl.when(at_source)
    def _():
        for slot in range(1, 5):
            dense_copy(0, dense_half(0), slot, x_mate).wait_recv()
        for way in range(2):
            own = dense_own.at[pl.ds(way * head_half, head_half)]
            add_into(own, (own, dense_recv.at[1 + way], dense_recv.at[3 + way]), head_half)
        for piece in range(per_head):
            @pl.when(first_owner + piece == c)
            def _(piece=piece):
                dense_store(piece).start()

            @pl.when(first_owner + piece != c)
            def _(piece=piece):
                dense_send_out(piece).start()

    first_step(5)
    last_step(3)
    send_panel(3)
    chain_step(0, levels - 3)
    chain_step(1, 2)
    first_step(6)
    last_step(4)
    send_panel(4)
    last_step(5)
    send_panel(5)
    last_step(6)
    send_panel(6)
    first_step(n_panels)
    chain_end()
    last_step(n_panels)
    for way in range(2):
        pltpu.make_async_copy(
            shrink_own.at[way, 0],
            shrink_out.at[pl.ds(way * shrink_half, shrink_half)],
            store_sem.at[n_panels + 2 + micro + way],
        ).start()

    board_load.wait()
    rest = board_recv.at[pl.ds(0, devices - 1)]
    remote(rest, rest, board_sem.at[0], board_sem.at[1], d, sibling).wait()
    tail_out[...] = jnp.sum(board_recv[...], axis=0)

    for index in range(n_panels + 1):
        close_unit(index)
    for panel in range(n_panels):
        end_panel(panel)
    for level in range(levels):
        for m in range(micro):
            core_copy(level, m).wait_send()
            for way in range(2):
                @pl.when(sends(way, level))
                def _(way=way, level=level, m=m):
                    chain_copy(way, level, m).wait_send()

    @pl.when(jnp.logical_not(at_source))
    def _():
        dense_copy(0, dense_half(0), 0, x_mate).wait_send()
        dense_copy(1, dense_half(1), 0, x_mate).wait_send()

    for piece in range(per_head):
        @pl.when(jnp.logical_and(at_source, first_owner + piece != c))
        def _(piece=piece):
            dense_send_out(piece).wait_send()

    stays = me // per_head == c

    @pl.when(stays)
    def _():
        dense_store(0).wait()

    @pl.when(jnp.logical_not(stays))
    def _():
        dense_send_out(0).wait_recv()

    for m in range(micro):
        pltpu.make_async_copy(back_own.at[0, m], back_out.at[m], store_sem.at[n_panels + 2 + m]).wait()
    for way in range(2):
        pltpu.make_async_copy(
            shrink_own.at[way, 0],
            shrink_out.at[pl.ds(way * shrink_half, shrink_half)],
            store_sem.at[n_panels + 2 + micro + way],
        ).wait()


def reduce_call(dp_size, ctx_size, back, qkv_grads, expand_grads, out_grads, board):
    micro, length, width = back.shape
    span = length // ctx_size
    n_panels = 3 + dp_size
    group_rows = qkv_grads.shape[0] // dp_size
    half = group_rows // 2
    rows = group_rows // ctx_size
    unit = (out_grads.shape[0] - HEAD) // dp_size
    levels = ctx_size // 2
    devices = dp_size * ctx_size
    dma = pltpu.SemaphoreType.DMA
    kind = back.dtype
    vmem = pltpu.VMEM
    out_shape = (
        jax.ShapeDtypeStruct((micro, span, width), kind),
        jax.ShapeDtypeStruct((n_panels, ctx_size, rows, HEAD), kind),
        jax.ShapeDtypeStruct((unit, width), kind),
        jax.ShapeDtypeStruct((HEAD // (HEAD // rows), width), kind),
        jax.ShapeDtypeStruct(board.shape[1:], jnp.float32),
    )
    anywhere = pl.BlockSpec(memory_space=pl.ANY)
    return pl.pallas_call(
        functools.partial(reduce_kernel, dp_size, ctx_size),
        out_shape=out_shape,
        in_specs=[anywhere] * 5,
        out_specs=(anywhere,) * 4 + (pl.BlockSpec(memory_space=pltpu.VMEM),),
        scratch_shapes=[
            vmem((levels, micro, span, width), kind),
            vmem((levels, micro, span, width), kind),
            vmem((2, levels, micro, span, width), kind),
            vmem((n_panels, 2, 2, half, HEAD), kind),
            vmem((n_panels, 2, 2, half, HEAD), kind),
            vmem((n_panels, 2, half, HEAD), kind),
            vmem((2, 2, unit // 2, width), kind),
            vmem((2, 2, unit // 2, width), kind),
            vmem((2, unit // 2, width), kind),
            vmem((HEAD, width), kind),
            vmem((5, HEAD // 2, width), kind),
            vmem((devices,) + board.shape[1:], jnp.float32),
            dma((n_panels + 2, levels * micro + 2)),
            dma((levels, micro)),
            dma((levels, micro)),
            dma((2, levels, micro)),
            dma((2, levels, micro)),
            dma((n_panels + 1, 2, 2)),
            dma((n_panels + 1, 2, 2)),
            dma((n_panels + 1, 2)),
            dma((n_panels + 1, 2)),
            dma((n_panels,)),
            dma((n_panels,)),
            dma((2 + HEAD // rows,)),
            dma((6,)),
            dma((2,)),
            dma((n_panels + 4 + micro,)),
        ],
        compiler_params=pltpu.CompilerParams(
            collective_id=2, has_side_effects=True, vmem_limit_bytes=56 * 1024 * 1024
        ),
        name="reduce_all",
    )(back, qkv_grads, expand_grads, out_grads, board)


def tensor_shards(
    layer_input,
    out_grad,
    prefix_len,
    qkv_weight,
    qkv_bias,
    dense_weight,
    dense_bias,
    expand_weight,
    expand_bias,
    shrink_weight,
    shrink_bias,
    attn_gain,
    attn_shift,
    mlp_gain,
    mlp_shift,
):
    dp_size = lax.axis_size("dp")
    ctx_size = lax.axis_size("ctx")
    devices = dp_size * ctx_size
    me = lax.axis_index("ctx")
    group = lax.axis_index("dp")
    micro, seq_count, span, width = layer_input.shape
    sequences = micro * seq_count
    tokens = sequences * SEQ
    row_share = qkv_weight.shape[0]
    scale = 1.0 / math.sqrt(HEAD)
    ff = expand_weight.shape[1]
    unit = shrink_weight.shape[0]
    lengths = tuple(
        member.shape[0]
        for member in (attn_gain, attn_shift, mlp_gain, mlp_shift, qkv_bias, dense_bias, expand_bias, shrink_bias)
    )
    packed = jnp.concatenate(
        [attn_gain, attn_shift, mlp_gain, mlp_shift, qkv_bias, dense_bias, expand_bias, shrink_bias]
    )
    own_x = layer_input.reshape(sequences, span, width)
    own_g = out_grad.reshape(sequences, span, width)
    g_all = lax.all_gather(own_g, "ctx", axis=1, tiled=True).reshape(tokens, width)
    count = packed.shape[0]
    packed = jnp.pad(packed, (0, -count % 2048)).reshape(-1, 128)
    x_all, panels, out_part, small = gather_call(
        dp_size, ctx_size, own_x, qkv_weight, expand_weight, dense_weight, shrink_weight, packed
    )
    x_all = x_all.reshape(tokens, width)
    qkv_part = panels[:3]
    expand_part = panels[3:]
    small = unpack_small(small.reshape(devices, -1)[:, :count], lengths, devices)
    gain_attn, shift_attn, gain_mlp, shift_mlp, qkv_shift, dense_shift, expand_shift, shrink_shift = small
    qkv_shift = lax.dynamic_slice_in_dim(qkv_shift.reshape(3, ctx_size, HEAD), me, 1, 1).reshape(-1)
    expand_shift = lax.dynamic_slice_in_dim(
        expand_shift.reshape(dp_size, ctx_size, unit), me, 1, 1
    ).reshape(-1)

    inputs = x_all.astype(jnp.float32)
    row_mean = jnp.mean(inputs, axis=-1, keepdims=True)
    centered = inputs - row_mean
    spread = lax.rsqrt(jnp.mean(centered * centered, axis=-1, keepdims=True) + 1e-05)
    normal = centered * spread
    hidden_attn = low(normal * gain_attn + shift_attn)
    hidden_mlp = low(normal * gain_mlp + shift_mlp)

    cos_table, sin_table = rope_tables(jnp.arange(SEQ, dtype=jnp.float32))
    joined = jnp.einsum("td,pde->tpe", hidden_attn, qkv_part, preferred_element_type=jnp.float32)
    joined = joined.reshape(tokens, -1) + qkv_shift
    joined = joined.reshape(sequences, SEQ, 3, HEAD)

    def turn(heads, sin_values):
        return rotate(heads[:, :, None, :], cos_table, sin_values)[:, :, 0]

    queries = low(turn(joined[:, :, 0], sin_table))
    key_rows = low(turn(joined[:, :, 1], sin_table))
    value_rows = low(joined[:, :, 2])
    positions = jnp.arange(SEQ, dtype=jnp.int32)
    prefix = prefix_len.reshape(sequences)
    allowed = (positions[None, :] <= positions[:, None])[None] | (
        positions[None, None, :] < prefix[:, None, None]
    )
    scores = jnp.einsum("sqe,ske->sqk", queries, key_rows, preferred_element_type=jnp.float32) * scale
    scores = jnp.where(allowed, scores, -1e30)
    expo = jnp.exp(scores - jnp.max(scores, axis=-1, keepdims=True))
    probs = expo / jnp.sum(expo, axis=-1, keepdims=True)
    probs_low = low(probs)
    mixed = low(
        jnp.einsum("sqk,ske->sqe", probs_low, value_rows, preferred_element_type=jnp.float32)
    ).reshape(tokens, HEAD)
    expanded = jnp.einsum("td,pde->tpe", hidden_mlp, expand_part, preferred_element_type=jnp.float32)
    expanded = expanded.reshape(tokens, -1) + expand_shift
    activated = low(gelu_exact(expanded))
    features = jnp.concatenate([mixed, activated], axis=1)
    partial = low(jnp.dot(features, out_part, preferred_element_type=jnp.float32))
    reduced = lax.psum_scatter(
        partial.reshape(sequences, SEQ, width), "ctx", scatter_dimension=1, tiled=True
    )
    layer_output = low(
        own_x.astype(jnp.float32) + reduced.astype(jnp.float32) + (dense_shift + shrink_shift)
    ).reshape(layer_input.shape)

    out_grads = low(contract_rows(features, g_all))
    grad_features = contract_cols(g_all, out_part)
    unused, gelu_back = jax.vjp(gelu_exact, expanded)
    grad_expanded = low(gelu_back(grad_features[:, HEAD:])[0])
    grad_mixed = low(grad_features[:, :HEAD]).reshape(sequences, SEQ, HEAD)
    expand_grads = low(contract_rows(hidden_mlp, grad_expanded))
    back_mlp = jnp.einsum(
        "tpe,pde->td",
        grad_expanded.reshape(tokens, -1, HEAD),
        expand_part,
        preferred_element_type=jnp.float32,
    )

    grad_probs = jnp.einsum("sqe,ske->sqk", grad_mixed, value_rows, preferred_element_type=jnp.float32)
    delta = jnp.sum(probs * grad_probs, axis=-1, keepdims=True)
    grad_scores = low(probs * (grad_probs - delta))
    grad_queries = (
        jnp.einsum("sqk,ske->sqe", grad_scores, key_rows, preferred_element_type=jnp.float32) * scale
    )
    grad_keys = (
        jnp.einsum("sqk,sqe->ske", grad_scores, queries, preferred_element_type=jnp.float32) * scale
    )
    grad_values = jnp.einsum("sqk,sqe->ske", probs_low, grad_mixed, preferred_element_type=jnp.float32)
    grad_joined = low(
        jnp.concatenate([turn(grad_queries, -sin_table), turn(grad_keys, -sin_table), grad_values], axis=-1)
    ).reshape(tokens, 3 * HEAD)
    qkv_grads = low(contract_rows(hidden_attn, grad_joined))
    back_attn = jnp.einsum(
        "tpe,pde->td",
        grad_joined.reshape(tokens, -1, HEAD),
        qkv_part,
        preferred_element_type=jnp.float32,
    )
    combined = low(back_attn * gain_attn + back_mlp * gain_mlp)
    def place(values, parts):
        board = jnp.zeros((parts, ctx_size, values.shape[0] // parts), jnp.float32)
        board = lax.dynamic_update_slice(board, values.reshape(parts, 1, -1), (0, me, 0))
        return board.reshape(devices, -1)

    joined_sum = jnp.sum(grad_joined.astype(jnp.float32), axis=0)
    expand_sum = jnp.sum(grad_expanded.astype(jnp.float32), axis=0)
    out_sum = jnp.sum(own_g.astype(jnp.float32), axis=(0, 1))
    board = jnp.concatenate(
        [
            place(joined_sum[: 2 * HEAD], 2),
            place(joined_sum[2 * HEAD :], 1),
            out_sum.reshape(devices, -1),
            place(expand_sum, dp_size),
            jnp.sum(back_attn * normal, axis=0).reshape(devices, -1),
            jnp.sum(back_attn, axis=0).reshape(devices, -1),
            jnp.sum(back_mlp * normal, axis=0).reshape(devices, -1),
            jnp.sum(back_mlp, axis=0).reshape(devices, -1),
        ],
        axis=1,
    )
    used = board.shape[1]
    board = jnp.pad(board, ((0, 0), (0, -used % 1024))).reshape(devices, -1, 128)
    combined, panel_grads, shrink_grad, dense_grad, tail = reduce_call(
        dp_size, ctx_size, combined.reshape(sequences, SEQ, width), qkv_grads, expand_grads, out_grads, board
    )
    combined = combined.astype(jnp.float32)
    panel_grads = jnp.transpose(panel_grads.astype(jnp.float32), (2, 0, 1, 3))
    qkv_grad = panel_grads[:, :3].reshape(row_share, 3 * width)
    expand_grad = panel_grads[:, 3:].reshape(row_share, ff)
    own = own_x.astype(jnp.float32)
    own_center = own - jnp.mean(own, axis=-1, keepdims=True)
    own_spread = lax.rsqrt(jnp.mean(own_center * own_center, axis=-1, keepdims=True) + 1e-05)
    own_normal = own_center * own_spread
    share = own_spread * (
        combined
        - jnp.mean(combined, axis=-1, keepdims=True)
        - own_normal * jnp.mean(combined * own_normal, axis=-1, keepdims=True)
    )
    input_grad = low(own_g.astype(jnp.float32) + share).reshape(layer_input.shape)

    tail = tail.reshape(-1)
    share_len = width // devices
    at = 0
    pieces = []
    for length in (2 * share_len, share_len, share_len, ff // devices, share_len, share_len, share_len, share_len):
        pieces.append(tail[at : at + length])
        at += length
    return (
        layer_output,
        input_grad,
        qkv_grad,
        pieces[0],
        pieces[1],
        dense_grad.astype(jnp.float32),
        pieces[2],
        expand_grad,
        pieces[3],
        shrink_grad.astype(jnp.float32),
        pieces[2],
        pieces[4],
        pieces[5],
        pieces[6],
        pieces[7],
    )


def solution(mesh):
    placed = (
        P(None, "dp", "ctx", None),
        P(None, "dp", "ctx", None),
        P(None, "dp"),
        P(("dp", "ctx"), None),
        P(("dp", "ctx")),
        P(("dp", "ctx"), None),
        P(("dp", "ctx")),
        P(("dp", "ctx"), None),
        P(("dp", "ctx")),
        P(("dp", "ctx"), None),
        P(("dp", "ctx")),
        P(("dp", "ctx")),
        P(("dp", "ctx")),
        P(("dp", "ctx")),
        P(("dp", "ctx")),
    )
    return jax.shard_map(
        tensor_shards if (mesh.shape["dp"], mesh.shape["ctx"]) == (4, HEADS) else shards,
        mesh=mesh,
        in_specs=placed,
        out_specs=(
            P(None, "dp", "ctx", None),
            P(None, "dp", "ctx", None),
            P(("dp", "ctx"), None),
            P(("dp", "ctx")),
            P(("dp", "ctx")),
            P(("dp", "ctx"), None),
            P(("dp", "ctx")),
            P(("dp", "ctx"), None),
            P(("dp", "ctx")),
            P(("dp", "ctx"), None),
            P(("dp", "ctx")),
            P(("dp", "ctx")),
            P(("dp", "ctx")),
            P(("dp", "ctx")),
            P(("dp", "ctx")),
        ),
        check_vma=False,
    )
```

```python
import functools
import math

import jax
import jax.numpy as jnp
from jax import lax
from jax.experimental import pallas as pl
from jax.experimental.pallas import tpu as pltpu
from jax.sharding import PartitionSpec as P

HEADS = 8
HEAD = 256
ROT = 64
SEQ = 1024


def norm_rows(inputs, norm_gain, norm_bias):
    row_mean = jnp.mean(inputs, axis=-1, keepdims=True)
    centered = inputs - row_mean
    variance = jnp.mean(centered * centered, axis=-1, keepdims=True)
    return centered * lax.rsqrt(variance + 1e-05) * norm_gain + norm_bias


def gelu_exact(values):
    return jax.nn.gelu(values, approximate=False)


def rope_tables(positions):
    freqs = jnp.exp(jnp.arange(ROT // 2, dtype=jnp.float32) * (-2.0 * math.log(10000.0) / ROT))
    angles = positions[:, None] * freqs[None, :]
    return (jnp.cos(angles), jnp.sin(angles))


def rotate(heads, cos_table, sin_table):
    half_rot = ROT // 2
    lower = heads[..., :half_rot]
    upper = heads[..., half_rot:ROT]
    cos_wide = cos_table[:, None, :]
    sin_wide = sin_table[:, None, :]
    return jnp.concatenate(
        [
            lower * cos_wide - upper * sin_wide,
            upper * cos_wide + lower * sin_wide,
            heads[..., ROT:],
        ],
        axis=-1,
    )


def unpack_small(packed, lengths, devices):
    table_rows = packed.reshape(devices, -1)
    members = []
    offset = 0
    for length in lengths:
        members.append(table_rows[:, offset : offset + length].reshape(-1).astype(jnp.float32))
        offset = offset + length
    return members


def contract_rows(left_mat, right_mat):
    return lax.dot_general(
        left_mat, right_mat, (((0,), (0,)), ((), ())), preferred_element_type=jnp.float32
    )


def contract_cols(left_mat, right_mat):
    return lax.dot_general(
        left_mat, right_mat, (((1,), (1,)), ((), ())), preferred_element_type=jnp.float32
    )


def shards(
    layer_input,
    out_grad,
    prefix_len,
    qkv_weight,
    qkv_bias,
    dense_weight,
    dense_bias,
    expand_weight,
    expand_bias,
    shrink_weight,
    shrink_bias,
    attn_gain,
    attn_shift,
    mlp_gain,
    mlp_shift,
):
    devices = lax.axis_size("dp") * lax.axis_size("ctx")
    ctx_index = lax.axis_index("ctx")
    micro, seq_count, span, width = layer_input.shape
    sequences = micro * seq_count
    rows = sequences * span
    heads_shape = (sequences, span, HEADS, HEAD)
    scale = 1.0 / math.sqrt(HEAD)
    attn_lengths = (attn_gain.shape[0], attn_shift.shape[0], qkv_bias.shape[0], dense_bias.shape[0])
    mlp_lengths = (
        mlp_gain.shape[0],
        mlp_shift.shape[0],
        expand_bias.shape[0],
        shrink_bias.shape[0],
    )
    attn_packed = jnp.concatenate([attn_gain, attn_shift, qkv_bias, dense_bias])
    mlp_packed = jnp.concatenate([mlp_gain, mlp_shift, expand_bias, shrink_bias])

    def fetch_attn():
        return (
            lax.all_gather(qkv_weight, ("dp", "ctx"), axis=0, tiled=True),
            lax.all_gather(dense_weight, ("dp", "ctx"), axis=0, tiled=True),
            lax.all_gather(attn_packed, ("dp", "ctx"), axis=0, tiled=True),
        )

    def fetch_mlp():
        return (
            lax.all_gather(expand_weight, ("dp", "ctx"), axis=0, tiled=True),
            lax.all_gather(shrink_weight, ("dp", "ctx"), axis=0, tiled=True),
            lax.all_gather(mlp_packed, ("dp", "ctx"), axis=0, tiled=True),
        )

    local_pos = ctx_index * span + jnp.arange(span, dtype=jnp.int32)
    cos_table, sin_table = rope_tables(local_pos.astype(jnp.float32))
    key_pos = jnp.arange(SEQ, dtype=jnp.int32)
    causal = key_pos[None, :] <= local_pos[:, None]
    inputs = layer_input.astype(jnp.float32).reshape(rows, width)
    cot_rows = out_grad.reshape(rows, width)
    cot_float = cot_rows.astype(jnp.float32)
    prefix = prefix_len.reshape(sequences)
    allowed = (causal[None] | (key_pos[None, None, :] < prefix[:, None, None]))[:, None]
    attn_set = fetch_attn()
    qkv_full, dense_full, attn_small = attn_set
    gain_attn, shift_attn, joined_shift, dense_shift = unpack_small(
        attn_small, attn_lengths, devices
    )
    hidden_attn = norm_rows(inputs, gain_attn, shift_attn).astype(jnp.bfloat16)
    joined = jnp.dot(hidden_attn, qkv_full, preferred_element_type=jnp.float32) + joined_shift
    queries = rotate(joined[:, :width].reshape(heads_shape), cos_table, sin_table).astype(
        jnp.bfloat16
    )
    key_rows = rotate(
        joined[:, width : 2 * width].reshape(heads_shape), cos_table, sin_table
    ).astype(jnp.bfloat16)
    value_rows = joined[:, 2 * width :].reshape(heads_shape).astype(jnp.bfloat16)
    all_keys, all_values = (
        lax.all_gather(key_rows, "ctx", axis=1, tiled=True),
        lax.all_gather(value_rows, "ctx", axis=1, tiled=True),
    )
    scores = (
        jnp.einsum("sqhe,skhe->shqk", queries, all_keys, preferred_element_type=jnp.float32) * scale
    )
    scores = jnp.where(allowed, scores, -1e30)
    row_max = jnp.max(scores, axis=-1, keepdims=True)
    expo = jnp.exp(scores - row_max)
    row_total = jnp.sum(expo, axis=-1, keepdims=True)
    log_total = row_max + jnp.log(row_total)
    probs_low = (expo / row_total).astype(jnp.bfloat16)
    mixed = jnp.einsum("shqk,skhe->sqhe", probs_low, all_values, preferred_element_type=jnp.float32)
    mixed = mixed.reshape(rows, width).astype(jnp.bfloat16)
    attn_out = jnp.dot(mixed, dense_full, preferred_element_type=jnp.float32) + dense_shift
    mlp_set = fetch_mlp()
    expand_full, shrink_full, mlp_small = mlp_set
    gain_mlp, shift_mlp, expand_shift, shrink_shift = unpack_small(mlp_small, mlp_lengths, devices)
    hidden_mlp = norm_rows(inputs, gain_mlp, shift_mlp).astype(jnp.bfloat16)
    expanded = jnp.dot(hidden_mlp, expand_full, preferred_element_type=jnp.float32) + expand_shift
    activated = gelu_exact(expanded).astype(jnp.bfloat16)
    mlp_out = jnp.dot(activated, shrink_full, preferred_element_type=jnp.float32) + shrink_shift
    layer_output = (
        (inputs + attn_out + mlp_out).astype(jnp.bfloat16).reshape(micro, seq_count, span, width)
    )
    attn_back_set = fetch_attn()
    qkv_back, dense_back, attn_small_back = attn_back_set
    gain_attn, shift_attn, joined_shift, dense_shift = unpack_small(
        attn_small_back, attn_lengths, devices
    )
    grad_out_shift = jnp.sum(cot_float, axis=0)
    grad_mixed = contract_cols(cot_rows, dense_back).astype(jnp.bfloat16).reshape(heads_shape)
    again = (
        jnp.einsum("sqhe,skhe->shqk", queries, all_keys, preferred_element_type=jnp.float32) * scale
    )
    again = jnp.where(allowed, again, -1e30)
    probs = jnp.exp(again - log_total)
    grad_probs = jnp.einsum(
        "sqhe,skhe->shqk", grad_mixed, all_values, preferred_element_type=jnp.float32
    )
    delta = jnp.sum(probs * grad_probs, axis=-1, keepdims=True)
    grad_scores = (probs * (grad_probs - delta)).astype(jnp.bfloat16)
    grad_queries = (
        jnp.einsum("shqk,skhe->sqhe", grad_scores, all_keys, preferred_element_type=jnp.float32)
        * scale
    )
    all_queries, all_grad_mixed = (
        lax.all_gather(queries, "ctx", axis=1, tiled=True),
        lax.all_gather(grad_mixed, "ctx", axis=1, tiled=True),
    )
    stat_lse = jnp.transpose(log_total[..., 0], (0, 2, 1))
    stat_delta = jnp.transpose(delta[..., 0], (0, 2, 1))
    lse_all, delta_all = (
        lax.all_gather(stat_lse, "ctx", axis=1, tiled=True),
        lax.all_gather(stat_delta, "ctx", axis=1, tiled=True),
    )
    lse_all = jnp.transpose(lse_all, (0, 2, 1))[..., None]
    delta_all = jnp.transpose(delta_all, (0, 2, 1))[..., None]
    key_allowed = (local_pos[None, :] <= key_pos[:, None])[None] | (
        local_pos[None, None, :] < prefix[:, None, None]
    )
    block_scores = (
        jnp.einsum("sqhe,skhe->shqk", all_queries, key_rows, preferred_element_type=jnp.float32)
        * scale
    )
    block_scores = jnp.where(key_allowed[:, None], block_scores, -1e30)
    block_probs = jnp.exp(block_scores - lse_all)
    block_grad_probs = jnp.einsum(
        "sqhe,skhe->shqk", all_grad_mixed, value_rows, preferred_element_type=jnp.float32
    )
    block_grad_scores = (block_probs * (block_grad_probs - delta_all)).astype(jnp.bfloat16)
    own_keys = (
        jnp.einsum(
            "shqk,sqhe->skhe", block_grad_scores, all_queries, preferred_element_type=jnp.float32
        )
        * scale
    )
    own_values = jnp.einsum(
        "shqk,sqhe->skhe",
        block_probs.astype(jnp.bfloat16),
        all_grad_mixed,
        preferred_element_type=jnp.float32,
    )
    grad_joined = jnp.concatenate(
        [
            rotate(grad_queries, cos_table, -sin_table).reshape(rows, width),
            rotate(own_keys, cos_table, -sin_table).reshape(rows, width),
            own_values.reshape(rows, width),
        ],
        axis=1,
    ).astype(jnp.bfloat16)
    grad_joined_shift = jnp.sum(grad_joined.astype(jnp.float32), axis=0)
    grad_hidden_attn = contract_cols(grad_joined, qkv_back)
    unused_attn, attn_back = jax.vjp(norm_rows, inputs, gain_attn, shift_attn)
    grad_in_attn, grad_gain_attn, grad_shift_attn = attn_back(grad_hidden_attn)
    attn_columns = jnp.concatenate(
        [
            grad_gain_attn[:, None],
            grad_shift_attn[:, None],
            grad_joined_shift[: 2 * width].reshape(width, 2),
            grad_joined_shift[2 * width :][:, None],
            grad_out_shift[:, None],
        ],
        axis=1,
    )
    hidden_part = hidden_attn
    small_part = attn_columns
    attn_grads = lax.psum_scatter(
        jnp.concatenate(
            [contract_rows(hidden_part, grad_joined), contract_rows(mixed, cot_rows), small_part],
            axis=1,
        ),
        ("dp", "ctx"),
        scatter_dimension=0,
        tiled=True,
    )
    qkv_grad = attn_grads[:, : 3 * width]
    dense_grad = attn_grads[:, 3 * width : 4 * width]
    attn_tail = attn_grads[:, 4 * width :]
    mlp_back_set = fetch_mlp()
    expand_back, shrink_back, mlp_small_back = mlp_back_set
    gain_mlp, shift_mlp, expand_shift, shrink_shift = unpack_small(
        mlp_small_back, mlp_lengths, devices
    )
    unused_gelu, gelu_back = jax.vjp(gelu_exact, expanded)
    grad_act = contract_cols(cot_rows, shrink_back)
    grad_expanded = gelu_back(grad_act)[0].astype(jnp.bfloat16)
    grad_expand_shift = jnp.sum(grad_expanded.astype(jnp.float32), axis=0)
    grad_hidden_mlp = contract_cols(grad_expanded, expand_back)
    unused_mlp, mlp_back = jax.vjp(norm_rows, inputs, gain_mlp, shift_mlp)
    grad_in_mlp, grad_gain_mlp, grad_shift_mlp = mlp_back(grad_hidden_mlp)
    ratio = expand_shift.shape[0] // width
    mlp_columns = jnp.concatenate(
        [
            grad_gain_mlp[:, None],
            grad_shift_mlp[:, None],
            grad_expand_shift.reshape(width, ratio),
            grad_out_shift[:, None],
        ],
        axis=1,
    )
    ff_width = expand_back.shape[1]
    hidden_part = hidden_mlp
    small_part = mlp_columns
    expand_grads = lax.psum_scatter(
        jnp.concatenate([contract_rows(hidden_part, grad_expanded), small_part], axis=1),
        ("dp", "ctx"),
        scatter_dimension=0,
        tiled=True,
    )
    shrink_grad = lax.psum_scatter(
        contract_rows(activated, cot_rows), ("dp", "ctx"), scatter_dimension=0, tiled=True
    )
    expand_grad = expand_grads[:, :ff_width]
    mlp_tail = expand_grads[:, ff_width:]
    input_grad = (
        (cot_float + grad_in_attn + grad_in_mlp)
        .astype(jnp.bfloat16)
        .reshape(micro, seq_count, span, width)
    )
    return (
        layer_output,
        input_grad,
        qkv_grad,
        attn_tail[:, 2:4].reshape(-1),
        attn_tail[:, 4],
        dense_grad,
        attn_tail[:, 5],
        expand_grad,
        mlp_tail[:, 2 : 2 + ratio].reshape(-1),
        shrink_grad,
        mlp_tail[:, 2 + ratio],
        attn_tail[:, 0],
        attn_tail[:, 1],
        mlp_tail[:, 0],
        mlp_tail[:, 1],
    )


def low(values):
    return values.astype(jnp.bfloat16)


MESH_ID = pl.DeviceIdType.MESH


def remote(src, dst, send_sem, recv_sem, dp, ctx):
    return pltpu.make_async_remote_copy(
        src_ref=src,
        dst_ref=dst,
        send_sem=send_sem,
        recv_sem=recv_sem,
        device_id=(dp, ctx),
        device_id_type=MESH_ID,
    )


def greet_all(dp, ctx, dp_size, ctx_size):
    barrier = pltpu.get_barrier_semaphore()
    devices = dp_size * ctx_size
    me = dp * ctx_size + ctx

    def greet(step, carry):
        other = lax.rem(me + step, devices)
        pl.semaphore_signal(
            barrier, inc=1, device_id=(other // ctx_size, lax.rem(other, ctx_size)), device_id_type=MESH_ID
        )
        return carry

    lax.fori_loop(1, devices, greet, 0)
    pl.semaphore_wait(barrier, devices - 1)


def gather_kernel(
    dp_size,
    ctx_size,
    x,
    qkv,
    expand,
    dense,
    shrink,
    packed,
    x_all,
    panels,
    out_w,
    small,
    local_sem,
    small_sem,
    block_send,
    block_recv,
    core_send,
    core_recv,
    panel_send,
    panel_recv,
    share_send,
    share_recv,
    pass_send,
    pass_recv,
):
    d = lax.axis_index("dp")
    c = lax.axis_index("ctx")
    z = c // 2
    sibling = c + 1 - 2 * lax.rem(c, 2)
    x_mate = d + 1 - 2 * lax.rem(d, 2)
    y_mate = lax.rem(d + 2, 4)
    micro, span = x.shape[0], x.shape[1]
    devices = dp_size * ctx_size
    me = d * ctx_size + c
    rows = qkv.shape[0]
    unit = shrink.shape[0]
    levels = ctx_size // 2
    panel_rows = ctx_size * rows
    n_panels = 3 + dp_size

    greet_all(d, c, dp_size, ctx_size)

    def column_block(panel, target):
        if panel < 3:
            start = panel * (qkv.shape[1] // 3) + target * HEAD
            return qkv.at[:, pl.ds(pl.multiple_of(start, HEAD), HEAD)]
        start = (panel - 3) * ctx_size * unit + target * unit
        return expand.at[:, pl.ds(pl.multiple_of(start, HEAD), HEAD)]

    own_rows = pl.ds(pl.multiple_of((d * ctx_size + c) * rows, rows), rows)

    for panel in range(n_panels):
        pltpu.make_async_copy(
            column_block(panel, c), panels.at[panel, own_rows], local_sem.at[panel]
        ).start()

        def push(step, carry, panel=panel):
            target = lax.rem(c + step, ctx_size)
            remote(
                column_block(panel, target),
                panels.at[panel, own_rows],
                panel_send.at[panel],
                panel_recv.at[panel],
                d,
                target,
            ).start()
            return carry

        lax.fori_loop(1, ctx_size, push, 0)

    def shrink_rows(owner, offset, count):
        return out_w.at[pl.ds(pl.multiple_of(HEAD + owner * unit + offset, 16), count)]

    shrink_local = pltpu.make_async_copy(shrink, shrink_rows(d, 0, unit), local_sem.at[n_panels])
    shrink_local.start()
    for way, mate in ((0, x_mate), (1, y_mate)):
        remote(
            shrink, shrink_rows(d, 0, unit), share_send.at[n_panels, way], share_recv.at[n_panels, way], mate, c
        ).start()

    per_head = HEAD // rows
    head_of = (d * ctx_size + c) // per_head
    dense_rows = pl.ds(pl.multiple_of(lax.rem(c, per_head) * rows, rows), rows)
    dense_out = remote(dense, out_w.at[dense_rows], panel_send.at[n_panels], panel_recv.at[n_panels], d, head_of)
    dense_own = pltpu.make_async_copy(dense, out_w.at[dense_rows], local_sem.at[n_panels + 1])
    stays = head_of == c

    @pl.when(stays)
    def _():
        dense_own.start()

    @pl.when(jnp.logical_not(stays))
    def _():
        dense_out.start()

    def block(origin, m):
        return x_all.at[m, pl.ds(pl.multiple_of(origin * span, span), span)]

    x_local = []
    for m in range(micro):
        copy = pltpu.make_async_copy(x.at[m], block(c, m), local_sem.at[n_panels + 2 + m])
        copy.start()
        x_local.append(copy)

    def chain(way, hop, m):
        step = 2 if way == 0 else -2
        origin = c - step * hop
        src = x.at[m] if hop == 0 else block(origin, m)
        exists = jnp.logical_and(z >= hop, z <= levels - 2) if way == 0 else jnp.logical_and(
            z + hop <= levels - 1, z >= 1
        )
        copy = remote(src, block(origin, m), block_send.at[way, hop, m], block_recv.at[way, hop, m], d, c + step)
        return exists, copy

    def arrives(way, hop):
        return z >= hop + 1 if way == 0 else z + hop + 1 <= levels - 1

    def core_copy(slot, origin, m):
        src = x.at[m] if slot == 0 else block(origin, m)
        return remote(src, block(origin, m), core_send.at[slot, m], core_recv.at[slot, m], d, sibling)

    for m in range(micro):
        core_copy(0, c, m).start()
        for way in range(2):
            exists, copy = chain(way, 0, m)

            @pl.when(exists)
            def _(copy=copy):
                copy.start()

    small_copy = pltpu.make_async_copy(packed, small.at[me], local_sem.at[n_panels + 2 + micro])
    small_copy.start()

    def push_small(step, carry):
        other = lax.rem(me + step, devices)
        remote(
            packed,
            small.at[me],
            small_sem.at[0],
            small_sem.at[1],
            other // ctx_size,
            lax.rem(other, ctx_size),
        ).start()
        return carry

    lax.fori_loop(1, devices, push_small, 0)

    def slot_of(way, hop):
        return 1 + way * (levels - 1) + hop

    def hop_step(hop):
        for m in range(micro):
            for way in range(2):
                step = 2 if way == 0 else -2

                @pl.when(arrives(way, hop))
                def _(way=way, m=m, step=step):
                    origin = c - step * (hop + 1)
                    remote(
                        block(origin, m), block(origin, m), block_send.at[way, hop, m], block_recv.at[way, hop, m], d, c - step
                    ).wait_recv()
                    core_copy(slot_of(way, hop), origin, m).start()

                if hop + 1 <= levels - 2:
                    exists, copy = chain(way, hop + 1, m)

                    @pl.when(exists)
                    def _(copy=copy):
                        copy.start()

    def group_rows(owner, offset, count):
        return pl.ds(pl.multiple_of(owner * panel_rows + offset, 16), count)

    def panel_share(panel, way, mate):
        view = panels.at[panel, group_rows(d, 0, panel_rows)]
        return remote(view, view, share_send.at[panel, way], share_recv.at[panel, way], mate, c)

    def panel_step(panel):
        pltpu.make_async_copy(column_block(panel, c), panels.at[panel, own_rows], local_sem.at[panel]).wait()
        whole = panels.at[panel, group_rows(d, 0, (ctx_size - 1) * rows)]
        remote(whole, whole, panel_send.at[panel], panel_recv.at[panel], d, sibling).wait_recv()
        panel_share(panel, 0, x_mate).start()
        panel_share(panel, 1, y_mate).start()

    half = panel_rows // 2

    def panel_pass(panel, way):
        owner, mate = ((x_mate, y_mate), (y_mate, x_mate))[way]
        view = panels.at[panel, group_rows(owner, way * half, half)]
        return remote(view, view, pass_send.at[panel, way], pass_recv.at[panel, way], mate, c)

    def panel_forward(panel):
        for way, owner in ((0, x_mate), (1, y_mate)):
            view = panels.at[panel, group_rows(owner, 0, panel_rows)]
            remote(view, view, share_send.at[panel, way], share_recv.at[panel, way], owner, c).wait_recv()
            panel_pass(panel, way).start()

    def shrink_share_wait(way, owner):
        view = shrink_rows(owner, 0, unit)
        remote(view, view, share_send.at[n_panels, way], share_recv.at[n_panels, way], owner, c).wait_recv()

    def shrink_pass(way):
        owner, mate = ((x_mate, y_mate), (y_mate, x_mate))[way]
        view = shrink_rows(owner, way * (unit // 2), unit // 2)
        return remote(view, view, pass_send.at[n_panels, way], pass_recv.at[n_panels, way], mate, c)

    source = c // (ctx_size // dp_size)
    at_source = d == source
    from_x = x_mate == source
    from_y = y_mate == source
    head_rows = out_w.at[pl.ds(0, HEAD)]
    half_head = HEAD // 2

    def dense_share(way, mate):
        return remote(head_rows, head_rows, share_send.at[n_panels + 1, way], share_recv.at[n_panels + 1, way], mate, c)

    def dense_pass(way, mate):
        view = out_w.at[pl.ds(way * half_head, half_head)]
        return remote(view, view, pass_send.at[n_panels + 1, way], pass_recv.at[n_panels + 1, way], mate, c)

    owns_share = jnp.logical_and(at_source, stays)

    def dense_gather_step():
        @pl.when(owns_share)
        def _():
            dense_own.wait()
            view = out_w.at[pl.ds(0, (per_head - 1) * rows)]
            remote(view, view, panel_send.at[n_panels], panel_recv.at[n_panels], d, sibling).wait_recv()

        @pl.when(jnp.logical_and(at_source, jnp.logical_not(stays)))
        def _():
            remote(head_rows, head_rows, panel_send.at[n_panels], panel_recv.at[n_panels], d, sibling).wait_recv()

        @pl.when(at_source)
        def _():
            dense_share(0, x_mate).start()
            dense_share(1, y_mate).start()

    def dense_forward_step():
        @pl.when(from_x)
        def _():
            dense_share(0, x_mate).wait_recv()
            dense_pass(0, y_mate).start()

        @pl.when(from_y)
        def _():
            dense_share(1, y_mate).wait_recv()
            dense_pass(1, x_mate).start()

    across = jnp.logical_not(jnp.logical_or(at_source, jnp.logical_or(from_x, from_y)))

    for panel in range(3):
        panel_step(panel)
    shrink_share_wait(0, x_mate)
    shrink_pass(0).start()
    shrink_share_wait(1, y_mate)
    shrink_pass(1).start()
    dense_gather_step()
    hop_step(0)
    for panel in range(3, n_panels):
        panel_step(panel)
        panel_forward(panel - 3)
    hop_step(1)
    dense_forward_step()
    for panel in range(n_panels - 3, n_panels):
        panel_forward(panel)
    for hop in range(2, levels - 1):
        hop_step(hop)

    for panel in range(n_panels):
        for way, mate in ((0, x_mate), (1, y_mate)):
            panel_share(panel, way, mate).wait_send()
            panel_pass(panel, way).wait_send()
        for way in range(2):
            diagonal = 3 - d
            view = panels.at[panel, group_rows(diagonal, way * half, half)]
            remote(view, view, pass_send.at[panel, way], pass_recv.at[panel, way], x_mate, c).wait_recv()
        whole = panels.at[panel, group_rows(d, 0, (ctx_size - 1) * rows)]
        remote(whole, whole, panel_send.at[panel], panel_recv.at[panel], x_mate, c).wait_send()
    shrink_local.wait()
    for way in range(2):
        mate = (x_mate, y_mate)[way]
        remote(
            shrink, shrink_rows(d, 0, unit), share_send.at[n_panels, way], share_recv.at[n_panels, way], mate, c
        ).wait_send()
        shrink_pass(way).wait_send()
        view = shrink_rows(3 - d, way * (unit // 2), unit // 2)
        remote(view, view, pass_send.at[n_panels, way], pass_recv.at[n_panels, way], mate, c).wait_recv()

    @pl.when(jnp.logical_not(stays))
    def _():
        dense_out.wait_send()

    @pl.when(at_source)
    def _():
        dense_share(0, x_mate).wait_send()
        dense_share(1, y_mate).wait_send()

    @pl.when(from_x)
    def _():
        dense_pass(0, y_mate).wait_send()

    @pl.when(from_y)
    def _():
        dense_pass(1, x_mate).wait_send()

    @pl.when(across)
    def _():
        dense_pass(0, y_mate).wait_recv()
        dense_pass(1, x_mate).wait_recv()

    for m in range(micro):
        x_local[m].wait()
        core_copy(0, c, m).wait_send()
        core_copy(0, sibling, m).wait_recv()
        for way in range(2):
            step = 2 if way == 0 else -2
            for hop in range(levels - 1):
                exists, copy = chain(way, hop, m)

                @pl.when(exists)
                def _(copy=copy):
                    copy.wait_send()

                @pl.when(arrives(way, hop))
                def _(way=way, hop=hop, m=m, step=step):
                    slot = slot_of(way, hop)
                    core_copy(slot, c - step * (hop + 1), m).wait_send()
                    core_copy(slot, sibling - step * (hop + 1), m).wait_recv()

    small_copy.wait()
    rest = small.at[pl.ds(0, devices - 1)]
    remote(rest, rest, small_sem.at[0], small_sem.at[1], d, sibling).wait()


def gather_call(dp_size, ctx_size, x, qkv, expand, dense, shrink, packed):
    micro, span, width = x.shape
    rows = qkv.shape[0]
    n_panels = 3 + dp_size
    levels = ctx_size // 2
    devices = dp_size * ctx_size
    dma = pltpu.SemaphoreType.DMA
    out_shape = (
        jax.ShapeDtypeStruct((micro, ctx_size * span, width), x.dtype),
        jax.ShapeDtypeStruct((n_panels, devices * rows, HEAD), x.dtype),
        jax.ShapeDtypeStruct((HEAD + dp_size * shrink.shape[0], width), x.dtype),
        jax.ShapeDtypeStruct((devices,) + packed.shape, x.dtype),
    )
    anywhere = pl.BlockSpec(memory_space=pl.ANY)
    return pl.pallas_call(
        functools.partial(gather_kernel, dp_size, ctx_size),
        out_shape=out_shape,
        in_specs=[anywhere] * 6,
        out_specs=(anywhere,) * 4,
        scratch_shapes=[
            dma((n_panels + 3 + micro,)),
            dma((2,)),
            dma((2, levels - 1, micro)),
            dma((2, levels - 1, micro)),
            dma((2 * levels - 1, micro)),
            dma((2 * levels - 1, micro)),
            dma((n_panels + 1,)),
            dma((n_panels + 1,)),
            dma((n_panels + 2, 2)),
            dma((n_panels + 2, 2)),
            dma((n_panels + 2, 2)),
            dma((n_panels + 2, 2)),
        ],
        compiler_params=pltpu.CompilerParams(collective_id=1, has_side_effects=True),
        name="gather_all",
    )(x, qkv, expand, dense, shrink, packed)


def add_into(dst, srcs, rows):
    chunk = 16 if dst.shape[-1] > 1024 else 64

    def step(index, carry):
        at = pl.ds(pl.multiple_of(index * chunk, 16), chunk)
        total = srcs[0][at, :].astype(jnp.float32)
        for src in srcs[1:]:
            total = total + src[at, :].astype(jnp.float32)
        dst[at, :] = total.astype(dst.dtype)
        return carry

    lax.fori_loop(0, rows // chunk, step, 0)


def reduce_kernel(
    dp_size,
    ctx_size,
    back,
    qkv_grads,
    expand_grads,
    out_grads,
    board,
    back_out,
    panel_out,
    shrink_out,
    dense_out,
    tail_out,
    back_own,
    back_core,
    back_chain,
    panel_own,
    panel_recv,
    panel_last,
    shrink_own,
    shrink_recv,
    shrink_last,
    dense_own,
    dense_recv,
    board_recv,
    load_sem,
    core_send,
    core_recv,
    chain_send,
    chain_recv,
    first_send,
    first_recv,
    last_send,
    last_recv,
    out_send,
    out_recv,
    dense_send,
    dense_sem,
    board_sem,
    store_sem,
):
    d = lax.axis_index("dp")
    c = lax.axis_index("ctx")
    z = c // 2
    core = lax.rem(c, 2)
    sibling = c + 1 - 2 * core
    x_mate = d + 1 - 2 * lax.rem(d, 2)
    y_mate = lax.rem(d + 2, 4)
    diagonal = 3 - d
    micro = back.shape[0]
    span = back.shape[1] // ctx_size
    levels = ctx_size // 2
    devices = dp_size * ctx_size
    me = d * ctx_size + c
    n_panels = 3 + dp_size
    group_rows = qkv_grads.shape[0] // dp_size
    half = group_rows // 2
    rows = group_rows // ctx_size
    unit = (out_grads.shape[0] - HEAD) // dp_size
    shrink_half = unit // 2
    head_half = HEAD // 2

    greet_all(d, c, dp_size, ctx_size)

    def back_view(parity, level, m):
        start = (2 * level + parity) * span
        return back.at[m, pl.ds(pl.multiple_of(start, span), span)]

    def back_load(level, m):
        return pltpu.make_async_copy(back_view(core, level, m), back_own.at[level, m], load_sem.at[0, level * micro + m])

    def core_copy(level, m):
        return remote(
            back_view(1 - core, level, m),
            back_core.at[level, m],
            core_send.at[level, m],
            core_recv.at[level, m],
            d,
            sibling,
        )

    order = []
    for pair in range((levels + 1) // 2):
        for level in (levels - 1 - pair, pair):
            if level not in order:
                order.append(level)
    for level in order:
        for m in range(micro):
            core_copy(level, m).start()
            back_load(level, m).start()

    mates = ((x_mate, y_mate), (y_mate, x_mate))

    def panel_view(panel, owner, way):
        at = pl.ds(pl.multiple_of(owner * group_rows + way * half, 16), half)
        if panel < 3:
            return qkv_grads.at[at, pl.ds(panel * HEAD, HEAD)]
        return expand_grads.at[at, pl.ds((panel - 3) * HEAD, HEAD)]

    def shrink_view(owner, way):
        return out_grads.at[pl.ds(pl.multiple_of(HEAD + owner * unit + way * shrink_half, 16), shrink_half)]

    def first_copies(index, view, recv):
        copies = []
        for way in range(2):
            mate = mates[way][0]
            for slot, owner in ((0, mate), (1, diagonal)):
                copies.append(
                    remote(
                        view(owner, way),
                        recv.at[way, slot],
                        first_send.at[index, way, slot],
                        first_recv.at[index, way, slot],
                        mate,
                        c,
                    )
                )
        return copies

    def own_loads(index, view, own):
        copies = []
        for way in range(2):
            for slot, owner in ((0, d), (1, mates[way][1])):
                copies.append(
                    pltpu.make_async_copy(view(owner, way), own.at[way, slot], load_sem.at[1 + index, way * 2 + slot])
                )
        return copies

    def last_copies(index, own, last):
        return [
            remote(
                own.at[way, 1], last.at[way], last_send.at[index, way], last_recv.at[index, way], mates[way][1], c
            )
            for way in range(2)
        ]

    def unit_parts(index):
        if index < n_panels:
            return (
                functools.partial(panel_view, index),
                panel_own.at[index],
                panel_recv.at[index],
                panel_last.at[index],
                half,
            )
        return shrink_view, shrink_own, shrink_recv, shrink_last, shrink_half

    def open_unit(index):
        view, own, recv, last, count = unit_parts(index)
        for copy in first_copies(index, view, recv) + own_loads(index, view, own):
            copy.start()

    def first_step(index):
        view, own, recv, last, count = unit_parts(index)
        arrivals = first_copies(index, view, recv)
        loads = own_loads(index, view, own)
        sends = last_copies(index, own, last)
        for way in range(2):
            arrivals[way * 2 + 1].wait_recv()
            loads[way * 2 + 1].wait()
            add_into(own.at[way, 1], (own.at[way, 1], recv.at[way, 1]), count)
            sends[way].start()

    def last_step(index):
        view, own, recv, last, count = unit_parts(index)
        arrivals = first_copies(index, view, recv)
        loads = own_loads(index, view, own)
        ends = last_copies(index, own, last)
        for way in range(2):
            arrivals[way * 2].wait_recv()
            loads[way * 2].wait()
            ends[way].wait_recv()
            add_into(own.at[way, 0], (own.at[way, 0], recv.at[way, 0], last.at[way]), count)

    def close_unit(index):
        view, own, recv, last, count = unit_parts(index)
        for copy in first_copies(index, view, recv) + last_copies(index, own, last):
            copy.wait_send()

    per_half = half // rows

    def panel_chunk(panel, target):
        start = pl.multiple_of(lax.rem(target, per_half) * rows, rows)
        return panel_own.at[panel, target // per_half, 0, pl.ds(start, rows)]

    def panel_local(panel):
        return pltpu.make_async_copy(panel_chunk(panel, c), panel_out.at[panel, c], store_sem.at[panel])

    def send_panel(panel):
        def push(step, carry):
            target = lax.rem(c + step, ctx_size)
            remote(
                panel_chunk(panel, target), panel_out.at[panel, c], out_send.at[panel], out_recv.at[panel], d, target
            ).start()
            return carry

        lax.fori_loop(1, ctx_size, push, 0)
        panel_local(panel).start()

    def end_panel(panel):
        rest = panel_out.at[panel, pl.ds(0, ctx_size - 1)]
        remote(rest, rest, out_send.at[panel], out_recv.at[panel], d, sibling).wait()
        panel_local(panel).wait()

    source = c // (ctx_size // dp_size)
    at_source = d == source
    from_x = x_mate == source
    from_y = y_mate == source
    across = diagonal == source
    per_head = HEAD // rows

    def dense_half(way):
        return out_grads.at[pl.ds(way * head_half, head_half)]

    def dense_copy(way, src, slot, mate):
        return remote(src, dense_recv.at[slot], dense_send.at[way], dense_sem.at[slot], mate, c)

    dense_load = pltpu.make_async_copy(out_grads.at[pl.ds(0, HEAD)], dense_own, load_sem.at[0, levels * micro])
    dense_load.start()

    @pl.when(across)
    def _():
        dense_copy(0, dense_half(0), 0, y_mate).start()
        dense_copy(1, dense_half(1), 0, x_mate).start()

    def middle(mate, mine, axis):
        own = dense_own.at[pl.ds(mine * head_half, head_half)]
        dense_copy(1 - mine, dense_half(1 - mine), 1 + 2 * axis + 1 - mine, mate).start()
        dense_copy(mine, own, 0, mate).wait_recv()
        add_into(own, (own, dense_recv.at[0]), head_half)
        dense_copy(mine, own, 1 + 2 * axis + mine, mate).start()

    def dense_chunk(piece):
        return dense_own.at[pl.ds(piece * rows, rows)]

    first_owner = lax.rem(c, ctx_size // per_head) * per_head

    def dense_send_out(piece):
        return remote(
            dense_chunk(piece), dense_out, dense_send.at[2 + piece], dense_sem.at[5], d, first_owner + piece
        )

    def dense_store(piece):
        return pltpu.make_async_copy(dense_chunk(piece), dense_out, store_sem.at[n_panels])

    board_load = pltpu.make_async_copy(board.at[me], board_recv.at[me], load_sem.at[0, levels * micro + 1])
    board_load.start()

    def push_board(step, carry):
        other = lax.rem(me + step, devices)
        remote(
            board.at[other],
            board_recv.at[me],
            board_sem.at[0],
            board_sem.at[1],
            other // ctx_size,
            lax.rem(other, ctx_size),
        ).start()
        return carry

    lax.fori_loop(1, devices, push_board, 0)

    for index in range(n_panels):
        open_unit(index)

    for level in order:
        for m in range(micro):
            back_load(level, m).wait()
            core_copy(level, m).wait_recv()
            add_into(back_own.at[level, m], (back_own.at[level, m], back_core.at[level, m]), span)

    def chain_copy(way, level, m):
        return remote(
            back_own.at[level, m],
            back_chain.at[way, level, m],
            chain_send.at[way, level, m],
            chain_recv.at[way, level, m],
            d,
            c + (2 if way == 0 else -2),
        )

    def sends(way, level):
        return z < level if way == 0 else z > level

    def hears(way, level):
        if way == 0:
            return jnp.logical_and(z >= 1, z <= level)
        return jnp.logical_and(z <= levels - 2, z >= level)

    def chain_step(way, level):
        for m in range(micro):
            @pl.when(jnp.logical_and(sends(way, level), hears(way, level)))
            def _(m=m):
                chain_copy(way, level, m).wait_recv()
                add_into(back_own.at[level, m], (back_own.at[level, m], back_chain.at[way, level, m]), span)

            @pl.when(sends(way, level))
            def _(m=m):
                chain_copy(way, level, m).start()

    def chain_end():
        for level in range(levels):
            for m in range(micro):
                for way in range(2):
                    @pl.when(jnp.logical_and(z == level, hears(way, level)))
                    def _(way=way, level=level, m=m):
                        chain_copy(way, level, m).wait_recv()
                        add_into(back_own.at[level, m], (back_own.at[level, m], back_chain.at[way, level, m]), span)

                @pl.when(z == level)
                def _(level=level, m=m):
                    pltpu.make_async_copy(back_own.at[level, m], back_out.at[m], store_sem.at[n_panels + 2 + m]).start()

    chain_step(0, levels - 1)
    chain_step(1, 0)
    first_step(0)
    first_step(1)
    dense_load.wait()

    @pl.when(from_x)
    def _():
        middle(x_mate, 0, 0)

    @pl.when(from_y)
    def _():
        middle(y_mate, 1, 1)

    first_step(2)
    last_step(0)
    send_panel(0)
    chain_step(0, levels - 2)
    chain_step(1, 1)
    first_step(3)
    last_step(1)
    send_panel(1)
    open_unit(n_panels)
    first_step(4)
    last_step(2)
    send_panel(2)

    @pl.when(at_source)
    def _():
        for slot in range(1, 5):
            dense_copy(0, dense_half(0), slot, x_mate).wait_recv()
        for way in range(2):
            own = dense_own.at[pl.ds(way * head_half, head_half)]
            add_into(own, (own, dense_recv.at[1 + way], dense_recv.at[3 + way]), head_half)
        for piece in range(per_head):
            @pl.when(first_owner + piece == c)
            def _(piece=piece):
                dense_store(piece).start()

            @pl.when(first_owner + piece != c)
            def _(piece=piece):
                dense_send_out(piece).start()

    first_step(5)
    last_step(3)
    send_panel(3)
    chain_step(0, levels - 3)
    chain_step(1, 2)
    first_step(6)
    last_step(4)
    send_panel(4)
    last_step(5)
    send_panel(5)
    last_step(6)
    send_panel(6)
    first_step(n_panels)
    chain_end()
    last_step(n_panels)
    for way in range(2):
        pltpu.make_async_copy(
            shrink_own.at[way, 0],
            shrink_out.at[pl.ds(way * shrink_half, shrink_half)],
            store_sem.at[n_panels + 2 + micro + way],
        ).start()

    board_load.wait()
    rest = board_recv.at[pl.ds(0, devices - 1)]
    remote(rest, rest, board_sem.at[0], board_sem.at[1], d, sibling).wait()
    tail_out[...] = jnp.sum(board_recv[...], axis=0)

    for index in range(n_panels + 1):
        close_unit(index)
    for panel in range(n_panels):
        end_panel(panel)
    for level in range(levels):
        for m in range(micro):
            core_copy(level, m).wait_send()
            for way in range(2):
                @pl.when(sends(way, level))
                def _(way=way, level=level, m=m):
                    chain_copy(way, level, m).wait_send()

    @pl.when(jnp.logical_not(at_source))
    def _():
        dense_copy(0, dense_half(0), 0, x_mate).wait_send()
        dense_copy(1, dense_half(1), 0, x_mate).wait_send()

    for piece in range(per_head):
        @pl.when(jnp.logical_and(at_source, first_owner + piece != c))
        def _(piece=piece):
            dense_send_out(piece).wait_send()

    stays = me // per_head == c

    @pl.when(stays)
    def _():
        dense_store(0).wait()

    @pl.when(jnp.logical_not(stays))
    def _():
        dense_send_out(0).wait_recv()

    for m in range(micro):
        pltpu.make_async_copy(back_own.at[0, m], back_out.at[m], store_sem.at[n_panels + 2 + m]).wait()
    for way in range(2):
        pltpu.make_async_copy(
            shrink_own.at[way, 0],
            shrink_out.at[pl.ds(way * shrink_half, shrink_half)],
            store_sem.at[n_panels + 2 + micro + way],
        ).wait()


def reduce_call(dp_size, ctx_size, back, qkv_grads, expand_grads, out_grads, board):
    micro, length, width = back.shape
    span = length // ctx_size
    n_panels = 3 + dp_size
    group_rows = qkv_grads.shape[0] // dp_size
    half = group_rows // 2
    rows = group_rows // ctx_size
    unit = (out_grads.shape[0] - HEAD) // dp_size
    levels = ctx_size // 2
    devices = dp_size * ctx_size
    dma = pltpu.SemaphoreType.DMA
    kind = back.dtype
    vmem = pltpu.VMEM
    out_shape = (
        jax.ShapeDtypeStruct((micro, span, width), kind),
        jax.ShapeDtypeStruct((n_panels, ctx_size, rows, HEAD), kind),
        jax.ShapeDtypeStruct((unit, width), kind),
        jax.ShapeDtypeStruct((HEAD // (HEAD // rows), width), kind),
        jax.ShapeDtypeStruct(board.shape[1:], jnp.float32),
    )
    anywhere = pl.BlockSpec(memory_space=pl.ANY)
    return pl.pallas_call(
        functools.partial(reduce_kernel, dp_size, ctx_size),
        out_shape=out_shape,
        in_specs=[anywhere] * 5,
        out_specs=(anywhere,) * 4 + (pl.BlockSpec(memory_space=pltpu.VMEM),),
        scratch_shapes=[
            vmem((levels, micro, span, width), kind),
            vmem((levels, micro, span, width), kind),
            vmem((2, levels, micro, span, width), kind),
            vmem((n_panels, 2, 2, half, HEAD), kind),
            vmem((n_panels, 2, 2, half, HEAD), kind),
            vmem((n_panels, 2, half, HEAD), kind),
            vmem((2, 2, unit // 2, width), kind),
            vmem((2, 2, unit // 2, width), kind),
            vmem((2, unit // 2, width), kind),
            vmem((HEAD, width), kind),
            vmem((5, HEAD // 2, width), kind),
            vmem((devices,) + board.shape[1:], jnp.float32),
            dma((n_panels + 2, levels * micro + 2)),
            dma((levels, micro)),
            dma((levels, micro)),
            dma((2, levels, micro)),
            dma((2, levels, micro)),
            dma((n_panels + 1, 2, 2)),
            dma((n_panels + 1, 2, 2)),
            dma((n_panels + 1, 2)),
            dma((n_panels + 1, 2)),
            dma((n_panels,)),
            dma((n_panels,)),
            dma((2 + HEAD // rows,)),
            dma((6,)),
            dma((2,)),
            dma((n_panels + 4 + micro,)),
        ],
        compiler_params=pltpu.CompilerParams(
            collective_id=2, has_side_effects=True, vmem_limit_bytes=56 * 1024 * 1024
        ),
        name="reduce_all",
    )(back, qkv_grads, expand_grads, out_grads, board)


TILE = 256


def turn_tables(length):
    freqs = jnp.exp(jnp.arange(ROT // 2, dtype=jnp.float32) * (-2.0 * math.log(10000.0) / ROT))
    angles = jnp.arange(length, dtype=jnp.float32)[:, None] * freqs[None, :]
    cos, sin = jnp.cos(angles), jnp.sin(angles)
    rest = jnp.zeros((length, 128 - ROT), jnp.float32)
    return (
        jnp.concatenate([cos, cos, rest + 1.0], axis=1),
        jnp.concatenate([-sin, sin, rest], axis=1),
    )


def turn(head, cos, sin):
    front = head[:, :128]
    lane = lax.broadcasted_iota(jnp.int32, front.shape, 1)
    other = jnp.where(lane < ROT // 2, pltpu.roll(front, 128 - ROT // 2, 1), pltpu.roll(front, ROT // 2, 1))
    return jnp.concatenate([front * cos + other * sin, head[:, 128:]], axis=1)


def dot_nn(a, b):
    return lax.dot_general(a, b, (((1,), (0,)), ((), ())), preferred_element_type=jnp.float32)


def dot_nt(a, b):
    return lax.dot_general(a, b, (((1,), (1,)), ((), ())), preferred_element_type=jnp.float32)


def dot_tn(a, b):
    return lax.dot_general(a, b, (((0,), (0,)), ((), ())), preferred_element_type=jnp.float32)


def forward_kernel(
    tiles,
    prefix,
    x,
    panels,
    out_w,
    gains,
    qkv_shift,
    expand_shift,
    cos,
    sin,
    hidden_attn,
    hidden_mlp,
    heads,
    probs,
    features,
    slopes,
    partial,
    head_rows,
    acts,
):
    step = pl.program_id(0)
    seq = step // (2 * tiles)
    phase = lax.rem(step, 2 * tiles) // tiles
    tile = lax.rem(step, tiles)
    rows = pl.ds(pl.multiple_of(tile * TILE, TILE), TILE)
    n_expand = panels.shape[0] - 3
    scale = 1.0 / math.sqrt(HEAD)

    @pl.when(phase == 0)
    def _():
        values_in = x[...].astype(jnp.float32)
        centered = values_in - jnp.mean(values_in, axis=1, keepdims=True)
        normal = centered * lax.rsqrt(jnp.mean(centered * centered, axis=1, keepdims=True) + 1e-05)
        hidden_attn[...] = (normal * gains[0:1, :] + gains[1:2, :]).astype(jnp.bfloat16)
        hidden_mlp[...] = (normal * gains[2:3, :] + gains[3:4, :]).astype(jnp.bfloat16)
        for part in range(3):
            joined = dot_nn(hidden_attn[...], panels[part]) + qkv_shift[:, part * HEAD : (part + 1) * HEAD]
            if part < 2:
                joined = turn(joined, cos[rows, :], sin[rows, :])
            joined = joined.astype(jnp.bfloat16)
            heads[part] = joined
            head_rows[part, rows, :] = joined
        for part in range(n_expand):
            columns = slice(part * HEAD, (part + 1) * HEAD)
            expanded = dot_nn(hidden_mlp[...], panels[3 + part]) + expand_shift[:, columns]
            cdf = 0.5 * (1.0 + lax.erf(expanded * (1.0 / math.sqrt(2.0))))
            acts[rows, columns] = (expanded * cdf).astype(jnp.bfloat16)
            bell = jnp.exp(-0.5 * expanded * expanded) * (1.0 / math.sqrt(2.0 * math.pi))
            slopes[:, columns] = (cdf + expanded * bell).astype(jnp.bfloat16)

    @pl.when(phase == 1)
    def _():
        scores = dot_nt(head_rows[0, rows, :], head_rows[1]) * scale
        key_at = lax.broadcasted_iota(jnp.int32, scores.shape, 1)
        query_at = lax.broadcasted_iota(jnp.int32, scores.shape, 0) + tile * TILE
        allowed = jnp.logical_or(key_at <= query_at, key_at < prefix[seq])
        scores = jnp.where(allowed, scores, -1e30)
        expo = jnp.exp(scores - jnp.max(scores, axis=1, keepdims=True))
        low_probs = (expo * (1.0 / jnp.sum(expo, axis=1, keepdims=True))).astype(jnp.bfloat16)
        probs[0] = low_probs
        features[:, :HEAD] = dot_nn(low_probs, head_rows[2]).astype(jnp.bfloat16)
        features[:, HEAD:] = acts[rows, :]
        width = out_w.shape[1]
        for start in range(0, width, 512):
            columns = slice(start, start + 512)
            partial[:, columns] = dot_nn(features[...], out_w[:, columns]).astype(jnp.bfloat16)


def whole_spec(array):
    zeros = (0,) * array.ndim
    return pl.BlockSpec(array.shape, lambda step: zeros, pipeline_mode=pl.Buffered(1))


def forward_call(prefix, x, panels, out_w, gains, qkv_shift, expand_shift, cos, sin):
    tokens, width = x.shape
    length = cos.shape[0]
    tiles = length // TILE
    steps = 2 * tokens // TILE
    hidden = expand_shift.shape[1]

    def early(step):
        seq, at = step // (2 * tiles), lax.rem(step, 2 * tiles)
        return seq * tiles + jnp.minimum(at, tiles - 1)

    def late(step):
        seq, at = step // (2 * tiles), lax.rem(step, 2 * tiles)
        return seq * tiles + jnp.maximum(at - tiles, 0)

    kind = jnp.bfloat16
    return pl.pallas_call(
        functools.partial(forward_kernel, tiles),
        grid=(steps,),
        out_shape=(
            jax.ShapeDtypeStruct((tokens, width), kind),
            jax.ShapeDtypeStruct((tokens, width), kind),
            jax.ShapeDtypeStruct((3, tokens, HEAD), kind),
            jax.ShapeDtypeStruct((tokens // length, length, length), kind),
            jax.ShapeDtypeStruct((tokens, HEAD + hidden), kind),
            jax.ShapeDtypeStruct((tokens, hidden), kind),
            jax.ShapeDtypeStruct((tokens, width), kind),
        ),
        in_specs=[
            pl.BlockSpec(memory_space=pltpu.SMEM),
            pl.BlockSpec((TILE, width), lambda step: (early(step), 0)),
            whole_spec(panels),
            whole_spec(out_w),
            whole_spec(gains),
            whole_spec(qkv_shift),
            whole_spec(expand_shift),
            whole_spec(cos),
            whole_spec(sin),
        ],
        out_specs=(
            pl.BlockSpec((TILE, width), lambda step: (early(step), 0)),
            pl.BlockSpec((TILE, width), lambda step: (early(step), 0)),
            pl.BlockSpec((3, TILE, HEAD), lambda step: (0, early(step), 0)),
            pl.BlockSpec((1, TILE, length), lambda step: (late(step) // tiles, lax.rem(late(step), tiles), 0)),
            pl.BlockSpec((TILE, HEAD + hidden), lambda step: (late(step), 0)),
            pl.BlockSpec((TILE, hidden), lambda step: (early(step), 0)),
            pl.BlockSpec((TILE, width), lambda step: (late(step), 0)),
        ),
        scratch_shapes=[
            pltpu.VMEM((3, length, HEAD), kind),
            pltpu.VMEM((length, hidden), kind),
        ],
        compiler_params=pltpu.CompilerParams(vmem_limit_bytes=56 * 1024 * 1024),
        cost_estimate=pl.CostEstimate(
            flops=2 * tokens * width * (2 * hidden + 4 * HEAD) + 4 * tokens * length * HEAD,
            bytes_accessed=64 * 1024 * 1024,
            transcendentals=0,
        ),
        name="forward_part",
    )(prefix, x, panels, out_w, gains, qkv_shift, expand_shift, cos, sin)


def backward_kernel(
    tiles,
    g,
    x,
    panels,
    out_w,
    gains,
    cos,
    sin,
    heads,
    probs,
    slopes,
    grad_expanded,
    grad_joined,
    combined,
    norm_sums,
    joined_sums,
    expand_sums,
    grad_mixed,
    back_mlp,
    grad_queries,
    grad_keys,
    grad_values,
):
    step = pl.program_id(0)
    phase = lax.rem(step, 3 * tiles) // tiles
    tile = lax.rem(step, tiles)
    rows = pl.ds(pl.multiple_of(tile * TILE, TILE), TILE)
    n_expand = panels.shape[0] - 3
    width = out_w.shape[1]
    scale = 1.0 / math.sqrt(HEAD)

    @pl.when(step == 0)
    def _():
        norm_sums[...] = jnp.zeros_like(norm_sums)
        joined_sums[...] = jnp.zeros_like(joined_sums)
        expand_sums[...] = jnp.zeros_like(expand_sums)

    @pl.when(phase == 0)
    def _():
        grad_mixed[rows, :] = dot_nt(g[...], out_w[:HEAD, :]).astype(jnp.bfloat16)
        for part in range(n_expand):
            columns = slice(part * HEAD, (part + 1) * HEAD)
            grad = dot_nt(g[...], out_w[(part + 1) * HEAD : (part + 2) * HEAD, :])
            grad = (grad * slopes[:, columns].astype(jnp.float32)).astype(jnp.bfloat16)
            grad_expanded[:, columns] = grad
            expand_sums[:, columns] += jnp.sum(grad.astype(jnp.float32), axis=0, keepdims=True)
        for start in range(0, width, 512):
            columns = slice(start, start + 512)
            total = dot_nt(grad_expanded[:, :HEAD], panels[3, columns, :])
            for part in range(1, n_expand):
                total += dot_nt(grad_expanded[:, part * HEAD : (part + 1) * HEAD], panels[3 + part, columns, :])
            back_mlp[rows, columns] = total

    @pl.when(phase == 1)
    def _():
        low_probs = probs[0]
        own = grad_mixed[rows, :]
        grad_probs = dot_nt(own, heads[2])
        wide = low_probs.astype(jnp.float32)
        delta = jnp.sum(wide * grad_probs, axis=1, keepdims=True)
        grad_scores = (wide * (grad_probs - delta)).astype(jnp.bfloat16)
        grad_queries[rows, :] = dot_nn(grad_scores, heads[1]) * scale
        more_keys = dot_tn(grad_scores, heads[0, rows, :]) * scale
        more_values = dot_tn(low_probs, own)

        @pl.when(tile == 0)
        def _():
            grad_keys[...] = more_keys
            grad_values[...] = more_values

        @pl.when(tile > 0)
        def _():
            grad_keys[...] += more_keys
            grad_values[...] += more_values

    @pl.when(phase == 2)
    def _():
        cos_rows, sin_rows = cos[rows, :], -sin[rows, :]
        parts = (
            turn(grad_queries[rows, :], cos_rows, sin_rows),
            turn(grad_keys[rows, :], cos_rows, sin_rows),
            grad_values[rows, :],
        )
        for part in range(3):
            columns = slice(part * HEAD, (part + 1) * HEAD)
            joined = parts[part].astype(jnp.bfloat16)
            grad_joined[:, columns] = joined
            joined_sums[:, columns] += jnp.sum(joined.astype(jnp.float32), axis=0, keepdims=True)
        values_in = x[...].astype(jnp.float32)
        mean = jnp.mean(values_in, axis=1, keepdims=True)
        centered = values_in - mean
        spread = lax.rsqrt(jnp.mean(centered * centered, axis=1, keepdims=True) + 1e-05)
        for start in range(0, width, 512):
            columns = slice(start, start + 512)
            normal = (x[:, columns].astype(jnp.float32) - mean) * spread
            total = dot_nt(grad_joined[:, :HEAD], panels[0, columns, :])
            for part in range(1, 3):
                total += dot_nt(grad_joined[:, part * HEAD : (part + 1) * HEAD], panels[part, columns, :])
            other = back_mlp[rows, columns]
            for row, value in ((0, total * normal), (1, total), (2, other * normal), (3, other)):
                norm_sums[row : row + 1, columns] += jnp.sum(value, axis=0, keepdims=True)
            combined[:, columns] = (total * gains[0:1, columns] + other * gains[2:3, columns]).astype(jnp.bfloat16)


def backward_call(g, x, panels, out_w, gains, cos, sin, heads, probs, slopes):
    tokens, width = x.shape
    length = cos.shape[0]
    tiles = length // TILE
    steps = 3 * tokens // TILE
    hidden = slopes.shape[1]

    def at_phase(phase):
        def index(step):
            seq, at = step // (3 * tiles), lax.rem(step, 3 * tiles)
            return seq * tiles + jnp.clip(at - phase * tiles, 0, tiles - 1)

        return index

    first, second, third = (at_phase(phase) for phase in range(3))
    kind = jnp.bfloat16
    fixed = lambda step: (0, 0)
    return pl.pallas_call(
        functools.partial(backward_kernel, tiles),
        grid=(steps,),
        out_shape=(
            jax.ShapeDtypeStruct((tokens, hidden), kind),
            jax.ShapeDtypeStruct((tokens, 3 * HEAD), kind),
            jax.ShapeDtypeStruct((tokens, width), kind),
            jax.ShapeDtypeStruct((8, width), jnp.float32),
            jax.ShapeDtypeStruct((1, 3 * HEAD), jnp.float32),
            jax.ShapeDtypeStruct((1, hidden), jnp.float32),
        ),
        in_specs=[
            pl.BlockSpec((TILE, width), lambda step: (first(step), 0)),
            pl.BlockSpec((TILE, width), lambda step: (third(step), 0)),
            whole_spec(panels),
            whole_spec(out_w),
            whole_spec(gains),
            whole_spec(cos),
            whole_spec(sin),
            pl.BlockSpec((3, length, HEAD), lambda step: (0, step // (3 * tiles), 0)),
            pl.BlockSpec((1, TILE, length), lambda step: (second(step) // tiles, lax.rem(second(step), tiles), 0)),
            pl.BlockSpec((TILE, hidden), lambda step: (first(step), 0)),
        ],
        out_specs=(
            pl.BlockSpec((TILE, hidden), lambda step: (first(step), 0)),
            pl.BlockSpec((TILE, 3 * HEAD), lambda step: (third(step), 0)),
            pl.BlockSpec((TILE, width), lambda step: (third(step), 0)),
            pl.BlockSpec((8, width), fixed),
            pl.BlockSpec((1, 3 * HEAD), fixed),
            pl.BlockSpec((1, hidden), fixed),
        ),
        scratch_shapes=[
            pltpu.VMEM((length, HEAD), kind),
            pltpu.VMEM((length, width), jnp.float32),
            pltpu.VMEM((length, HEAD), jnp.float32),
            pltpu.VMEM((length, HEAD), jnp.float32),
            pltpu.VMEM((length, HEAD), jnp.float32),
        ],
        compiler_params=pltpu.CompilerParams(vmem_limit_bytes=56 * 1024 * 1024),
        cost_estimate=pl.CostEstimate(
            flops=2 * tokens * width * (2 * hidden + 4 * HEAD) + 10 * tokens * length * HEAD,
            bytes_accessed=48 * 1024 * 1024,
            transcendentals=0,
        ),
        name="backward_part",
    )(g, x, panels, out_w, gains, cos, sin, heads, probs, slopes)


def tensor_shards(
    layer_input,
    out_grad,
    prefix_len,
    qkv_weight,
    qkv_bias,
    dense_weight,
    dense_bias,
    expand_weight,
    expand_bias,
    shrink_weight,
    shrink_bias,
    attn_gain,
    attn_shift,
    mlp_gain,
    mlp_shift,
):
    dp_size = lax.axis_size("dp")
    ctx_size = lax.axis_size("ctx")
    devices = dp_size * ctx_size
    me = lax.axis_index("ctx")
    group = lax.axis_index("dp")
    micro, seq_count, span, width = layer_input.shape
    sequences = micro * seq_count
    tokens = sequences * SEQ
    row_share = qkv_weight.shape[0]
    scale = 1.0 / math.sqrt(HEAD)
    ff = expand_weight.shape[1]
    unit = shrink_weight.shape[0]
    lengths = tuple(
        member.shape[0]
        for member in (attn_gain, attn_shift, mlp_gain, mlp_shift, qkv_bias, dense_bias, expand_bias, shrink_bias)
    )
    packed = jnp.concatenate(
        [attn_gain, attn_shift, mlp_gain, mlp_shift, qkv_bias, dense_bias, expand_bias, shrink_bias]
    )
    own_x = layer_input.reshape(sequences, span, width)
    own_g = out_grad.reshape(sequences, span, width)
    g_all = lax.all_gather(own_g, "ctx", axis=1, tiled=True).reshape(tokens, width)
    count = packed.shape[0]
    packed = jnp.pad(packed, (0, -count % 2048)).reshape(-1, 128)
    x_all, panels, out_part, small = gather_call(
        dp_size, ctx_size, own_x, qkv_weight, expand_weight, dense_weight, shrink_weight, packed
    )
    x_all = x_all.reshape(tokens, width)
    small = unpack_small(small.reshape(devices, -1)[:, :count], lengths, devices)
    gain_attn, shift_attn, gain_mlp, shift_mlp, qkv_shift, dense_shift, expand_shift, shrink_shift = small
    qkv_shift = lax.dynamic_slice_in_dim(qkv_shift.reshape(3, ctx_size, HEAD), me, 1, 1).reshape(-1)
    expand_shift = lax.dynamic_slice_in_dim(
        expand_shift.reshape(dp_size, ctx_size, unit), me, 1, 1
    ).reshape(-1)

    gains = jnp.stack([gain_attn, shift_attn, gain_mlp, shift_mlp])
    cos, sin = turn_tables(SEQ)
    hidden_attn, hidden_mlp, heads, probs, features, slopes, partial = forward_call(
        prefix_len.reshape(sequences), x_all, panels, out_part, gains, qkv_shift[None], expand_shift[None], cos, sin
    )
    reduced = lax.psum_scatter(
        partial.reshape(sequences, SEQ, width), "ctx", scatter_dimension=1, tiled=True
    )
    layer_output = low(
        own_x.astype(jnp.float32) + reduced.astype(jnp.float32) + (dense_shift + shrink_shift)
    ).reshape(layer_input.shape)

    out_grads = low(contract_rows(features, g_all))
    grad_expanded, grad_joined, combined, norm_sums, joined_sum, expand_sum = backward_call(
        g_all, x_all, panels, out_part, gains, cos, sin, heads, probs, slopes
    )
    expand_grads = low(contract_rows(hidden_mlp, grad_expanded))
    qkv_grads = low(contract_rows(hidden_attn, grad_joined))
    joined_sum, expand_sum = joined_sum[0], expand_sum[0]

    def place(values, parts):
        board = jnp.zeros((parts, ctx_size, values.shape[0] // parts), jnp.float32)
        board = lax.dynamic_update_slice(board, values.reshape(parts, 1, -1), (0, me, 0))
        return board.reshape(devices, -1)

    out_sum = jnp.sum(own_g.astype(jnp.float32), axis=(0, 1))
    board = jnp.concatenate(
        [
            place(joined_sum[: 2 * HEAD], 2),
            place(joined_sum[2 * HEAD :], 1),
            out_sum.reshape(devices, -1),
            place(expand_sum, dp_size),
            norm_sums[0].reshape(devices, -1),
            norm_sums[1].reshape(devices, -1),
            norm_sums[2].reshape(devices, -1),
            norm_sums[3].reshape(devices, -1),
        ],
        axis=1,
    )
    used = board.shape[1]
    board = jnp.pad(board, ((0, 0), (0, -used % 1024))).reshape(devices, -1, 128)
    combined, panel_grads, shrink_grad, dense_grad, tail = reduce_call(
        dp_size, ctx_size, combined.reshape(sequences, SEQ, width), qkv_grads, expand_grads, out_grads, board
    )
    combined = combined.astype(jnp.float32)
    panel_grads = jnp.transpose(panel_grads.astype(jnp.float32), (2, 0, 1, 3))
    qkv_grad = panel_grads[:, :3].reshape(row_share, 3 * width)
    expand_grad = panel_grads[:, 3:].reshape(row_share, ff)
    own = own_x.astype(jnp.float32)
    own_center = own - jnp.mean(own, axis=-1, keepdims=True)
    own_spread = lax.rsqrt(jnp.mean(own_center * own_center, axis=-1, keepdims=True) + 1e-05)
    own_normal = own_center * own_spread
    share = own_spread * (
        combined
        - jnp.mean(combined, axis=-1, keepdims=True)
        - own_normal * jnp.mean(combined * own_normal, axis=-1, keepdims=True)
    )
    input_grad = low(own_g.astype(jnp.float32) + share).reshape(layer_input.shape)

    tail = tail.reshape(-1)
    share_len = width // devices
    at = 0
    pieces = []
    for length in (2 * share_len, share_len, share_len, ff // devices, share_len, share_len, share_len, share_len):
        pieces.append(tail[at : at + length])
        at += length
    return (
        layer_output,
        input_grad,
        qkv_grad,
        pieces[0],
        pieces[1],
        dense_grad.astype(jnp.float32),
        pieces[2],
        expand_grad,
        pieces[3],
        shrink_grad.astype(jnp.float32),
        pieces[2],
        pieces[4],
        pieces[5],
        pieces[6],
        pieces[7],
    )


def solution(mesh):
    placed = (
        P(None, "dp", "ctx", None),
        P(None, "dp", "ctx", None),
        P(None, "dp"),
        P(("dp", "ctx"), None),
        P(("dp", "ctx")),
        P(("dp", "ctx"), None),
        P(("dp", "ctx")),
        P(("dp", "ctx"), None),
        P(("dp", "ctx")),
        P(("dp", "ctx"), None),
        P(("dp", "ctx")),
        P(("dp", "ctx")),
        P(("dp", "ctx")),
        P(("dp", "ctx")),
        P(("dp", "ctx")),
    )
    return jax.shard_map(
        tensor_shards if (mesh.shape["dp"], mesh.shape["ctx"]) == (4, HEADS) else shards,
        mesh=mesh,
        in_specs=placed,
        out_specs=(
            P(None, "dp", "ctx", None),
            P(None, "dp", "ctx", None),
            P(("dp", "ctx"), None),
            P(("dp", "ctx")),
            P(("dp", "ctx")),
            P(("dp", "ctx"), None),
            P(("dp", "ctx")),
            P(("dp", "ctx"), None),
            P(("dp", "ctx")),
            P(("dp", "ctx"), None),
            P(("dp", "ctx")),
            P(("dp", "ctx")),
            P(("dp", "ctx")),
            P(("dp", "ctx")),
            P(("dp", "ctx")),
        ),
        check_vma=False,
    )
```

```python
import functools
import math

import jax
import jax.numpy as jnp
from jax import lax
from jax.experimental import pallas as pl
from jax.experimental.pallas import tpu as pltpu
from jax.sharding import PartitionSpec as P

HEADS = 8
HEAD = 256
ROT = 64
SEQ = 1024


def norm_rows(inputs, norm_gain, norm_bias):
    row_mean = jnp.mean(inputs, axis=-1, keepdims=True)
    centered = inputs - row_mean
    variance = jnp.mean(centered * centered, axis=-1, keepdims=True)
    return centered * lax.rsqrt(variance + 1e-05) * norm_gain + norm_bias


def gelu_exact(values):
    return jax.nn.gelu(values, approximate=False)


def rope_tables(positions):
    freqs = jnp.exp(jnp.arange(ROT // 2, dtype=jnp.float32) * (-2.0 * math.log(10000.0) / ROT))
    angles = positions[:, None] * freqs[None, :]
    return (jnp.cos(angles), jnp.sin(angles))


def rotate(heads, cos_table, sin_table):
    half_rot = ROT // 2
    lower = heads[..., :half_rot]
    upper = heads[..., half_rot:ROT]
    cos_wide = cos_table[:, None, :]
    sin_wide = sin_table[:, None, :]
    return jnp.concatenate(
        [
            lower * cos_wide - upper * sin_wide,
            upper * cos_wide + lower * sin_wide,
            heads[..., ROT:],
        ],
        axis=-1,
    )


def unpack_small(packed, lengths, devices):
    table_rows = packed.reshape(devices, -1)
    members = []
    offset = 0
    for length in lengths:
        members.append(table_rows[:, offset : offset + length].reshape(-1).astype(jnp.float32))
        offset = offset + length
    return members


def contract_rows(left_mat, right_mat):
    return lax.dot_general(
        left_mat, right_mat, (((0,), (0,)), ((), ())), preferred_element_type=jnp.float32
    )


def contract_cols(left_mat, right_mat):
    return lax.dot_general(
        left_mat, right_mat, (((1,), (1,)), ((), ())), preferred_element_type=jnp.float32
    )


def shards(
    layer_input,
    out_grad,
    prefix_len,
    qkv_weight,
    qkv_bias,
    dense_weight,
    dense_bias,
    expand_weight,
    expand_bias,
    shrink_weight,
    shrink_bias,
    attn_gain,
    attn_shift,
    mlp_gain,
    mlp_shift,
):
    devices = lax.axis_size("dp") * lax.axis_size("ctx")
    ctx_index = lax.axis_index("ctx")
    micro, seq_count, span, width = layer_input.shape
    sequences = micro * seq_count
    rows = sequences * span
    heads_shape = (sequences, span, HEADS, HEAD)
    scale = 1.0 / math.sqrt(HEAD)
    attn_lengths = (attn_gain.shape[0], attn_shift.shape[0], qkv_bias.shape[0], dense_bias.shape[0])
    mlp_lengths = (
        mlp_gain.shape[0],
        mlp_shift.shape[0],
        expand_bias.shape[0],
        shrink_bias.shape[0],
    )
    attn_packed = jnp.concatenate([attn_gain, attn_shift, qkv_bias, dense_bias])
    mlp_packed = jnp.concatenate([mlp_gain, mlp_shift, expand_bias, shrink_bias])

    def fetch_attn():
        return (
            lax.all_gather(qkv_weight, ("dp", "ctx"), axis=0, tiled=True),
            lax.all_gather(dense_weight, ("dp", "ctx"), axis=0, tiled=True),
            lax.all_gather(attn_packed, ("dp", "ctx"), axis=0, tiled=True),
        )

    def fetch_mlp():
        return (
            lax.all_gather(expand_weight, ("dp", "ctx"), axis=0, tiled=True),
            lax.all_gather(shrink_weight, ("dp", "ctx"), axis=0, tiled=True),
            lax.all_gather(mlp_packed, ("dp", "ctx"), axis=0, tiled=True),
        )

    local_pos = ctx_index * span + jnp.arange(span, dtype=jnp.int32)
    cos_table, sin_table = rope_tables(local_pos.astype(jnp.float32))
    key_pos = jnp.arange(SEQ, dtype=jnp.int32)
    causal = key_pos[None, :] <= local_pos[:, None]
    inputs = layer_input.astype(jnp.float32).reshape(rows, width)
    cot_rows = out_grad.reshape(rows, width)
    cot_float = cot_rows.astype(jnp.float32)
    prefix = prefix_len.reshape(sequences)
    allowed = (causal[None] | (key_pos[None, None, :] < prefix[:, None, None]))[:, None]
    attn_set = fetch_attn()
    qkv_full, dense_full, attn_small = attn_set
    gain_attn, shift_attn, joined_shift, dense_shift = unpack_small(
        attn_small, attn_lengths, devices
    )
    hidden_attn = norm_rows(inputs, gain_attn, shift_attn).astype(jnp.bfloat16)
    joined = jnp.dot(hidden_attn, qkv_full, preferred_element_type=jnp.float32) + joined_shift
    queries = rotate(joined[:, :width].reshape(heads_shape), cos_table, sin_table).astype(
        jnp.bfloat16
    )
    key_rows = rotate(
        joined[:, width : 2 * width].reshape(heads_shape), cos_table, sin_table
    ).astype(jnp.bfloat16)
    value_rows = joined[:, 2 * width :].reshape(heads_shape).astype(jnp.bfloat16)
    all_keys, all_values = (
        lax.all_gather(key_rows, "ctx", axis=1, tiled=True),
        lax.all_gather(value_rows, "ctx", axis=1, tiled=True),
    )
    scores = (
        jnp.einsum("sqhe,skhe->shqk", queries, all_keys, preferred_element_type=jnp.float32) * scale
    )
    scores = jnp.where(allowed, scores, -1e30)
    row_max = jnp.max(scores, axis=-1, keepdims=True)
    expo = jnp.exp(scores - row_max)
    row_total = jnp.sum(expo, axis=-1, keepdims=True)
    log_total = row_max + jnp.log(row_total)
    probs_low = (expo / row_total).astype(jnp.bfloat16)
    mixed = jnp.einsum("shqk,skhe->sqhe", probs_low, all_values, preferred_element_type=jnp.float32)
    mixed = mixed.reshape(rows, width).astype(jnp.bfloat16)
    attn_out = jnp.dot(mixed, dense_full, preferred_element_type=jnp.float32) + dense_shift
    mlp_set = fetch_mlp()
    expand_full, shrink_full, mlp_small = mlp_set
    gain_mlp, shift_mlp, expand_shift, shrink_shift = unpack_small(mlp_small, mlp_lengths, devices)
    hidden_mlp = norm_rows(inputs, gain_mlp, shift_mlp).astype(jnp.bfloat16)
    expanded = jnp.dot(hidden_mlp, expand_full, preferred_element_type=jnp.float32) + expand_shift
    activated = gelu_exact(expanded).astype(jnp.bfloat16)
    mlp_out = jnp.dot(activated, shrink_full, preferred_element_type=jnp.float32) + shrink_shift
    layer_output = (
        (inputs + attn_out + mlp_out).astype(jnp.bfloat16).reshape(micro, seq_count, span, width)
    )
    attn_back_set = fetch_attn()
    qkv_back, dense_back, attn_small_back = attn_back_set
    gain_attn, shift_attn, joined_shift, dense_shift = unpack_small(
        attn_small_back, attn_lengths, devices
    )
    grad_out_shift = jnp.sum(cot_float, axis=0)
    grad_mixed = contract_cols(cot_rows, dense_back).astype(jnp.bfloat16).reshape(heads_shape)
    again = (
        jnp.einsum("sqhe,skhe->shqk", queries, all_keys, preferred_element_type=jnp.float32) * scale
    )
    again = jnp.where(allowed, again, -1e30)
    probs = jnp.exp(again - log_total)
    grad_probs = jnp.einsum(
        "sqhe,skhe->shqk", grad_mixed, all_values, preferred_element_type=jnp.float32
    )
    delta = jnp.sum(probs * grad_probs, axis=-1, keepdims=True)
    grad_scores = (probs * (grad_probs - delta)).astype(jnp.bfloat16)
    grad_queries = (
        jnp.einsum("shqk,skhe->sqhe", grad_scores, all_keys, preferred_element_type=jnp.float32)
        * scale
    )
    all_queries, all_grad_mixed = (
        lax.all_gather(queries, "ctx", axis=1, tiled=True),
        lax.all_gather(grad_mixed, "ctx", axis=1, tiled=True),
    )
    stat_lse = jnp.transpose(log_total[..., 0], (0, 2, 1))
    stat_delta = jnp.transpose(delta[..., 0], (0, 2, 1))
    lse_all, delta_all = (
        lax.all_gather(stat_lse, "ctx", axis=1, tiled=True),
        lax.all_gather(stat_delta, "ctx", axis=1, tiled=True),
    )
    lse_all = jnp.transpose(lse_all, (0, 2, 1))[..., None]
    delta_all = jnp.transpose(delta_all, (0, 2, 1))[..., None]
    key_allowed = (local_pos[None, :] <= key_pos[:, None])[None] | (
        local_pos[None, None, :] < prefix[:, None, None]
    )
    block_scores = (
        jnp.einsum("sqhe,skhe->shqk", all_queries, key_rows, preferred_element_type=jnp.float32)
        * scale
    )
    block_scores = jnp.where(key_allowed[:, None], block_scores, -1e30)
    block_probs = jnp.exp(block_scores - lse_all)
    block_grad_probs = jnp.einsum(
        "sqhe,skhe->shqk", all_grad_mixed, value_rows, preferred_element_type=jnp.float32
    )
    block_grad_scores = (block_probs * (block_grad_probs - delta_all)).astype(jnp.bfloat16)
    own_keys = (
        jnp.einsum(
            "shqk,sqhe->skhe", block_grad_scores, all_queries, preferred_element_type=jnp.float32
        )
        * scale
    )
    own_values = jnp.einsum(
        "shqk,sqhe->skhe",
        block_probs.astype(jnp.bfloat16),
        all_grad_mixed,
        preferred_element_type=jnp.float32,
    )
    grad_joined = jnp.concatenate(
        [
            rotate(grad_queries, cos_table, -sin_table).reshape(rows, width),
            rotate(own_keys, cos_table, -sin_table).reshape(rows, width),
            own_values.reshape(rows, width),
        ],
        axis=1,
    ).astype(jnp.bfloat16)
    grad_joined_shift = jnp.sum(grad_joined.astype(jnp.float32), axis=0)
    grad_hidden_attn = contract_cols(grad_joined, qkv_back)
    unused_attn, attn_back = jax.vjp(norm_rows, inputs, gain_attn, shift_attn)
    grad_in_attn, grad_gain_attn, grad_shift_attn = attn_back(grad_hidden_attn)
    attn_columns = jnp.concatenate(
        [
            grad_gain_attn[:, None],
            grad_shift_attn[:, None],
            grad_joined_shift[: 2 * width].reshape(width, 2),
            grad_joined_shift[2 * width :][:, None],
            grad_out_shift[:, None],
        ],
        axis=1,
    )
    hidden_part = hidden_attn
    small_part = attn_columns
    attn_grads = lax.psum_scatter(
        jnp.concatenate(
            [contract_rows(hidden_part, grad_joined), contract_rows(mixed, cot_rows), small_part],
            axis=1,
        ),
        ("dp", "ctx"),
        scatter_dimension=0,
        tiled=True,
    )
    qkv_grad = attn_grads[:, : 3 * width]
    dense_grad = attn_grads[:, 3 * width : 4 * width]
    attn_tail = attn_grads[:, 4 * width :]
    mlp_back_set = fetch_mlp()
    expand_back, shrink_back, mlp_small_back = mlp_back_set
    gain_mlp, shift_mlp, expand_shift, shrink_shift = unpack_small(
        mlp_small_back, mlp_lengths, devices
    )
    unused_gelu, gelu_back = jax.vjp(gelu_exact, expanded)
    grad_act = contract_cols(cot_rows, shrink_back)
    grad_expanded = gelu_back(grad_act)[0].astype(jnp.bfloat16)
    grad_expand_shift = jnp.sum(grad_expanded.astype(jnp.float32), axis=0)
    grad_hidden_mlp = contract_cols(grad_expanded, expand_back)
    unused_mlp, mlp_back = jax.vjp(norm_rows, inputs, gain_mlp, shift_mlp)
    grad_in_mlp, grad_gain_mlp, grad_shift_mlp = mlp_back(grad_hidden_mlp)
    ratio = expand_shift.shape[0] // width
    mlp_columns = jnp.concatenate(
        [
            grad_gain_mlp[:, None],
            grad_shift_mlp[:, None],
            grad_expand_shift.reshape(width, ratio),
            grad_out_shift[:, None],
        ],
        axis=1,
    )
    ff_width = expand_back.shape[1]
    hidden_part = hidden_mlp
    small_part = mlp_columns
    expand_grads = lax.psum_scatter(
        jnp.concatenate([contract_rows(hidden_part, grad_expanded), small_part], axis=1),
        ("dp", "ctx"),
        scatter_dimension=0,
        tiled=True,
    )
    shrink_grad = lax.psum_scatter(
        contract_rows(activated, cot_rows), ("dp", "ctx"), scatter_dimension=0, tiled=True
    )
    expand_grad = expand_grads[:, :ff_width]
    mlp_tail = expand_grads[:, ff_width:]
    input_grad = (
        (cot_float + grad_in_attn + grad_in_mlp)
        .astype(jnp.bfloat16)
        .reshape(micro, seq_count, span, width)
    )
    return (
        layer_output,
        input_grad,
        qkv_grad,
        attn_tail[:, 2:4].reshape(-1),
        attn_tail[:, 4],
        dense_grad,
        attn_tail[:, 5],
        expand_grad,
        mlp_tail[:, 2 : 2 + ratio].reshape(-1),
        shrink_grad,
        mlp_tail[:, 2 + ratio],
        attn_tail[:, 0],
        attn_tail[:, 1],
        mlp_tail[:, 0],
        mlp_tail[:, 1],
    )


def low(values):
    return values.astype(jnp.bfloat16)


MESH_ID = pl.DeviceIdType.MESH


def remote(src, dst, send_sem, recv_sem, dp, ctx):
    return pltpu.make_async_remote_copy(
        src_ref=src,
        dst_ref=dst,
        send_sem=send_sem,
        recv_sem=recv_sem,
        device_id=(dp, ctx),
        device_id_type=MESH_ID,
    )


def greet_all(dp, ctx, dp_size, ctx_size):
    barrier = pltpu.get_barrier_semaphore()
    devices = dp_size * ctx_size
    me = dp * ctx_size + ctx

    def greet(step, carry):
        other = lax.rem(me + step, devices)
        pl.semaphore_signal(
            barrier, inc=1, device_id=(other // ctx_size, lax.rem(other, ctx_size)), device_id_type=MESH_ID
        )
        return carry

    lax.fori_loop(1, devices, greet, 0)
    pl.semaphore_wait(barrier, devices - 1)


def chain_gather(src, dst, sems, d, c, levels):
    block_send, block_recv, core_send, core_recv, local = sems
    micro, span = src.shape[0], src.shape[1]
    z = c // 2
    sibling = c + 1 - 2 * lax.rem(c, 2)

    def block(origin, m):
        return dst.at[m, pl.ds(pl.multiple_of(origin * span, span), span)]

    def link(way, hop, m):
        step = 2 if way == 0 else -2
        origin = c - step * hop
        view = src.at[m] if hop == 0 else block(origin, m)
        return remote(view, block(origin, m), block_send.at[way, hop, m], block_recv.at[way, hop, m], d, c + step)

    def leaves(way, hop):
        if way == 0:
            return jnp.logical_and(z >= hop, z <= levels - 2)
        return jnp.logical_and(z + hop <= levels - 1, z >= 1)

    def arrives(way, hop):
        return z >= hop + 1 if way == 0 else z + hop + 1 <= levels - 1

    def slot_of(way, hop):
        return 1 + way * (levels - 1) + hop

    def core_copy(slot, origin, m):
        view = src.at[m] if slot == 0 else block(origin, m)
        return remote(view, block(origin, m), core_send.at[slot, m], core_recv.at[slot, m], d, sibling)

    def own_copy(m):
        return pltpu.make_async_copy(src.at[m], block(c, m), local.at[m])

    def start(m):
        for way in range(2):
            @pl.when(leaves(way, 0))
            def _(way=way):
                link(way, 0, m).start()

        core_copy(0, c, m).start()
        own_copy(m).start()

    def hop_step(hop, m):
        for way in range(2):
            step = 2 if way == 0 else -2

            @pl.when(arrives(way, hop))
            def _(way=way, step=step):
                link(way, hop, m).wait_recv()
                if hop + 1 <= levels - 2:
                    @pl.when(leaves(way, hop + 1))
                    def _():
                        link(way, hop + 1, m).start()

                core_copy(slot_of(way, hop), c - step * (hop + 1), m).start()

    def finish(m):
        own_copy(m).wait()
        core_copy(0, c, m).wait_send()
        core_copy(0, sibling, m).wait_recv()
        for way in range(2):
            step = 2 if way == 0 else -2
            for hop in range(levels - 1):
                @pl.when(leaves(way, hop))
                def _(way=way, hop=hop):
                    link(way, hop, m).wait_send()

                @pl.when(arrives(way, hop))
                def _(way=way, hop=hop, step=step):
                    slot = slot_of(way, hop)
                    core_copy(slot, c - step * (hop + 1), m).wait_send()
                    core_copy(slot, sibling - step * (hop + 1), m).wait_recv()

    return start, hop_step, finish


def chain_scratch(levels, micro):
    dma = pltpu.SemaphoreType.DMA
    return [
        dma((2, levels - 1, micro)),
        dma((2, levels - 1, micro)),
        dma((2 * levels - 1, micro)),
        dma((2 * levels - 1, micro)),
        dma((micro,)),
    ]


def greet_line(d, c, levels):
    barrier = pltpu.get_barrier_semaphore()
    z = c // 2
    sibling = c + 1 - 2 * lax.rem(c, 2)
    pl.semaphore_signal(barrier, inc=1, device_id=(d, sibling), device_id_type=MESH_ID)

    @pl.when(z >= 1)
    def _():
        pl.semaphore_signal(barrier, inc=1, device_id=(d, c - 2), device_id_type=MESH_ID)

    @pl.when(z <= levels - 2)
    def _():
        pl.semaphore_signal(barrier, inc=1, device_id=(d, c + 2), device_id_type=MESH_ID)

    peers = 1 + (z >= 1).astype(jnp.int32) + (z <= levels - 2).astype(jnp.int32)
    pl.semaphore_wait(barrier, peers)


def gather_kernel(
    dp_size,
    ctx_size,
    x,
    qkv,
    expand,
    dense,
    shrink,
    packed,
    x_all,
    panels,
    out_w,
    small,
    local_sem,
    small_sem,
    block_send,
    block_recv,
    core_send,
    core_recv,
    block_local,
    panel_send,
    panel_recv,
    share_send,
    share_recv,
    pass_send,
    pass_recv,
):
    d = lax.axis_index("dp")
    c = lax.axis_index("ctx")
    z = c // 2
    sibling = c + 1 - 2 * lax.rem(c, 2)
    x_mate = d + 1 - 2 * lax.rem(d, 2)
    y_mate = lax.rem(d + 2, 4)
    micro, span = x.shape[0], x.shape[1]
    devices = dp_size * ctx_size
    me = d * ctx_size + c
    rows = qkv.shape[0]
    unit = shrink.shape[0]
    levels = ctx_size // 2
    panel_rows = ctx_size * rows
    n_panels = 3 + dp_size

    greet_all(d, c, dp_size, ctx_size)

    def column_block(panel, target):
        if panel < 3:
            start = panel * (qkv.shape[1] // 3) + target * HEAD
            return qkv.at[:, pl.ds(pl.multiple_of(start, HEAD), HEAD)]
        start = (panel - 3) * ctx_size * unit + target * unit
        return expand.at[:, pl.ds(pl.multiple_of(start, HEAD), HEAD)]

    own_rows = pl.ds(pl.multiple_of((d * ctx_size + c) * rows, rows), rows)

    for panel in range(n_panels):
        pltpu.make_async_copy(
            column_block(panel, c), panels.at[panel, own_rows], local_sem.at[panel]
        ).start()

        def push(step, carry, panel=panel):
            target = lax.rem(c + step, ctx_size)
            remote(
                column_block(panel, target),
                panels.at[panel, own_rows],
                panel_send.at[panel],
                panel_recv.at[panel],
                d,
                target,
            ).start()
            return carry

        lax.fori_loop(1, ctx_size, push, 0)

    def shrink_rows(owner, offset, count):
        return out_w.at[pl.ds(pl.multiple_of(HEAD + owner * unit + offset, 16), count)]

    shrink_local = pltpu.make_async_copy(shrink, shrink_rows(d, 0, unit), local_sem.at[n_panels])
    shrink_local.start()
    for way, mate in ((0, x_mate), (1, y_mate)):
        remote(
            shrink, shrink_rows(d, 0, unit), share_send.at[n_panels, way], share_recv.at[n_panels, way], mate, c
        ).start()

    per_head = HEAD // rows
    head_of = (d * ctx_size + c) // per_head
    dense_rows = pl.ds(pl.multiple_of(lax.rem(c, per_head) * rows, rows), rows)
    dense_out = remote(dense, out_w.at[dense_rows], panel_send.at[n_panels], panel_recv.at[n_panels], d, head_of)
    dense_own = pltpu.make_async_copy(dense, out_w.at[dense_rows], local_sem.at[n_panels + 1])
    stays = head_of == c

    @pl.when(stays)
    def _():
        dense_own.start()

    @pl.when(jnp.logical_not(stays))
    def _():
        dense_out.start()

    x_start, x_hop, x_finish = chain_gather(
        x, x_all, (block_send, block_recv, core_send, core_recv, block_local), d, c, levels
    )
    for m in range(micro):
        x_start(m)

    small_copy = pltpu.make_async_copy(packed, small.at[me], local_sem.at[n_panels + 2])
    small_copy.start()

    def push_small(step, carry):
        other = lax.rem(me + step, devices)
        remote(
            packed,
            small.at[me],
            small_sem.at[0],
            small_sem.at[1],
            other // ctx_size,
            lax.rem(other, ctx_size),
        ).start()
        return carry

    lax.fori_loop(1, devices, push_small, 0)

    def group_rows(owner, offset, count):
        return pl.ds(pl.multiple_of(owner * panel_rows + offset, 16), count)

    def panel_share(panel, way, mate):
        view = panels.at[panel, group_rows(d, 0, panel_rows)]
        return remote(view, view, share_send.at[panel, way], share_recv.at[panel, way], mate, c)

    def panel_step(panel):
        pltpu.make_async_copy(column_block(panel, c), panels.at[panel, own_rows], local_sem.at[panel]).wait()
        whole = panels.at[panel, group_rows(d, 0, (ctx_size - 1) * rows)]
        remote(whole, whole, panel_send.at[panel], panel_recv.at[panel], d, sibling).wait_recv()
        panel_share(panel, 0, x_mate).start()
        panel_share(panel, 1, y_mate).start()

    half = panel_rows // 2

    def panel_pass(panel, way):
        owner, mate = ((x_mate, y_mate), (y_mate, x_mate))[way]
        view = panels.at[panel, group_rows(owner, way * half, half)]
        return remote(view, view, pass_send.at[panel, way], pass_recv.at[panel, way], mate, c)

    def panel_forward(panel):
        for way, owner in ((0, x_mate), (1, y_mate)):
            view = panels.at[panel, group_rows(owner, 0, panel_rows)]
            remote(view, view, share_send.at[panel, way], share_recv.at[panel, way], owner, c).wait_recv()
            panel_pass(panel, way).start()

    def shrink_share_wait(way, owner):
        view = shrink_rows(owner, 0, unit)
        remote(view, view, share_send.at[n_panels, way], share_recv.at[n_panels, way], owner, c).wait_recv()

    def shrink_pass(way):
        owner, mate = ((x_mate, y_mate), (y_mate, x_mate))[way]
        view = shrink_rows(owner, way * (unit // 2), unit // 2)
        return remote(view, view, pass_send.at[n_panels, way], pass_recv.at[n_panels, way], mate, c)

    source = c // (ctx_size // dp_size)
    at_source = d == source
    from_x = x_mate == source
    from_y = y_mate == source
    head_rows = out_w.at[pl.ds(0, HEAD)]
    half_head = HEAD // 2

    def dense_share(way, mate):
        view = out_w.at[pl.ds(way * half_head, half_head)]
        return remote(view, view, share_send.at[n_panels + 1, way], share_recv.at[n_panels + 1, way], mate, c)

    owns_share = jnp.logical_and(at_source, stays)

    def dense_gather_step():
        @pl.when(owns_share)
        def _():
            dense_own.wait()
            view = out_w.at[pl.ds(0, (per_head - 1) * rows)]
            remote(view, view, panel_send.at[n_panels], panel_recv.at[n_panels], d, sibling).wait_recv()

        @pl.when(jnp.logical_and(at_source, jnp.logical_not(stays)))
        def _():
            remote(head_rows, head_rows, panel_send.at[n_panels], panel_recv.at[n_panels], d, sibling).wait_recv()

        @pl.when(at_source)
        def _():
            dense_share(0, x_mate).start()
            dense_share(1, y_mate).start()

    def dense_forward_step():
        @pl.when(from_x)
        def _():
            dense_share(0, x_mate).wait_recv()
            dense_share(0, y_mate).start()

        @pl.when(from_y)
        def _():
            dense_share(1, y_mate).wait_recv()
            dense_share(1, x_mate).start()

    def dense_last_step():
        @pl.when(across)
        def _():
            dense_share(0, y_mate).wait_recv()
            dense_share(0, x_mate).start()
            dense_share(1, x_mate).wait_recv()
            dense_share(1, y_mate).start()

    across = jnp.logical_not(jnp.logical_or(at_source, jnp.logical_or(from_x, from_y)))

    for panel in range(3):
        panel_step(panel)
    shrink_share_wait(0, x_mate)
    shrink_pass(0).start()
    shrink_share_wait(1, y_mate)
    shrink_pass(1).start()
    for panel in range(3, n_panels):
        panel_step(panel)
    dense_gather_step()
    panel_forward(0)
    panel_forward(1)
    x_hop(0, 0)
    panel_forward(2)
    x_hop(0, 1)
    dense_forward_step()
    panel_forward(3)
    panel_forward(4)
    x_hop(1, 0)
    panel_forward(5)
    x_hop(1, 1)
    dense_last_step()
    panel_forward(6)
    for hop in range(2, levels - 1):
        for m in range(micro):
            x_hop(hop, m)

    for panel in range(n_panels):
        for way, mate in ((0, x_mate), (1, y_mate)):
            panel_share(panel, way, mate).wait_send()
            panel_pass(panel, way).wait_send()
        for way in range(2):
            diagonal = 3 - d
            view = panels.at[panel, group_rows(diagonal, way * half, half)]
            remote(view, view, pass_send.at[panel, way], pass_recv.at[panel, way], x_mate, c).wait_recv()
        whole = panels.at[panel, group_rows(d, 0, (ctx_size - 1) * rows)]
        remote(whole, whole, panel_send.at[panel], panel_recv.at[panel], x_mate, c).wait_send()
    shrink_local.wait()
    for way in range(2):
        mate = (x_mate, y_mate)[way]
        remote(
            shrink, shrink_rows(d, 0, unit), share_send.at[n_panels, way], share_recv.at[n_panels, way], mate, c
        ).wait_send()
        shrink_pass(way).wait_send()
        view = shrink_rows(3 - d, way * (unit // 2), unit // 2)
        remote(view, view, pass_send.at[n_panels, way], pass_recv.at[n_panels, way], mate, c).wait_recv()

    @pl.when(jnp.logical_not(stays))
    def _():
        dense_out.wait_send()

    @pl.when(at_source)
    def _():
        dense_share(0, x_mate).wait_send()
        dense_share(1, y_mate).wait_send()

    @pl.when(from_x)
    def _():
        dense_share(0, y_mate).wait_send()
        dense_share(1, y_mate).wait_recv()

    @pl.when(from_y)
    def _():
        dense_share(1, x_mate).wait_send()
        dense_share(0, x_mate).wait_recv()

    @pl.when(across)
    def _():
        dense_share(0, x_mate).wait_send()
        dense_share(1, y_mate).wait_send()

    for m in range(micro):
        x_finish(m)

    small_copy.wait()
    rest = small.at[pl.ds(0, devices - 1)]
    remote(rest, rest, small_sem.at[0], small_sem.at[1], d, sibling).wait()


def gather_call(dp_size, ctx_size, x, qkv, expand, dense, shrink, packed):
    micro, span, width = x.shape
    rows = qkv.shape[0]
    n_panels = 3 + dp_size
    levels = ctx_size // 2
    devices = dp_size * ctx_size
    dma = pltpu.SemaphoreType.DMA
    out_shape = (
        jax.ShapeDtypeStruct((micro, ctx_size * span, width), x.dtype),
        jax.ShapeDtypeStruct((n_panels, devices * rows, HEAD), x.dtype),
        jax.ShapeDtypeStruct((HEAD + dp_size * shrink.shape[0], width), x.dtype),
        jax.ShapeDtypeStruct((devices,) + packed.shape, x.dtype),
    )
    anywhere = pl.BlockSpec(memory_space=pl.ANY)
    return pl.pallas_call(
        functools.partial(gather_kernel, dp_size, ctx_size),
        out_shape=out_shape,
        in_specs=[anywhere] * 6,
        out_specs=(anywhere,) * 4,
        scratch_shapes=[
            dma((n_panels + 3,)),
            dma((2,)),
            *chain_scratch(levels, micro),
            dma((n_panels + 1,)),
            dma((n_panels + 1,)),
            dma((n_panels + 2, 2)),
            dma((n_panels + 2, 2)),
            dma((n_panels + 2, 2)),
            dma((n_panels + 2, 2)),
        ],
        compiler_params=pltpu.CompilerParams(collective_id=1, has_side_effects=True),
        name="gather_all",
    )(x, qkv, expand, dense, shrink, packed)


def add_into(dst, srcs, rows):
    chunk = 16 if dst.shape[-1] > 1024 else 64

    def step(index, carry):
        at = pl.ds(pl.multiple_of(index * chunk, 16), chunk)
        total = srcs[0][at, :].astype(jnp.float32)
        for src in srcs[1:]:
            total = total + src[at, :].astype(jnp.float32)
        dst[at, :] = total.astype(dst.dtype)
        return carry

    lax.fori_loop(0, rows // chunk, step, 0)


TILE = 256


def turn_tables(length):
    freqs = jnp.exp(jnp.arange(ROT // 2, dtype=jnp.float32) * (-2.0 * math.log(10000.0) / ROT))
    angles = jnp.arange(length, dtype=jnp.float32)[:, None] * freqs[None, :]
    cos, sin = jnp.cos(angles), jnp.sin(angles)
    rest = jnp.zeros((length, 128 - ROT), jnp.float32)
    return (
        jnp.concatenate([cos, cos, rest + 1.0], axis=1),
        jnp.concatenate([-sin, sin, rest], axis=1),
    )


def turn(head, cos, sin):
    front = head[:, :128]
    lane = lax.broadcasted_iota(jnp.int32, front.shape, 1)
    other = jnp.where(lane < ROT // 2, pltpu.roll(front, 128 - ROT // 2, 1), pltpu.roll(front, ROT // 2, 1))
    return jnp.concatenate([front * cos + other * sin, head[:, 128:]], axis=1)


def dot_nn(a, b):
    return lax.dot_general(a, b, (((1,), (0,)), ((), ())), preferred_element_type=jnp.float32)


def dot_nt(a, b):
    return lax.dot_general(a, b, (((1,), (1,)), ((), ())), preferred_element_type=jnp.float32)


def dot_tn(a, b):
    return lax.dot_general(a, b, (((0,), (0,)), ((), ())), preferred_element_type=jnp.float32)


def forward_kernel(
    tiles,
    levels,
    prefix,
    x,
    own_g,
    panels,
    out_w,
    gains,
    qkv_shift,
    expand_shift,
    cos,
    sin,
    hidden_attn,
    hidden_mlp,
    heads,
    probs,
    features,
    slopes,
    partial,
    g_all,
    head_rows,
    acts,
    *g_sems,
):
    step = pl.program_id(0)
    micro = own_g.shape[0]
    d = lax.axis_index("dp")
    c = lax.axis_index("ctx")
    g_start, g_hop, g_finish = chain_gather(own_g, g_all, g_sems, d, c, levels)

    @pl.when(step == 0)
    def _():
        greet_line(d, c, levels)
        for m in range(micro):
            g_start(m)

    last = 4 * tiles - 1
    for at, hop, m in ((4, 0, 0), (7, 0, 1), (11, 1, 0), (14, 1, 1)):
        @pl.when(step == at)
        def _(hop=hop, m=m):
            g_hop(hop, m)

    seq = step // (2 * tiles)
    phase = lax.rem(step, 2 * tiles) // tiles
    tile = lax.rem(step, tiles)
    rows = pl.ds(pl.multiple_of(tile * TILE, TILE), TILE)
    n_expand = panels.shape[0] - 3
    scale = 1.0 / math.sqrt(HEAD)

    @pl.when(phase == 0)
    def _():
        values_in = x[...].astype(jnp.float32)
        centered = values_in - jnp.mean(values_in, axis=1, keepdims=True)
        normal = centered * lax.rsqrt(jnp.mean(centered * centered, axis=1, keepdims=True) + 1e-05)
        hidden_attn[...] = (normal * gains[0:1, :] + gains[1:2, :]).astype(jnp.bfloat16)
        hidden_mlp[...] = (normal * gains[2:3, :] + gains[3:4, :]).astype(jnp.bfloat16)
        for part in range(3):
            joined = dot_nn(hidden_attn[...], panels[part]) + qkv_shift[:, part * HEAD : (part + 1) * HEAD]
            if part < 2:
                joined = turn(joined, cos[rows, :], sin[rows, :])
            joined = joined.astype(jnp.bfloat16)
            heads[part] = joined
            head_rows[part, rows, :] = joined
        for part in range(n_expand):
            columns = slice(part * HEAD, (part + 1) * HEAD)
            expanded = dot_nn(hidden_mlp[...], panels[3 + part]) + expand_shift[:, columns]
            cdf = 0.5 * (1.0 + lax.erf(expanded * (1.0 / math.sqrt(2.0))))
            acts[rows, columns] = (expanded * cdf).astype(jnp.bfloat16)
            bell = jnp.exp(-0.5 * expanded * expanded) * (1.0 / math.sqrt(2.0 * math.pi))
            slopes[:, columns] = (cdf + expanded * bell).astype(jnp.bfloat16)

    @pl.when(phase == 1)
    def _():
        scores = dot_nt(head_rows[0, rows, :], head_rows[1]) * scale
        key_at = lax.broadcasted_iota(jnp.int32, scores.shape, 1)
        query_at = lax.broadcasted_iota(jnp.int32, scores.shape, 0) + tile * TILE
        allowed = jnp.logical_or(key_at <= query_at, key_at < prefix[seq])
        scores = jnp.where(allowed, scores, -1e30)
        expo = jnp.exp(scores - jnp.max(scores, axis=1, keepdims=True))
        low_probs = (expo * (1.0 / jnp.sum(expo, axis=1, keepdims=True))).astype(jnp.bfloat16)
        probs[0] = low_probs
        features[:, :HEAD] = dot_nn(low_probs, head_rows[2]).astype(jnp.bfloat16)
        features[:, HEAD:] = acts[rows, :]
        width = out_w.shape[1]
        for start in range(0, width, 512):
            columns = slice(start, start + 512)
            partial[:, columns] = dot_nn(features[...], out_w[:, columns]).astype(jnp.bfloat16)

    @pl.when(step == last)
    def _():
        for m in range(micro):
            for hop in range(2, levels - 1):
                g_hop(hop, m)
        for m in range(micro):
            g_finish(m)


def whole_spec(array):
    zeros = (0,) * array.ndim
    return pl.BlockSpec(array.shape, lambda step: zeros, pipeline_mode=pl.Buffered(1))


def forward_call(levels, prefix, x, own_g, panels, out_w, gains, qkv_shift, expand_shift, cos, sin):
    tokens, width = x.shape
    length = cos.shape[0]
    tiles = length // TILE
    steps = 2 * tokens // TILE
    hidden = expand_shift.shape[1]

    def early(step):
        seq, at = step // (2 * tiles), lax.rem(step, 2 * tiles)
        return seq * tiles + jnp.minimum(at, tiles - 1)

    def late(step):
        seq, at = step // (2 * tiles), lax.rem(step, 2 * tiles)
        return seq * tiles + jnp.maximum(at - tiles, 0)

    kind = jnp.bfloat16
    return pl.pallas_call(
        functools.partial(forward_kernel, tiles, levels),
        grid=(steps,),
        out_shape=(
            jax.ShapeDtypeStruct((tokens, width), kind),
            jax.ShapeDtypeStruct((tokens, width), kind),
            jax.ShapeDtypeStruct((3, tokens, HEAD), kind),
            jax.ShapeDtypeStruct((tokens // length, length, length), kind),
            jax.ShapeDtypeStruct((tokens, HEAD + hidden), kind),
            jax.ShapeDtypeStruct((tokens, hidden), kind),
            jax.ShapeDtypeStruct((tokens, width), kind),
            jax.ShapeDtypeStruct((tokens // length, length, width), kind),
        ),
        in_specs=[
            pl.BlockSpec(memory_space=pltpu.SMEM),
            pl.BlockSpec((TILE, width), lambda step: (early(step), 0)),
            pl.BlockSpec(memory_space=pl.ANY),
            whole_spec(panels),
            whole_spec(out_w),
            whole_spec(gains),
            whole_spec(qkv_shift),
            whole_spec(expand_shift),
            whole_spec(cos),
            whole_spec(sin),
        ],
        out_specs=(
            pl.BlockSpec((TILE, width), lambda step: (early(step), 0)),
            pl.BlockSpec((TILE, width), lambda step: (early(step), 0)),
            pl.BlockSpec((3, TILE, HEAD), lambda step: (0, early(step), 0)),
            pl.BlockSpec((1, TILE, length), lambda step: (late(step) // tiles, lax.rem(late(step), tiles), 0)),
            pl.BlockSpec((TILE, HEAD + hidden), lambda step: (late(step), 0)),
            pl.BlockSpec((TILE, hidden), lambda step: (early(step), 0)),
            pl.BlockSpec((TILE, width), lambda step: (late(step), 0)),
            pl.BlockSpec(memory_space=pl.ANY),
        ),
        scratch_shapes=[
            pltpu.VMEM((3, length, HEAD), kind),
            pltpu.VMEM((length, hidden), kind),
            *chain_scratch(levels, tokens // length),
        ],
        compiler_params=pltpu.CompilerParams(
            collective_id=3, has_side_effects=True, vmem_limit_bytes=56 * 1024 * 1024
        ),
        cost_estimate=pl.CostEstimate(
            flops=2 * tokens * width * (2 * hidden + 4 * HEAD) + 4 * tokens * length * HEAD,
            bytes_accessed=64 * 1024 * 1024,
            transcendentals=0,
        ),
        name="forward_part",
    )(prefix, x, own_g, panels, out_w, gains, qkv_shift, expand_shift, cos, sin)


def outside_in(levels):
    return [levels - 1 - place // 2 if place % 2 == 0 else place // 2 for place in range(levels)]


def chain_reduce(own, recv, sems, d, c, levels):
    chain_send, chain_recv = sems
    z = c // 2
    span = recv.shape[2]

    def copy(way, level):
        return remote(
            own(level),
            recv.at[way, level - 1 + way],
            chain_send.at[way, level],
            chain_recv.at[way, level],
            d,
            c + (2 if way == 0 else -2),
        )

    def sends(way, level):
        return z < level if way == 0 else z > level

    def hears(way, level):
        if way == 0:
            return jnp.logical_and(z >= 1, z <= level)
        return jnp.logical_and(z <= levels - 2, z >= level)

    def add(way, level):
        copy(way, level).wait_recv()
        add_into(own(level), (own(level), recv.at[way, level - 1 + way]), span)

    def open_level(level):
        for way, place in ((0, 0), (1, levels - 1)):
            if place != level:
                @pl.when(z == place)
                def _(way=way):
                    copy(way, level).start()

    def turn_round(index):
        for level in range(levels):
            for way in range(2):
                behind = levels - 1 - level if way == 0 else level
                place = index - behind if way == 0 else levels - 1 - (index - behind)
                if behind < index and (place < level if way == 0 else place > level):
                    @pl.when(z == place)
                    def _(way=way, level=level):
                        add(way, level)
                        copy(way, level).start()

    def end(store):
        for level in range(levels):
            for way in range(2):
                if 0 <= level - 1 + way < levels - 1:
                    @pl.when(jnp.logical_and(z == level, hears(way, level)))
                    def _(way=way, level=level):
                        add(way, level)

            @pl.when(z == level)
            def _(level=level):
                store(level).start()

    def finish(store):
        for level in range(levels):
            for way in range(2):
                if 0 <= level - 1 + way < levels - 1:
                    @pl.when(sends(way, level))
                    def _(way=way, level=level):
                        copy(way, level).wait_send()

        store(0).wait()

    return open_level, turn_round, end, finish


def square_sum(first, passing, recv, last, final, sems, d, c, count):
    first_send, first_recv, last_send, last_recv = sems
    x_mate = d + 1 - 2 * lax.rem(d, 2)
    y_mate = lax.rem(d + 2, 4)
    mates = ((x_mate, y_mate), (y_mate, x_mate))

    def first_copy(way, slot):
        return remote(
            first(way, slot), recv.at[way, slot], first_send.at[way, slot], first_recv.at[way, slot], mates[way][0], c
        )

    def last_copy(way):
        return remote(passing(way), last.at[way], last_send.at[way], last_recv.at[way], mates[way][1], c)

    def pass_on(way):
        first_copy(way, 1).wait_recv()
        add_into(passing(way), (passing(way), recv.at[way, 1]), count)
        last_copy(way).start()

    def arrive(way):
        first_copy(way, 0).wait_recv()
        last_copy(way).wait_recv()

    def add_final(way, start, rows):
        at = pl.ds(start, rows)
        own = final(way).at[at]
        add_into(own, (own, recv.at[way, 0, at], last.at[way, at]), rows)

    def finish():
        for way in range(2):
            first_copy(way, 0).wait_send()
            first_copy(way, 1).wait_send()
            last_copy(way).wait_send()

    return first_copy, pass_on, arrive, add_final, finish


def square_scratch():
    dma = pltpu.SemaphoreType.DMA
    return [dma((2, 2)), dma((2, 2)), dma((2,)), dma((2,))]


def backward_kernel(
    tiles,
    dp_size,
    ctx_size,
    g,
    x,
    panels,
    out_w,
    gains,
    cos,
    sin,
    heads,
    probs,
    slopes,
    features,
    grads,
    grad_expanded,
    grad_joined,
    combined,
    norm_sums,
    joined_sums,
    expand_sums,
    back_out,
    shrink_out,
    dense_out,
    grad_queries,
    grad_keys,
    grad_values,
    board,
    back_core,
    back_chain,
    left,
    right,
    out_own,
    out_recv,
    out_last,
    dense_own,
    dense_recv,
    left_sem,
    right_sem,
    core_send,
    core_recv,
    chain_send,
    chain_recv,
    first_send,
    first_recv,
    last_send,
    last_recv,
    dense_send,
    dense_sem,
    store_sem,
):
    step = pl.program_id(0)
    seq = step // (2 * tiles)
    phase = lax.rem(step, 2 * tiles) // tiles
    tile = lax.rem(step, tiles)
    tile = jnp.where(phase == 0, tile, jnp.where(lax.rem(tile, 2) == 0, tiles - 1 - tile // 2, tile // 2))
    rows = pl.ds(pl.multiple_of(tile * TILE, TILE), TILE)
    n_expand = panels.shape[0] - 3
    width = out_w.shape[1]
    scale = 1.0 / math.sqrt(HEAD)

    d = lax.axis_index("dp")
    c = lax.axis_index("ctx")
    z = c // 2
    core = lax.rem(c, 2)
    sibling = c + 1 - 2 * core
    x_mate = d + 1 - 2 * lax.rem(d, 2)
    y_mate = lax.rem(d + 2, 4)
    diagonal = 3 - d
    levels = ctx_size // 2
    me = d * ctx_size + c
    span = board.shape[2]
    share = dense_out.shape[0]
    unit = (features.shape[1] - HEAD) // dp_size
    out_half = unit // 2
    head_half = HEAD // 2

    def left_copy(index):
        if index == 0:
            columns = pl.ds(0, HEAD)
        else:
            owner = (diagonal, x_mate, y_mate, d)[index - 1]
            columns = pl.ds(pl.multiple_of(HEAD + owner * unit, HEAD), unit)
        return pltpu.make_async_copy(features.at[:, columns], left.at[index % 2], left_sem.at[index % 2])

    right_copy = pltpu.make_async_copy(grads, right, right_sem.at[0])

    def compute(index):
        if index < dp_size:
            left_copy(index + 1).start()
        left_copy(index).wait()
        target = dense_own if index == 0 else out_own.at[index - 1]
        for start in range(0, width, 1024):
            columns = slice(start, start + 1024)
            target[:, columns] = dot_tn(left[index % 2], right[:, columns]).astype(jnp.bfloat16)

    def out_rows(index, way):
        return out_own.at[index, pl.ds(way * out_half, out_half)]

    first_copy, pass_on, arrive, add_final, square_finish = square_sum(
        lambda way, slot: out_rows(0 if slot == 1 else 1 + way, way),
        lambda way: out_rows(2 - way, way),
        out_recv,
        out_last,
        lambda way: out_rows(3, way),
        (first_send, first_recv, last_send, last_recv),
        d,
        c,
        out_half,
    )

    def out_store(way):
        return pltpu.make_async_copy(
            out_rows(3, way), shrink_out.at[pl.ds(way * out_half, out_half)], store_sem.at[way]
        )

    source = c // (ctx_size // dp_size)
    at_source = d == source
    from_x = x_mate == source
    from_y = y_mate == source
    across = diagonal == source
    per_head = HEAD // share

    def dense_half(way):
        return dense_own.at[pl.ds(way * head_half, head_half)]

    def dense_copy(way, mate):
        return remote(dense_half(way), dense_recv.at[way], dense_send.at[way], dense_sem.at[way], mate, c)

    def dense_add(way, mate):
        dense_copy(way, mate).wait_recv()
        add_into(dense_half(way), (dense_half(way), dense_recv.at[way]), head_half)

    def dense_open():
        @pl.when(from_y)
        def _():
            dense_copy(0, x_mate).start()

        @pl.when(from_x)
        def _():
            dense_copy(1, y_mate).start()

    def dense_second():
        @pl.when(across)
        def _():
            dense_add(0, y_mate)
            dense_copy(0, y_mate).start()
            dense_add(1, x_mate)
            dense_copy(1, x_mate).start()

    def dense_third():
        @pl.when(from_x)
        def _():
            dense_add(0, x_mate)
            dense_copy(0, x_mate).start()

        @pl.when(from_y)
        def _():
            dense_add(1, y_mate)
            dense_copy(1, y_mate).start()

    first_owner = lax.rem(c, ctx_size // per_head) * per_head

    def dense_chunk(piece):
        return dense_own.at[pl.ds(piece * share, share)]

    def dense_send_out(piece):
        return remote(
            dense_chunk(piece), dense_out, dense_send.at[2 + piece], dense_sem.at[2], d, first_owner + piece
        )

    def dense_store(piece):
        return pltpu.make_async_copy(dense_chunk(piece), dense_out, store_sem.at[2])

    def dense_fourth():
        @pl.when(at_source)
        def _():
            dense_add(0, x_mate)
            dense_add(1, y_mate)
            for piece in range(per_head):
                @pl.when(first_owner + piece == c)
                def _(piece=piece):
                    dense_store(piece).start()

                @pl.when(first_owner + piece != c)
                def _(piece=piece):
                    dense_send_out(piece).start()

    def dense_finish():
        @pl.when(jnp.logical_or(jnp.logical_or(from_y, across), from_x))
        def _():
            dense_copy(0, x_mate).wait_send()
            dense_copy(1, x_mate).wait_send()

        for piece in range(per_head):
            @pl.when(jnp.logical_and(at_source, first_owner + piece != c))
            def _(piece=piece):
                dense_send_out(piece).wait_send()

        stays = me // per_head == c

        @pl.when(stays)
        def _():
            dense_store(0).wait()

        @pl.when(jnp.logical_not(stays))
        def _():
            dense_send_out(0).wait_recv()

    def own_block(level):
        return board.at[level, core]

    def core_copy(level):
        return remote(
            board.at[level, 1 - core], back_core.at[level], core_send.at[level], core_recv.at[level], d, sibling
        )

    def core_add(level):
        core_copy(level).wait_recv()
        add_into(own_block(level), (own_block(level), back_core.at[level]), span)

    chain_open, chain_round, chain_end, chain_finish = chain_reduce(
        own_block, back_chain, (chain_send, chain_recv), d, c, levels
    )

    def back_store(level):
        return pltpu.make_async_copy(own_block(level), back_out, store_sem.at[3])

    def at(when):
        return pl.when(step == when)

    @at(0)
    def _():
        greet_all(d, c, dp_size, ctx_size)
        left_copy(0).start()
        right_copy.start()
        norm_sums[...] = jnp.zeros_like(norm_sums)
        joined_sums[...] = jnp.zeros_like(joined_sums)
        expand_sums[...] = jnp.zeros_like(expand_sums)

    @at(1)
    def _():
        right_copy.wait()
        compute(0)
        dense_open()

    @at(2)
    def _():
        compute(1)
        first_copy(0, 1).start()
        first_copy(1, 1).start()

    @at(3)
    def _():
        compute(2)
        first_copy(0, 0).start()
        compute(3)
        first_copy(1, 0).start()

    @at(4)
    def _():
        compute(4)

    for place, level in enumerate(outside_in(levels)):
        @at(tiles + 1 + place)
        def _(level=level):
            core_copy(level).start()

        @at(tiles + 2 + place)
        def _(level=level):
            core_add(level)
            chain_open(level)

    @at(6)
    def _():
        dense_second()

    @at(7)
    def _():
        pass_on(0)
        pass_on(1)

    @at(10)
    def _():
        chain_round(1)
        dense_third()

    @at(13)
    def _():
        chain_round(2)
        for way in range(2):
            arrive(way)
            add_final(way, 0, out_half)
            out_store(way).start()

    @at(14)
    def _():
        dense_fourth()

    @pl.when(phase == 0)
    def _():
        low_probs = probs[0]
        own = dot_nt(g[...], out_w[:HEAD, :]).astype(jnp.bfloat16)
        grad_probs = dot_nt(own, heads[2])
        wide = low_probs.astype(jnp.float32)
        delta = jnp.sum(wide * grad_probs, axis=1, keepdims=True)
        grad_scores = (wide * (grad_probs - delta)).astype(jnp.bfloat16)
        grad_queries[rows, :] = dot_nn(grad_scores, heads[1]) * scale
        more_keys = dot_tn(grad_scores, heads[0, rows, :]) * scale
        more_values = dot_tn(low_probs, own)

        @pl.when(tile == 0)
        def _():
            grad_keys[...] = more_keys
            grad_values[...] = more_values

        @pl.when(tile > 0)
        def _():
            grad_keys[...] += more_keys
            grad_values[...] += more_values

    @pl.when(phase == 1)
    def _():
        for part in range(n_expand):
            columns = slice(part * HEAD, (part + 1) * HEAD)
            grad = dot_nt(g[...], out_w[(part + 1) * HEAD : (part + 2) * HEAD, :])
            grad = (grad * slopes[:, columns].astype(jnp.float32)).astype(jnp.bfloat16)
            grad_expanded[:, columns] = grad
            expand_sums[:, columns] += jnp.sum(grad.astype(jnp.float32), axis=0, keepdims=True)
        cos_rows, sin_rows = cos[rows, :], -sin[rows, :]
        parts = (
            turn(grad_queries[rows, :], cos_rows, sin_rows),
            turn(grad_keys[rows, :], cos_rows, sin_rows),
            grad_values[rows, :],
        )
        for part in range(3):
            columns = slice(part * HEAD, (part + 1) * HEAD)
            joined = parts[part].astype(jnp.bfloat16)
            grad_joined[:, columns] = joined
            joined_sums[:, columns] += jnp.sum(joined.astype(jnp.float32), axis=0, keepdims=True)
        values_in = x[...].astype(jnp.float32)
        mean = jnp.mean(values_in, axis=1, keepdims=True)
        centered = values_in - mean
        spread = lax.rsqrt(jnp.mean(centered * centered, axis=1, keepdims=True) + 1e-05)
        for start in range(0, width, 512):
            columns = slice(start, start + 512)
            normal = (x[:, columns].astype(jnp.float32) - mean) * spread
            total = dot_nt(grad_joined[:, :HEAD], panels[0, columns, :])
            for part in range(1, 3):
                total += dot_nt(grad_joined[:, part * HEAD : (part + 1) * HEAD], panels[part, columns, :])
            other = dot_nt(grad_expanded[:, :HEAD], panels[3, columns, :])
            for part in range(1, n_expand):
                other += dot_nt(grad_expanded[:, part * HEAD : (part + 1) * HEAD], panels[3 + part, columns, :])
            for row, value in ((0, total * normal), (1, total), (2, other * normal), (3, other)):
                norm_sums[row : row + 1, columns] += jnp.sum(value, axis=0, keepdims=True)
            value = (total * gains[0:1, columns] + other * gains[2:3, columns]).astype(jnp.bfloat16)

            @pl.when(seq == 0)
            def _(columns=columns, value=value):
                for parity in range(2):
                    board[tile, parity, :, columns] = value[parity * span : (parity + 1) * span]

            @pl.when(seq > 0)
            def _(columns=columns, value=value):
                combined[:, columns] = value

    @at(4 * tiles - 1)
    def _():
        chain_end(back_store)
        square_finish()
        for way in range(2):
            out_store(way).wait()
        dense_finish()
        for level in range(levels):
            core_copy(level).wait_send()
        chain_finish(back_store)


def backward_call(dp_size, ctx_size, g, x, panels, out_w, gains, cos, sin, heads, probs, slopes, features):
    tokens, width = x.shape
    length = cos.shape[0]
    tiles = length // TILE
    steps = 2 * tokens // TILE
    hidden = slopes.shape[1]
    levels = ctx_size // 2
    span = length // ctx_size
    unit = hidden // dp_size
    share = width // (dp_size * ctx_size)
    dma = pltpu.SemaphoreType.DMA
    vmem = pltpu.VMEM

    def first(step):
        seq, at = step // (2 * tiles), lax.rem(step, 2 * tiles)
        return seq * tiles + jnp.minimum(at, tiles - 1)

    def mixed_order(place):
        return jnp.where(lax.rem(place, 2) == 0, tiles - 1 - place // 2, place // 2)

    def second(step):
        seq, at = step // (2 * tiles), lax.rem(step, 2 * tiles)
        return seq * tiles + mixed_order(jnp.maximum(at - tiles, 0))

    def both(step):
        seq, at = step // (2 * tiles), lax.rem(step, 2 * tiles)
        return seq * tiles + jnp.where(at < tiles, at, mixed_order(at - tiles))

    def late(step):
        return jnp.where(step < 2 * tiles, mixed_order(0), second(step) - tiles)

    kind = jnp.bfloat16
    fixed = lambda step: (0, 0)
    anywhere = pl.BlockSpec(memory_space=pl.ANY)
    return pl.pallas_call(
        functools.partial(backward_kernel, tiles, dp_size, ctx_size),
        grid=(steps,),
        out_shape=(
            jax.ShapeDtypeStruct((tokens, hidden), kind),
            jax.ShapeDtypeStruct((tokens, 3 * HEAD), kind),
            jax.ShapeDtypeStruct((length, width), kind),
            jax.ShapeDtypeStruct((8, width), jnp.float32),
            jax.ShapeDtypeStruct((1, 3 * HEAD), jnp.float32),
            jax.ShapeDtypeStruct((1, hidden), jnp.float32),
            jax.ShapeDtypeStruct((span, width), kind),
            jax.ShapeDtypeStruct((unit, width), kind),
            jax.ShapeDtypeStruct((share, width), kind),
        ),
        in_specs=[
            pl.BlockSpec((TILE, width), lambda step: (both(step), 0)),
            pl.BlockSpec((TILE, width), lambda step: (second(step), 0)),
            whole_spec(panels),
            whole_spec(out_w),
            whole_spec(gains),
            whole_spec(cos),
            whole_spec(sin),
            pl.BlockSpec((3, length, HEAD), lambda step: (0, step // (2 * tiles), 0)),
            pl.BlockSpec((1, TILE, length), lambda step: (first(step) // tiles, lax.rem(first(step), tiles), 0)),
            pl.BlockSpec((TILE, hidden), lambda step: (second(step), 0)),
            anywhere,
            anywhere,
        ],
        out_specs=(
            pl.BlockSpec((TILE, hidden), lambda step: (second(step), 0)),
            pl.BlockSpec((TILE, 3 * HEAD), lambda step: (second(step), 0)),
            pl.BlockSpec((TILE, width), lambda step: (late(step), 0)),
            pl.BlockSpec((8, width), fixed),
            pl.BlockSpec((1, 3 * HEAD), fixed),
            pl.BlockSpec((1, hidden), fixed),
            anywhere,
            anywhere,
            anywhere,
        ),
        scratch_shapes=[
            vmem((length, HEAD), jnp.float32),
            vmem((length, HEAD), jnp.float32),
            vmem((length, HEAD), jnp.float32),
            vmem((levels, 2, span, width), kind),
            vmem((levels, span, width), kind),
            vmem((2, levels - 1, span, width), kind),
            vmem((2, tokens, HEAD), kind),
            vmem((tokens, width), kind),
            vmem((dp_size, unit, width), kind),
            vmem((2, 2, unit // 2, width), kind),
            vmem((2, unit // 2, width), kind),
            vmem((HEAD, width), kind),
            vmem((2, HEAD // 2, width), kind),
            dma((2,)),
            dma((1,)),
            dma((levels,)),
            dma((levels,)),
            dma((2, levels)),
            dma((2, levels)),
            *square_scratch(),
            dma((2 + HEAD // share,)),
            dma((3,)),
            dma((4,)),
        ],
        compiler_params=pltpu.CompilerParams(
            collective_id=4, has_side_effects=True, vmem_limit_bytes=60 * 1024 * 1024
        ),
        name="backward_part",
    )(g, x, panels, out_w, gains, cos, sin, heads, probs, slopes, features, g)


def reduce_kernel(
    dp_size,
    ctx_size,
    back,
    hidden_attn,
    hidden_mlp,
    grad_joined,
    grad_expanded,
    board,
    back_out,
    attn_out,
    mlp_out,
    tail_out,
    back_own,
    back_core,
    back_chain,
    left,
    right_attn,
    right_mlp,
    attn_own,
    attn_recv,
    attn_last,
    mlp_own,
    mlp_recv,
    mlp_last,
    board_recv,
    load_sem,
    left_sem,
    right_sem,
    core_send,
    core_recv,
    chain_send,
    chain_recv,
    first_send_a,
    first_recv_a,
    last_send_a,
    last_recv_a,
    first_send_m,
    first_recv_m,
    last_send_m,
    last_recv_m,
    row_send,
    row_recv,
    board_sem,
    store_sem,
):
    d = lax.axis_index("dp")
    c = lax.axis_index("ctx")
    core = lax.rem(c, 2)
    sibling = c + 1 - 2 * core
    x_mate = d + 1 - 2 * lax.rem(d, 2)
    y_mate = lax.rem(d + 2, 4)
    diagonal = 3 - d
    span = back.shape[0] // ctx_size
    levels = ctx_size // 2
    devices = dp_size * ctx_size
    me = d * ctx_size + c
    group_rows = hidden_attn.shape[1] // dp_size
    half = group_rows // 2
    rows = group_rows // ctx_size

    greet_all(d, c, dp_size, ctx_size)

    def back_view(parity, level):
        start = (2 * level + parity) * span
        return back.at[pl.ds(pl.multiple_of(start, span), span)]

    def back_load(level):
        return pltpu.make_async_copy(back_view(core, level), back_own.at[level], load_sem.at[level])

    def core_copy(level):
        return remote(
            back_view(1 - core, level), back_core.at[level], core_send.at[level], core_recv.at[level], d, sibling
        )

    order = outside_in(levels)

    tile_of = []
    for owners in ((diagonal, diagonal), (x_mate, y_mate), (y_mate, x_mate), (d, d)):
        for way in range(2):
            tile_of.append((owners[way], way))
    sequence = [(0, index) for index in range(6)]
    sequence += [(1, index) for index in range(4)]
    sequence += [(0, index) for index in range(6, 8)]
    sequence += [(1, index) for index in range(4, 8)]

    def left_copy(place):
        kind, index = sequence[place]
        owner, way = tile_of[index]
        columns = pl.ds(pl.multiple_of(owner * group_rows + way * half, half), half)
        source = (hidden_attn, hidden_mlp)[kind]
        return pltpu.make_async_copy(source.at[:, columns], left.at[place % 2], left_sem.at[place % 2])

    right_copies = (
        pltpu.make_async_copy(grad_joined, right_attn, right_sem.at[0]),
        pltpu.make_async_copy(grad_expanded, right_mlp, right_sem.at[1]),
    )

    def compute(kind, index):
        place = sequence.index((kind, index))
        if place + 1 < len(sequence):
            left_copy(place + 1).start()
        left_copy(place).wait()
        if index == 0:
            right_copies[kind].wait()
        target, right = ((attn_own, right_attn), (mlp_own, right_mlp))[kind]
        target[index] = dot_tn(left[place % 2], right[...]).astype(jnp.bfloat16)

    def square(own, recv, last, sems):
        return square_sum(
            lambda way, slot: own.at[way + 2 * (1 - slot)],
            lambda way: own.at[4 + way],
            recv,
            last,
            lambda way: own.at[6 + way],
            sems,
            d,
            c,
            half,
        )

    squares = (
        square(attn_own, attn_recv, attn_last, (first_send_a, first_recv_a, last_send_a, last_recv_a)),
        square(mlp_own, mlp_recv, mlp_last, (first_send_m, first_recv_m, last_send_m, last_recv_m)),
    )

    per_half = half // rows

    def row_chunk(kind, way, piece):
        return (attn_own, mlp_own)[kind].at[6 + way, pl.ds(piece * rows, rows)]

    def row_copy(kind, way, piece):
        target = way * per_half + piece
        out = (attn_out, mlp_out)[kind]
        return remote(
            row_chunk(kind, way, piece), out.at[c], row_send.at[kind, target], row_recv.at[kind], d, target
        )

    def row_local(kind, way, piece):
        out = (attn_out, mlp_out)[kind]
        return pltpu.make_async_copy(row_chunk(kind, way, piece), out.at[c], store_sem.at[kind])

    def tile_end(kind):
        first_copy, pass_on, arrive, add_final, finish = squares[kind]
        for way in range(2):
            arrive(way)
            for piece in range(per_half):
                add_final(way, piece * rows, rows)
                target = way * per_half + piece

                @pl.when(c != target)
                def _(way=way, piece=piece):
                    row_copy(kind, way, piece).start()

                @pl.when(c == target)
                def _(way=way, piece=piece):
                    row_local(kind, way, piece).start()

    board_load = pltpu.make_async_copy(board.at[me], board_recv.at[me], load_sem.at[levels])

    def board_start():
        board_load.start()

        def push_board(step, carry):
            other = lax.rem(me + step, devices)
            remote(
                board.at[other],
                board_recv.at[me],
                board_sem.at[0],
                board_sem.at[1],
                other // ctx_size,
                lax.rem(other, ctx_size),
            ).start()
            return carry

        lax.fori_loop(1, devices, push_board, 0)

    def board_end():
        board_load.wait()
        rest = board_recv.at[pl.ds(0, devices - 1)]
        remote(rest, rest, board_sem.at[0], board_sem.at[1], d, sibling).wait()
        tail_out[...] = jnp.sum(board_recv[...], axis=0)

    chain_open, chain_round, chain_end, chain_finish = chain_reduce(
        lambda level: back_own.at[level], back_chain, (chain_send, chain_recv), d, c, levels
    )

    def back_store(level):
        return pltpu.make_async_copy(back_own.at[level], back_out, store_sem.at[2])

    right_copies[0].start()
    left_copy(0).start()
    for level in order:
        core_copy(level).start()
        back_load(level).start()
    right_copies[1].start()

    for way in range(2):
        compute(0, way)
        squares[0][0](way, 1).start()
    for way in range(2):
        compute(0, 2 + way)
        squares[0][0](way, 0).start()
    for level in order:
        back_load(level).wait()
        core_copy(level).wait_recv()
        own = back_own.at[level]
        add_into(own, (own, back_core.at[level]), span)
        chain_open(level)
    compute(0, 4)
    compute(0, 5)
    squares[0][1](0)
    squares[0][1](1)
    for way in range(2):
        compute(1, way)
        squares[1][0](way, 1).start()
    for way in range(2):
        compute(1, 2 + way)
        squares[1][0](way, 0).start()
    chain_round(1)
    board_start()
    compute(0, 6)
    compute(0, 7)
    compute(1, 4)
    compute(1, 5)
    tile_end(0)
    chain_round(2)
    compute(1, 6)
    compute(1, 7)
    squares[1][1](0)
    squares[1][1](1)
    chain_end(back_store)
    tile_end(1)
    board_end()

    for kind in range(2):
        squares[kind][4]()
        for way in range(2):
            for piece in range(per_half):
                target = way * per_half + piece

                @pl.when(c != target)
                def _(kind=kind, way=way, piece=piece):
                    row_copy(kind, way, piece).wait_send()

        out = (attn_out, mlp_out)[kind]
        rest = out.at[pl.ds(0, ctx_size - 1)]
        remote(rest, rest, row_send.at[kind, 0], row_recv.at[kind], d, sibling).wait_recv()
        row_local(kind, 0, 0).wait()
    for level in range(levels):
        core_copy(level).wait_send()
    chain_finish(back_store)


def reduce_call(dp_size, ctx_size, back, hidden_attn, hidden_mlp, grad_joined, grad_expanded, board):
    length, width = back.shape
    tokens = hidden_attn.shape[0]
    span = length // ctx_size
    group_rows = width // dp_size
    half = group_rows // 2
    rows = group_rows // ctx_size
    joined, hidden = grad_joined.shape[1], grad_expanded.shape[1]
    levels = ctx_size // 2
    devices = dp_size * ctx_size
    dma = pltpu.SemaphoreType.DMA
    kind = back.dtype
    vmem = pltpu.VMEM
    out_shape = (
        jax.ShapeDtypeStruct((span, width), kind),
        jax.ShapeDtypeStruct((ctx_size, rows, joined), kind),
        jax.ShapeDtypeStruct((ctx_size, rows, hidden), kind),
        jax.ShapeDtypeStruct(board.shape[1:], jnp.float32),
    )
    anywhere = pl.BlockSpec(memory_space=pl.ANY)
    return pl.pallas_call(
        functools.partial(reduce_kernel, dp_size, ctx_size),
        out_shape=out_shape,
        in_specs=[anywhere] * 6,
        out_specs=(anywhere,) * 3 + (pl.BlockSpec(memory_space=pltpu.VMEM),),
        scratch_shapes=[
            vmem((levels, span, width), kind),
            vmem((levels, span, width), kind),
            vmem((2, levels - 1, span, width), kind),
            vmem((2, tokens, HEAD), kind),
            vmem((tokens, joined), kind),
            vmem((tokens, hidden), kind),
            vmem((8, half, joined), kind),
            vmem((2, 2, half, joined), kind),
            vmem((2, half, joined), kind),
            vmem((8, half, hidden), kind),
            vmem((2, 2, half, hidden), kind),
            vmem((2, half, hidden), kind),
            vmem((devices,) + board.shape[1:], jnp.float32),
            dma((levels + 1,)),
            dma((2,)),
            dma((2,)),
            dma((levels,)),
            dma((levels,)),
            dma((2, levels)),
            dma((2, levels)),
            *square_scratch(),
            *square_scratch(),
            dma((2, ctx_size)),
            dma((2,)),
            dma((2,)),
            dma((3,)),
        ],
        compiler_params=pltpu.CompilerParams(
            collective_id=2, has_side_effects=True, vmem_limit_bytes=60 * 1024 * 1024
        ),
        name="reduce_all",
    )(back, hidden_attn, hidden_mlp, grad_joined, grad_expanded, board)


def finish_kernel(
    attn_rows,
    mlp_rows,
    shrink_rows,
    dense_rows,
    back_first,
    back_last,
    x,
    g,
    reduced,
    out_shift,
    qkv_grad,
    expand_grad,
    shrink_grad,
    dense_grad,
    layer_output,
    input_grad,
):
    ctx_size = attn_rows.shape[0]
    for rows, target in ((attn_rows, qkv_grad), (mlp_rows, expand_grad)):
        for member in range(ctx_size):
            for part in range(rows.shape[2] // HEAD):
                start = (part * ctx_size + member) * HEAD
                target[:, start : start + HEAD] = rows[member, :, part * HEAD : (part + 1) * HEAD].astype(jnp.float32)
    shrink_grad[...] = shrink_rows[...].astype(jnp.float32)
    dense_grad[...] = dense_rows[...].astype(jnp.float32)
    for m, back in enumerate((back_first, back_last)):
        own = x[m].astype(jnp.float32)
        layer_output[m] = (own + reduced[m].astype(jnp.float32) + out_shift[...]).astype(jnp.bfloat16)
        centered = own - jnp.mean(own, axis=1, keepdims=True)
        spread = lax.rsqrt(jnp.mean(centered * centered, axis=1, keepdims=True) + 1e-05)
        normal = centered * spread
        grad = back[...].astype(jnp.float32)
        share = spread * (
            grad
            - jnp.mean(grad, axis=1, keepdims=True)
            - normal * jnp.mean(grad * normal, axis=1, keepdims=True)
        )
        input_grad[m] = (g[m].astype(jnp.float32) + share).astype(jnp.bfloat16)


def finish_call(attn_rows, mlp_rows, shrink_rows, dense_rows, back_first, back_last, x, g, reduced, out_shift):
    steps = 4
    arrays = (attn_rows, mlp_rows, shrink_rows, dense_rows, back_first, back_last, x, g, reduced)
    micro = x.shape[0]
    ctx_size, rows, joined = attn_rows.shape

    def spec(shape):
        block = shape[:-2] + (shape[-2] // steps, shape[-1])
        lead = (0,) * (len(shape) - 2)
        return pl.BlockSpec(block, lambda step: lead + (step, 0))

    outs = (
        jax.ShapeDtypeStruct((rows, joined * ctx_size), jnp.float32),
        jax.ShapeDtypeStruct((rows, mlp_rows.shape[2] * ctx_size), jnp.float32),
        jax.ShapeDtypeStruct(shrink_rows.shape, jnp.float32),
        jax.ShapeDtypeStruct(dense_rows.shape, jnp.float32),
        jax.ShapeDtypeStruct(x.shape, jnp.bfloat16),
        jax.ShapeDtypeStruct(x.shape, jnp.bfloat16),
    )
    return pl.pallas_call(
        finish_kernel,
        grid=(steps,),
        out_shape=outs,
        in_specs=[spec(array.shape) for array in arrays] + [whole_spec(out_shift)],
        out_specs=tuple(spec(out.shape) for out in outs),
        compiler_params=pltpu.CompilerParams(vmem_limit_bytes=40 * 1024 * 1024),
        name="finish_part",
    )(*arrays, out_shift)


def tensor_shards(
    layer_input,
    out_grad,
    prefix_len,
    qkv_weight,
    qkv_bias,
    dense_weight,
    dense_bias,
    expand_weight,
    expand_bias,
    shrink_weight,
    shrink_bias,
    attn_gain,
    attn_shift,
    mlp_gain,
    mlp_shift,
):
    dp_size = lax.axis_size("dp")
    ctx_size = lax.axis_size("ctx")
    devices = dp_size * ctx_size
    me = lax.axis_index("ctx")
    group = lax.axis_index("dp")
    micro, seq_count, span, width = layer_input.shape
    sequences = micro * seq_count
    tokens = sequences * SEQ
    row_share = qkv_weight.shape[0]
    scale = 1.0 / math.sqrt(HEAD)
    ff = expand_weight.shape[1]
    unit = shrink_weight.shape[0]
    lengths = tuple(
        member.shape[0]
        for member in (attn_gain, attn_shift, mlp_gain, mlp_shift, qkv_bias, dense_bias, expand_bias, shrink_bias)
    )
    packed = jnp.concatenate(
        [attn_gain, attn_shift, mlp_gain, mlp_shift, qkv_bias, dense_bias, expand_bias, shrink_bias]
    )
    own_x = layer_input.reshape(sequences, span, width)
    own_g = out_grad.reshape(sequences, span, width)
    count = packed.shape[0]
    packed = jnp.pad(packed, (0, -count % 2048)).reshape(-1, 128)
    x_all, panels, out_part, small = gather_call(
        dp_size, ctx_size, own_x, qkv_weight, expand_weight, dense_weight, shrink_weight, packed
    )
    x_all = x_all.reshape(tokens, width)
    small = unpack_small(small.reshape(devices, -1)[:, :count], lengths, devices)
    gain_attn, shift_attn, gain_mlp, shift_mlp, qkv_shift, dense_shift, expand_shift, shrink_shift = small
    qkv_shift = lax.dynamic_slice_in_dim(qkv_shift.reshape(3, ctx_size, HEAD), me, 1, 1).reshape(-1)
    expand_shift = lax.dynamic_slice_in_dim(
        expand_shift.reshape(dp_size, ctx_size, unit), me, 1, 1
    ).reshape(-1)

    gains = jnp.stack([gain_attn, shift_attn, gain_mlp, shift_mlp])
    cos, sin = turn_tables(SEQ)
    hidden_attn, hidden_mlp, heads, probs, features, slopes, partial, g_all = forward_call(
        ctx_size // 2,
        prefix_len.reshape(sequences),
        x_all,
        own_g,
        panels,
        out_part,
        gains,
        qkv_shift[None],
        expand_shift[None],
        cos,
        sin,
    )
    g_all = g_all.reshape(tokens, width)
    reduced = lax.psum_scatter(
        partial.reshape(sequences, SEQ, width), "ctx", scatter_dimension=1, tiled=True
    )

    (
        grad_expanded,
        grad_joined,
        combined,
        norm_sums,
        joined_sum,
        expand_sum,
        back_first,
        shrink_rows,
        dense_rows,
    ) = backward_call(
        dp_size, ctx_size, g_all, x_all, panels, out_part, gains, cos, sin, heads, probs, slopes, features
    )
    joined_sum, expand_sum = joined_sum[0], expand_sum[0]

    def place(values, parts):
        board = jnp.zeros((parts, ctx_size, values.shape[0] // parts), jnp.float32)
        board = lax.dynamic_update_slice(board, values.reshape(parts, 1, -1), (0, me, 0))
        return board.reshape(devices, -1)

    out_sum = jnp.sum(own_g.astype(jnp.float32), axis=(0, 1))
    board = jnp.concatenate(
        [
            place(joined_sum[: 2 * HEAD], 2),
            place(joined_sum[2 * HEAD :], 1),
            out_sum.reshape(devices, -1),
            place(expand_sum, dp_size),
            norm_sums[0].reshape(devices, -1),
            norm_sums[1].reshape(devices, -1),
            norm_sums[2].reshape(devices, -1),
            norm_sums[3].reshape(devices, -1),
        ],
        axis=1,
    )
    used = board.shape[1]
    board = jnp.pad(board, ((0, 0), (0, -used % 1024))).reshape(devices, -1, 128)
    back_last, attn_rows, mlp_rows, tail = reduce_call(
        dp_size, ctx_size, combined, hidden_attn, hidden_mlp, grad_joined, grad_expanded, board
    )
    qkv_grad, expand_grad, shrink_grad, dense_grad, layer_output, input_grad = finish_call(
        attn_rows,
        mlp_rows,
        shrink_rows,
        dense_rows,
        back_first,
        back_last,
        own_x,
        own_g,
        reduced,
        (dense_shift + shrink_shift)[None],
    )
    layer_output = layer_output.reshape(layer_input.shape)
    input_grad = input_grad.reshape(layer_input.shape)
    tail = tail.reshape(-1)
    share_len = width // devices
    at = 0
    pieces = []
    for length in (2 * share_len, share_len, share_len, ff // devices, share_len, share_len, share_len, share_len):
        pieces.append(tail[at : at + length])
        at += length
    return (
        layer_output,
        input_grad,
        qkv_grad,
        pieces[0],
        pieces[1],
        dense_grad,
        pieces[2],
        expand_grad,
        pieces[3],
        shrink_grad,
        pieces[2],
        pieces[4],
        pieces[5],
        pieces[6],
        pieces[7],
    )


def solution(mesh):
    placed = (
        P(None, "dp", "ctx", None),
        P(None, "dp", "ctx", None),
        P(None, "dp"),
        P(("dp", "ctx"), None),
        P(("dp", "ctx")),
        P(("dp", "ctx"), None),
        P(("dp", "ctx")),
        P(("dp", "ctx"), None),
        P(("dp", "ctx")),
        P(("dp", "ctx"), None),
        P(("dp", "ctx")),
        P(("dp", "ctx")),
        P(("dp", "ctx")),
        P(("dp", "ctx")),
        P(("dp", "ctx")),
    )
    return jax.shard_map(
        tensor_shards if (mesh.shape["dp"], mesh.shape["ctx"]) == (4, HEADS) else shards,
        mesh=mesh,
        in_specs=placed,
        out_specs=(
            P(None, "dp", "ctx", None),
            P(None, "dp", "ctx", None),
            P(("dp", "ctx"), None),
            P(("dp", "ctx")),
            P(("dp", "ctx")),
            P(("dp", "ctx"), None),
            P(("dp", "ctx")),
            P(("dp", "ctx"), None),
            P(("dp", "ctx")),
            P(("dp", "ctx"), None),
            P(("dp", "ctx")),
            P(("dp", "ctx")),
            P(("dp", "ctx")),
            P(("dp", "ctx")),
            P(("dp", "ctx")),
        ),
        check_vma=False,
    )
```

```python
import functools
import math

import jax
import jax.numpy as jnp
from jax import lax
from jax.experimental import pallas as pl
from jax.experimental.pallas import tpu as pltpu
from jax.sharding import PartitionSpec as P

HEADS = 8
HEAD = 256
ROT = 64
SEQ = 1024


def norm_rows(inputs, norm_gain, norm_bias):
    row_mean = jnp.mean(inputs, axis=-1, keepdims=True)
    centered = inputs - row_mean
    variance = jnp.mean(centered * centered, axis=-1, keepdims=True)
    return centered * lax.rsqrt(variance + 1e-05) * norm_gain + norm_bias


def gelu_exact(values):
    return jax.nn.gelu(values, approximate=False)


def rope_tables(positions):
    freqs = jnp.exp(jnp.arange(ROT // 2, dtype=jnp.float32) * (-2.0 * math.log(10000.0) / ROT))
    angles = positions[:, None] * freqs[None, :]
    return (jnp.cos(angles), jnp.sin(angles))


def rotate(heads, cos_table, sin_table):
    half_rot = ROT // 2
    lower = heads[..., :half_rot]
    upper = heads[..., half_rot:ROT]
    cos_wide = cos_table[:, None, :]
    sin_wide = sin_table[:, None, :]
    return jnp.concatenate(
        [
            lower * cos_wide - upper * sin_wide,
            upper * cos_wide + lower * sin_wide,
            heads[..., ROT:],
        ],
        axis=-1,
    )


def unpack_small(packed, lengths, devices):
    table_rows = packed.reshape(devices, -1)
    members = []
    offset = 0
    for length in lengths:
        members.append(table_rows[:, offset : offset + length].reshape(-1).astype(jnp.float32))
        offset = offset + length
    return members


def contract_rows(left_mat, right_mat):
    return lax.dot_general(
        left_mat, right_mat, (((0,), (0,)), ((), ())), preferred_element_type=jnp.float32
    )


def contract_cols(left_mat, right_mat):
    return lax.dot_general(
        left_mat, right_mat, (((1,), (1,)), ((), ())), preferred_element_type=jnp.float32
    )


def shards(
    layer_input,
    out_grad,
    prefix_len,
    qkv_weight,
    qkv_bias,
    dense_weight,
    dense_bias,
    expand_weight,
    expand_bias,
    shrink_weight,
    shrink_bias,
    attn_gain,
    attn_shift,
    mlp_gain,
    mlp_shift,
):
    devices = lax.axis_size("dp") * lax.axis_size("ctx")
    ctx_index = lax.axis_index("ctx")
    micro, seq_count, span, width = layer_input.shape
    sequences = micro * seq_count
    rows = sequences * span
    heads_shape = (sequences, span, HEADS, HEAD)
    scale = 1.0 / math.sqrt(HEAD)
    attn_lengths = (attn_gain.shape[0], attn_shift.shape[0], qkv_bias.shape[0], dense_bias.shape[0])
    mlp_lengths = (
        mlp_gain.shape[0],
        mlp_shift.shape[0],
        expand_bias.shape[0],
        shrink_bias.shape[0],
    )
    attn_packed = jnp.concatenate([attn_gain, attn_shift, qkv_bias, dense_bias])
    mlp_packed = jnp.concatenate([mlp_gain, mlp_shift, expand_bias, shrink_bias])

    def fetch_attn():
        return (
            lax.all_gather(qkv_weight, ("dp", "ctx"), axis=0, tiled=True),
            lax.all_gather(dense_weight, ("dp", "ctx"), axis=0, tiled=True),
            lax.all_gather(attn_packed, ("dp", "ctx"), axis=0, tiled=True),
        )

    def fetch_mlp():
        return (
            lax.all_gather(expand_weight, ("dp", "ctx"), axis=0, tiled=True),
            lax.all_gather(shrink_weight, ("dp", "ctx"), axis=0, tiled=True),
            lax.all_gather(mlp_packed, ("dp", "ctx"), axis=0, tiled=True),
        )

    local_pos = ctx_index * span + jnp.arange(span, dtype=jnp.int32)
    cos_table, sin_table = rope_tables(local_pos.astype(jnp.float32))
    key_pos = jnp.arange(SEQ, dtype=jnp.int32)
    causal = key_pos[None, :] <= local_pos[:, None]
    inputs = layer_input.astype(jnp.float32).reshape(rows, width)
    cot_rows = out_grad.reshape(rows, width)
    cot_float = cot_rows.astype(jnp.float32)
    prefix = prefix_len.reshape(sequences)
    allowed = (causal[None] | (key_pos[None, None, :] < prefix[:, None, None]))[:, None]
    attn_set = fetch_attn()
    qkv_full, dense_full, attn_small = attn_set
    gain_attn, shift_attn, joined_shift, dense_shift = unpack_small(
        attn_small, attn_lengths, devices
    )
    hidden_attn = norm_rows(inputs, gain_attn, shift_attn).astype(jnp.bfloat16)
    joined = jnp.dot(hidden_attn, qkv_full, preferred_element_type=jnp.float32) + joined_shift
    queries = rotate(joined[:, :width].reshape(heads_shape), cos_table, sin_table).astype(
        jnp.bfloat16
    )
    key_rows = rotate(
        joined[:, width : 2 * width].reshape(heads_shape), cos_table, sin_table
    ).astype(jnp.bfloat16)
    value_rows = joined[:, 2 * width :].reshape(heads_shape).astype(jnp.bfloat16)
    all_keys, all_values = (
        lax.all_gather(key_rows, "ctx", axis=1, tiled=True),
        lax.all_gather(value_rows, "ctx", axis=1, tiled=True),
    )
    scores = (
        jnp.einsum("sqhe,skhe->shqk", queries, all_keys, preferred_element_type=jnp.float32) * scale
    )
    scores = jnp.where(allowed, scores, -1e30)
    row_max = jnp.max(scores, axis=-1, keepdims=True)
    expo = jnp.exp(scores - row_max)
    row_total = jnp.sum(expo, axis=-1, keepdims=True)
    log_total = row_max + jnp.log(row_total)
    probs_low = (expo / row_total).astype(jnp.bfloat16)
    mixed = jnp.einsum("shqk,skhe->sqhe", probs_low, all_values, preferred_element_type=jnp.float32)
    mixed = mixed.reshape(rows, width).astype(jnp.bfloat16)
    attn_out = jnp.dot(mixed, dense_full, preferred_element_type=jnp.float32) + dense_shift
    mlp_set = fetch_mlp()
    expand_full, shrink_full, mlp_small = mlp_set
    gain_mlp, shift_mlp, expand_shift, shrink_shift = unpack_small(mlp_small, mlp_lengths, devices)
    hidden_mlp = norm_rows(inputs, gain_mlp, shift_mlp).astype(jnp.bfloat16)
    expanded = jnp.dot(hidden_mlp, expand_full, preferred_element_type=jnp.float32) + expand_shift
    activated = gelu_exact(expanded).astype(jnp.bfloat16)
    mlp_out = jnp.dot(activated, shrink_full, preferred_element_type=jnp.float32) + shrink_shift
    layer_output = (
        (inputs + attn_out + mlp_out).astype(jnp.bfloat16).reshape(micro, seq_count, span, width)
    )
    attn_back_set = fetch_attn()
    qkv_back, dense_back, attn_small_back = attn_back_set
    gain_attn, shift_attn, joined_shift, dense_shift = unpack_small(
        attn_small_back, attn_lengths, devices
    )
    grad_out_shift = jnp.sum(cot_float, axis=0)
    grad_mixed = contract_cols(cot_rows, dense_back).astype(jnp.bfloat16).reshape(heads_shape)
    again = (
        jnp.einsum("sqhe,skhe->shqk", queries, all_keys, preferred_element_type=jnp.float32) * scale
    )
    again = jnp.where(allowed, again, -1e30)
    probs = jnp.exp(again - log_total)
    grad_probs = jnp.einsum(
        "sqhe,skhe->shqk", grad_mixed, all_values, preferred_element_type=jnp.float32
    )
    delta = jnp.sum(probs * grad_probs, axis=-1, keepdims=True)
    grad_scores = (probs * (grad_probs - delta)).astype(jnp.bfloat16)
    grad_queries = (
        jnp.einsum("shqk,skhe->sqhe", grad_scores, all_keys, preferred_element_type=jnp.float32)
        * scale
    )
    all_queries, all_grad_mixed = (
        lax.all_gather(queries, "ctx", axis=1, tiled=True),
        lax.all_gather(grad_mixed, "ctx", axis=1, tiled=True),
    )
    stat_lse = jnp.transpose(log_total[..., 0], (0, 2, 1))
    stat_delta = jnp.transpose(delta[..., 0], (0, 2, 1))
    lse_all, delta_all = (
        lax.all_gather(stat_lse, "ctx", axis=1, tiled=True),
        lax.all_gather(stat_delta, "ctx", axis=1, tiled=True),
    )
    lse_all = jnp.transpose(lse_all, (0, 2, 1))[..., None]
    delta_all = jnp.transpose(delta_all, (0, 2, 1))[..., None]
    key_allowed = (local_pos[None, :] <= key_pos[:, None])[None] | (
        local_pos[None, None, :] < prefix[:, None, None]
    )
    block_scores = (
        jnp.einsum("sqhe,skhe->shqk", all_queries, key_rows, preferred_element_type=jnp.float32)
        * scale
    )
    block_scores = jnp.where(key_allowed[:, None], block_scores, -1e30)
    block_probs = jnp.exp(block_scores - lse_all)
    block_grad_probs = jnp.einsum(
        "sqhe,skhe->shqk", all_grad_mixed, value_rows, preferred_element_type=jnp.float32
    )
    block_grad_scores = (block_probs * (block_grad_probs - delta_all)).astype(jnp.bfloat16)
    own_keys = (
        jnp.einsum(
            "shqk,sqhe->skhe", block_grad_scores, all_queries, preferred_element_type=jnp.float32
        )
        * scale
    )
    own_values = jnp.einsum(
        "shqk,sqhe->skhe",
        block_probs.astype(jnp.bfloat16),
        all_grad_mixed,
        preferred_element_type=jnp.float32,
    )
    grad_joined = jnp.concatenate(
        [
            rotate(grad_queries, cos_table, -sin_table).reshape(rows, width),
            rotate(own_keys, cos_table, -sin_table).reshape(rows, width),
            own_values.reshape(rows, width),
        ],
        axis=1,
    ).astype(jnp.bfloat16)
    grad_joined_shift = jnp.sum(grad_joined.astype(jnp.float32), axis=0)
    grad_hidden_attn = contract_cols(grad_joined, qkv_back)
    unused_attn, attn_back = jax.vjp(norm_rows, inputs, gain_attn, shift_attn)
    grad_in_attn, grad_gain_attn, grad_shift_attn = attn_back(grad_hidden_attn)
    attn_columns = jnp.concatenate(
        [
            grad_gain_attn[:, None],
            grad_shift_attn[:, None],
            grad_joined_shift[: 2 * width].reshape(width, 2),
            grad_joined_shift[2 * width :][:, None],
            grad_out_shift[:, None],
        ],
        axis=1,
    )
    hidden_part = hidden_attn
    small_part = attn_columns
    attn_grads = lax.psum_scatter(
        jnp.concatenate(
            [contract_rows(hidden_part, grad_joined), contract_rows(mixed, cot_rows), small_part],
            axis=1,
        ),
        ("dp", "ctx"),
        scatter_dimension=0,
        tiled=True,
    )
    qkv_grad = attn_grads[:, : 3 * width]
    dense_grad = attn_grads[:, 3 * width : 4 * width]
    attn_tail = attn_grads[:, 4 * width :]
    mlp_back_set = fetch_mlp()
    expand_back, shrink_back, mlp_small_back = mlp_back_set
    gain_mlp, shift_mlp, expand_shift, shrink_shift = unpack_small(
        mlp_small_back, mlp_lengths, devices
    )
    unused_gelu, gelu_back = jax.vjp(gelu_exact, expanded)
    grad_act = contract_cols(cot_rows, shrink_back)
    grad_expanded = gelu_back(grad_act)[0].astype(jnp.bfloat16)
    grad_expand_shift = jnp.sum(grad_expanded.astype(jnp.float32), axis=0)
    grad_hidden_mlp = contract_cols(grad_expanded, expand_back)
    unused_mlp, mlp_back = jax.vjp(norm_rows, inputs, gain_mlp, shift_mlp)
    grad_in_mlp, grad_gain_mlp, grad_shift_mlp = mlp_back(grad_hidden_mlp)
    ratio = expand_shift.shape[0] // width
    mlp_columns = jnp.concatenate(
        [
            grad_gain_mlp[:, None],
            grad_shift_mlp[:, None],
            grad_expand_shift.reshape(width, ratio),
            grad_out_shift[:, None],
        ],
        axis=1,
    )
    ff_width = expand_back.shape[1]
    hidden_part = hidden_mlp
    small_part = mlp_columns
    expand_grads = lax.psum_scatter(
        jnp.concatenate([contract_rows(hidden_part, grad_expanded), small_part], axis=1),
        ("dp", "ctx"),
        scatter_dimension=0,
        tiled=True,
    )
    shrink_grad = lax.psum_scatter(
        contract_rows(activated, cot_rows), ("dp", "ctx"), scatter_dimension=0, tiled=True
    )
    expand_grad = expand_grads[:, :ff_width]
    mlp_tail = expand_grads[:, ff_width:]
    input_grad = (
        (cot_float + grad_in_attn + grad_in_mlp)
        .astype(jnp.bfloat16)
        .reshape(micro, seq_count, span, width)
    )
    return (
        layer_output,
        input_grad,
        qkv_grad,
        attn_tail[:, 2:4].reshape(-1),
        attn_tail[:, 4],
        dense_grad,
        attn_tail[:, 5],
        expand_grad,
        mlp_tail[:, 2 : 2 + ratio].reshape(-1),
        shrink_grad,
        mlp_tail[:, 2 + ratio],
        attn_tail[:, 0],
        attn_tail[:, 1],
        mlp_tail[:, 0],
        mlp_tail[:, 1],
    )


def low(values):
    return values.astype(jnp.bfloat16)


MESH_ID = pl.DeviceIdType.MESH


def remote(src, dst, send_sem, recv_sem, dp, ctx):
    return pltpu.make_async_remote_copy(
        src_ref=src,
        dst_ref=dst,
        send_sem=send_sem,
        recv_sem=recv_sem,
        device_id=(dp, ctx),
        device_id_type=MESH_ID,
    )


def greet_all(dp, ctx, dp_size, ctx_size):
    barrier = pltpu.get_barrier_semaphore()
    devices = dp_size * ctx_size
    me = dp * ctx_size + ctx

    def greet(step, carry):
        other = lax.rem(me + step, devices)
        pl.semaphore_signal(
            barrier, inc=1, device_id=(other // ctx_size, lax.rem(other, ctx_size)), device_id_type=MESH_ID
        )
        return carry

    lax.fori_loop(1, devices, greet, 0)
    pl.semaphore_wait(barrier, devices - 1)


def chain_gather(src, dst, sems, d, c, levels):
    block_send, block_recv, core_send, core_recv, local = sems
    micro, span = src.shape[0], src.shape[1]
    z = c // 2
    sibling = c + 1 - 2 * lax.rem(c, 2)

    def block(origin, m):
        return dst.at[m, pl.ds(pl.multiple_of(origin * span, span), span)]

    def link(way, hop, m):
        step = 2 if way == 0 else -2
        origin = c - step * hop
        view = src.at[m] if hop == 0 else block(origin, m)
        return remote(view, block(origin, m), block_send.at[way, hop, m], block_recv.at[way, hop, m], d, c + step)

    def leaves(way, hop):
        if way == 0:
            return jnp.logical_and(z >= hop, z <= levels - 2)
        return jnp.logical_and(z + hop <= levels - 1, z >= 1)

    def arrives(way, hop):
        return z >= hop + 1 if way == 0 else z + hop + 1 <= levels - 1

    def slot_of(way, hop):
        return 1 + way * (levels - 1) + hop

    def core_copy(slot, origin, m):
        view = src.at[m] if slot == 0 else block(origin, m)
        return remote(view, block(origin, m), core_send.at[slot, m], core_recv.at[slot, m], d, sibling)

    def own_copy(m):
        return pltpu.make_async_copy(src.at[m], block(c, m), local.at[m])

    def start(m):
        for way in range(2):
            @pl.when(leaves(way, 0))
            def _(way=way):
                link(way, 0, m).start()

        core_copy(0, c, m).start()
        own_copy(m).start()

    def hop_step(hop, m):
        for way in range(2):
            step = 2 if way == 0 else -2

            @pl.when(arrives(way, hop))
            def _(way=way, step=step):
                link(way, hop, m).wait_recv()
                if hop + 1 <= levels - 2:
                    @pl.when(leaves(way, hop + 1))
                    def _():
                        link(way, hop + 1, m).start()

                core_copy(slot_of(way, hop), c - step * (hop + 1), m).start()

    def finish(m):
        own_copy(m).wait()
        core_copy(0, c, m).wait_send()
        core_copy(0, sibling, m).wait_recv()
        for way in range(2):
            step = 2 if way == 0 else -2
            for hop in range(levels - 1):
                @pl.when(leaves(way, hop))
                def _(way=way, hop=hop):
                    link(way, hop, m).wait_send()

                @pl.when(arrives(way, hop))
                def _(way=way, hop=hop, step=step):
                    slot = slot_of(way, hop)
                    core_copy(slot, c - step * (hop + 1), m).wait_send()
                    core_copy(slot, sibling - step * (hop + 1), m).wait_recv()

    return start, hop_step, finish


def chain_scratch(levels, micro):
    dma = pltpu.SemaphoreType.DMA
    return [
        dma((2, levels - 1, micro)),
        dma((2, levels - 1, micro)),
        dma((2 * levels - 1, micro)),
        dma((2 * levels - 1, micro)),
        dma((micro,)),
    ]


def greet_line(d, c, levels):
    barrier = pltpu.get_barrier_semaphore()
    z = c // 2
    sibling = c + 1 - 2 * lax.rem(c, 2)
    pl.semaphore_signal(barrier, inc=1, device_id=(d, sibling), device_id_type=MESH_ID)

    @pl.when(z >= 1)
    def _():
        pl.semaphore_signal(barrier, inc=1, device_id=(d, c - 2), device_id_type=MESH_ID)

    @pl.when(z <= levels - 2)
    def _():
        pl.semaphore_signal(barrier, inc=1, device_id=(d, c + 2), device_id_type=MESH_ID)

    peers = 1 + (z >= 1).astype(jnp.int32) + (z <= levels - 2).astype(jnp.int32)
    pl.semaphore_wait(barrier, peers)


def gather_kernel(
    dp_size,
    ctx_size,
    x,
    qkv,
    expand,
    dense,
    shrink,
    packed,
    x_all,
    panels,
    out_w,
    small,
    local_sem,
    small_sem,
    block_send,
    block_recv,
    core_send,
    core_recv,
    block_local,
    panel_send,
    panel_recv,
    share_send,
    share_recv,
    pass_send,
    pass_recv,
):
    d = lax.axis_index("dp")
    c = lax.axis_index("ctx")
    z = c // 2
    sibling = c + 1 - 2 * lax.rem(c, 2)
    x_mate = d + 1 - 2 * lax.rem(d, 2)
    y_mate = lax.rem(d + 2, 4)
    micro, span = x.shape[0], x.shape[1]
    devices = dp_size * ctx_size
    me = d * ctx_size + c
    rows = qkv.shape[0]
    unit = shrink.shape[0]
    levels = ctx_size // 2
    panel_rows = ctx_size * rows
    n_panels = 3 + dp_size

    greet_all(d, c, dp_size, ctx_size)

    def column_block(panel, target):
        if panel < 3:
            start = panel * (qkv.shape[1] // 3) + target * HEAD
            return qkv.at[:, pl.ds(pl.multiple_of(start, HEAD), HEAD)]
        start = (panel - 3) * ctx_size * unit + target * unit
        return expand.at[:, pl.ds(pl.multiple_of(start, HEAD), HEAD)]

    own_rows = pl.ds(pl.multiple_of((d * ctx_size + c) * rows, rows), rows)

    for panel in range(n_panels):
        pltpu.make_async_copy(
            column_block(panel, c), panels.at[panel, own_rows], local_sem.at[panel]
        ).start()

        def push(step, carry, panel=panel):
            target = lax.rem(c + step, ctx_size)
            remote(
                column_block(panel, target),
                panels.at[panel, own_rows],
                panel_send.at[panel],
                panel_recv.at[panel],
                d,
                target,
            ).start()
            return carry

        lax.fori_loop(1, ctx_size, push, 0)

    def shrink_rows(owner, offset, count):
        return out_w.at[pl.ds(pl.multiple_of(HEAD + owner * unit + offset, 16), count)]

    shrink_local = pltpu.make_async_copy(shrink, shrink_rows(d, 0, unit), local_sem.at[n_panels])
    shrink_local.start()
    for way, mate in ((0, x_mate), (1, y_mate)):
        remote(
            shrink, shrink_rows(d, 0, unit), share_send.at[n_panels, way], share_recv.at[n_panels, way], mate, c
        ).start()

    per_head = HEAD // rows
    head_of = (d * ctx_size + c) // per_head
    dense_rows = pl.ds(pl.multiple_of(lax.rem(c, per_head) * rows, rows), rows)
    dense_out = remote(dense, out_w.at[dense_rows], panel_send.at[n_panels], panel_recv.at[n_panels], d, head_of)
    dense_own = pltpu.make_async_copy(dense, out_w.at[dense_rows], local_sem.at[n_panels + 1])
    stays = head_of == c

    @pl.when(stays)
    def _():
        dense_own.start()

    @pl.when(jnp.logical_not(stays))
    def _():
        dense_out.start()

    x_start, x_hop, x_finish = chain_gather(
        x, x_all, (block_send, block_recv, core_send, core_recv, block_local), d, c, levels
    )
    for m in range(micro):
        x_start(m)

    small_copy = pltpu.make_async_copy(packed, small.at[me], local_sem.at[n_panels + 2])
    small_copy.start()

    def push_small(step, carry):
        other = lax.rem(me + step, devices)
        remote(
            packed,
            small.at[me],
            small_sem.at[0],
            small_sem.at[1],
            other // ctx_size,
            lax.rem(other, ctx_size),
        ).start()
        return carry

    lax.fori_loop(1, devices, push_small, 0)

    def group_rows(owner, offset, count):
        return pl.ds(pl.multiple_of(owner * panel_rows + offset, 16), count)

    def panel_share(panel, way, mate):
        view = panels.at[panel, group_rows(d, 0, panel_rows)]
        return remote(view, view, share_send.at[panel, way], share_recv.at[panel, way], mate, c)

    def panel_step(panel):
        pltpu.make_async_copy(column_block(panel, c), panels.at[panel, own_rows], local_sem.at[panel]).wait()
        whole = panels.at[panel, group_rows(d, 0, (ctx_size - 1) * rows)]
        remote(whole, whole, panel_send.at[panel], panel_recv.at[panel], d, sibling).wait_recv()
        panel_share(panel, 0, x_mate).start()
        panel_share(panel, 1, y_mate).start()

    half = panel_rows // 2

    def panel_pass(panel, way):
        owner, mate = ((x_mate, y_mate), (y_mate, x_mate))[way]
        view = panels.at[panel, group_rows(owner, way * half, half)]
        return remote(view, view, pass_send.at[panel, way], pass_recv.at[panel, way], mate, c)

    def panel_forward(panel):
        for way, owner in ((0, x_mate), (1, y_mate)):
            view = panels.at[panel, group_rows(owner, 0, panel_rows)]
            remote(view, view, share_send.at[panel, way], share_recv.at[panel, way], owner, c).wait_recv()
            panel_pass(panel, way).start()

    def shrink_share_wait(way, owner):
        view = shrink_rows(owner, 0, unit)
        remote(view, view, share_send.at[n_panels, way], share_recv.at[n_panels, way], owner, c).wait_recv()

    def shrink_pass(way):
        owner, mate = ((x_mate, y_mate), (y_mate, x_mate))[way]
        view = shrink_rows(owner, way * (unit // 2), unit // 2)
        return remote(view, view, pass_send.at[n_panels, way], pass_recv.at[n_panels, way], mate, c)

    source = c // (ctx_size // dp_size)
    at_source = d == source
    from_x = x_mate == source
    from_y = y_mate == source
    head_rows = out_w.at[pl.ds(0, HEAD)]
    half_head = HEAD // 2

    def dense_share(way, mate):
        view = out_w.at[pl.ds(way * half_head, half_head)]
        return remote(view, view, share_send.at[n_panels + 1, way], share_recv.at[n_panels + 1, way], mate, c)

    owns_share = jnp.logical_and(at_source, stays)

    def dense_gather_step():
        @pl.when(owns_share)
        def _():
            dense_own.wait()
            view = out_w.at[pl.ds(0, (per_head - 1) * rows)]
            remote(view, view, panel_send.at[n_panels], panel_recv.at[n_panels], d, sibling).wait_recv()

        @pl.when(jnp.logical_and(at_source, jnp.logical_not(stays)))
        def _():
            remote(head_rows, head_rows, panel_send.at[n_panels], panel_recv.at[n_panels], d, sibling).wait_recv()

        @pl.when(at_source)
        def _():
            dense_share(0, x_mate).start()
            dense_share(1, y_mate).start()

    def dense_forward_step():
        @pl.when(from_x)
        def _():
            dense_share(0, x_mate).wait_recv()
            dense_share(0, y_mate).start()

        @pl.when(from_y)
        def _():
            dense_share(1, y_mate).wait_recv()
            dense_share(1, x_mate).start()

    def dense_last_step():
        @pl.when(across)
        def _():
            dense_share(0, y_mate).wait_recv()
            dense_share(0, x_mate).start()
            dense_share(1, x_mate).wait_recv()
            dense_share(1, y_mate).start()

    across = jnp.logical_not(jnp.logical_or(at_source, jnp.logical_or(from_x, from_y)))

    for panel in range(3):
        panel_step(panel)
    shrink_share_wait(0, x_mate)
    shrink_pass(0).start()
    shrink_share_wait(1, y_mate)
    shrink_pass(1).start()
    for panel in range(3, n_panels):
        panel_step(panel)
    dense_gather_step()
    panel_forward(0)
    panel_forward(1)
    x_hop(0, 0)
    panel_forward(2)
    x_hop(0, 1)
    dense_forward_step()
    panel_forward(3)
    panel_forward(4)
    x_hop(1, 0)
    panel_forward(5)
    x_hop(1, 1)
    dense_last_step()
    panel_forward(6)
    for hop in range(2, levels - 1):
        for m in range(micro):
            x_hop(hop, m)

    for panel in range(n_panels):
        for way, mate in ((0, x_mate), (1, y_mate)):
            panel_share(panel, way, mate).wait_send()
            panel_pass(panel, way).wait_send()
        for way in range(2):
            diagonal = 3 - d
            view = panels.at[panel, group_rows(diagonal, way * half, half)]
            remote(view, view, pass_send.at[panel, way], pass_recv.at[panel, way], x_mate, c).wait_recv()
        whole = panels.at[panel, group_rows(d, 0, (ctx_size - 1) * rows)]
        remote(whole, whole, panel_send.at[panel], panel_recv.at[panel], x_mate, c).wait_send()
    shrink_local.wait()
    for way in range(2):
        mate = (x_mate, y_mate)[way]
        remote(
            shrink, shrink_rows(d, 0, unit), share_send.at[n_panels, way], share_recv.at[n_panels, way], mate, c
        ).wait_send()
        shrink_pass(way).wait_send()
        view = shrink_rows(3 - d, way * (unit // 2), unit // 2)
        remote(view, view, pass_send.at[n_panels, way], pass_recv.at[n_panels, way], mate, c).wait_recv()

    @pl.when(jnp.logical_not(stays))
    def _():
        dense_out.wait_send()

    @pl.when(at_source)
    def _():
        dense_share(0, x_mate).wait_send()
        dense_share(1, y_mate).wait_send()

    @pl.when(from_x)
    def _():
        dense_share(0, y_mate).wait_send()
        dense_share(1, y_mate).wait_recv()

    @pl.when(from_y)
    def _():
        dense_share(1, x_mate).wait_send()
        dense_share(0, x_mate).wait_recv()

    @pl.when(across)
    def _():
        dense_share(0, x_mate).wait_send()
        dense_share(1, y_mate).wait_send()

    for m in range(micro):
        x_finish(m)

    small_copy.wait()
    rest = small.at[pl.ds(0, devices - 1)]
    remote(rest, rest, small_sem.at[0], small_sem.at[1], d, sibling).wait()


def gather_call(dp_size, ctx_size, x, qkv, expand, dense, shrink, packed):
    micro, span, width = x.shape
    rows = qkv.shape[0]
    n_panels = 3 + dp_size
    levels = ctx_size // 2
    devices = dp_size * ctx_size
    dma = pltpu.SemaphoreType.DMA
    out_shape = (
        jax.ShapeDtypeStruct((micro, ctx_size * span, width), x.dtype),
        jax.ShapeDtypeStruct((n_panels, devices * rows, HEAD), x.dtype),
        jax.ShapeDtypeStruct((HEAD + dp_size * shrink.shape[0], width), x.dtype),
        jax.ShapeDtypeStruct((devices,) + packed.shape, x.dtype),
    )
    anywhere = pl.BlockSpec(memory_space=pl.ANY)
    return pl.pallas_call(
        functools.partial(gather_kernel, dp_size, ctx_size),
        out_shape=out_shape,
        in_specs=[anywhere] * 6,
        out_specs=(anywhere,) * 4,
        scratch_shapes=[
            dma((n_panels + 3,)),
            dma((2,)),
            *chain_scratch(levels, micro),
            dma((n_panels + 1,)),
            dma((n_panels + 1,)),
            dma((n_panels + 2, 2)),
            dma((n_panels + 2, 2)),
            dma((n_panels + 2, 2)),
            dma((n_panels + 2, 2)),
        ],
        compiler_params=pltpu.CompilerParams(collective_id=1, has_side_effects=True),
        name="gather_all",
    )(x, qkv, expand, dense, shrink, packed)


def add_into(dst, srcs, rows):
    chunk = 16 if dst.shape[-1] > 1024 else 64

    def step(index, carry):
        at = pl.ds(pl.multiple_of(index * chunk, 16), chunk)
        total = srcs[0][at, :].astype(jnp.float32)
        for src in srcs[1:]:
            total = total + src[at, :].astype(jnp.float32)
        dst[at, :] = total.astype(dst.dtype)
        return carry

    lax.fori_loop(0, rows // chunk, step, 0)


TILE = 256


def turn_tables(length):
    freqs = jnp.exp(jnp.arange(ROT // 2, dtype=jnp.float32) * (-2.0 * math.log(10000.0) / ROT))
    angles = jnp.arange(length, dtype=jnp.float32)[:, None] * freqs[None, :]
    cos, sin = jnp.cos(angles), jnp.sin(angles)
    rest = jnp.zeros((length, 128 - ROT), jnp.float32)
    return (
        jnp.concatenate([cos, cos, rest + 1.0], axis=1),
        jnp.concatenate([-sin, sin, rest], axis=1),
    )


def turn(head, cos, sin):
    front = head[:, :128]
    lane = lax.broadcasted_iota(jnp.int32, front.shape, 1)
    other = jnp.where(lane < ROT // 2, pltpu.roll(front, 128 - ROT // 2, 1), pltpu.roll(front, ROT // 2, 1))
    return jnp.concatenate([front * cos + other * sin, head[:, 128:]], axis=1)


def dot_nn(a, b):
    return lax.dot_general(a, b, (((1,), (0,)), ((), ())), preferred_element_type=jnp.float32)


def dot_nt(a, b):
    return lax.dot_general(a, b, (((1,), (1,)), ((), ())), preferred_element_type=jnp.float32)


def dot_tn(a, b):
    return lax.dot_general(a, b, (((0,), (0,)), ((), ())), preferred_element_type=jnp.float32)


def forward_kernel(
    tiles,
    levels,
    prefix,
    x,
    own_g,
    panels,
    out_w,
    gains,
    qkv_shift,
    expand_shift,
    cos,
    sin,
    hidden_attn,
    hidden_mlp,
    heads,
    probs,
    features,
    slopes,
    partial,
    g_all,
    first_out,
    head_rows,
    acts,
    board,
    out_core,
    out_chain,
    core_send,
    core_recv,
    chain_send,
    chain_recv,
    store_sem,
    *g_sems,
):
    step = pl.program_id(0)
    micro = own_g.shape[0]
    d = lax.axis_index("dp")
    c = lax.axis_index("ctx")
    g_start, g_hop, g_finish = chain_gather(own_g, g_all, g_sems, d, c, levels)

    core = lax.rem(c, 2)
    span = board.shape[2]

    def own_block(level):
        return board.at[level, core]

    def core_copy(level):
        return remote(
            board.at[level, 1 - core],
            out_core.at[level],
            core_send.at[level],
            core_recv.at[level],
            d,
            c + 1 - 2 * core,
        )

    chain_open, chain_round, chain_end, chain_finish = chain_reduce(
        own_block, out_chain, (chain_send, chain_recv), d, c, levels
    )

    def out_store(level):
        return pltpu.make_async_copy(own_block(level), first_out, store_sem.at[0])

    @pl.when(step == 0)
    def _():
        greet_line(d, c, levels)
        for m in range(micro):
            g_start(m)

    for place, level in enumerate(outside_in(levels)):
        @pl.when(step == tiles + 1 + place)
        def _(level=level):
            core_copy(level).start()

        @pl.when(step == tiles + 2 + place)
        def _(level=level):
            core_copy(level).wait_recv()
            add_into(own_block(level), (own_block(level), out_core.at[level]), span)
            chain_open(level)

    @pl.when(step == 12)
    def _():
        chain_round(1)

    last = 4 * tiles - 1
    for at, hop, m in ((4, 0, 0), (7, 0, 1), (11, 1, 0), (14, 1, 1)):
        @pl.when(step == at)
        def _(hop=hop, m=m):
            g_hop(hop, m)

    seq = step // (2 * tiles)
    phase = lax.rem(step, 2 * tiles) // tiles
    tile = lax.rem(step, tiles)
    tile = jnp.where(phase == 0, tile, jnp.where(lax.rem(tile, 2) == 0, tiles - 1 - tile // 2, tile // 2))
    rows = pl.ds(pl.multiple_of(tile * TILE, TILE), TILE)
    n_expand = panels.shape[0] - 3
    scale = 1.0 / math.sqrt(HEAD)

    @pl.when(phase == 0)
    def _():
        values_in = x[...].astype(jnp.float32)
        centered = values_in - jnp.mean(values_in, axis=1, keepdims=True)
        normal = centered * lax.rsqrt(jnp.mean(centered * centered, axis=1, keepdims=True) + 1e-05)
        hidden_attn[...] = (normal * gains[0:1, :] + gains[1:2, :]).astype(jnp.bfloat16)
        hidden_mlp[...] = (normal * gains[2:3, :] + gains[3:4, :]).astype(jnp.bfloat16)
        wide = jnp.concatenate([panels[part] for part in range(3)], axis=1)
        all_joined = dot_nn(hidden_attn[...], wide) + qkv_shift[...]
        for part in range(3):
            joined = all_joined[:, part * HEAD : (part + 1) * HEAD]
            if part < 2:
                joined = turn(joined, cos[rows, :], sin[rows, :])
            joined = joined.astype(jnp.bfloat16)
            heads[part] = joined
            head_rows[part, rows, :] = joined
        for part in range(0, n_expand, 2):
            columns = slice(part * HEAD, (part + 2) * HEAD)
            wide = jnp.concatenate([panels[3 + part], panels[4 + part]], axis=1)
            expanded = dot_nn(hidden_mlp[...], wide) + expand_shift[:, columns]
            cdf = 0.5 * (1.0 + lax.erf(expanded * (1.0 / math.sqrt(2.0))))
            acts[rows, columns] = (expanded * cdf).astype(jnp.bfloat16)
            bell = jnp.exp(-0.5 * expanded * expanded) * (1.0 / math.sqrt(2.0 * math.pi))
            slopes[:, columns] = (cdf + expanded * bell).astype(jnp.bfloat16)

    @pl.when(phase == 1)
    def _():
        scores = dot_nt(head_rows[0, rows, :], head_rows[1]) * scale
        key_at = lax.broadcasted_iota(jnp.int32, scores.shape, 1)
        query_at = lax.broadcasted_iota(jnp.int32, scores.shape, 0) + tile * TILE
        allowed = jnp.logical_or(key_at <= query_at, key_at < prefix[seq])
        scores = jnp.where(allowed, scores, -1e30)
        expo = jnp.exp(scores - jnp.max(scores, axis=1, keepdims=True))
        low_probs = (expo * (1.0 / jnp.sum(expo, axis=1, keepdims=True))).astype(jnp.bfloat16)
        probs[0] = low_probs
        features[:, :HEAD] = dot_nn(low_probs, head_rows[2]).astype(jnp.bfloat16)
        features[:, HEAD:] = acts[rows, :]
        width = out_w.shape[1]
        for start in range(0, width, 1024):
            columns = slice(start, start + 1024)
            value = dot_nn(features[...], out_w[:, columns]).astype(jnp.bfloat16)

            @pl.when(seq == 0)
            def _(columns=columns, value=value):
                for parity in range(2):
                    board[tile, parity, :, columns] = value[parity * span : (parity + 1) * span]

            @pl.when(seq > 0)
            def _(columns=columns, value=value):
                partial[:, columns] = value

    @pl.when(step == last)
    def _():
        chain_round(2)
        for m in range(micro):
            for hop in range(2, levels - 1):
                g_hop(hop, m)
        chain_end(out_store)
        for m in range(micro):
            g_finish(m)
        for level in range(levels):
            core_copy(level).wait_send()
        chain_finish(out_store)


def whole_spec(array):
    zeros = (0,) * array.ndim
    return pl.BlockSpec(array.shape, lambda step: zeros, pipeline_mode=pl.Buffered(1))


def forward_call(levels, prefix, x, own_g, panels, out_w, gains, qkv_shift, expand_shift, cos, sin):
    tokens, width = x.shape
    length = cos.shape[0]
    tiles = length // TILE
    steps = 2 * tokens // TILE
    hidden = expand_shift.shape[1]
    span = own_g.shape[1]
    dma = pltpu.SemaphoreType.DMA

    def early(step):
        seq, at = step // (2 * tiles), lax.rem(step, 2 * tiles)
        return seq * tiles + jnp.minimum(at, tiles - 1)

    def late(step):
        seq, at = step // (2 * tiles), lax.rem(step, 2 * tiles)
        place = jnp.maximum(at - tiles, 0)
        return seq * tiles + jnp.where(lax.rem(place, 2) == 0, tiles - 1 - place // 2, place // 2)

    def last_only(step):
        return jnp.where(step < 2 * tiles, tiles - 1, late(step) - tiles)

    kind = jnp.bfloat16
    return pl.pallas_call(
        functools.partial(forward_kernel, tiles, levels),
        grid=(steps,),
        out_shape=(
            jax.ShapeDtypeStruct((tokens, width), kind),
            jax.ShapeDtypeStruct((tokens, width), kind),
            jax.ShapeDtypeStruct((3, tokens, HEAD), kind),
            jax.ShapeDtypeStruct((tokens // length, length, length), kind),
            jax.ShapeDtypeStruct((tokens, HEAD + hidden), kind),
            jax.ShapeDtypeStruct((tokens, hidden), kind),
            jax.ShapeDtypeStruct((length, width), kind),
            jax.ShapeDtypeStruct((tokens // length, length, width), kind),
            jax.ShapeDtypeStruct((span, width), kind),
        ),
        in_specs=[
            pl.BlockSpec(memory_space=pltpu.SMEM),
            pl.BlockSpec((TILE, width), lambda step: (early(step), 0)),
            pl.BlockSpec(memory_space=pl.ANY),
            whole_spec(panels),
            whole_spec(out_w),
            whole_spec(gains),
            whole_spec(qkv_shift),
            whole_spec(expand_shift),
            whole_spec(cos),
            whole_spec(sin),
        ],
        out_specs=(
            pl.BlockSpec((TILE, width), lambda step: (early(step), 0)),
            pl.BlockSpec((TILE, width), lambda step: (early(step), 0)),
            pl.BlockSpec((3, TILE, HEAD), lambda step: (0, early(step), 0)),
            pl.BlockSpec((1, TILE, length), lambda step: (late(step) // tiles, lax.rem(late(step), tiles), 0)),
            pl.BlockSpec((TILE, HEAD + hidden), lambda step: (late(step), 0)),
            pl.BlockSpec((TILE, hidden), lambda step: (early(step), 0)),
            pl.BlockSpec((TILE, width), lambda step: (last_only(step), 0)),
            pl.BlockSpec(memory_space=pl.ANY),
            pl.BlockSpec(memory_space=pl.ANY),
        ),
        scratch_shapes=[
            pltpu.VMEM((3, length, HEAD), kind),
            pltpu.VMEM((length, hidden), kind),
            pltpu.VMEM((levels, 2, span, width), kind),
            pltpu.VMEM((levels, span, width), kind),
            pltpu.VMEM((2, levels - 1, span, width), kind),
            dma((levels,)),
            dma((levels,)),
            dma((2, levels)),
            dma((2, levels)),
            dma((1,)),
            *chain_scratch(levels, tokens // length),
        ],
        compiler_params=pltpu.CompilerParams(
            collective_id=3, has_side_effects=True, vmem_limit_bytes=60 * 1024 * 1024
        ),
        cost_estimate=pl.CostEstimate(
            flops=2 * tokens * width * (2 * hidden + 4 * HEAD) + 4 * tokens * length * HEAD,
            bytes_accessed=64 * 1024 * 1024,
            transcendentals=0,
        ),
        name="forward_part",
    )(prefix, x, own_g, panels, out_w, gains, qkv_shift, expand_shift, cos, sin)


def outside_in(levels):
    return [levels - 1 - place // 2 if place % 2 == 0 else place // 2 for place in range(levels)]


def chain_reduce(own, recv, sems, d, c, levels):
    chain_send, chain_recv = sems
    z = c // 2
    span = recv.shape[2]

    def copy(way, level):
        return remote(
            own(level),
            recv.at[way, level - 1 + way],
            chain_send.at[way, level],
            chain_recv.at[way, level],
            d,
            c + (2 if way == 0 else -2),
        )

    def sends(way, level):
        return z < level if way == 0 else z > level

    def hears(way, level):
        if way == 0:
            return jnp.logical_and(z >= 1, z <= level)
        return jnp.logical_and(z <= levels - 2, z >= level)

    def add(way, level):
        copy(way, level).wait_recv()
        add_into(own(level), (own(level), recv.at[way, level - 1 + way]), span)

    def open_level(level):
        for way, place in ((0, 0), (1, levels - 1)):
            if place != level:
                @pl.when(z == place)
                def _(way=way):
                    copy(way, level).start()

    def turn_round(index):
        for level in range(levels):
            for way in range(2):
                behind = levels - 1 - level if way == 0 else level
                place = index - behind if way == 0 else levels - 1 - (index - behind)
                if behind < index and (place < level if way == 0 else place > level):
                    @pl.when(z == place)
                    def _(way=way, level=level):
                        add(way, level)
                        copy(way, level).start()

    def end(store):
        for level in range(levels):
            for way in range(2):
                if 0 <= level - 1 + way < levels - 1:
                    @pl.when(jnp.logical_and(z == level, hears(way, level)))
                    def _(way=way, level=level):
                        add(way, level)

            @pl.when(z == level)
            def _(level=level):
                store(level).start()

    def finish(store):
        for level in range(levels):
            for way in range(2):
                if 0 <= level - 1 + way < levels - 1:
                    @pl.when(sends(way, level))
                    def _(way=way, level=level):
                        copy(way, level).wait_send()

        store(0).wait()

    return open_level, turn_round, end, finish


def square_sum(first, passing, recv, last, final, sems, d, c, count):
    first_send, first_recv, last_send, last_recv = sems
    x_mate = d + 1 - 2 * lax.rem(d, 2)
    y_mate = lax.rem(d + 2, 4)
    mates = ((x_mate, y_mate), (y_mate, x_mate))

    def first_copy(way, slot):
        return remote(
            first(way, slot), recv.at[way, slot], first_send.at[way, slot], first_recv.at[way, slot], mates[way][0], c
        )

    def last_copy(way):
        return remote(passing(way), last.at[way], last_send.at[way], last_recv.at[way], mates[way][1], c)

    def pass_on(way):
        first_copy(way, 1).wait_recv()
        add_into(passing(way), (passing(way), recv.at[way, 1]), count)
        last_copy(way).start()

    def arrive(way):
        first_copy(way, 0).wait_recv()
        last_copy(way).wait_recv()

    def add_final(way, start, rows):
        at = pl.ds(start, rows)
        own = final(way).at[at]
        add_into(own, (own, recv.at[way, 0, at], last.at[way, at]), rows)

    def finish():
        for way in range(2):
            first_copy(way, 0).wait_send()
            first_copy(way, 1).wait_send()
            last_copy(way).wait_send()

    return first_copy, pass_on, arrive, add_final, finish


def square_scratch():
    dma = pltpu.SemaphoreType.DMA
    return [dma((2, 2)), dma((2, 2)), dma((2,)), dma((2,))]


def backward_kernel(
    tiles,
    dp_size,
    ctx_size,
    g,
    x,
    panels,
    out_w,
    gains,
    cos,
    sin,
    heads,
    probs,
    slopes,
    features,
    grads,
    grad_expanded,
    grad_joined,
    combined,
    norm_sums,
    joined_sums,
    expand_sums,
    back_out,
    shrink_out,
    dense_out,
    grad_queries,
    grad_keys,
    grad_values,
    board,
    back_core,
    back_chain,
    left,
    right,
    out_own,
    out_recv,
    out_last,
    dense_own,
    dense_recv,
    left_sem,
    right_sem,
    core_send,
    core_recv,
    chain_send,
    chain_recv,
    first_send,
    first_recv,
    last_send,
    last_recv,
    dense_send,
    dense_sem,
    store_sem,
):
    step = pl.program_id(0)
    seq = step // (2 * tiles)
    phase = lax.rem(step, 2 * tiles) // tiles
    tile = lax.rem(step, tiles)
    tile = jnp.where(phase == 0, tile, jnp.where(lax.rem(tile, 2) == 0, tiles - 1 - tile // 2, tile // 2))
    rows = pl.ds(pl.multiple_of(tile * TILE, TILE), TILE)
    n_expand = panels.shape[0] - 3
    width = out_w.shape[1]
    scale = 1.0 / math.sqrt(HEAD)

    d = lax.axis_index("dp")
    c = lax.axis_index("ctx")
    z = c // 2
    core = lax.rem(c, 2)
    sibling = c + 1 - 2 * core
    x_mate = d + 1 - 2 * lax.rem(d, 2)
    y_mate = lax.rem(d + 2, 4)
    diagonal = 3 - d
    levels = ctx_size // 2
    me = d * ctx_size + c
    span = board.shape[2]
    share = dense_out.shape[0]
    unit = (features.shape[1] - HEAD) // dp_size
    out_half = unit // 2
    head_half = HEAD // 2

    def left_copy(index):
        if index == 0:
            columns = pl.ds(0, HEAD)
        else:
            owner = (diagonal, x_mate, y_mate, d)[index - 1]
            columns = pl.ds(pl.multiple_of(HEAD + owner * unit, HEAD), unit)
        return pltpu.make_async_copy(features.at[:, columns], left.at[index % 2], left_sem.at[index % 2])

    right_copy = pltpu.make_async_copy(grads, right, right_sem.at[0])

    def compute(index):
        if index < dp_size:
            left_copy(index + 1).start()
        left_copy(index).wait()
        target = dense_own if index == 0 else out_own.at[index - 1]
        for start in range(0, width, 1024):
            columns = slice(start, start + 1024)
            target[:, columns] = dot_tn(left[index % 2], right[:, columns]).astype(jnp.bfloat16)

    def out_rows(index, way):
        return out_own.at[index, pl.ds(way * out_half, out_half)]

    first_copy, pass_on, arrive, add_final, square_finish = square_sum(
        lambda way, slot: out_rows(0 if slot == 1 else 1 + way, way),
        lambda way: out_rows(2 - way, way),
        out_recv,
        out_last,
        lambda way: out_rows(3, way),
        (first_send, first_recv, last_send, last_recv),
        d,
        c,
        out_half,
    )

    def out_store(way):
        return pltpu.make_async_copy(
            out_rows(3, way), shrink_out.at[pl.ds(way * out_half, out_half)], store_sem.at[way]
        )

    source = c // (ctx_size // dp_size)
    at_source = d == source
    from_x = x_mate == source
    from_y = y_mate == source
    across = diagonal == source
    per_head = HEAD // share

    def dense_half(way):
        return dense_own.at[pl.ds(way * head_half, head_half)]

    def dense_copy(way, mate):
        return remote(dense_half(way), dense_recv.at[way], dense_send.at[way], dense_sem.at[way], mate, c)

    def dense_add(way, mate):
        dense_copy(way, mate).wait_recv()
        add_into(dense_half(way), (dense_half(way), dense_recv.at[way]), head_half)

    def dense_open():
        @pl.when(from_y)
        def _():
            dense_copy(0, x_mate).start()

        @pl.when(from_x)
        def _():
            dense_copy(1, y_mate).start()

    def dense_second():
        @pl.when(across)
        def _():
            dense_add(0, y_mate)
            dense_copy(0, y_mate).start()
            dense_add(1, x_mate)
            dense_copy(1, x_mate).start()

    def dense_third():
        @pl.when(from_x)
        def _():
            dense_add(0, x_mate)
            dense_copy(0, x_mate).start()

        @pl.when(from_y)
        def _():
            dense_add(1, y_mate)
            dense_copy(1, y_mate).start()

    first_owner = lax.rem(c, ctx_size // per_head) * per_head

    def dense_chunk(piece):
        return dense_own.at[pl.ds(piece * share, share)]

    def dense_send_out(piece):
        return remote(
            dense_chunk(piece), dense_out, dense_send.at[2 + piece], dense_sem.at[2], d, first_owner + piece
        )

    def dense_store(piece):
        return pltpu.make_async_copy(dense_chunk(piece), dense_out, store_sem.at[2])

    def dense_fourth():
        @pl.when(at_source)
        def _():
            dense_add(0, x_mate)
            dense_add(1, y_mate)
            for piece in range(per_head):
                @pl.when(first_owner + piece == c)
                def _(piece=piece):
                    dense_store(piece).start()

                @pl.when(first_owner + piece != c)
                def _(piece=piece):
                    dense_send_out(piece).start()

    def dense_finish():
        @pl.when(jnp.logical_or(jnp.logical_or(from_y, across), from_x))
        def _():
            dense_copy(0, x_mate).wait_send()
            dense_copy(1, x_mate).wait_send()

        for piece in range(per_head):
            @pl.when(jnp.logical_and(at_source, first_owner + piece != c))
            def _(piece=piece):
                dense_send_out(piece).wait_send()

        stays = me // per_head == c

        @pl.when(stays)
        def _():
            dense_store(0).wait()

        @pl.when(jnp.logical_not(stays))
        def _():
            dense_send_out(0).wait_recv()

    def own_block(level):
        return board.at[level, core]

    def core_copy(level):
        return remote(
            board.at[level, 1 - core], back_core.at[level], core_send.at[level], core_recv.at[level], d, sibling
        )

    def core_add(level):
        core_copy(level).wait_recv()
        add_into(own_block(level), (own_block(level), back_core.at[level]), span)

    chain_open, chain_round, chain_end, chain_finish = chain_reduce(
        own_block, back_chain, (chain_send, chain_recv), d, c, levels
    )

    def back_store(level):
        return pltpu.make_async_copy(own_block(level), back_out, store_sem.at[3])

    def at(when):
        return pl.when(step == when)

    @at(0)
    def _():
        greet_all(d, c, dp_size, ctx_size)
        left_copy(0).start()
        right_copy.start()
        norm_sums[...] = jnp.zeros_like(norm_sums)
        joined_sums[...] = jnp.zeros_like(joined_sums)
        expand_sums[...] = jnp.zeros_like(expand_sums)

    @at(1)
    def _():
        right_copy.wait()
        compute(0)
        dense_open()

    @at(2)
    def _():
        compute(1)
        first_copy(0, 1).start()
        first_copy(1, 1).start()

    @at(3)
    def _():
        compute(2)
        first_copy(0, 0).start()
        compute(3)
        first_copy(1, 0).start()

    @at(4)
    def _():
        compute(4)

    for place, level in enumerate(outside_in(levels)):
        @at(tiles + 1 + place)
        def _(level=level):
            core_copy(level).start()

        @at(tiles + 2 + place)
        def _(level=level):
            core_add(level)
            chain_open(level)

    @at(6)
    def _():
        dense_second()

    @at(7)
    def _():
        pass_on(0)
        pass_on(1)

    @at(10)
    def _():
        chain_round(1)
        dense_third()

    @at(13)
    def _():
        chain_round(2)
        for way in range(2):
            arrive(way)
            add_final(way, 0, out_half)
            out_store(way).start()

    @at(14)
    def _():
        dense_fourth()

    @pl.when(phase == 0)
    def _():
        low_probs = probs[0]
        own = dot_nt(g[...], out_w[:HEAD, :]).astype(jnp.bfloat16)
        grad_probs = dot_nt(own, heads[2])
        wide = low_probs.astype(jnp.float32)
        delta = jnp.sum(wide * grad_probs, axis=1, keepdims=True)
        grad_scores = (wide * (grad_probs - delta)).astype(jnp.bfloat16)
        grad_queries[rows, :] = dot_nn(grad_scores, heads[1]) * scale
        more_keys = dot_tn(grad_scores, heads[0, rows, :]) * scale
        more_values = dot_tn(low_probs, own)

        @pl.when(tile == 0)
        def _():
            grad_keys[...] = more_keys
            grad_values[...] = more_values

        @pl.when(tile > 0)
        def _():
            grad_keys[...] += more_keys
            grad_values[...] += more_values

    @pl.when(phase == 1)
    def _():
        grad = dot_nt(g[...], out_w[HEAD:, :])
        grad = (grad * slopes[...].astype(jnp.float32)).astype(jnp.bfloat16)
        grad_expanded[...] = grad
        expand_sums[...] += jnp.sum(grad.astype(jnp.float32), axis=0, keepdims=True)
        cos_rows, sin_rows = cos[rows, :], -sin[rows, :]
        parts = (
            turn(grad_queries[rows, :], cos_rows, sin_rows),
            turn(grad_keys[rows, :], cos_rows, sin_rows),
            grad_values[rows, :],
        )
        for part in range(3):
            columns = slice(part * HEAD, (part + 1) * HEAD)
            joined = parts[part].astype(jnp.bfloat16)
            grad_joined[:, columns] = joined
            joined_sums[:, columns] += jnp.sum(joined.astype(jnp.float32), axis=0, keepdims=True)
        values_in = x[...].astype(jnp.float32)
        mean = jnp.mean(values_in, axis=1, keepdims=True)
        centered = values_in - mean
        spread = lax.rsqrt(jnp.mean(centered * centered, axis=1, keepdims=True) + 1e-05)
        for start in range(0, width, 1024):
            columns = slice(start, start + 1024)
            normal = (x[:, columns].astype(jnp.float32) - mean) * spread
            wide = jnp.concatenate([panels[part, columns, :] for part in range(3)], axis=1)
            total = dot_nt(grad_joined[...], wide)
            wide = jnp.concatenate([panels[3 + part, columns, :] for part in range(n_expand)], axis=1)
            other = dot_nt(grad_expanded[...], wide)
            for row, value in ((0, total * normal), (1, total), (2, other * normal), (3, other)):
                norm_sums[row : row + 1, columns] += jnp.sum(value, axis=0, keepdims=True)
            value = (total * gains[0:1, columns] + other * gains[2:3, columns]).astype(jnp.bfloat16)

            @pl.when(seq == 0)
            def _(columns=columns, value=value):
                for parity in range(2):
                    board[tile, parity, :, columns] = value[parity * span : (parity + 1) * span]

            @pl.when(seq > 0)
            def _(columns=columns, value=value):
                combined[:, columns] = value

    @at(4 * tiles - 1)
    def _():
        chain_end(back_store)
        square_finish()
        for way in range(2):
            out_store(way).wait()
        dense_finish()
        for level in range(levels):
            core_copy(level).wait_send()
        chain_finish(back_store)


def backward_call(dp_size, ctx_size, g, x, panels, out_w, gains, cos, sin, heads, probs, slopes, features):
    tokens, width = x.shape
    length = cos.shape[0]
    tiles = length // TILE
    steps = 2 * tokens // TILE
    hidden = slopes.shape[1]
    levels = ctx_size // 2
    span = length // ctx_size
    unit = hidden // dp_size
    share = width // (dp_size * ctx_size)
    dma = pltpu.SemaphoreType.DMA
    vmem = pltpu.VMEM

    def first(step):
        seq, at = step // (2 * tiles), lax.rem(step, 2 * tiles)
        return seq * tiles + jnp.minimum(at, tiles - 1)

    def mixed_order(place):
        return jnp.where(lax.rem(place, 2) == 0, tiles - 1 - place // 2, place // 2)

    def second(step):
        seq, at = step // (2 * tiles), lax.rem(step, 2 * tiles)
        return seq * tiles + mixed_order(jnp.maximum(at - tiles, 0))

    def both(step):
        seq, at = step // (2 * tiles), lax.rem(step, 2 * tiles)
        return seq * tiles + jnp.where(at < tiles, at, mixed_order(at - tiles))

    def late(step):
        return jnp.where(step < 2 * tiles, mixed_order(0), second(step) - tiles)

    kind = jnp.bfloat16
    fixed = lambda step: (0, 0)
    anywhere = pl.BlockSpec(memory_space=pl.ANY)
    return pl.pallas_call(
        functools.partial(backward_kernel, tiles, dp_size, ctx_size),
        grid=(steps,),
        out_shape=(
            jax.ShapeDtypeStruct((tokens, hidden), kind),
            jax.ShapeDtypeStruct((tokens, 3 * HEAD), kind),
            jax.ShapeDtypeStruct((length, width), kind),
            jax.ShapeDtypeStruct((8, width), jnp.float32),
            jax.ShapeDtypeStruct((1, 3 * HEAD), jnp.float32),
            jax.ShapeDtypeStruct((1, hidden), jnp.float32),
            jax.ShapeDtypeStruct((span, width), kind),
            jax.ShapeDtypeStruct((unit, width), kind),
            jax.ShapeDtypeStruct((share, width), kind),
        ),
        in_specs=[
            pl.BlockSpec((TILE, width), lambda step: (both(step), 0)),
            pl.BlockSpec((TILE, width), lambda step: (second(step), 0)),
            whole_spec(panels),
            whole_spec(out_w),
            whole_spec(gains),
            whole_spec(cos),
            whole_spec(sin),
            pl.BlockSpec((3, length, HEAD), lambda step: (0, step // (2 * tiles), 0)),
            pl.BlockSpec((1, TILE, length), lambda step: (first(step) // tiles, lax.rem(first(step), tiles), 0)),
            pl.BlockSpec((TILE, hidden), lambda step: (second(step), 0)),
            anywhere,
            anywhere,
        ],
        out_specs=(
            pl.BlockSpec((TILE, hidden), lambda step: (second(step), 0)),
            pl.BlockSpec((TILE, 3 * HEAD), lambda step: (second(step), 0)),
            pl.BlockSpec((TILE, width), lambda step: (late(step), 0)),
            pl.BlockSpec((8, width), fixed),
            pl.BlockSpec((1, 3 * HEAD), fixed),
            pl.BlockSpec((1, hidden), fixed),
            anywhere,
            anywhere,
            anywhere,
        ),
        scratch_shapes=[
            vmem((length, HEAD), jnp.float32),
            vmem((length, HEAD), jnp.float32),
            vmem((length, HEAD), jnp.float32),
            vmem((levels, 2, span, width), kind),
            vmem((levels, span, width), kind),
            vmem((2, levels - 1, span, width), kind),
            vmem((2, tokens, HEAD), kind),
            vmem((tokens, width), kind),
            vmem((dp_size, unit, width), kind),
            vmem((2, 2, unit // 2, width), kind),
            vmem((2, unit // 2, width), kind),
            vmem((HEAD, width), kind),
            vmem((2, HEAD // 2, width), kind),
            dma((2,)),
            dma((1,)),
            dma((levels,)),
            dma((levels,)),
            dma((2, levels)),
            dma((2, levels)),
            *square_scratch(),
            dma((2 + HEAD // share,)),
            dma((3,)),
            dma((4,)),
        ],
        compiler_params=pltpu.CompilerParams(
            collective_id=4, has_side_effects=True, vmem_limit_bytes=60 * 1024 * 1024
        ),
        name="backward_part",
    )(g, x, panels, out_w, gains, cos, sin, heads, probs, slopes, features, g)


def reduce_kernel(
    dp_size,
    ctx_size,
    back,
    hidden_attn,
    hidden_mlp,
    grad_joined,
    grad_expanded,
    board,
    back_out,
    attn_out,
    mlp_out,
    tail_out,
    back_own,
    back_core,
    back_chain,
    left,
    right_attn,
    right_mlp,
    attn_own,
    attn_recv,
    attn_last,
    mlp_own,
    mlp_recv,
    mlp_last,
    board_recv,
    load_sem,
    left_sem,
    right_sem,
    core_send,
    core_recv,
    chain_send,
    chain_recv,
    first_send_a,
    first_recv_a,
    last_send_a,
    last_recv_a,
    first_send_m,
    first_recv_m,
    last_send_m,
    last_recv_m,
    row_send,
    row_recv,
    board_sem,
    store_sem,
):
    d = lax.axis_index("dp")
    c = lax.axis_index("ctx")
    core = lax.rem(c, 2)
    sibling = c + 1 - 2 * core
    x_mate = d + 1 - 2 * lax.rem(d, 2)
    y_mate = lax.rem(d + 2, 4)
    diagonal = 3 - d
    span = back.shape[0] // ctx_size
    levels = ctx_size // 2
    devices = dp_size * ctx_size
    me = d * ctx_size + c
    group_rows = hidden_attn.shape[1] // dp_size
    half = group_rows // 2
    rows = group_rows // ctx_size

    greet_all(d, c, dp_size, ctx_size)

    def back_view(parity, level):
        start = (2 * level + parity) * span
        return back.at[pl.ds(pl.multiple_of(start, span), span)]

    def back_load(level):
        return pltpu.make_async_copy(back_view(core, level), back_own.at[level], load_sem.at[level])

    def core_copy(level):
        return remote(
            back_view(1 - core, level), back_core.at[level], core_send.at[level], core_recv.at[level], d, sibling
        )

    order = outside_in(levels)

    tile_of = []
    for owners in ((diagonal, diagonal), (x_mate, y_mate), (y_mate, x_mate), (d, d)):
        for way in range(2):
            tile_of.append((owners[way], way))
    sequence = [(0, index) for index in range(6)]
    sequence += [(1, index) for index in range(4)]
    sequence += [(0, index) for index in range(6, 8)]
    sequence += [(1, index) for index in range(4, 8)]

    def left_copy(place):
        kind, index = sequence[place]
        owner, way = tile_of[index]
        columns = pl.ds(pl.multiple_of(owner * group_rows + way * half, half), half)
        source = (hidden_attn, hidden_mlp)[kind]
        return pltpu.make_async_copy(source.at[:, columns], left.at[place % 2], left_sem.at[place % 2])

    right_copies = (
        pltpu.make_async_copy(grad_joined, right_attn, right_sem.at[0]),
        pltpu.make_async_copy(grad_expanded, right_mlp, right_sem.at[1]),
    )

    def compute(kind, index):
        place = sequence.index((kind, index))
        if place + 1 < len(sequence):
            left_copy(place + 1).start()
        left_copy(place).wait()
        if index == 0:
            right_copies[kind].wait()
        target, right = ((attn_own, right_attn), (mlp_own, right_mlp))[kind]
        target[index] = dot_tn(left[place % 2], right[...]).astype(jnp.bfloat16)

    def square(own, recv, last, sems):
        return square_sum(
            lambda way, slot: own.at[way + 2 * (1 - slot)],
            lambda way: own.at[4 + way],
            recv,
            last,
            lambda way: own.at[6 + way],
            sems,
            d,
            c,
            half,
        )

    squares = (
        square(attn_own, attn_recv, attn_last, (first_send_a, first_recv_a, last_send_a, last_recv_a)),
        square(mlp_own, mlp_recv, mlp_last, (first_send_m, first_recv_m, last_send_m, last_recv_m)),
    )

    per_half = half // rows

    def row_chunk(kind, way, piece):
        return (attn_own, mlp_own)[kind].at[6 + way, pl.ds(piece * rows, rows)]

    def row_copy(kind, way, piece):
        target = way * per_half + piece
        out = (attn_out, mlp_out)[kind]
        return remote(
            row_chunk(kind, way, piece), out.at[c], row_send.at[kind, target], row_recv.at[kind], d, target
        )

    def row_local(kind, way, piece):
        out = (attn_out, mlp_out)[kind]
        return pltpu.make_async_copy(row_chunk(kind, way, piece), out.at[c], store_sem.at[kind])

    def tile_end(kind):
        first_copy, pass_on, arrive, add_final, finish = squares[kind]
        for way in range(2):
            arrive(way)
            for piece in range(per_half):
                add_final(way, piece * rows, rows)
                target = way * per_half + piece

                @pl.when(c != target)
                def _(way=way, piece=piece):
                    row_copy(kind, way, piece).start()

                @pl.when(c == target)
                def _(way=way, piece=piece):
                    row_local(kind, way, piece).start()

    board_load = pltpu.make_async_copy(board.at[me], board_recv.at[me], load_sem.at[levels])

    def board_start():
        board_load.start()

        def push_board(step, carry):
            other = lax.rem(me + step, devices)
            remote(
                board.at[other],
                board_recv.at[me],
                board_sem.at[0],
                board_sem.at[1],
                other // ctx_size,
                lax.rem(other, ctx_size),
            ).start()
            return carry

        lax.fori_loop(1, devices, push_board, 0)

    def board_end():
        board_load.wait()
        rest = board_recv.at[pl.ds(0, devices - 1)]
        remote(rest, rest, board_sem.at[0], board_sem.at[1], d, sibling).wait()
        tail_out[...] = jnp.sum(board_recv[...], axis=0)

    chain_open, chain_round, chain_end, chain_finish = chain_reduce(
        lambda level: back_own.at[level], back_chain, (chain_send, chain_recv), d, c, levels
    )

    def back_store(level):
        return pltpu.make_async_copy(back_own.at[level], back_out, store_sem.at[2])

    right_copies[0].start()
    left_copy(0).start()
    for level in order:
        core_copy(level).start()
        back_load(level).start()
    right_copies[1].start()

    for way in range(2):
        compute(0, way)
        squares[0][0](way, 1).start()
    for way in range(2):
        compute(0, 2 + way)
        squares[0][0](way, 0).start()
    for level in order:
        back_load(level).wait()
        core_copy(level).wait_recv()
        own = back_own.at[level]
        add_into(own, (own, back_core.at[level]), span)
        chain_open(level)
    compute(0, 4)
    compute(0, 5)
    squares[0][1](0)
    squares[0][1](1)
    for way in range(2):
        compute(1, way)
        squares[1][0](way, 1).start()
    for way in range(2):
        compute(1, 2 + way)
        squares[1][0](way, 0).start()
    chain_round(1)
    board_start()
    compute(0, 6)
    compute(0, 7)
    compute(1, 4)
    compute(1, 5)
    tile_end(0)
    chain_round(2)
    compute(1, 6)
    compute(1, 7)
    squares[1][1](0)
    squares[1][1](1)
    chain_end(back_store)
    tile_end(1)
    board_end()

    for kind in range(2):
        squares[kind][4]()
        for way in range(2):
            for piece in range(per_half):
                target = way * per_half + piece

                @pl.when(c != target)
                def _(kind=kind, way=way, piece=piece):
                    row_copy(kind, way, piece).wait_send()

        out = (attn_out, mlp_out)[kind]
        rest = out.at[pl.ds(0, ctx_size - 1)]
        remote(rest, rest, row_send.at[kind, 0], row_recv.at[kind], d, sibling).wait_recv()
        row_local(kind, 0, 0).wait()
    for level in range(levels):
        core_copy(level).wait_send()
    chain_finish(back_store)


def reduce_call(dp_size, ctx_size, back, hidden_attn, hidden_mlp, grad_joined, grad_expanded, board):
    length, width = back.shape
    tokens = hidden_attn.shape[0]
    span = length // ctx_size
    group_rows = width // dp_size
    half = group_rows // 2
    rows = group_rows // ctx_size
    joined, hidden = grad_joined.shape[1], grad_expanded.shape[1]
    levels = ctx_size // 2
    devices = dp_size * ctx_size
    dma = pltpu.SemaphoreType.DMA
    kind = back.dtype
    vmem = pltpu.VMEM
    out_shape = (
        jax.ShapeDtypeStruct((span, width), kind),
        jax.ShapeDtypeStruct((ctx_size, rows, joined), kind),
        jax.ShapeDtypeStruct((ctx_size, rows, hidden), kind),
        jax.ShapeDtypeStruct(board.shape[1:], jnp.float32),
    )
    anywhere = pl.BlockSpec(memory_space=pl.ANY)
    return pl.pallas_call(
        functools.partial(reduce_kernel, dp_size, ctx_size),
        out_shape=out_shape,
        in_specs=[anywhere] * 6,
        out_specs=(anywhere,) * 3 + (pl.BlockSpec(memory_space=pltpu.VMEM),),
        scratch_shapes=[
            vmem((levels, span, width), kind),
            vmem((levels, span, width), kind),
            vmem((2, levels - 1, span, width), kind),
            vmem((2, tokens, HEAD), kind),
            vmem((tokens, joined), kind),
            vmem((tokens, hidden), kind),
            vmem((8, half, joined), kind),
            vmem((2, 2, half, joined), kind),
            vmem((2, half, joined), kind),
            vmem((8, half, hidden), kind),
            vmem((2, 2, half, hidden), kind),
            vmem((2, half, hidden), kind),
            vmem((devices,) + board.shape[1:], jnp.float32),
            dma((levels + 1,)),
            dma((2,)),
            dma((2,)),
            dma((levels,)),
            dma((levels,)),
            dma((2, levels)),
            dma((2, levels)),
            *square_scratch(),
            *square_scratch(),
            dma((2, ctx_size)),
            dma((2,)),
            dma((2,)),
            dma((3,)),
        ],
        compiler_params=pltpu.CompilerParams(
            collective_id=2, has_side_effects=True, vmem_limit_bytes=60 * 1024 * 1024
        ),
        name="reduce_all",
    )(back, hidden_attn, hidden_mlp, grad_joined, grad_expanded, board)


def finish_kernel(
    attn_rows,
    mlp_rows,
    shrink_rows,
    dense_rows,
    back_first,
    back_last,
    x,
    g,
    out_first,
    out_last,
    out_shift,
    tail,
    qkv_grad,
    expand_grad,
    shrink_grad,
    dense_grad,
    layer_output,
    input_grad,
    *small_grads,
):
    ctx_size = attn_rows.shape[0]
    at = 0
    for target in small_grads:
        size = target.shape[0] * target.shape[1]
        for row in range(target.shape[0]):
            start = at + row * target.shape[1]
            lane = start % 128
            target[row : row + 1, :] = tail[start // 128 : start // 128 + 1, lane : lane + target.shape[1]]
        at += size
    for rows, target in ((attn_rows, qkv_grad), (mlp_rows, expand_grad)):
        for member in range(ctx_size):
            for part in range(rows.shape[2] // HEAD):
                start = (part * ctx_size + member) * HEAD
                target[:, start : start + HEAD] = rows[member, :, part * HEAD : (part + 1) * HEAD].astype(jnp.float32)
    shrink_grad[...] = shrink_rows[...].astype(jnp.float32)
    dense_grad[...] = dense_rows[...].astype(jnp.float32)
    for m, (back, out) in enumerate(((back_first, out_first), (back_last, out_last))):
        own = x[m].astype(jnp.float32)
        layer_output[m] = (own + out[...].astype(jnp.float32) + out_shift[...]).astype(jnp.bfloat16)
        centered = own - jnp.mean(own, axis=1, keepdims=True)
        spread = lax.rsqrt(jnp.mean(centered * centered, axis=1, keepdims=True) + 1e-05)
        normal = centered * spread
        grad = back[...].astype(jnp.float32)
        share = spread * (
            grad
            - jnp.mean(grad, axis=1, keepdims=True)
            - normal * jnp.mean(grad * normal, axis=1, keepdims=True)
        )
        input_grad[m] = (g[m].astype(jnp.float32) + share).astype(jnp.bfloat16)


def finish_call(attn_rows, mlp_rows, shrink_rows, dense_rows, back_first, back_last, x, g, out_first, out_last, out_shift, tail, lengths):
    steps = 4
    arrays = (attn_rows, mlp_rows, shrink_rows, dense_rows, back_first, back_last, x, g, out_first, out_last)
    micro = x.shape[0]
    ctx_size, rows, joined = attn_rows.shape

    def spec(shape):
        block = shape[:-2] + (shape[-2] // steps, shape[-1])
        lead = (0,) * (len(shape) - 2)
        return pl.BlockSpec(block, lambda step: lead + (step, 0))

    outs = (
        jax.ShapeDtypeStruct((rows, joined * ctx_size), jnp.float32),
        jax.ShapeDtypeStruct((rows, mlp_rows.shape[2] * ctx_size), jnp.float32),
        jax.ShapeDtypeStruct(shrink_rows.shape, jnp.float32),
        jax.ShapeDtypeStruct(dense_rows.shape, jnp.float32),
        jax.ShapeDtypeStruct(x.shape, jnp.bfloat16),
        jax.ShapeDtypeStruct(x.shape, jnp.bfloat16),
    )
    smalls = tuple(
        jax.ShapeDtypeStruct((max(1, length // 128), min(length, 128)), jnp.float32) for length in lengths
    )
    return pl.pallas_call(
        finish_kernel,
        grid=(steps,),
        out_shape=outs + smalls,
        in_specs=[spec(array.shape) for array in arrays] + [whole_spec(out_shift), whole_spec(tail)],
        out_specs=tuple(spec(out.shape) for out in outs)
        + tuple(pl.BlockSpec(out.shape, lambda step: (0, 0)) for out in smalls),
        compiler_params=pltpu.CompilerParams(vmem_limit_bytes=60 * 1024 * 1024),
        name="finish_part",
    )(*arrays, out_shift, tail)


def tensor_shards(
    layer_input,
    out_grad,
    prefix_len,
    qkv_weight,
    qkv_bias,
    dense_weight,
    dense_bias,
    expand_weight,
    expand_bias,
    shrink_weight,
    shrink_bias,
    attn_gain,
    attn_shift,
    mlp_gain,
    mlp_shift,
):
    dp_size = lax.axis_size("dp")
    ctx_size = lax.axis_size("ctx")
    devices = dp_size * ctx_size
    me = lax.axis_index("ctx")
    group = lax.axis_index("dp")
    micro, seq_count, span, width = layer_input.shape
    sequences = micro * seq_count
    tokens = sequences * SEQ
    row_share = qkv_weight.shape[0]
    scale = 1.0 / math.sqrt(HEAD)
    ff = expand_weight.shape[1]
    unit = shrink_weight.shape[0]
    lengths = tuple(
        member.shape[0]
        for member in (attn_gain, attn_shift, mlp_gain, mlp_shift, qkv_bias, dense_bias, expand_bias, shrink_bias)
    )
    packed = jnp.concatenate(
        [attn_gain, attn_shift, mlp_gain, mlp_shift, qkv_bias, dense_bias, expand_bias, shrink_bias]
    )
    own_x = layer_input.reshape(sequences, span, width)
    own_g = out_grad.reshape(sequences, span, width)
    count = packed.shape[0]
    packed = jnp.pad(packed, (0, -count % 2048)).reshape(-1, 128)
    x_all, panels, out_part, small = gather_call(
        dp_size, ctx_size, own_x, qkv_weight, expand_weight, dense_weight, shrink_weight, packed
    )
    x_all = x_all.reshape(tokens, width)
    small = unpack_small(small.reshape(devices, -1)[:, :count], lengths, devices)
    gain_attn, shift_attn, gain_mlp, shift_mlp, qkv_shift, dense_shift, expand_shift, shrink_shift = small
    qkv_shift = lax.dynamic_slice_in_dim(qkv_shift.reshape(3, ctx_size, HEAD), me, 1, 1).reshape(-1)
    expand_shift = lax.dynamic_slice_in_dim(
        expand_shift.reshape(dp_size, ctx_size, unit), me, 1, 1
    ).reshape(-1)

    gains = jnp.stack([gain_attn, shift_attn, gain_mlp, shift_mlp])
    cos, sin = turn_tables(SEQ)
    hidden_attn, hidden_mlp, heads, probs, features, slopes, partial, g_all, out_first = forward_call(
        ctx_size // 2,
        prefix_len.reshape(sequences),
        x_all,
        own_g,
        panels,
        out_part,
        gains,
        qkv_shift[None],
        expand_shift[None],
        cos,
        sin,
    )
    g_all = g_all.reshape(tokens, width)
    out_last = lax.psum_scatter(partial, "ctx", scatter_dimension=0, tiled=True)

    (
        grad_expanded,
        grad_joined,
        combined,
        norm_sums,
        joined_sum,
        expand_sum,
        back_first,
        shrink_rows,
        dense_rows,
    ) = backward_call(
        dp_size, ctx_size, g_all, x_all, panels, out_part, gains, cos, sin, heads, probs, slopes, features
    )
    joined_sum, expand_sum = joined_sum[0], expand_sum[0]

    def place(values, parts):
        board = jnp.zeros((parts, ctx_size, values.shape[0] // parts), jnp.float32)
        board = lax.dynamic_update_slice(board, values.reshape(parts, 1, -1), (0, me, 0))
        return board.reshape(devices, -1)

    out_sum = jnp.sum(own_g.astype(jnp.float32), axis=(0, 1))
    board = jnp.concatenate(
        [
            place(joined_sum[: 2 * HEAD], 2),
            place(joined_sum[2 * HEAD :], 1),
            out_sum.reshape(devices, -1),
            place(expand_sum, dp_size),
            norm_sums[0].reshape(devices, -1),
            norm_sums[1].reshape(devices, -1),
            norm_sums[2].reshape(devices, -1),
            norm_sums[3].reshape(devices, -1),
        ],
        axis=1,
    )
    used = board.shape[1]
    board = jnp.pad(board, ((0, 0), (0, -used % 1024))).reshape(devices, -1, 128)
    back_last, attn_rows, mlp_rows, tail = reduce_call(
        dp_size, ctx_size, combined, hidden_attn, hidden_mlp, grad_joined, grad_expanded, board
    )
    share_len = width // devices
    small_lengths = (2 * share_len, share_len, share_len, ff // devices) + (share_len,) * 4
    qkv_grad, expand_grad, shrink_grad, dense_grad, layer_output, input_grad, *pieces = finish_call(
        attn_rows,
        mlp_rows,
        shrink_rows,
        dense_rows,
        back_first,
        back_last,
        own_x,
        own_g,
        out_first,
        out_last,
        (dense_shift + shrink_shift)[None],
        tail,
        small_lengths,
    )
    pieces = [piece.reshape(-1) for piece in pieces]
    layer_output = layer_output.reshape(layer_input.shape)
    input_grad = input_grad.reshape(layer_input.shape)
    return (
        layer_output,
        input_grad,
        qkv_grad,
        pieces[0],
        pieces[1],
        dense_grad,
        pieces[2],
        expand_grad,
        pieces[3],
        shrink_grad,
        pieces[2],
        pieces[4],
        pieces[5],
        pieces[6],
        pieces[7],
    )


def solution(mesh):
    placed = (
        P(None, "dp", "ctx", None),
        P(None, "dp", "ctx", None),
        P(None, "dp"),
        P(("dp", "ctx"), None),
        P(("dp", "ctx")),
        P(("dp", "ctx"), None),
        P(("dp", "ctx")),
        P(("dp", "ctx"), None),
        P(("dp", "ctx")),
        P(("dp", "ctx"), None),
        P(("dp", "ctx")),
        P(("dp", "ctx")),
        P(("dp", "ctx")),
        P(("dp", "ctx")),
        P(("dp", "ctx")),
    )
    return jax.shard_map(
        tensor_shards if (mesh.shape["dp"], mesh.shape["ctx"]) == (4, HEADS) else shards,
        mesh=mesh,
        in_specs=placed,
        out_specs=(
            P(None, "dp", "ctx", None),
            P(None, "dp", "ctx", None),
            P(("dp", "ctx"), None),
            P(("dp", "ctx")),
            P(("dp", "ctx")),
            P(("dp", "ctx"), None),
            P(("dp", "ctx")),
            P(("dp", "ctx"), None),
            P(("dp", "ctx")),
            P(("dp", "ctx"), None),
            P(("dp", "ctx")),
            P(("dp", "ctx")),
            P(("dp", "ctx")),
            P(("dp", "ctx")),
            P(("dp", "ctx")),
        ),
        check_vma=False,
    )
```

```python
import functools
import math

import jax
import jax.numpy as jnp
import numpy as np
from jax import lax
from jax.experimental import pallas as pl
from jax.experimental.pallas import tpu as pltpu
from jax.sharding import PartitionSpec as P

HEADS = 8
HEAD = 256
ROT = 64
SEQ = 1024


def norm_rows(inputs, norm_gain, norm_bias):
    row_mean = jnp.mean(inputs, axis=-1, keepdims=True)
    centered = inputs - row_mean
    variance = jnp.mean(centered * centered, axis=-1, keepdims=True)
    return centered * lax.rsqrt(variance + 1e-05) * norm_gain + norm_bias


def gelu_exact(values):
    return jax.nn.gelu(values, approximate=False)


def rope_tables(positions):
    freqs = jnp.exp(jnp.arange(ROT // 2, dtype=jnp.float32) * (-2.0 * math.log(10000.0) / ROT))
    angles = positions[:, None] * freqs[None, :]
    return (jnp.cos(angles), jnp.sin(angles))


def rotate(heads, cos_table, sin_table):
    half_rot = ROT // 2
    lower = heads[..., :half_rot]
    upper = heads[..., half_rot:ROT]
    cos_wide = cos_table[:, None, :]
    sin_wide = sin_table[:, None, :]
    return jnp.concatenate(
        [
            lower * cos_wide - upper * sin_wide,
            upper * cos_wide + lower * sin_wide,
            heads[..., ROT:],
        ],
        axis=-1,
    )


def unpack_small(packed, lengths, devices):
    table_rows = packed.reshape(devices, -1)
    members = []
    offset = 0
    for length in lengths:
        members.append(table_rows[:, offset : offset + length].reshape(-1).astype(jnp.float32))
        offset = offset + length
    return members


def contract_rows(left_mat, right_mat):
    return lax.dot_general(
        left_mat, right_mat, (((0,), (0,)), ((), ())), preferred_element_type=jnp.float32
    )


def contract_cols(left_mat, right_mat):
    return lax.dot_general(
        left_mat, right_mat, (((1,), (1,)), ((), ())), preferred_element_type=jnp.float32
    )


def shards(
    layer_input,
    out_grad,
    prefix_len,
    qkv_weight,
    qkv_bias,
    dense_weight,
    dense_bias,
    expand_weight,
    expand_bias,
    shrink_weight,
    shrink_bias,
    attn_gain,
    attn_shift,
    mlp_gain,
    mlp_shift,
):
    devices = lax.axis_size("dp") * lax.axis_size("ctx")
    ctx_index = lax.axis_index("ctx")
    micro, seq_count, span, width = layer_input.shape
    sequences = micro * seq_count
    rows = sequences * span
    heads_shape = (sequences, span, HEADS, HEAD)
    scale = 1.0 / math.sqrt(HEAD)
    attn_lengths = (attn_gain.shape[0], attn_shift.shape[0], qkv_bias.shape[0], dense_bias.shape[0])
    mlp_lengths = (
        mlp_gain.shape[0],
        mlp_shift.shape[0],
        expand_bias.shape[0],
        shrink_bias.shape[0],
    )
    attn_packed = jnp.concatenate([attn_gain, attn_shift, qkv_bias, dense_bias])
    mlp_packed = jnp.concatenate([mlp_gain, mlp_shift, expand_bias, shrink_bias])

    def fetch_attn():
        return (
            lax.all_gather(qkv_weight, ("dp", "ctx"), axis=0, tiled=True),
            lax.all_gather(dense_weight, ("dp", "ctx"), axis=0, tiled=True),
            lax.all_gather(attn_packed, ("dp", "ctx"), axis=0, tiled=True),
        )

    def fetch_mlp():
        return (
            lax.all_gather(expand_weight, ("dp", "ctx"), axis=0, tiled=True),
            lax.all_gather(shrink_weight, ("dp", "ctx"), axis=0, tiled=True),
            lax.all_gather(mlp_packed, ("dp", "ctx"), axis=0, tiled=True),
        )

    local_pos = ctx_index * span + jnp.arange(span, dtype=jnp.int32)
    cos_table, sin_table = rope_tables(local_pos.astype(jnp.float32))
    key_pos = jnp.arange(SEQ, dtype=jnp.int32)
    causal = key_pos[None, :] <= local_pos[:, None]
    inputs = layer_input.astype(jnp.float32).reshape(rows, width)
    cot_rows = out_grad.reshape(rows, width)
    cot_float = cot_rows.astype(jnp.float32)
    prefix = prefix_len.reshape(sequences)
    allowed = (causal[None] | (key_pos[None, None, :] < prefix[:, None, None]))[:, None]
    attn_set = fetch_attn()
    qkv_full, dense_full, attn_small = attn_set
    gain_attn, shift_attn, joined_shift, dense_shift = unpack_small(
        attn_small, attn_lengths, devices
    )
    hidden_attn = norm_rows(inputs, gain_attn, shift_attn).astype(jnp.bfloat16)
    joined = jnp.dot(hidden_attn, qkv_full, preferred_element_type=jnp.float32) + joined_shift
    queries = rotate(joined[:, :width].reshape(heads_shape), cos_table, sin_table).astype(
        jnp.bfloat16
    )
    key_rows = rotate(
        joined[:, width : 2 * width].reshape(heads_shape), cos_table, sin_table
    ).astype(jnp.bfloat16)
    value_rows = joined[:, 2 * width :].reshape(heads_shape).astype(jnp.bfloat16)
    all_keys, all_values = (
        lax.all_gather(key_rows, "ctx", axis=1, tiled=True),
        lax.all_gather(value_rows, "ctx", axis=1, tiled=True),
    )
    scores = (
        jnp.einsum("sqhe,skhe->shqk", queries, all_keys, preferred_element_type=jnp.float32) * scale
    )
    scores = jnp.where(allowed, scores, -1e30)
    row_max = jnp.max(scores, axis=-1, keepdims=True)
    expo = jnp.exp(scores - row_max)
    row_total = jnp.sum(expo, axis=-1, keepdims=True)
    log_total = row_max + jnp.log(row_total)
    probs_low = (expo / row_total).astype(jnp.bfloat16)
    mixed = jnp.einsum("shqk,skhe->sqhe", probs_low, all_values, preferred_element_type=jnp.float32)
    mixed = mixed.reshape(rows, width).astype(jnp.bfloat16)
    attn_out = jnp.dot(mixed, dense_full, preferred_element_type=jnp.float32) + dense_shift
    mlp_set = fetch_mlp()
    expand_full, shrink_full, mlp_small = mlp_set
    gain_mlp, shift_mlp, expand_shift, shrink_shift = unpack_small(mlp_small, mlp_lengths, devices)
    hidden_mlp = norm_rows(inputs, gain_mlp, shift_mlp).astype(jnp.bfloat16)
    expanded = jnp.dot(hidden_mlp, expand_full, preferred_element_type=jnp.float32) + expand_shift
    activated = gelu_exact(expanded).astype(jnp.bfloat16)
    mlp_out = jnp.dot(activated, shrink_full, preferred_element_type=jnp.float32) + shrink_shift
    layer_output = (
        (inputs + attn_out + mlp_out).astype(jnp.bfloat16).reshape(micro, seq_count, span, width)
    )
    attn_back_set = fetch_attn()
    qkv_back, dense_back, attn_small_back = attn_back_set
    gain_attn, shift_attn, joined_shift, dense_shift = unpack_small(
        attn_small_back, attn_lengths, devices
    )
    grad_out_shift = jnp.sum(cot_float, axis=0)
    grad_mixed = contract_cols(cot_rows, dense_back).astype(jnp.bfloat16).reshape(heads_shape)
    again = (
        jnp.einsum("sqhe,skhe->shqk", queries, all_keys, preferred_element_type=jnp.float32) * scale
    )
    again = jnp.where(allowed, again, -1e30)
    probs = jnp.exp(again - log_total)
    grad_probs = jnp.einsum(
        "sqhe,skhe->shqk", grad_mixed, all_values, preferred_element_type=jnp.float32
    )
    delta = jnp.sum(probs * grad_probs, axis=-1, keepdims=True)
    grad_scores = (probs * (grad_probs - delta)).astype(jnp.bfloat16)
    grad_queries = (
        jnp.einsum("shqk,skhe->sqhe", grad_scores, all_keys, preferred_element_type=jnp.float32)
        * scale
    )
    all_queries, all_grad_mixed = (
        lax.all_gather(queries, "ctx", axis=1, tiled=True),
        lax.all_gather(grad_mixed, "ctx", axis=1, tiled=True),
    )
    stat_lse = jnp.transpose(log_total[..., 0], (0, 2, 1))
    stat_delta = jnp.transpose(delta[..., 0], (0, 2, 1))
    lse_all, delta_all = (
        lax.all_gather(stat_lse, "ctx", axis=1, tiled=True),
        lax.all_gather(stat_delta, "ctx", axis=1, tiled=True),
    )
    lse_all = jnp.transpose(lse_all, (0, 2, 1))[..., None]
    delta_all = jnp.transpose(delta_all, (0, 2, 1))[..., None]
    key_allowed = (local_pos[None, :] <= key_pos[:, None])[None] | (
        local_pos[None, None, :] < prefix[:, None, None]
    )
    block_scores = (
        jnp.einsum("sqhe,skhe->shqk", all_queries, key_rows, preferred_element_type=jnp.float32)
        * scale
    )
    block_scores = jnp.where(key_allowed[:, None], block_scores, -1e30)
    block_probs = jnp.exp(block_scores - lse_all)
    block_grad_probs = jnp.einsum(
        "sqhe,skhe->shqk", all_grad_mixed, value_rows, preferred_element_type=jnp.float32
    )
    block_grad_scores = (block_probs * (block_grad_probs - delta_all)).astype(jnp.bfloat16)
    own_keys = (
        jnp.einsum(
            "shqk,sqhe->skhe", block_grad_scores, all_queries, preferred_element_type=jnp.float32
        )
        * scale
    )
    own_values = jnp.einsum(
        "shqk,sqhe->skhe",
        block_probs.astype(jnp.bfloat16),
        all_grad_mixed,
        preferred_element_type=jnp.float32,
    )
    grad_joined = jnp.concatenate(
        [
            rotate(grad_queries, cos_table, -sin_table).reshape(rows, width),
            rotate(own_keys, cos_table, -sin_table).reshape(rows, width),
            own_values.reshape(rows, width),
        ],
        axis=1,
    ).astype(jnp.bfloat16)
    grad_joined_shift = jnp.sum(grad_joined.astype(jnp.float32), axis=0)
    grad_hidden_attn = contract_cols(grad_joined, qkv_back)
    unused_attn, attn_back = jax.vjp(norm_rows, inputs, gain_attn, shift_attn)
    grad_in_attn, grad_gain_attn, grad_shift_attn = attn_back(grad_hidden_attn)
    attn_columns = jnp.concatenate(
        [
            grad_gain_attn[:, None],
            grad_shift_attn[:, None],
            grad_joined_shift[: 2 * width].reshape(width, 2),
            grad_joined_shift[2 * width :][:, None],
            grad_out_shift[:, None],
        ],
        axis=1,
    )
    hidden_part = hidden_attn
    small_part = attn_columns
    attn_grads = lax.psum_scatter(
        jnp.concatenate(
            [contract_rows(hidden_part, grad_joined), contract_rows(mixed, cot_rows), small_part],
            axis=1,
        ),
        ("dp", "ctx"),
        scatter_dimension=0,
        tiled=True,
    )
    qkv_grad = attn_grads[:, : 3 * width]
    dense_grad = attn_grads[:, 3 * width : 4 * width]
    attn_tail = attn_grads[:, 4 * width :]
    mlp_back_set = fetch_mlp()
    expand_back, shrink_back, mlp_small_back = mlp_back_set
    gain_mlp, shift_mlp, expand_shift, shrink_shift = unpack_small(
        mlp_small_back, mlp_lengths, devices
    )
    unused_gelu, gelu_back = jax.vjp(gelu_exact, expanded)
    grad_act = contract_cols(cot_rows, shrink_back)
    grad_expanded = gelu_back(grad_act)[0].astype(jnp.bfloat16)
    grad_expand_shift = jnp.sum(grad_expanded.astype(jnp.float32), axis=0)
    grad_hidden_mlp = contract_cols(grad_expanded, expand_back)
    unused_mlp, mlp_back = jax.vjp(norm_rows, inputs, gain_mlp, shift_mlp)
    grad_in_mlp, grad_gain_mlp, grad_shift_mlp = mlp_back(grad_hidden_mlp)
    ratio = expand_shift.shape[0] // width
    mlp_columns = jnp.concatenate(
        [
            grad_gain_mlp[:, None],
            grad_shift_mlp[:, None],
            grad_expand_shift.reshape(width, ratio),
            grad_out_shift[:, None],
        ],
        axis=1,
    )
    ff_width = expand_back.shape[1]
    hidden_part = hidden_mlp
    small_part = mlp_columns
    expand_grads = lax.psum_scatter(
        jnp.concatenate([contract_rows(hidden_part, grad_expanded), small_part], axis=1),
        ("dp", "ctx"),
        scatter_dimension=0,
        tiled=True,
    )
    shrink_grad = lax.psum_scatter(
        contract_rows(activated, cot_rows), ("dp", "ctx"), scatter_dimension=0, tiled=True
    )
    expand_grad = expand_grads[:, :ff_width]
    mlp_tail = expand_grads[:, ff_width:]
    input_grad = (
        (cot_float + grad_in_attn + grad_in_mlp)
        .astype(jnp.bfloat16)
        .reshape(micro, seq_count, span, width)
    )
    return (
        layer_output,
        input_grad,
        qkv_grad,
        attn_tail[:, 2:4].reshape(-1),
        attn_tail[:, 4],
        dense_grad,
        attn_tail[:, 5],
        expand_grad,
        mlp_tail[:, 2 : 2 + ratio].reshape(-1),
        shrink_grad,
        mlp_tail[:, 2 + ratio],
        attn_tail[:, 0],
        attn_tail[:, 1],
        mlp_tail[:, 0],
        mlp_tail[:, 1],
    )


def low(values):
    return values.astype(jnp.bfloat16)


MESH_ID = pl.DeviceIdType.MESH


def remote(src, dst, send_sem, recv_sem, dp, ctx):
    return pltpu.make_async_remote_copy(
        src_ref=src,
        dst_ref=dst,
        send_sem=send_sem,
        recv_sem=recv_sem,
        device_id=(dp, ctx),
        device_id_type=MESH_ID,
    )


def greet_all(dp, ctx, dp_size, ctx_size):
    barrier = pltpu.get_barrier_semaphore()
    devices = dp_size * ctx_size
    me = dp * ctx_size + ctx

    def greet(step, carry):
        other = lax.rem(me + step, devices)
        pl.semaphore_signal(
            barrier, inc=1, device_id=(other // ctx_size, lax.rem(other, ctx_size)), device_id_type=MESH_ID
        )
        return carry

    lax.fori_loop(1, devices, greet, 0)
    pl.semaphore_wait(barrier, devices - 1)


def chain_gather(src, dst, sems, d, c, levels):
    block_send, block_recv, core_send, core_recv, local = sems
    micro, span = src.shape[0], src.shape[1]
    z = c // 2
    sibling = c + 1 - 2 * lax.rem(c, 2)

    def block(origin, m):
        return dst.at[m, pl.ds(pl.multiple_of(origin * span, span), span)]

    def link(way, hop, m):
        step = 2 if way == 0 else -2
        origin = c - step * hop
        view = src.at[m] if hop == 0 else block(origin, m)
        return remote(view, block(origin, m), block_send.at[way, hop, m], block_recv.at[way, hop, m], d, c + step)

    def leaves(way, hop):
        if way == 0:
            return jnp.logical_and(z >= hop, z <= levels - 2)
        return jnp.logical_and(z + hop <= levels - 1, z >= 1)

    def arrives(way, hop):
        return z >= hop + 1 if way == 0 else z + hop + 1 <= levels - 1

    def slot_of(way, hop):
        return 1 + way * (levels - 1) + hop

    def core_copy(slot, origin, m):
        view = src.at[m] if slot == 0 else block(origin, m)
        return remote(view, block(origin, m), core_send.at[slot, m], core_recv.at[slot, m], d, sibling)

    def own_copy(m):
        return pltpu.make_async_copy(src.at[m], block(c, m), local.at[m])

    def start(m):
        for way in range(2):
            @pl.when(leaves(way, 0))
            def _(way=way):
                link(way, 0, m).start()

        core_copy(0, c, m).start()
        own_copy(m).start()

    def hop_step(hop, m):
        for way in range(2):
            step = 2 if way == 0 else -2

            @pl.when(arrives(way, hop))
            def _(way=way, step=step):
                link(way, hop, m).wait_recv()
                if hop + 1 <= levels - 2:
                    @pl.when(leaves(way, hop + 1))
                    def _():
                        link(way, hop + 1, m).start()

                core_copy(slot_of(way, hop), c - step * (hop + 1), m).start()

    def finish(m):
        own_copy(m).wait()
        core_copy(0, c, m).wait_send()
        core_copy(0, sibling, m).wait_recv()
        for way in range(2):
            step = 2 if way == 0 else -2
            for hop in range(levels - 1):
                @pl.when(leaves(way, hop))
                def _(way=way, hop=hop):
                    link(way, hop, m).wait_send()

                @pl.when(arrives(way, hop))
                def _(way=way, hop=hop, step=step):
                    slot = slot_of(way, hop)
                    core_copy(slot, c - step * (hop + 1), m).wait_send()
                    core_copy(slot, sibling - step * (hop + 1), m).wait_recv()

    return start, hop_step, finish


def chain_scratch(levels, micro):
    dma = pltpu.SemaphoreType.DMA
    return [
        dma((2, levels - 1, micro)),
        dma((2, levels - 1, micro)),
        dma((2 * levels - 1, micro)),
        dma((2 * levels - 1, micro)),
        dma((micro,)),
    ]


def greet_line(d, c, levels):
    barrier = pltpu.get_barrier_semaphore()
    z = c // 2
    sibling = c + 1 - 2 * lax.rem(c, 2)
    pl.semaphore_signal(barrier, inc=1, device_id=(d, sibling), device_id_type=MESH_ID)

    @pl.when(z >= 1)
    def _():
        pl.semaphore_signal(barrier, inc=1, device_id=(d, c - 2), device_id_type=MESH_ID)

    @pl.when(z <= levels - 2)
    def _():
        pl.semaphore_signal(barrier, inc=1, device_id=(d, c + 2), device_id_type=MESH_ID)

    peers = 1 + (z >= 1).astype(jnp.int32) + (z <= levels - 2).astype(jnp.int32)
    pl.semaphore_wait(barrier, peers)


def gather_kernel(
    dp_size,
    ctx_size,
    x,
    qkv,
    expand,
    dense,
    shrink,
    packed,
    x_all,
    panels,
    out_w,
    small,
    local_sem,
    small_sem,
    block_send,
    block_recv,
    core_send,
    core_recv,
    block_local,
    panel_send,
    panel_recv,
    share_send,
    share_recv,
    pass_send,
    pass_recv,
):
    d = lax.axis_index("dp")
    c = lax.axis_index("ctx")
    z = c // 2
    sibling = c + 1 - 2 * lax.rem(c, 2)
    x_mate = d + 1 - 2 * lax.rem(d, 2)
    y_mate = lax.rem(d + 2, 4)
    micro, span = x.shape[0], x.shape[1]
    devices = dp_size * ctx_size
    me = d * ctx_size + c
    rows = qkv.shape[0]
    unit = shrink.shape[0]
    levels = ctx_size // 2
    panel_rows = ctx_size * rows
    n_panels = 3 + dp_size

    greet_all(d, c, dp_size, ctx_size)

    def column_block(panel, target):
        if panel < 3:
            start = panel * (qkv.shape[1] // 3) + target * HEAD
            return qkv.at[:, pl.ds(pl.multiple_of(start, HEAD), HEAD)]
        start = (panel - 3) * ctx_size * unit + target * unit
        return expand.at[:, pl.ds(pl.multiple_of(start, HEAD), HEAD)]

    own_rows = pl.ds(pl.multiple_of((d * ctx_size + c) * rows, rows), rows)

    for panel in range(n_panels):
        pltpu.make_async_copy(
            column_block(panel, c), panels.at[panel, own_rows], local_sem.at[panel]
        ).start()

        def push(step, carry, panel=panel):
            target = lax.rem(c + step, ctx_size)
            remote(
                column_block(panel, target),
                panels.at[panel, own_rows],
                panel_send.at[panel],
                panel_recv.at[panel],
                d,
                target,
            ).start()
            return carry

        lax.fori_loop(1, ctx_size, push, 0)

    def shrink_rows(owner, offset, count):
        return out_w.at[pl.ds(pl.multiple_of(HEAD + owner * unit + offset, 16), count)]

    shrink_local = pltpu.make_async_copy(shrink, shrink_rows(d, 0, unit), local_sem.at[n_panels])
    shrink_local.start()
    for way, mate in ((0, x_mate), (1, y_mate)):
        remote(
            shrink, shrink_rows(d, 0, unit), share_send.at[n_panels, way], share_recv.at[n_panels, way], mate, c
        ).start()

    per_head = HEAD // rows
    head_of = (d * ctx_size + c) // per_head
    dense_rows = pl.ds(pl.multiple_of(lax.rem(c, per_head) * rows, rows), rows)
    dense_out = remote(dense, out_w.at[dense_rows], panel_send.at[n_panels], panel_recv.at[n_panels], d, head_of)
    dense_own = pltpu.make_async_copy(dense, out_w.at[dense_rows], local_sem.at[n_panels + 1])
    stays = head_of == c

    @pl.when(stays)
    def _():
        dense_own.start()

    @pl.when(jnp.logical_not(stays))
    def _():
        dense_out.start()

    x_start, x_hop, x_finish = chain_gather(
        x, x_all, (block_send, block_recv, core_send, core_recv, block_local), d, c, levels
    )
    for m in range(micro):
        x_start(m)

    small_copy = pltpu.make_async_copy(packed, small.at[me], local_sem.at[n_panels + 2])
    small_copy.start()

    def push_small(step, carry):
        other = lax.rem(me + step, devices)
        remote(
            packed,
            small.at[me],
            small_sem.at[0],
            small_sem.at[1],
            other // ctx_size,
            lax.rem(other, ctx_size),
        ).start()
        return carry

    lax.fori_loop(1, devices, push_small, 0)

    def group_rows(owner, offset, count):
        return pl.ds(pl.multiple_of(owner * panel_rows + offset, 16), count)

    def panel_share(panel, way, mate):
        view = panels.at[panel, group_rows(d, 0, panel_rows)]
        return remote(view, view, share_send.at[panel, way], share_recv.at[panel, way], mate, c)

    def panel_step(panel):
        pltpu.make_async_copy(column_block(panel, c), panels.at[panel, own_rows], local_sem.at[panel]).wait()
        whole = panels.at[panel, group_rows(d, 0, (ctx_size - 1) * rows)]
        remote(whole, whole, panel_send.at[panel], panel_recv.at[panel], d, sibling).wait_recv()
        panel_share(panel, 0, x_mate).start()
        panel_share(panel, 1, y_mate).start()

    half = panel_rows // 2

    def panel_pass(panel, way):
        owner, mate = ((x_mate, y_mate), (y_mate, x_mate))[way]
        view = panels.at[panel, group_rows(owner, way * half, half)]
        return remote(view, view, pass_send.at[panel, way], pass_recv.at[panel, way], mate, c)

    def panel_forward(panel):
        for way, owner in ((0, x_mate), (1, y_mate)):
            view = panels.at[panel, group_rows(owner, 0, panel_rows)]
            remote(view, view, share_send.at[panel, way], share_recv.at[panel, way], owner, c).wait_recv()
            panel_pass(panel, way).start()

    def shrink_share_wait(way, owner):
        view = shrink_rows(owner, 0, unit)
        remote(view, view, share_send.at[n_panels, way], share_recv.at[n_panels, way], owner, c).wait_recv()

    def shrink_pass(way):
        owner, mate = ((x_mate, y_mate), (y_mate, x_mate))[way]
        view = shrink_rows(owner, way * (unit // 2), unit // 2)
        return remote(view, view, pass_send.at[n_panels, way], pass_recv.at[n_panels, way], mate, c)

    source = c // (ctx_size // dp_size)
    at_source = d == source
    from_x = x_mate == source
    from_y = y_mate == source
    head_rows = out_w.at[pl.ds(0, HEAD)]
    half_head = HEAD // 2

    def dense_share(way, mate):
        view = out_w.at[pl.ds(way * half_head, half_head)]
        return remote(view, view, share_send.at[n_panels + 1, way], share_recv.at[n_panels + 1, way], mate, c)

    owns_share = jnp.logical_and(at_source, stays)

    def dense_gather_step():
        @pl.when(owns_share)
        def _():
            dense_own.wait()
            view = out_w.at[pl.ds(0, (per_head - 1) * rows)]
            remote(view, view, panel_send.at[n_panels], panel_recv.at[n_panels], d, sibling).wait_recv()

        @pl.when(jnp.logical_and(at_source, jnp.logical_not(stays)))
        def _():
            remote(head_rows, head_rows, panel_send.at[n_panels], panel_recv.at[n_panels], d, sibling).wait_recv()

        @pl.when(at_source)
        def _():
            dense_share(0, x_mate).start()
            dense_share(1, y_mate).start()

    def dense_forward_step():
        @pl.when(from_x)
        def _():
            dense_share(0, x_mate).wait_recv()
            dense_share(0, y_mate).start()

        @pl.when(from_y)
        def _():
            dense_share(1, y_mate).wait_recv()
            dense_share(1, x_mate).start()

    def dense_last_step():
        @pl.when(across)
        def _():
            dense_share(0, y_mate).wait_recv()
            dense_share(0, x_mate).start()
            dense_share(1, x_mate).wait_recv()
            dense_share(1, y_mate).start()

    across = jnp.logical_not(jnp.logical_or(at_source, jnp.logical_or(from_x, from_y)))

    for panel in range(3):
        panel_step(panel)
    shrink_share_wait(0, x_mate)
    shrink_pass(0).start()
    shrink_share_wait(1, y_mate)
    shrink_pass(1).start()
    for panel in range(3, n_panels):
        panel_step(panel)
    dense_gather_step()
    panel_forward(0)
    panel_forward(1)
    x_hop(0, 0)
    panel_forward(2)
    x_hop(0, 1)
    dense_forward_step()
    panel_forward(3)
    panel_forward(4)
    x_hop(1, 0)
    panel_forward(5)
    x_hop(1, 1)
    dense_last_step()
    panel_forward(6)
    for hop in range(2, levels - 1):
        for m in range(micro):
            x_hop(hop, m)

    for panel in range(n_panels):
        for way, mate in ((0, x_mate), (1, y_mate)):
            panel_share(panel, way, mate).wait_send()
            panel_pass(panel, way).wait_send()
        for way in range(2):
            diagonal = 3 - d
            view = panels.at[panel, group_rows(diagonal, way * half, half)]
            remote(view, view, pass_send.at[panel, way], pass_recv.at[panel, way], x_mate, c).wait_recv()
        whole = panels.at[panel, group_rows(d, 0, (ctx_size - 1) * rows)]
        remote(whole, whole, panel_send.at[panel], panel_recv.at[panel], x_mate, c).wait_send()
    shrink_local.wait()
    for way in range(2):
        mate = (x_mate, y_mate)[way]
        remote(
            shrink, shrink_rows(d, 0, unit), share_send.at[n_panels, way], share_recv.at[n_panels, way], mate, c
        ).wait_send()
        shrink_pass(way).wait_send()
        view = shrink_rows(3 - d, way * (unit // 2), unit // 2)
        remote(view, view, pass_send.at[n_panels, way], pass_recv.at[n_panels, way], mate, c).wait_recv()

    @pl.when(jnp.logical_not(stays))
    def _():
        dense_out.wait_send()

    @pl.when(at_source)
    def _():
        dense_share(0, x_mate).wait_send()
        dense_share(1, y_mate).wait_send()

    @pl.when(from_x)
    def _():
        dense_share(0, y_mate).wait_send()
        dense_share(1, y_mate).wait_recv()

    @pl.when(from_y)
    def _():
        dense_share(1, x_mate).wait_send()
        dense_share(0, x_mate).wait_recv()

    @pl.when(across)
    def _():
        dense_share(0, x_mate).wait_send()
        dense_share(1, y_mate).wait_send()

    for m in range(micro):
        x_finish(m)

    small_copy.wait()
    rest = small.at[pl.ds(0, devices - 1)]
    remote(rest, rest, small_sem.at[0], small_sem.at[1], d, sibling).wait()


def gather_call(dp_size, ctx_size, x, qkv, expand, dense, shrink, packed):
    micro, span, width = x.shape
    rows = qkv.shape[0]
    n_panels = 3 + dp_size
    levels = ctx_size // 2
    devices = dp_size * ctx_size
    dma = pltpu.SemaphoreType.DMA
    out_shape = (
        jax.ShapeDtypeStruct((micro, ctx_size * span, width), x.dtype),
        jax.ShapeDtypeStruct((n_panels, devices * rows, HEAD), x.dtype),
        jax.ShapeDtypeStruct((HEAD + dp_size * shrink.shape[0], width), x.dtype),
        jax.ShapeDtypeStruct((devices,) + packed.shape, x.dtype),
    )
    anywhere = pl.BlockSpec(memory_space=pl.ANY)
    return pl.pallas_call(
        functools.partial(gather_kernel, dp_size, ctx_size),
        out_shape=out_shape,
        in_specs=[anywhere] * 6,
        out_specs=(anywhere,) * 4,
        scratch_shapes=[
            dma((n_panels + 3,)),
            dma((2,)),
            *chain_scratch(levels, micro),
            dma((n_panels + 1,)),
            dma((n_panels + 1,)),
            dma((n_panels + 2, 2)),
            dma((n_panels + 2, 2)),
            dma((n_panels + 2, 2)),
            dma((n_panels + 2, 2)),
        ],
        compiler_params=pltpu.CompilerParams(collective_id=1, has_side_effects=True),
        name="gather_all",
    )(x, qkv, expand, dense, shrink, packed)


def add_into(dst, srcs, rows):
    chunk = 16 if dst.shape[-1] > 1024 else 64

    def step(index, carry):
        at = pl.ds(pl.multiple_of(index * chunk, 16), chunk)
        total = srcs[0][at, :].astype(jnp.float32)
        for src in srcs[1:]:
            total = total + src[at, :].astype(jnp.float32)
        dst[at, :] = total.astype(dst.dtype)
        return carry

    lax.fori_loop(0, rows // chunk, step, 0)


TILE = 256


def turn_tables(length):
    freqs = np.exp(np.arange(ROT // 2) * (-2.0 * math.log(10000.0) / ROT))
    angles = np.arange(length)[:, None] * freqs[None, :]
    cos, sin = np.cos(angles), np.sin(angles)
    rest = np.zeros((length, 128 - ROT))
    return (
        jnp.asarray(np.concatenate([cos, cos, rest + 1.0], axis=1), jnp.float32),
        jnp.asarray(np.concatenate([-sin, sin, rest], axis=1), jnp.float32),
    )


def turn(head, cos, sin):
    front = head[:, :128]
    lane = lax.broadcasted_iota(jnp.int32, front.shape, 1)
    other = jnp.where(lane < ROT // 2, pltpu.roll(front, 128 - ROT // 2, 1), pltpu.roll(front, ROT // 2, 1))
    return jnp.concatenate([front * cos + other * sin, head[:, 128:]], axis=1)


def dot_nn(a, b):
    return lax.dot_general(a, b, (((1,), (0,)), ((), ())), preferred_element_type=jnp.float32)


def dot_nt(a, b):
    return lax.dot_general(a, b, (((1,), (1,)), ((), ())), preferred_element_type=jnp.float32)


def dot_tn(a, b):
    return lax.dot_general(a, b, (((0,), (0,)), ((), ())), preferred_element_type=jnp.float32)


def forward_kernel(
    tiles,
    levels,
    prefix,
    x,
    own_g,
    panels,
    out_w,
    gains,
    qkv_shift,
    expand_shift,
    cos,
    sin,
    hidden_attn,
    hidden_mlp,
    heads,
    probs,
    features,
    slopes,
    partial,
    g_all,
    first_out,
    head_rows,
    acts,
    board,
    out_core,
    out_chain,
    core_send,
    core_recv,
    chain_send,
    chain_recv,
    store_sem,
    *g_sems,
):
    step = pl.program_id(0)
    micro = own_g.shape[0]
    d = lax.axis_index("dp")
    c = lax.axis_index("ctx")
    g_start, g_hop, g_finish = chain_gather(own_g, g_all, g_sems, d, c, levels)

    core = lax.rem(c, 2)
    span = board.shape[2]

    def own_block(level):
        return board.at[level, core]

    def core_copy(level):
        return remote(
            board.at[level, 1 - core],
            out_core.at[level],
            core_send.at[level],
            core_recv.at[level],
            d,
            c + 1 - 2 * core,
        )

    chain_open, chain_round, chain_end, chain_finish = chain_reduce(
        own_block, out_chain, (chain_send, chain_recv), d, c, levels
    )

    def out_store(level):
        return pltpu.make_async_copy(own_block(level), first_out, store_sem.at[0])

    @pl.when(step == 0)
    def _():
        greet_line(d, c, levels)
        for m in range(micro):
            g_start(m)

    for place, level in enumerate(outside_in(levels)):
        @pl.when(step == tiles + 1 + place)
        def _(level=level):
            core_copy(level).start()

        @pl.when(step == tiles + 2 + place)
        def _(level=level):
            core_copy(level).wait_recv()
            add_into(own_block(level), (own_block(level), out_core.at[level]), span)
            chain_open(level)

    @pl.when(step == 12)
    def _():
        chain_round(1)

    last = 4 * tiles - 1
    for at, hop, m in ((4, 0, 0), (7, 0, 1), (11, 1, 0), (14, 1, 1)):
        @pl.when(step == at)
        def _(hop=hop, m=m):
            g_hop(hop, m)

    seq = step // (2 * tiles)
    phase = lax.rem(step, 2 * tiles) // tiles
    tile = lax.rem(step, tiles)
    tile = jnp.where(phase == 0, tile, jnp.where(lax.rem(tile, 2) == 0, tiles - 1 - tile // 2, tile // 2))
    rows = pl.ds(pl.multiple_of(tile * TILE, TILE), TILE)
    n_expand = panels.shape[0] - 3
    scale = 1.0 / math.sqrt(HEAD)

    @pl.when(phase == 0)
    def _():
        values_in = x[...].astype(jnp.float32)
        centered = values_in - jnp.mean(values_in, axis=1, keepdims=True)
        normal = centered * lax.rsqrt(jnp.mean(centered * centered, axis=1, keepdims=True) + 1e-05)
        hidden_attn[...] = (normal * gains[0:1, :] + gains[1:2, :]).astype(jnp.bfloat16)
        hidden_mlp[...] = (normal * gains[2:3, :] + gains[3:4, :]).astype(jnp.bfloat16)
        wide = jnp.concatenate([panels[part] for part in range(3)], axis=1)
        all_joined = dot_nn(hidden_attn[...], wide) + qkv_shift[...]
        for part in range(3):
            joined = all_joined[:, part * HEAD : (part + 1) * HEAD]
            if part < 2:
                joined = turn(joined, cos[rows, :], sin[rows, :])
            joined = joined.astype(jnp.bfloat16)
            heads[part] = joined
            head_rows[part, rows, :] = joined
        for part in range(0, n_expand, 2):
            columns = slice(part * HEAD, (part + 2) * HEAD)
            wide = jnp.concatenate([panels[3 + part], panels[4 + part]], axis=1)
            expanded = dot_nn(hidden_mlp[...], wide) + expand_shift[:, columns]
            cdf = 0.5 * (1.0 + lax.erf(expanded * (1.0 / math.sqrt(2.0))))
            acts[rows, columns] = (expanded * cdf).astype(jnp.bfloat16)
            bell = jnp.exp(-0.5 * expanded * expanded) * (1.0 / math.sqrt(2.0 * math.pi))
            slopes[:, columns] = (cdf + expanded * bell).astype(jnp.bfloat16)

    @pl.when(phase == 1)
    def _():
        scores = dot_nt(head_rows[0, rows, :], head_rows[1]) * scale
        key_at = lax.broadcasted_iota(jnp.int32, scores.shape, 1)
        query_at = lax.broadcasted_iota(jnp.int32, scores.shape, 0) + tile * TILE
        allowed = jnp.logical_or(key_at <= query_at, key_at < prefix[seq])
        scores = jnp.where(allowed, scores, -1e30)
        expo = jnp.exp(scores - jnp.max(scores, axis=1, keepdims=True))
        low_probs = (expo * (1.0 / jnp.sum(expo, axis=1, keepdims=True))).astype(jnp.bfloat16)
        probs[0] = low_probs
        features[:, :HEAD] = dot_nn(low_probs, head_rows[2]).astype(jnp.bfloat16)
        features[:, HEAD:] = acts[rows, :]
        width = out_w.shape[1]
        for start in range(0, width, 1024):
            columns = slice(start, start + 1024)
            value = dot_nn(features[...], out_w[:, columns]).astype(jnp.bfloat16)

            @pl.when(seq == 0)
            def _(columns=columns, value=value):
                for parity in range(2):
                    board[tile, parity, :, columns] = value[parity * span : (parity + 1) * span]

            @pl.when(seq > 0)
            def _(columns=columns, value=value):
                partial[:, columns] = value

    @pl.when(step == last)
    def _():
        chain_round(2)
        for m in range(micro):
            for hop in range(2, levels - 1):
                g_hop(hop, m)
        chain_end(out_store)
        for m in range(micro):
            g_finish(m)
        for level in range(levels):
            core_copy(level).wait_send()
        chain_finish(out_store)


def whole_spec(array):
    zeros = (0,) * array.ndim
    return pl.BlockSpec(array.shape, lambda step: zeros, pipeline_mode=pl.Buffered(1))


def forward_call(levels, prefix, x, own_g, panels, out_w, gains, qkv_shift, expand_shift, cos, sin):
    tokens, width = x.shape
    length = cos.shape[0]
    tiles = length // TILE
    steps = 2 * tokens // TILE
    hidden = expand_shift.shape[1]
    span = own_g.shape[1]
    dma = pltpu.SemaphoreType.DMA

    def early(step):
        seq, at = step // (2 * tiles), lax.rem(step, 2 * tiles)
        return seq * tiles + jnp.minimum(at, tiles - 1)

    def late(step):
        seq, at = step // (2 * tiles), lax.rem(step, 2 * tiles)
        place = jnp.maximum(at - tiles, 0)
        return seq * tiles + jnp.where(lax.rem(place, 2) == 0, tiles - 1 - place // 2, place // 2)

    def last_only(step):
        return jnp.where(step < 2 * tiles, tiles - 1, late(step) - tiles)

    kind = jnp.bfloat16
    return pl.pallas_call(
        functools.partial(forward_kernel, tiles, levels),
        grid=(steps,),
        out_shape=(
            jax.ShapeDtypeStruct((tokens, width), kind),
            jax.ShapeDtypeStruct((tokens, width), kind),
            jax.ShapeDtypeStruct((3, tokens, HEAD), kind),
            jax.ShapeDtypeStruct((tokens // length, length, length), kind),
            jax.ShapeDtypeStruct((tokens, HEAD + hidden), kind),
            jax.ShapeDtypeStruct((tokens, hidden), kind),
            jax.ShapeDtypeStruct((length, width), kind),
            jax.ShapeDtypeStruct((tokens // length, length, width), kind),
            jax.ShapeDtypeStruct((span, width), kind),
        ),
        in_specs=[
            pl.BlockSpec(memory_space=pltpu.SMEM),
            pl.BlockSpec((TILE, width), lambda step: (early(step), 0)),
            pl.BlockSpec(memory_space=pl.ANY),
            whole_spec(panels),
            whole_spec(out_w),
            whole_spec(gains),
            whole_spec(qkv_shift),
            whole_spec(expand_shift),
            whole_spec(cos),
            whole_spec(sin),
        ],
        out_specs=(
            pl.BlockSpec((TILE, width), lambda step: (early(step), 0)),
            pl.BlockSpec((TILE, width), lambda step: (early(step), 0)),
            pl.BlockSpec((3, TILE, HEAD), lambda step: (0, early(step), 0)),
            pl.BlockSpec((1, TILE, length), lambda step: (late(step) // tiles, lax.rem(late(step), tiles), 0)),
            pl.BlockSpec((TILE, HEAD + hidden), lambda step: (late(step), 0)),
            pl.BlockSpec((TILE, hidden), lambda step: (early(step), 0)),
            pl.BlockSpec((TILE, width), lambda step: (last_only(step), 0)),
            pl.BlockSpec(memory_space=pl.ANY),
            pl.BlockSpec(memory_space=pl.ANY),
        ),
        scratch_shapes=[
            pltpu.VMEM((3, length, HEAD), kind),
            pltpu.VMEM((length, hidden), kind),
            pltpu.VMEM((levels, 2, span, width), kind),
            pltpu.VMEM((levels, span, width), kind),
            pltpu.VMEM((2, levels - 1, span, width), kind),
            dma((levels,)),
            dma((levels,)),
            dma((2, levels)),
            dma((2, levels)),
            dma((1,)),
            *chain_scratch(levels, tokens // length),
        ],
        compiler_params=pltpu.CompilerParams(
            collective_id=3, has_side_effects=True, vmem_limit_bytes=60 * 1024 * 1024
        ),
        cost_estimate=pl.CostEstimate(
            flops=2 * tokens * width * (2 * hidden + 4 * HEAD) + 4 * tokens * length * HEAD,
            bytes_accessed=64 * 1024 * 1024,
            transcendentals=0,
        ),
        name="forward_part",
    )(prefix, x, own_g, panels, out_w, gains, qkv_shift, expand_shift, cos, sin)


def outside_in(levels):
    return [levels - 1 - place // 2 if place % 2 == 0 else place // 2 for place in range(levels)]


def chain_reduce(own, recv, sems, d, c, levels):
    chain_send, chain_recv = sems
    z = c // 2
    span = recv.shape[2]

    def copy(way, level):
        return remote(
            own(level),
            recv.at[way, level - 1 + way],
            chain_send.at[way, level],
            chain_recv.at[way, level],
            d,
            c + (2 if way == 0 else -2),
        )

    def sends(way, level):
        return z < level if way == 0 else z > level

    def hears(way, level):
        if way == 0:
            return jnp.logical_and(z >= 1, z <= level)
        return jnp.logical_and(z <= levels - 2, z >= level)

    def add(way, level):
        copy(way, level).wait_recv()
        add_into(own(level), (own(level), recv.at[way, level - 1 + way]), span)

    def open_level(level):
        for way, place in ((0, 0), (1, levels - 1)):
            if place != level:
                @pl.when(z == place)
                def _(way=way):
                    copy(way, level).start()

    def turn_round(index):
        for level in range(levels):
            for way in range(2):
                behind = levels - 1 - level if way == 0 else level
                place = index - behind if way == 0 else levels - 1 - (index - behind)
                if behind < index and (place < level if way == 0 else place > level):
                    @pl.when(z == place)
                    def _(way=way, level=level):
                        add(way, level)
                        copy(way, level).start()

    def end(store):
        for level in range(levels):
            for way in range(2):
                if 0 <= level - 1 + way < levels - 1:
                    @pl.when(jnp.logical_and(z == level, hears(way, level)))
                    def _(way=way, level=level):
                        add(way, level)

            @pl.when(z == level)
            def _(level=level):
                store(level).start()

    def finish(store):
        for level in range(levels):
            for way in range(2):
                if 0 <= level - 1 + way < levels - 1:
                    @pl.when(sends(way, level))
                    def _(way=way, level=level):
                        copy(way, level).wait_send()

        store(0).wait()

    return open_level, turn_round, end, finish


def square_sum(first, passing, recv, last, final, sems, d, c, count):
    first_send, first_recv, last_send, last_recv = sems
    x_mate = d + 1 - 2 * lax.rem(d, 2)
    y_mate = lax.rem(d + 2, 4)
    mates = ((x_mate, y_mate), (y_mate, x_mate))

    def first_copy(way, slot):
        return remote(
            first(way, slot), recv.at[way, slot], first_send.at[way, slot], first_recv.at[way, slot], mates[way][0], c
        )

    def last_copy(way):
        return remote(passing(way), last.at[way], last_send.at[way], last_recv.at[way], mates[way][1], c)

    def pass_on(way):
        first_copy(way, 1).wait_recv()
        add_into(passing(way), (passing(way), recv.at[way, 1]), count)
        last_copy(way).start()

    def arrive(way):
        first_copy(way, 0).wait_recv()
        last_copy(way).wait_recv()

    def add_final(way, start, rows):
        at = pl.ds(start, rows)
        own = final(way).at[at]
        add_into(own, (own, recv.at[way, 0, at], last.at[way, at]), rows)

    def finish():
        for way in range(2):
            first_copy(way, 0).wait_send()
            first_copy(way, 1).wait_send()
            last_copy(way).wait_send()

    return first_copy, pass_on, arrive, add_final, finish


def square_scratch():
    dma = pltpu.SemaphoreType.DMA
    return [dma((2, 2)), dma((2, 2)), dma((2,)), dma((2,))]


def backward_kernel(
    tiles,
    dp_size,
    ctx_size,
    g,
    x,
    panels,
    out_w,
    gains,
    cos,
    sin,
    heads,
    probs,
    slopes,
    features,
    grads,
    grad_expanded,
    grad_joined,
    combined,
    norm_sums,
    joined_sums,
    expand_sums,
    back_out,
    shrink_out,
    dense_out,
    grad_queries,
    grad_keys,
    grad_values,
    board,
    back_core,
    back_chain,
    left,
    right,
    out_own,
    out_recv,
    out_last,
    dense_own,
    dense_recv,
    left_sem,
    right_sem,
    core_send,
    core_recv,
    chain_send,
    chain_recv,
    first_send,
    first_recv,
    last_send,
    last_recv,
    dense_send,
    dense_sem,
    store_sem,
):
    step = pl.program_id(0)
    seq = step // (2 * tiles)
    phase = lax.rem(step, 2 * tiles) // tiles
    tile = lax.rem(step, tiles)
    tile = jnp.where(phase == 0, tile, jnp.where(lax.rem(tile, 2) == 0, tiles - 1 - tile // 2, tile // 2))
    rows = pl.ds(pl.multiple_of(tile * TILE, TILE), TILE)
    n_expand = panels.shape[0] - 3
    width = out_w.shape[1]
    scale = 1.0 / math.sqrt(HEAD)

    d = lax.axis_index("dp")
    c = lax.axis_index("ctx")
    z = c // 2
    core = lax.rem(c, 2)
    sibling = c + 1 - 2 * core
    x_mate = d + 1 - 2 * lax.rem(d, 2)
    y_mate = lax.rem(d + 2, 4)
    diagonal = 3 - d
    levels = ctx_size // 2
    me = d * ctx_size + c
    span = board.shape[2]
    share = dense_out.shape[0]
    unit = (features.shape[1] - HEAD) // dp_size
    out_half = unit // 2
    head_half = HEAD // 2

    def left_copy(index):
        if index == 0:
            columns = pl.ds(0, HEAD)
        else:
            owner = (diagonal, x_mate, y_mate, d)[index - 1]
            columns = pl.ds(pl.multiple_of(HEAD + owner * unit, HEAD), unit)
        return pltpu.make_async_copy(features.at[:, columns], left.at[index % 2], left_sem.at[index % 2])

    right_copy = pltpu.make_async_copy(grads, right, right_sem.at[0])

    def compute(index):
        if index < dp_size:
            left_copy(index + 1).start()
        left_copy(index).wait()
        target = dense_own if index == 0 else out_own.at[index - 1]
        for start in range(0, width, 1024):
            columns = slice(start, start + 1024)
            target[:, columns] = dot_tn(left[index % 2], right[:, columns]).astype(jnp.bfloat16)

    def out_rows(index, way):
        return out_own.at[index, pl.ds(way * out_half, out_half)]

    first_copy, pass_on, arrive, add_final, square_finish = square_sum(
        lambda way, slot: out_rows(0 if slot == 1 else 1 + way, way),
        lambda way: out_rows(2 - way, way),
        out_recv,
        out_last,
        lambda way: out_rows(3, way),
        (first_send, first_recv, last_send, last_recv),
        d,
        c,
        out_half,
    )

    def out_store(way):
        return pltpu.make_async_copy(
            out_rows(3, way), shrink_out.at[pl.ds(way * out_half, out_half)], store_sem.at[way]
        )

    source = c // (ctx_size // dp_size)
    at_source = d == source
    from_x = x_mate == source
    from_y = y_mate == source
    across = diagonal == source
    per_head = HEAD // share

    def dense_half(way):
        return dense_own.at[pl.ds(way * head_half, head_half)]

    def dense_copy(way, mate):
        return remote(dense_half(way), dense_recv.at[way], dense_send.at[way], dense_sem.at[way], mate, c)

    def dense_add(way, mate):
        dense_copy(way, mate).wait_recv()
        add_into(dense_half(way), (dense_half(way), dense_recv.at[way]), head_half)

    def dense_open():
        @pl.when(from_y)
        def _():
            dense_copy(0, x_mate).start()

        @pl.when(from_x)
        def _():
            dense_copy(1, y_mate).start()

    def dense_second():
        @pl.when(across)
        def _():
            dense_add(0, y_mate)
            dense_copy(0, y_mate).start()
            dense_add(1, x_mate)
            dense_copy(1, x_mate).start()

    def dense_third():
        @pl.when(from_x)
        def _():
            dense_add(0, x_mate)
            dense_copy(0, x_mate).start()

        @pl.when(from_y)
        def _():
            dense_add(1, y_mate)
            dense_copy(1, y_mate).start()

    first_owner = lax.rem(c, ctx_size // per_head) * per_head

    def dense_chunk(piece):
        return dense_own.at[pl.ds(piece * share, share)]

    def dense_send_out(piece):
        return remote(
            dense_chunk(piece), dense_out, dense_send.at[2 + piece], dense_sem.at[2], d, first_owner + piece
        )

    def dense_store(piece):
        return pltpu.make_async_copy(dense_chunk(piece), dense_out, store_sem.at[2])

    def dense_fourth():
        @pl.when(at_source)
        def _():
            dense_add(0, x_mate)
            dense_add(1, y_mate)
            for piece in range(per_head):
                @pl.when(first_owner + piece == c)
                def _(piece=piece):
                    dense_store(piece).start()

                @pl.when(first_owner + piece != c)
                def _(piece=piece):
                    dense_send_out(piece).start()

    def dense_finish():
        @pl.when(jnp.logical_or(jnp.logical_or(from_y, across), from_x))
        def _():
            dense_copy(0, x_mate).wait_send()
            dense_copy(1, x_mate).wait_send()

        for piece in range(per_head):
            @pl.when(jnp.logical_and(at_source, first_owner + piece != c))
            def _(piece=piece):
                dense_send_out(piece).wait_send()

        stays = me // per_head == c

        @pl.when(stays)
        def _():
            dense_store(0).wait()

        @pl.when(jnp.logical_not(stays))
        def _():
            dense_send_out(0).wait_recv()

    def own_block(level):
        return board.at[level, core]

    def core_copy(level):
        return remote(
            board.at[level, 1 - core], back_core.at[level], core_send.at[level], core_recv.at[level], d, sibling
        )

    def core_add(level):
        core_copy(level).wait_recv()
        add_into(own_block(level), (own_block(level), back_core.at[level]), span)

    chain_open, chain_round, chain_end, chain_finish = chain_reduce(
        own_block, back_chain, (chain_send, chain_recv), d, c, levels
    )

    def back_store(level):
        return pltpu.make_async_copy(own_block(level), back_out, store_sem.at[3])

    def at(when):
        return pl.when(step == when)

    @at(0)
    def _():
        greet_all(d, c, dp_size, ctx_size)
        left_copy(0).start()
        right_copy.start()
        norm_sums[...] = jnp.zeros_like(norm_sums)
        joined_sums[...] = jnp.zeros_like(joined_sums)
        expand_sums[...] = jnp.zeros_like(expand_sums)

    @at(1)
    def _():
        right_copy.wait()
        compute(0)
        dense_open()

    @at(2)
    def _():
        compute(1)
        first_copy(0, 1).start()
        first_copy(1, 1).start()

    @at(3)
    def _():
        compute(2)
        first_copy(0, 0).start()
        compute(3)
        first_copy(1, 0).start()

    @at(4)
    def _():
        compute(4)

    for place, level in enumerate(outside_in(levels)):
        @at(tiles + 1 + place)
        def _(level=level):
            core_copy(level).start()

        @at(tiles + 2 + place)
        def _(level=level):
            core_add(level)
            chain_open(level)

    @at(6)
    def _():
        dense_second()

    @at(7)
    def _():
        pass_on(0)
        pass_on(1)

    @at(10)
    def _():
        chain_round(1)
        dense_third()

    @at(13)
    def _():
        chain_round(2)
        for way in range(2):
            arrive(way)
            add_final(way, 0, out_half)
            out_store(way).start()

    @at(14)
    def _():
        dense_fourth()

    @pl.when(phase == 0)
    def _():
        low_probs = probs[0]
        own = dot_nt(g[...], out_w[:HEAD, :]).astype(jnp.bfloat16)
        grad_probs = dot_nt(own, heads[2])
        wide = low_probs.astype(jnp.float32)
        delta = jnp.sum(wide * grad_probs, axis=1, keepdims=True)
        grad_scores = (wide * (grad_probs - delta)).astype(jnp.bfloat16)
        grad_queries[rows, :] = dot_nn(grad_scores, heads[1]) * scale
        more_keys = dot_tn(grad_scores, heads[0, rows, :]) * scale
        more_values = dot_tn(low_probs, own)

        @pl.when(tile == 0)
        def _():
            grad_keys[...] = more_keys
            grad_values[...] = more_values

        @pl.when(tile > 0)
        def _():
            grad_keys[...] += more_keys
            grad_values[...] += more_values

    @pl.when(phase == 1)
    def _():
        grad = dot_nt(g[...], out_w[HEAD:, :])
        grad = (grad * slopes[...].astype(jnp.float32)).astype(jnp.bfloat16)
        grad_expanded[...] = grad
        expand_sums[...] += jnp.sum(grad.astype(jnp.float32), axis=0, keepdims=True)
        cos_rows, sin_rows = cos[rows, :], -sin[rows, :]
        parts = (
            turn(grad_queries[rows, :], cos_rows, sin_rows),
            turn(grad_keys[rows, :], cos_rows, sin_rows),
            grad_values[rows, :],
        )
        for part in range(3):
            columns = slice(part * HEAD, (part + 1) * HEAD)
            joined = parts[part].astype(jnp.bfloat16)
            grad_joined[:, columns] = joined
            joined_sums[:, columns] += jnp.sum(joined.astype(jnp.float32), axis=0, keepdims=True)
        values_in = x[...].astype(jnp.float32)
        mean = jnp.mean(values_in, axis=1, keepdims=True)
        centered = values_in - mean
        spread = lax.rsqrt(jnp.mean(centered * centered, axis=1, keepdims=True) + 1e-05)
        for start in range(0, width, 1024):
            columns = slice(start, start + 1024)
            normal = (x[:, columns].astype(jnp.float32) - mean) * spread
            wide = jnp.concatenate([panels[part, columns, :] for part in range(3)], axis=1)
            total = dot_nt(grad_joined[...], wide)
            wide = jnp.concatenate([panels[3 + part, columns, :] for part in range(n_expand)], axis=1)
            other = dot_nt(grad_expanded[...], wide)
            for row, value in ((0, total * normal), (1, total), (2, other * normal), (3, other)):
                norm_sums[row : row + 1, columns] += jnp.sum(value, axis=0, keepdims=True)
            value = (total * gains[0:1, columns] + other * gains[2:3, columns]).astype(jnp.bfloat16)

            @pl.when(seq == 0)
            def _(columns=columns, value=value):
                for parity in range(2):
                    board[tile, parity, :, columns] = value[parity * span : (parity + 1) * span]

            @pl.when(seq > 0)
            def _(columns=columns, value=value):
                combined[:, columns] = value

    @at(4 * tiles - 1)
    def _():
        chain_end(back_store)
        square_finish()
        for way in range(2):
            out_store(way).wait()
        dense_finish()
        for level in range(levels):
            core_copy(level).wait_send()
        chain_finish(back_store)


def backward_call(dp_size, ctx_size, g, x, panels, out_w, gains, cos, sin, heads, probs, slopes, features):
    tokens, width = x.shape
    length = cos.shape[0]
    tiles = length // TILE
    steps = 2 * tokens // TILE
    hidden = slopes.shape[1]
    levels = ctx_size // 2
    span = length // ctx_size
    unit = hidden // dp_size
    share = width // (dp_size * ctx_size)
    dma = pltpu.SemaphoreType.DMA
    vmem = pltpu.VMEM

    def first(step):
        seq, at = step // (2 * tiles), lax.rem(step, 2 * tiles)
        return seq * tiles + jnp.minimum(at, tiles - 1)

    def mixed_order(place):
        return jnp.where(lax.rem(place, 2) == 0, tiles - 1 - place // 2, place // 2)

    def second(step):
        seq, at = step // (2 * tiles), lax.rem(step, 2 * tiles)
        return seq * tiles + mixed_order(jnp.maximum(at - tiles, 0))

    def both(step):
        seq, at = step // (2 * tiles), lax.rem(step, 2 * tiles)
        return seq * tiles + jnp.where(at < tiles, at, mixed_order(at - tiles))

    def late(step):
        return jnp.where(step < 2 * tiles, mixed_order(0), second(step) - tiles)

    kind = jnp.bfloat16
    fixed = lambda step: (0, 0)
    anywhere = pl.BlockSpec(memory_space=pl.ANY)
    return pl.pallas_call(
        functools.partial(backward_kernel, tiles, dp_size, ctx_size),
        grid=(steps,),
        out_shape=(
            jax.ShapeDtypeStruct((tokens, hidden), kind),
            jax.ShapeDtypeStruct((tokens, 3 * HEAD), kind),
            jax.ShapeDtypeStruct((length, width), kind),
            jax.ShapeDtypeStruct((8, width), jnp.float32),
            jax.ShapeDtypeStruct((1, 3 * HEAD), jnp.float32),
            jax.ShapeDtypeStruct((1, hidden), jnp.float32),
            jax.ShapeDtypeStruct((span, width), kind),
            jax.ShapeDtypeStruct((unit, width), kind),
            jax.ShapeDtypeStruct((share, width), kind),
        ),
        in_specs=[
            pl.BlockSpec((TILE, width), lambda step: (both(step), 0)),
            pl.BlockSpec((TILE, width), lambda step: (second(step), 0)),
            whole_spec(panels),
            whole_spec(out_w),
            whole_spec(gains),
            whole_spec(cos),
            whole_spec(sin),
            pl.BlockSpec((3, length, HEAD), lambda step: (0, step // (2 * tiles), 0)),
            pl.BlockSpec((1, TILE, length), lambda step: (first(step) // tiles, lax.rem(first(step), tiles), 0)),
            pl.BlockSpec((TILE, hidden), lambda step: (second(step), 0)),
            anywhere,
            anywhere,
        ],
        out_specs=(
            pl.BlockSpec((TILE, hidden), lambda step: (second(step), 0)),
            pl.BlockSpec((TILE, 3 * HEAD), lambda step: (second(step), 0)),
            pl.BlockSpec((TILE, width), lambda step: (late(step), 0)),
            pl.BlockSpec((8, width), fixed),
            pl.BlockSpec((1, 3 * HEAD), fixed),
            pl.BlockSpec((1, hidden), fixed),
            anywhere,
            anywhere,
            anywhere,
        ),
        scratch_shapes=[
            vmem((length, HEAD), jnp.float32),
            vmem((length, HEAD), jnp.float32),
            vmem((length, HEAD), jnp.float32),
            vmem((levels, 2, span, width), kind),
            vmem((levels, span, width), kind),
            vmem((2, levels - 1, span, width), kind),
            vmem((2, tokens, HEAD), kind),
            vmem((tokens, width), kind),
            vmem((dp_size, unit, width), kind),
            vmem((2, 2, unit // 2, width), kind),
            vmem((2, unit // 2, width), kind),
            vmem((HEAD, width), kind),
            vmem((2, HEAD // 2, width), kind),
            dma((2,)),
            dma((1,)),
            dma((levels,)),
            dma((levels,)),
            dma((2, levels)),
            dma((2, levels)),
            *square_scratch(),
            dma((2 + HEAD // share,)),
            dma((3,)),
            dma((4,)),
        ],
        compiler_params=pltpu.CompilerParams(
            collective_id=4, has_side_effects=True, vmem_limit_bytes=60 * 1024 * 1024
        ),
        name="backward_part",
    )(g, x, panels, out_w, gains, cos, sin, heads, probs, slopes, features, g)


def reduce_kernel(
    dp_size,
    ctx_size,
    back,
    hidden_attn,
    hidden_mlp,
    grad_joined,
    grad_expanded,
    board,
    back_out,
    attn_out,
    mlp_out,
    tail_out,
    back_own,
    back_core,
    back_chain,
    left,
    right_attn,
    right_mlp,
    attn_own,
    attn_recv,
    attn_last,
    mlp_own,
    mlp_recv,
    mlp_last,
    board_recv,
    load_sem,
    left_sem,
    right_sem,
    core_send,
    core_recv,
    chain_send,
    chain_recv,
    first_send_a,
    first_recv_a,
    last_send_a,
    last_recv_a,
    first_send_m,
    first_recv_m,
    last_send_m,
    last_recv_m,
    row_send,
    row_recv,
    board_sem,
    store_sem,
):
    d = lax.axis_index("dp")
    c = lax.axis_index("ctx")
    core = lax.rem(c, 2)
    sibling = c + 1 - 2 * core
    x_mate = d + 1 - 2 * lax.rem(d, 2)
    y_mate = lax.rem(d + 2, 4)
    diagonal = 3 - d
    span = back.shape[0] // ctx_size
    levels = ctx_size // 2
    devices = dp_size * ctx_size
    me = d * ctx_size + c
    group_rows = hidden_attn.shape[1] // dp_size
    half = group_rows // 2
    rows = group_rows // ctx_size

    greet_all(d, c, dp_size, ctx_size)

    def back_view(parity, level):
        start = (2 * level + parity) * span
        return back.at[pl.ds(pl.multiple_of(start, span), span)]

    def back_load(level):
        return pltpu.make_async_copy(back_view(core, level), back_own.at[level], load_sem.at[level])

    def core_copy(level):
        return remote(
            back_view(1 - core, level), back_core.at[level], core_send.at[level], core_recv.at[level], d, sibling
        )

    order = outside_in(levels)

    tile_of = []
    for owners in ((diagonal, diagonal), (x_mate, y_mate), (y_mate, x_mate), (d, d)):
        for way in range(2):
            tile_of.append((owners[way], way))
    sequence = [(0, index) for index in range(6)]
    sequence += [(1, index) for index in range(4)]
    sequence += [(0, index) for index in range(6, 8)]
    sequence += [(1, index) for index in range(4, 8)]

    def left_copy(place):
        kind, index = sequence[place]
        owner, way = tile_of[index]
        columns = pl.ds(pl.multiple_of(owner * group_rows + way * half, half), half)
        source = (hidden_attn, hidden_mlp)[kind]
        return pltpu.make_async_copy(source.at[:, columns], left.at[place % 2], left_sem.at[place % 2])

    right_copies = (
        pltpu.make_async_copy(grad_joined, right_attn, right_sem.at[0]),
        pltpu.make_async_copy(grad_expanded, right_mlp, right_sem.at[1]),
    )

    def compute(kind, index):
        place = sequence.index((kind, index))
        if place + 1 < len(sequence):
            left_copy(place + 1).start()
        left_copy(place).wait()
        if index == 0:
            right_copies[kind].wait()
        target, right = ((attn_own, right_attn), (mlp_own, right_mlp))[kind]
        target[index] = dot_tn(left[place % 2], right[...]).astype(jnp.bfloat16)

    def square(own, recv, last, sems):
        return square_sum(
            lambda way, slot: own.at[way + 2 * (1 - slot)],
            lambda way: own.at[4 + way],
            recv,
            last,
            lambda way: own.at[6 + way],
            sems,
            d,
            c,
            half,
        )

    squares = (
        square(attn_own, attn_recv, attn_last, (first_send_a, first_recv_a, last_send_a, last_recv_a)),
        square(mlp_own, mlp_recv, mlp_last, (first_send_m, first_recv_m, last_send_m, last_recv_m)),
    )

    per_half = half // rows

    def row_chunk(kind, way, piece):
        return (attn_own, mlp_own)[kind].at[6 + way, pl.ds(piece * rows, rows)]

    def row_copy(kind, way, piece):
        target = way * per_half + piece
        out = (attn_out, mlp_out)[kind]
        return remote(
            row_chunk(kind, way, piece), out.at[c], row_send.at[kind, target], row_recv.at[kind], d, target
        )

    def row_local(kind, way, piece):
        out = (attn_out, mlp_out)[kind]
        return pltpu.make_async_copy(row_chunk(kind, way, piece), out.at[c], store_sem.at[kind])

    def tile_end(kind):
        first_copy, pass_on, arrive, add_final, finish = squares[kind]
        for way in range(2):
            arrive(way)
            for piece in range(per_half):
                add_final(way, piece * rows, rows)
                target = way * per_half + piece

                @pl.when(c != target)
                def _(way=way, piece=piece):
                    row_copy(kind, way, piece).start()

                @pl.when(c == target)
                def _(way=way, piece=piece):
                    row_local(kind, way, piece).start()

    board_load = pltpu.make_async_copy(board.at[me], board_recv.at[me], load_sem.at[levels])

    def board_start():
        board_load.start()

        def push_board(step, carry):
            other = lax.rem(me + step, devices)
            remote(
                board.at[other],
                board_recv.at[me],
                board_sem.at[0],
                board_sem.at[1],
                other // ctx_size,
                lax.rem(other, ctx_size),
            ).start()
            return carry

        lax.fori_loop(1, devices, push_board, 0)

    def board_end():
        board_load.wait()
        rest = board_recv.at[pl.ds(0, devices - 1)]
        remote(rest, rest, board_sem.at[0], board_sem.at[1], d, sibling).wait()
        tail_out[...] = jnp.sum(board_recv[...], axis=0)

    chain_open, chain_round, chain_end, chain_finish = chain_reduce(
        lambda level: back_own.at[level], back_chain, (chain_send, chain_recv), d, c, levels
    )

    def back_store(level):
        return pltpu.make_async_copy(back_own.at[level], back_out, store_sem.at[2])

    right_copies[0].start()
    left_copy(0).start()
    for level in order:
        core_copy(level).start()
        back_load(level).start()
    right_copies[1].start()

    for way in range(2):
        compute(0, way)
        squares[0][0](way, 1).start()
    for way in range(2):
        compute(0, 2 + way)
        squares[0][0](way, 0).start()
    for level in order:
        back_load(level).wait()
        core_copy(level).wait_recv()
        own = back_own.at[level]
        add_into(own, (own, back_core.at[level]), span)
        chain_open(level)
    compute(0, 4)
    compute(0, 5)
    squares[0][1](0)
    squares[0][1](1)
    for way in range(2):
        compute(1, way)
        squares[1][0](way, 1).start()
    for way in range(2):
        compute(1, 2 + way)
        squares[1][0](way, 0).start()
    chain_round(1)
    board_start()
    compute(0, 6)
    compute(0, 7)
    compute(1, 4)
    compute(1, 5)
    tile_end(0)
    chain_round(2)
    compute(1, 6)
    compute(1, 7)
    squares[1][1](0)
    squares[1][1](1)
    chain_end(back_store)
    tile_end(1)
    board_end()

    for kind in range(2):
        squares[kind][4]()
        for way in range(2):
            for piece in range(per_half):
                target = way * per_half + piece

                @pl.when(c != target)
                def _(kind=kind, way=way, piece=piece):
                    row_copy(kind, way, piece).wait_send()

        out = (attn_out, mlp_out)[kind]
        rest = out.at[pl.ds(0, ctx_size - 1)]
        remote(rest, rest, row_send.at[kind, 0], row_recv.at[kind], d, sibling).wait_recv()
        row_local(kind, 0, 0).wait()
    for level in range(levels):
        core_copy(level).wait_send()
    chain_finish(back_store)


def reduce_call(dp_size, ctx_size, back, hidden_attn, hidden_mlp, grad_joined, grad_expanded, board):
    length, width = back.shape
    tokens = hidden_attn.shape[0]
    span = length // ctx_size
    group_rows = width // dp_size
    half = group_rows // 2
    rows = group_rows // ctx_size
    joined, hidden = grad_joined.shape[1], grad_expanded.shape[1]
    levels = ctx_size // 2
    devices = dp_size * ctx_size
    dma = pltpu.SemaphoreType.DMA
    kind = back.dtype
    vmem = pltpu.VMEM
    out_shape = (
        jax.ShapeDtypeStruct((span, width), kind),
        jax.ShapeDtypeStruct((ctx_size, rows, joined), kind),
        jax.ShapeDtypeStruct((ctx_size, rows, hidden), kind),
        jax.ShapeDtypeStruct(board.shape[1:], jnp.float32),
    )
    anywhere = pl.BlockSpec(memory_space=pl.ANY)
    return pl.pallas_call(
        functools.partial(reduce_kernel, dp_size, ctx_size),
        out_shape=out_shape,
        in_specs=[anywhere] * 6,
        out_specs=(anywhere,) * 3 + (pl.BlockSpec(memory_space=pltpu.VMEM),),
        scratch_shapes=[
            vmem((levels, span, width), kind),
            vmem((levels, span, width), kind),
            vmem((2, levels - 1, span, width), kind),
            vmem((2, tokens, HEAD), kind),
            vmem((tokens, joined), kind),
            vmem((tokens, hidden), kind),
            vmem((8, half, joined), kind),
            vmem((2, 2, half, joined), kind),
            vmem((2, half, joined), kind),
            vmem((8, half, hidden), kind),
            vmem((2, 2, half, hidden), kind),
            vmem((2, half, hidden), kind),
            vmem((devices,) + board.shape[1:], jnp.float32),
            dma((levels + 1,)),
            dma((2,)),
            dma((2,)),
            dma((levels,)),
            dma((levels,)),
            dma((2, levels)),
            dma((2, levels)),
            *square_scratch(),
            *square_scratch(),
            dma((2, ctx_size)),
            dma((2,)),
            dma((2,)),
            dma((3,)),
        ],
        compiler_params=pltpu.CompilerParams(
            collective_id=2, has_side_effects=True, vmem_limit_bytes=60 * 1024 * 1024
        ),
        name="reduce_all",
    )(back, hidden_attn, hidden_mlp, grad_joined, grad_expanded, board)


def finish_kernel(
    attn_rows,
    mlp_rows,
    shrink_rows,
    dense_rows,
    back_first,
    back_last,
    x,
    g,
    out_first,
    out_last,
    out_shift,
    tail,
    qkv_grad,
    expand_grad,
    shrink_grad,
    dense_grad,
    layer_output,
    input_grad,
    *small_grads,
):
    ctx_size = attn_rows.shape[0]
    at = 0
    for target in small_grads:
        size = target.shape[0] * target.shape[1]
        for row in range(target.shape[0]):
            start = at + row * target.shape[1]
            lane = start % 128
            target[row : row + 1, :] = tail[start // 128 : start // 128 + 1, lane : lane + target.shape[1]]
        at += size
    for rows, target in ((attn_rows, qkv_grad), (mlp_rows, expand_grad)):
        for member in range(ctx_size):
            for part in range(rows.shape[2] // HEAD):
                start = (part * ctx_size + member) * HEAD
                target[:, start : start + HEAD] = rows[member, :, part * HEAD : (part + 1) * HEAD].astype(jnp.float32)
    shrink_grad[...] = shrink_rows[...].astype(jnp.float32)
    dense_grad[...] = dense_rows[...].astype(jnp.float32)
    for m, (back, out) in enumerate(((back_first, out_first), (back_last, out_last))):
        own = x[m].astype(jnp.float32)
        layer_output[m] = (own + out[...].astype(jnp.float32) + out_shift[...]).astype(jnp.bfloat16)
        centered = own - jnp.mean(own, axis=1, keepdims=True)
        spread = lax.rsqrt(jnp.mean(centered * centered, axis=1, keepdims=True) + 1e-05)
        normal = centered * spread
        grad = back[...].astype(jnp.float32)
        share = spread * (
            grad
            - jnp.mean(grad, axis=1, keepdims=True)
            - normal * jnp.mean(grad * normal, axis=1, keepdims=True)
        )
        input_grad[m] = (g[m].astype(jnp.float32) + share).astype(jnp.bfloat16)


def finish_call(attn_rows, mlp_rows, shrink_rows, dense_rows, back_first, back_last, x, g, out_first, out_last, out_shift, tail, lengths):
    steps = 4
    arrays = (attn_rows, mlp_rows, shrink_rows, dense_rows, back_first, back_last, x, g, out_first, out_last)
    micro = x.shape[0]
    ctx_size, rows, joined = attn_rows.shape

    def spec(shape):
        block = shape[:-2] + (shape[-2] // steps, shape[-1])
        lead = (0,) * (len(shape) - 2)
        return pl.BlockSpec(block, lambda step: lead + (step, 0))

    outs = (
        jax.ShapeDtypeStruct((rows, joined * ctx_size), jnp.float32),
        jax.ShapeDtypeStruct((rows, mlp_rows.shape[2] * ctx_size), jnp.float32),
        jax.ShapeDtypeStruct(shrink_rows.shape, jnp.float32),
        jax.ShapeDtypeStruct(dense_rows.shape, jnp.float32),
        jax.ShapeDtypeStruct(x.shape, jnp.bfloat16),
        jax.ShapeDtypeStruct(x.shape, jnp.bfloat16),
    )
    smalls = tuple(
        jax.ShapeDtypeStruct((max(1, length // 128), min(length, 128)), jnp.float32) for length in lengths
    )
    return pl.pallas_call(
        finish_kernel,
        grid=(steps,),
        out_shape=outs + smalls,
        in_specs=[spec(array.shape) for array in arrays] + [whole_spec(out_shift), whole_spec(tail)],
        out_specs=tuple(spec(out.shape) for out in outs)
        + tuple(pl.BlockSpec(out.shape, lambda step: (0, 0)) for out in smalls),
        compiler_params=pltpu.CompilerParams(vmem_limit_bytes=60 * 1024 * 1024),
        name="finish_part",
    )(*arrays, out_shift, tail)


def tensor_shards(
    layer_input,
    out_grad,
    prefix_len,
    qkv_weight,
    qkv_bias,
    dense_weight,
    dense_bias,
    expand_weight,
    expand_bias,
    shrink_weight,
    shrink_bias,
    attn_gain,
    attn_shift,
    mlp_gain,
    mlp_shift,
):
    dp_size = lax.axis_size("dp")
    ctx_size = lax.axis_size("ctx")
    devices = dp_size * ctx_size
    me = lax.axis_index("ctx")
    group = lax.axis_index("dp")
    micro, seq_count, span, width = layer_input.shape
    sequences = micro * seq_count
    tokens = sequences * SEQ
    row_share = qkv_weight.shape[0]
    scale = 1.0 / math.sqrt(HEAD)
    ff = expand_weight.shape[1]
    unit = shrink_weight.shape[0]
    members = (attn_gain, attn_shift, mlp_gain, mlp_shift, qkv_bias, dense_bias, expand_bias, shrink_bias)
    columns = max(member.shape[0] for member in members)
    packed = sum(
        jnp.pad(member[None], ((row, 15 - row), (0, columns - member.shape[0])))
        for row, member in enumerate(members)
    )
    own_x = layer_input.reshape(sequences, span, width)
    own_g = out_grad.reshape(sequences, span, width)
    x_all, panels, out_part, small = gather_call(
        dp_size, ctx_size, own_x, qkv_weight, expand_weight, dense_weight, shrink_weight, packed
    )
    x_all = x_all.reshape(tokens, width)
    small = small.astype(jnp.float32)
    gains = jnp.transpose(small[:, :4, : attn_gain.shape[0]], (1, 0, 2)).reshape(4, width)
    qkv_shift = small[:, 4, : qkv_bias.shape[0]].reshape(3, ctx_size, HEAD)
    qkv_shift = lax.dynamic_slice_in_dim(qkv_shift, me, 1, 1).reshape(-1)
    expand_shift = small.reshape(dp_size, ctx_size, 16, columns)[:, :, 6, :unit]
    expand_shift = lax.dynamic_slice_in_dim(expand_shift, me, 1, 1).reshape(-1)
    out_shift = (small[:, 5, : dense_bias.shape[0]] + small[:, 7, : shrink_bias.shape[0]]).reshape(1, width)
    cos, sin = turn_tables(SEQ)
    hidden_attn, hidden_mlp, heads, probs, features, slopes, partial, g_all, out_first = forward_call(
        ctx_size // 2,
        prefix_len.reshape(sequences),
        x_all,
        own_g,
        panels,
        out_part,
        gains,
        qkv_shift[None],
        expand_shift[None],
        cos,
        sin,
    )
    g_all = g_all.reshape(tokens, width)
    out_last = lax.psum_scatter(partial, "ctx", scatter_dimension=0, tiled=True)

    (
        grad_expanded,
        grad_joined,
        combined,
        norm_sums,
        joined_sum,
        expand_sum,
        back_first,
        shrink_rows,
        dense_rows,
    ) = backward_call(
        dp_size, ctx_size, g_all, x_all, panels, out_part, gains, cos, sin, heads, probs, slopes, features
    )
    joined_sum, expand_sum = joined_sum[0], expand_sum[0]

    def place(values, parts):
        board = jnp.zeros((parts, ctx_size, values.shape[0] // parts), jnp.float32)
        board = lax.dynamic_update_slice(board, values.reshape(parts, 1, -1), (0, me, 0))
        return board.reshape(devices, -1)

    out_sum = jnp.sum(own_g.astype(jnp.float32), axis=(0, 1))
    board = jnp.concatenate(
        [
            place(joined_sum[: 2 * HEAD], 2),
            place(joined_sum[2 * HEAD :], 1),
            out_sum.reshape(devices, -1),
            place(expand_sum, dp_size),
            norm_sums[0].reshape(devices, -1),
            norm_sums[1].reshape(devices, -1),
            norm_sums[2].reshape(devices, -1),
            norm_sums[3].reshape(devices, -1),
        ],
        axis=1,
    )
    used = board.shape[1]
    board = jnp.pad(board, ((0, 0), (0, -used % 1024))).reshape(devices, -1, 128)
    back_last, attn_rows, mlp_rows, tail = reduce_call(
        dp_size, ctx_size, combined, hidden_attn, hidden_mlp, grad_joined, grad_expanded, board
    )
    share_len = width // devices
    small_lengths = (2 * share_len, share_len, share_len, ff // devices) + (share_len,) * 4
    qkv_grad, expand_grad, shrink_grad, dense_grad, layer_output, input_grad, *pieces = finish_call(
        attn_rows,
        mlp_rows,
        shrink_rows,
        dense_rows,
        back_first,
        back_last,
        own_x,
        own_g,
        out_first,
        out_last,
        out_shift,
        tail,
        small_lengths,
    )
    pieces = [piece.reshape(-1) for piece in pieces]
    layer_output = layer_output.reshape(layer_input.shape)
    input_grad = input_grad.reshape(layer_input.shape)
    return (
        layer_output,
        input_grad,
        qkv_grad,
        pieces[0],
        pieces[1],
        dense_grad,
        pieces[2],
        expand_grad,
        pieces[3],
        shrink_grad,
        pieces[2],
        pieces[4],
        pieces[5],
        pieces[6],
        pieces[7],
    )


def solution(mesh):
    placed = (
        P(None, "dp", "ctx", None),
        P(None, "dp", "ctx", None),
        P(None, "dp"),
        P(("dp", "ctx"), None),
        P(("dp", "ctx")),
        P(("dp", "ctx"), None),
        P(("dp", "ctx")),
        P(("dp", "ctx"), None),
        P(("dp", "ctx")),
        P(("dp", "ctx"), None),
        P(("dp", "ctx")),
        P(("dp", "ctx")),
        P(("dp", "ctx")),
        P(("dp", "ctx")),
        P(("dp", "ctx")),
    )
    return jax.shard_map(
        tensor_shards if (mesh.shape["dp"], mesh.shape["ctx"]) == (4, HEADS) else shards,
        mesh=mesh,
        in_specs=placed,
        out_specs=(
            P(None, "dp", "ctx", None),
            P(None, "dp", "ctx", None),
            P(("dp", "ctx"), None),
            P(("dp", "ctx")),
            P(("dp", "ctx")),
            P(("dp", "ctx"), None),
            P(("dp", "ctx")),
            P(("dp", "ctx"), None),
            P(("dp", "ctx")),
            P(("dp", "ctx"), None),
            P(("dp", "ctx")),
            P(("dp", "ctx")),
            P(("dp", "ctx")),
            P(("dp", "ctx")),
            P(("dp", "ctx")),
        ),
        check_vma=False,
    )
```

```python
import functools
import math

import jax
import jax.numpy as jnp
import numpy as np
from jax import lax
from jax.experimental import pallas as pl
from jax.experimental.pallas import tpu as pltpu
from jax.sharding import PartitionSpec as P

HEADS = 8
HEAD = 256
ROT = 64
SEQ = 1024


def norm_rows(inputs, norm_gain, norm_bias):
    row_mean = jnp.mean(inputs, axis=-1, keepdims=True)
    centered = inputs - row_mean
    variance = jnp.mean(centered * centered, axis=-1, keepdims=True)
    return centered * lax.rsqrt(variance + 1e-05) * norm_gain + norm_bias


def gelu_exact(values):
    return jax.nn.gelu(values, approximate=False)


def rope_tables(positions):
    freqs = jnp.exp(jnp.arange(ROT // 2, dtype=jnp.float32) * (-2.0 * math.log(10000.0) / ROT))
    angles = positions[:, None] * freqs[None, :]
    return (jnp.cos(angles), jnp.sin(angles))


def rotate(heads, cos_table, sin_table):
    half_rot = ROT // 2
    lower = heads[..., :half_rot]
    upper = heads[..., half_rot:ROT]
    cos_wide = cos_table[:, None, :]
    sin_wide = sin_table[:, None, :]
    return jnp.concatenate(
        [
            lower * cos_wide - upper * sin_wide,
            upper * cos_wide + lower * sin_wide,
            heads[..., ROT:],
        ],
        axis=-1,
    )


def unpack_small(packed, lengths, devices):
    table_rows = packed.reshape(devices, -1)
    members = []
    offset = 0
    for length in lengths:
        members.append(table_rows[:, offset : offset + length].reshape(-1).astype(jnp.float32))
        offset = offset + length
    return members


def contract_rows(left_mat, right_mat):
    return lax.dot_general(
        left_mat, right_mat, (((0,), (0,)), ((), ())), preferred_element_type=jnp.float32
    )


def contract_cols(left_mat, right_mat):
    return lax.dot_general(
        left_mat, right_mat, (((1,), (1,)), ((), ())), preferred_element_type=jnp.float32
    )


def shards(
    layer_input,
    out_grad,
    prefix_len,
    qkv_weight,
    qkv_bias,
    dense_weight,
    dense_bias,
    expand_weight,
    expand_bias,
    shrink_weight,
    shrink_bias,
    attn_gain,
    attn_shift,
    mlp_gain,
    mlp_shift,
):
    devices = lax.axis_size("dp") * lax.axis_size("ctx")
    ctx_index = lax.axis_index("ctx")
    micro, seq_count, span, width = layer_input.shape
    sequences = micro * seq_count
    rows = sequences * span
    heads_shape = (sequences, span, HEADS, HEAD)
    scale = 1.0 / math.sqrt(HEAD)
    attn_lengths = (attn_gain.shape[0], attn_shift.shape[0], qkv_bias.shape[0], dense_bias.shape[0])
    mlp_lengths = (
        mlp_gain.shape[0],
        mlp_shift.shape[0],
        expand_bias.shape[0],
        shrink_bias.shape[0],
    )
    attn_packed = jnp.concatenate([attn_gain, attn_shift, qkv_bias, dense_bias])
    mlp_packed = jnp.concatenate([mlp_gain, mlp_shift, expand_bias, shrink_bias])

    def fetch_attn():
        return (
            lax.all_gather(qkv_weight, ("dp", "ctx"), axis=0, tiled=True),
            lax.all_gather(dense_weight, ("dp", "ctx"), axis=0, tiled=True),
            lax.all_gather(attn_packed, ("dp", "ctx"), axis=0, tiled=True),
        )

    def fetch_mlp():
        return (
            lax.all_gather(expand_weight, ("dp", "ctx"), axis=0, tiled=True),
            lax.all_gather(shrink_weight, ("dp", "ctx"), axis=0, tiled=True),
            lax.all_gather(mlp_packed, ("dp", "ctx"), axis=0, tiled=True),
        )

    local_pos = ctx_index * span + jnp.arange(span, dtype=jnp.int32)
    cos_table, sin_table = rope_tables(local_pos.astype(jnp.float32))
    key_pos = jnp.arange(SEQ, dtype=jnp.int32)
    causal = key_pos[None, :] <= local_pos[:, None]
    inputs = layer_input.astype(jnp.float32).reshape(rows, width)
    cot_rows = out_grad.reshape(rows, width)
    cot_float = cot_rows.astype(jnp.float32)
    prefix = prefix_len.reshape(sequences)
    allowed = (causal[None] | (key_pos[None, None, :] < prefix[:, None, None]))[:, None]
    attn_set = fetch_attn()
    qkv_full, dense_full, attn_small = attn_set
    gain_attn, shift_attn, joined_shift, dense_shift = unpack_small(
        attn_small, attn_lengths, devices
    )
    hidden_attn = norm_rows(inputs, gain_attn, shift_attn).astype(jnp.bfloat16)
    joined = jnp.dot(hidden_attn, qkv_full, preferred_element_type=jnp.float32) + joined_shift
    queries = rotate(joined[:, :width].reshape(heads_shape), cos_table, sin_table).astype(
        jnp.bfloat16
    )
    key_rows = rotate(
        joined[:, width : 2 * width].reshape(heads_shape), cos_table, sin_table
    ).astype(jnp.bfloat16)
    value_rows = joined[:, 2 * width :].reshape(heads_shape).astype(jnp.bfloat16)
    all_keys, all_values = (
        lax.all_gather(key_rows, "ctx", axis=1, tiled=True),
        lax.all_gather(value_rows, "ctx", axis=1, tiled=True),
    )
    scores = (
        jnp.einsum("sqhe,skhe->shqk", queries, all_keys, preferred_element_type=jnp.float32) * scale
    )
    scores = jnp.where(allowed, scores, -1e30)
    row_max = jnp.max(scores, axis=-1, keepdims=True)
    expo = jnp.exp(scores - row_max)
    row_total = jnp.sum(expo, axis=-1, keepdims=True)
    log_total = row_max + jnp.log(row_total)
    probs_low = (expo / row_total).astype(jnp.bfloat16)
    mixed = jnp.einsum("shqk,skhe->sqhe", probs_low, all_values, preferred_element_type=jnp.float32)
    mixed = mixed.reshape(rows, width).astype(jnp.bfloat16)
    attn_out = jnp.dot(mixed, dense_full, preferred_element_type=jnp.float32) + dense_shift
    mlp_set = fetch_mlp()
    expand_full, shrink_full, mlp_small = mlp_set
    gain_mlp, shift_mlp, expand_shift, shrink_shift = unpack_small(mlp_small, mlp_lengths, devices)
    hidden_mlp = norm_rows(inputs, gain_mlp, shift_mlp).astype(jnp.bfloat16)
    expanded = jnp.dot(hidden_mlp, expand_full, preferred_element_type=jnp.float32) + expand_shift
    activated = gelu_exact(expanded).astype(jnp.bfloat16)
    mlp_out = jnp.dot(activated, shrink_full, preferred_element_type=jnp.float32) + shrink_shift
    layer_output = (
        (inputs + attn_out + mlp_out).astype(jnp.bfloat16).reshape(micro, seq_count, span, width)
    )
    attn_back_set = fetch_attn()
    qkv_back, dense_back, attn_small_back = attn_back_set
    gain_attn, shift_attn, joined_shift, dense_shift = unpack_small(
        attn_small_back, attn_lengths, devices
    )
    grad_out_shift = jnp.sum(cot_float, axis=0)
    grad_mixed = contract_cols(cot_rows, dense_back).astype(jnp.bfloat16).reshape(heads_shape)
    again = (
        jnp.einsum("sqhe,skhe->shqk", queries, all_keys, preferred_element_type=jnp.float32) * scale
    )
    again = jnp.where(allowed, again, -1e30)
    probs = jnp.exp(again - log_total)
    grad_probs = jnp.einsum(
        "sqhe,skhe->shqk", grad_mixed, all_values, preferred_element_type=jnp.float32
    )
    delta = jnp.sum(probs * grad_probs, axis=-1, keepdims=True)
    grad_scores = (probs * (grad_probs - delta)).astype(jnp.bfloat16)
    grad_queries = (
        jnp.einsum("shqk,skhe->sqhe", grad_scores, all_keys, preferred_element_type=jnp.float32)
        * scale
    )
    all_queries, all_grad_mixed = (
        lax.all_gather(queries, "ctx", axis=1, tiled=True),
        lax.all_gather(grad_mixed, "ctx", axis=1, tiled=True),
    )
    stat_lse = jnp.transpose(log_total[..., 0], (0, 2, 1))
    stat_delta = jnp.transpose(delta[..., 0], (0, 2, 1))
    lse_all, delta_all = (
        lax.all_gather(stat_lse, "ctx", axis=1, tiled=True),
        lax.all_gather(stat_delta, "ctx", axis=1, tiled=True),
    )
    lse_all = jnp.transpose(lse_all, (0, 2, 1))[..., None]
    delta_all = jnp.transpose(delta_all, (0, 2, 1))[..., None]
    key_allowed = (local_pos[None, :] <= key_pos[:, None])[None] | (
        local_pos[None, None, :] < prefix[:, None, None]
    )
    block_scores = (
        jnp.einsum("sqhe,skhe->shqk", all_queries, key_rows, preferred_element_type=jnp.float32)
        * scale
    )
    block_scores = jnp.where(key_allowed[:, None], block_scores, -1e30)
    block_probs = jnp.exp(block_scores - lse_all)
    block_grad_probs = jnp.einsum(
        "sqhe,skhe->shqk", all_grad_mixed, value_rows, preferred_element_type=jnp.float32
    )
    block_grad_scores = (block_probs * (block_grad_probs - delta_all)).astype(jnp.bfloat16)
    own_keys = (
        jnp.einsum(
            "shqk,sqhe->skhe", block_grad_scores, all_queries, preferred_element_type=jnp.float32
        )
        * scale
    )
    own_values = jnp.einsum(
        "shqk,sqhe->skhe",
        block_probs.astype(jnp.bfloat16),
        all_grad_mixed,
        preferred_element_type=jnp.float32,
    )
    grad_joined = jnp.concatenate(
        [
            rotate(grad_queries, cos_table, -sin_table).reshape(rows, width),
            rotate(own_keys, cos_table, -sin_table).reshape(rows, width),
            own_values.reshape(rows, width),
        ],
        axis=1,
    ).astype(jnp.bfloat16)
    grad_joined_shift = jnp.sum(grad_joined.astype(jnp.float32), axis=0)
    grad_hidden_attn = contract_cols(grad_joined, qkv_back)
    unused_attn, attn_back = jax.vjp(norm_rows, inputs, gain_attn, shift_attn)
    grad_in_attn, grad_gain_attn, grad_shift_attn = attn_back(grad_hidden_attn)
    attn_columns = jnp.concatenate(
        [
            grad_gain_attn[:, None],
            grad_shift_attn[:, None],
            grad_joined_shift[: 2 * width].reshape(width, 2),
            grad_joined_shift[2 * width :][:, None],
            grad_out_shift[:, None],
        ],
        axis=1,
    )
    hidden_part = hidden_attn
    small_part = attn_columns
    attn_grads = lax.psum_scatter(
        jnp.concatenate(
            [contract_rows(hidden_part, grad_joined), contract_rows(mixed, cot_rows), small_part],
            axis=1,
        ),
        ("dp", "ctx"),
        scatter_dimension=0,
        tiled=True,
    )
    qkv_grad = attn_grads[:, : 3 * width]
    dense_grad = attn_grads[:, 3 * width : 4 * width]
    attn_tail = attn_grads[:, 4 * width :]
    mlp_back_set = fetch_mlp()
    expand_back, shrink_back, mlp_small_back = mlp_back_set
    gain_mlp, shift_mlp, expand_shift, shrink_shift = unpack_small(
        mlp_small_back, mlp_lengths, devices
    )
    unused_gelu, gelu_back = jax.vjp(gelu_exact, expanded)
    grad_act = contract_cols(cot_rows, shrink_back)
    grad_expanded = gelu_back(grad_act)[0].astype(jnp.bfloat16)
    grad_expand_shift = jnp.sum(grad_expanded.astype(jnp.float32), axis=0)
    grad_hidden_mlp = contract_cols(grad_expanded, expand_back)
    unused_mlp, mlp_back = jax.vjp(norm_rows, inputs, gain_mlp, shift_mlp)
    grad_in_mlp, grad_gain_mlp, grad_shift_mlp = mlp_back(grad_hidden_mlp)
    ratio = expand_shift.shape[0] // width
    mlp_columns = jnp.concatenate(
        [
            grad_gain_mlp[:, None],
            grad_shift_mlp[:, None],
            grad_expand_shift.reshape(width, ratio),
            grad_out_shift[:, None],
        ],
        axis=1,
    )
    ff_width = expand_back.shape[1]
    hidden_part = hidden_mlp
    small_part = mlp_columns
    expand_grads = lax.psum_scatter(
        jnp.concatenate([contract_rows(hidden_part, grad_expanded), small_part], axis=1),
        ("dp", "ctx"),
        scatter_dimension=0,
        tiled=True,
    )
    shrink_grad = lax.psum_scatter(
        contract_rows(activated, cot_rows), ("dp", "ctx"), scatter_dimension=0, tiled=True
    )
    expand_grad = expand_grads[:, :ff_width]
    mlp_tail = expand_grads[:, ff_width:]
    input_grad = (
        (cot_float + grad_in_attn + grad_in_mlp)
        .astype(jnp.bfloat16)
        .reshape(micro, seq_count, span, width)
    )
    return (
        layer_output,
        input_grad,
        qkv_grad,
        attn_tail[:, 2:4].reshape(-1),
        attn_tail[:, 4],
        dense_grad,
        attn_tail[:, 5],
        expand_grad,
        mlp_tail[:, 2 : 2 + ratio].reshape(-1),
        shrink_grad,
        mlp_tail[:, 2 + ratio],
        attn_tail[:, 0],
        attn_tail[:, 1],
        mlp_tail[:, 0],
        mlp_tail[:, 1],
    )


def low(values):
    return values.astype(jnp.bfloat16)


MESH_ID = pl.DeviceIdType.MESH


def remote(src, dst, send_sem, recv_sem, dp, ctx):
    return pltpu.make_async_remote_copy(
        src_ref=src,
        dst_ref=dst,
        send_sem=send_sem,
        recv_sem=recv_sem,
        device_id=(dp, ctx),
        device_id_type=MESH_ID,
    )


def greet_all(dp, ctx, dp_size, ctx_size):
    barrier = pltpu.get_barrier_semaphore()
    devices = dp_size * ctx_size
    me = dp * ctx_size + ctx

    def greet(step, carry):
        other = lax.rem(me + step, devices)
        pl.semaphore_signal(
            barrier, inc=1, device_id=(other // ctx_size, lax.rem(other, ctx_size)), device_id_type=MESH_ID
        )
        return carry

    lax.fori_loop(1, devices, greet, 0)
    pl.semaphore_wait(barrier, devices - 1)


def chain_gather(src, dst, sems, d, c, levels):
    block_send, block_recv, core_send, core_recv, local = sems
    micro, span = src.shape[0], src.shape[1]
    z = c // 2
    sibling = c + 1 - 2 * lax.rem(c, 2)

    def block(origin, m):
        return dst.at[m, pl.ds(pl.multiple_of(origin * span, span), span)]

    def link(way, hop, m):
        step = 2 if way == 0 else -2
        origin = c - step * hop
        view = src.at[m] if hop == 0 else block(origin, m)
        return remote(view, block(origin, m), block_send.at[way, hop, m], block_recv.at[way, hop, m], d, c + step)

    def leaves(way, hop):
        if way == 0:
            return jnp.logical_and(z >= hop, z <= levels - 2)
        return jnp.logical_and(z + hop <= levels - 1, z >= 1)

    def arrives(way, hop):
        return z >= hop + 1 if way == 0 else z + hop + 1 <= levels - 1

    def slot_of(way, hop):
        return 1 + way * (levels - 1) + hop

    def core_copy(slot, origin, m):
        view = src.at[m] if slot == 0 else block(origin, m)
        return remote(view, block(origin, m), core_send.at[slot, m], core_recv.at[slot, m], d, sibling)

    def own_copy(m):
        return pltpu.make_async_copy(src.at[m], block(c, m), local.at[m])

    def start(m):
        for way in range(2):
            @pl.when(leaves(way, 0))
            def _(way=way):
                link(way, 0, m).start()

        core_copy(0, c, m).start()
        own_copy(m).start()

    def hop_step(hop, m):
        for way in range(2):
            step = 2 if way == 0 else -2

            @pl.when(arrives(way, hop))
            def _(way=way, step=step):
                link(way, hop, m).wait_recv()
                if hop + 1 <= levels - 2:
                    @pl.when(leaves(way, hop + 1))
                    def _():
                        link(way, hop + 1, m).start()

                core_copy(slot_of(way, hop), c - step * (hop + 1), m).start()

    def finish(m):
        own_copy(m).wait()
        core_copy(0, c, m).wait_send()
        core_copy(0, sibling, m).wait_recv()
        for way in range(2):
            step = 2 if way == 0 else -2
            for hop in range(levels - 1):
                @pl.when(leaves(way, hop))
                def _(way=way, hop=hop):
                    link(way, hop, m).wait_send()

                @pl.when(arrives(way, hop))
                def _(way=way, hop=hop, step=step):
                    slot = slot_of(way, hop)
                    core_copy(slot, c - step * (hop + 1), m).wait_send()
                    core_copy(slot, sibling - step * (hop + 1), m).wait_recv()

    return start, hop_step, finish


def chain_scratch(levels, micro):
    dma = pltpu.SemaphoreType.DMA
    return [
        dma((2, levels - 1, micro)),
        dma((2, levels - 1, micro)),
        dma((2 * levels - 1, micro)),
        dma((2 * levels - 1, micro)),
        dma((micro,)),
    ]


def greet_line(d, c, levels):
    barrier = pltpu.get_barrier_semaphore()
    z = c // 2
    sibling = c + 1 - 2 * lax.rem(c, 2)
    pl.semaphore_signal(barrier, inc=1, device_id=(d, sibling), device_id_type=MESH_ID)

    @pl.when(z >= 1)
    def _():
        pl.semaphore_signal(barrier, inc=1, device_id=(d, c - 2), device_id_type=MESH_ID)

    @pl.when(z <= levels - 2)
    def _():
        pl.semaphore_signal(barrier, inc=1, device_id=(d, c + 2), device_id_type=MESH_ID)

    peers = 1 + (z >= 1).astype(jnp.int32) + (z <= levels - 2).astype(jnp.int32)
    pl.semaphore_wait(barrier, peers)


def gather_kernel(
    dp_size,
    ctx_size,
    x,
    qkv,
    expand,
    dense,
    shrink,
    packed,
    x_all,
    panels,
    out_w,
    small,
    local_sem,
    small_sem,
    block_send,
    block_recv,
    core_send,
    core_recv,
    block_local,
    panel_send,
    panel_recv,
    share_send,
    share_recv,
    pass_send,
    pass_recv,
):
    d = lax.axis_index("dp")
    c = lax.axis_index("ctx")
    z = c // 2
    sibling = c + 1 - 2 * lax.rem(c, 2)
    x_mate = d + 1 - 2 * lax.rem(d, 2)
    y_mate = lax.rem(d + 2, 4)
    micro, span = x.shape[0], x.shape[1]
    devices = dp_size * ctx_size
    me = d * ctx_size + c
    rows = qkv.shape[0]
    unit = shrink.shape[0]
    levels = ctx_size // 2
    panel_rows = ctx_size * rows
    n_panels = 3 + dp_size

    greet_all(d, c, dp_size, ctx_size)

    def column_block(panel, target):
        if panel < 3:
            start = panel * (qkv.shape[1] // 3) + target * HEAD
            return qkv.at[:, pl.ds(pl.multiple_of(start, HEAD), HEAD)]
        start = (panel - 3) * ctx_size * unit + target * unit
        return expand.at[:, pl.ds(pl.multiple_of(start, HEAD), HEAD)]

    own_rows = pl.ds(pl.multiple_of((d * ctx_size + c) * rows, rows), rows)

    for panel in range(n_panels):
        pltpu.make_async_copy(
            column_block(panel, c), panels.at[panel, own_rows], local_sem.at[panel]
        ).start()

        def push(step, carry, panel=panel):
            target = lax.rem(c + step, ctx_size)
            remote(
                column_block(panel, target),
                panels.at[panel, own_rows],
                panel_send.at[panel],
                panel_recv.at[panel],
                d,
                target,
            ).start()
            return carry

        lax.fori_loop(1, ctx_size, push, 0)

    def shrink_rows(owner, offset, count):
        return out_w.at[pl.ds(pl.multiple_of(HEAD + owner * unit + offset, 16), count)]

    shrink_local = pltpu.make_async_copy(shrink, shrink_rows(d, 0, unit), local_sem.at[n_panels])
    shrink_local.start()
    for way, mate in ((0, x_mate), (1, y_mate)):
        remote(
            shrink, shrink_rows(d, 0, unit), share_send.at[n_panels, way], share_recv.at[n_panels, way], mate, c
        ).start()

    per_head = HEAD // rows
    head_of = (d * ctx_size + c) // per_head
    dense_rows = pl.ds(pl.multiple_of(lax.rem(c, per_head) * rows, rows), rows)
    dense_out = remote(dense, out_w.at[dense_rows], panel_send.at[n_panels], panel_recv.at[n_panels], d, head_of)
    dense_own = pltpu.make_async_copy(dense, out_w.at[dense_rows], local_sem.at[n_panels + 1])
    stays = head_of == c

    @pl.when(stays)
    def _():
        dense_own.start()

    @pl.when(jnp.logical_not(stays))
    def _():
        dense_out.start()

    x_start, x_hop, x_finish = chain_gather(
        x, x_all, (block_send, block_recv, core_send, core_recv, block_local), d, c, levels
    )
    for m in range(micro):
        x_start(m)

    small_copy = pltpu.make_async_copy(packed, small.at[me], local_sem.at[n_panels + 2])
    small_copy.start()

    def push_small(step, carry):
        other = lax.rem(me + step, devices)
        remote(
            packed,
            small.at[me],
            small_sem.at[0],
            small_sem.at[1],
            other // ctx_size,
            lax.rem(other, ctx_size),
        ).start()
        return carry

    lax.fori_loop(1, devices, push_small, 0)

    def group_rows(owner, offset, count):
        return pl.ds(pl.multiple_of(owner * panel_rows + offset, 16), count)

    def panel_share(panel, way, mate):
        view = panels.at[panel, group_rows(d, 0, panel_rows)]
        return remote(view, view, share_send.at[panel, way], share_recv.at[panel, way], mate, c)

    def panel_step(panel):
        pltpu.make_async_copy(column_block(panel, c), panels.at[panel, own_rows], local_sem.at[panel]).wait()
        whole = panels.at[panel, group_rows(d, 0, (ctx_size - 1) * rows)]
        remote(whole, whole, panel_send.at[panel], panel_recv.at[panel], d, sibling).wait_recv()
        panel_share(panel, 0, x_mate).start()
        panel_share(panel, 1, y_mate).start()

    half = panel_rows // 2

    def panel_pass(panel, way):
        owner, mate = ((x_mate, y_mate), (y_mate, x_mate))[way]
        view = panels.at[panel, group_rows(owner, way * half, half)]
        return remote(view, view, pass_send.at[panel, way], pass_recv.at[panel, way], mate, c)

    def panel_forward(panel):
        for way, owner in ((0, x_mate), (1, y_mate)):
            view = panels.at[panel, group_rows(owner, 0, panel_rows)]
            remote(view, view, share_send.at[panel, way], share_recv.at[panel, way], owner, c).wait_recv()
            panel_pass(panel, way).start()

    def shrink_share_wait(way, owner):
        view = shrink_rows(owner, 0, unit)
        remote(view, view, share_send.at[n_panels, way], share_recv.at[n_panels, way], owner, c).wait_recv()

    def shrink_pass(way):
        owner, mate = ((x_mate, y_mate), (y_mate, x_mate))[way]
        view = shrink_rows(owner, way * (unit // 2), unit // 2)
        return remote(view, view, pass_send.at[n_panels, way], pass_recv.at[n_panels, way], mate, c)

    source = c // (ctx_size // dp_size)
    at_source = d == source
    from_x = x_mate == source
    from_y = y_mate == source
    head_rows = out_w.at[pl.ds(0, HEAD)]
    half_head = HEAD // 2

    def dense_share(way, mate):
        view = out_w.at[pl.ds(way * half_head, half_head)]
        return remote(view, view, share_send.at[n_panels + 1, way], share_recv.at[n_panels + 1, way], mate, c)

    owns_share = jnp.logical_and(at_source, stays)

    def dense_gather_step():
        @pl.when(owns_share)
        def _():
            dense_own.wait()
            view = out_w.at[pl.ds(0, (per_head - 1) * rows)]
            remote(view, view, panel_send.at[n_panels], panel_recv.at[n_panels], d, sibling).wait_recv()

        @pl.when(jnp.logical_and(at_source, jnp.logical_not(stays)))
        def _():
            remote(head_rows, head_rows, panel_send.at[n_panels], panel_recv.at[n_panels], d, sibling).wait_recv()

        @pl.when(at_source)
        def _():
            dense_share(0, x_mate).start()
            dense_share(1, y_mate).start()

    def dense_forward_step():
        @pl.when(from_x)
        def _():
            dense_share(0, x_mate).wait_recv()
            dense_share(0, y_mate).start()

        @pl.when(from_y)
        def _():
            dense_share(1, y_mate).wait_recv()
            dense_share(1, x_mate).start()

    def dense_last_step():
        @pl.when(across)
        def _():
            dense_share(0, y_mate).wait_recv()
            dense_share(0, x_mate).start()
            dense_share(1, x_mate).wait_recv()
            dense_share(1, y_mate).start()

    across = jnp.logical_not(jnp.logical_or(at_source, jnp.logical_or(from_x, from_y)))

    for panel in range(3):
        panel_step(panel)
    shrink_share_wait(0, x_mate)
    shrink_pass(0).start()
    shrink_share_wait(1, y_mate)
    shrink_pass(1).start()
    for panel in range(3, n_panels):
        panel_step(panel)
    dense_gather_step()
    panel_forward(0)
    panel_forward(1)
    x_hop(0, 0)
    panel_forward(2)
    x_hop(0, 1)
    dense_forward_step()
    panel_forward(3)
    panel_forward(4)
    x_hop(1, 0)
    panel_forward(5)
    x_hop(1, 1)
    dense_last_step()
    panel_forward(6)
    for hop in range(2, levels - 1):
        for m in range(micro):
            x_hop(hop, m)

    for panel in range(n_panels):
        for way, mate in ((0, x_mate), (1, y_mate)):
            panel_share(panel, way, mate).wait_send()
            panel_pass(panel, way).wait_send()
        for way in range(2):
            diagonal = 3 - d
            view = panels.at[panel, group_rows(diagonal, way * half, half)]
            remote(view, view, pass_send.at[panel, way], pass_recv.at[panel, way], x_mate, c).wait_recv()
        whole = panels.at[panel, group_rows(d, 0, (ctx_size - 1) * rows)]
        remote(whole, whole, panel_send.at[panel], panel_recv.at[panel], x_mate, c).wait_send()
    shrink_local.wait()
    for way in range(2):
        mate = (x_mate, y_mate)[way]
        remote(
            shrink, shrink_rows(d, 0, unit), share_send.at[n_panels, way], share_recv.at[n_panels, way], mate, c
        ).wait_send()
        shrink_pass(way).wait_send()
        view = shrink_rows(3 - d, way * (unit // 2), unit // 2)
        remote(view, view, pass_send.at[n_panels, way], pass_recv.at[n_panels, way], mate, c).wait_recv()

    @pl.when(jnp.logical_not(stays))
    def _():
        dense_out.wait_send()

    @pl.when(at_source)
    def _():
        dense_share(0, x_mate).wait_send()
        dense_share(1, y_mate).wait_send()

    @pl.when(from_x)
    def _():
        dense_share(0, y_mate).wait_send()
        dense_share(1, y_mate).wait_recv()

    @pl.when(from_y)
    def _():
        dense_share(1, x_mate).wait_send()
        dense_share(0, x_mate).wait_recv()

    @pl.when(across)
    def _():
        dense_share(0, x_mate).wait_send()
        dense_share(1, y_mate).wait_send()

    for m in range(micro):
        x_finish(m)

    small_copy.wait()
    rest = small.at[pl.ds(0, devices - 1)]
    remote(rest, rest, small_sem.at[0], small_sem.at[1], d, sibling).wait()


def gather_call(dp_size, ctx_size, x, qkv, expand, dense, shrink, packed):
    micro, span, width = x.shape
    rows = qkv.shape[0]
    n_panels = 3 + dp_size
    levels = ctx_size // 2
    devices = dp_size * ctx_size
    dma = pltpu.SemaphoreType.DMA
    out_shape = (
        jax.ShapeDtypeStruct((micro, ctx_size * span, width), x.dtype),
        jax.ShapeDtypeStruct((n_panels, devices * rows, HEAD), x.dtype),
        jax.ShapeDtypeStruct((HEAD + dp_size * shrink.shape[0], width), x.dtype),
        jax.ShapeDtypeStruct((devices,) + packed.shape, x.dtype),
    )
    anywhere = pl.BlockSpec(memory_space=pl.ANY)
    return pl.pallas_call(
        functools.partial(gather_kernel, dp_size, ctx_size),
        out_shape=out_shape,
        in_specs=[anywhere] * 6,
        out_specs=(anywhere,) * 4,
        scratch_shapes=[
            dma((n_panels + 3,)),
            dma((2,)),
            *chain_scratch(levels, micro),
            dma((n_panels + 1,)),
            dma((n_panels + 1,)),
            dma((n_panels + 2, 2)),
            dma((n_panels + 2, 2)),
            dma((n_panels + 2, 2)),
            dma((n_panels + 2, 2)),
        ],
        compiler_params=pltpu.CompilerParams(collective_id=1, has_side_effects=True),
        name="gather_all",
    )(x, qkv, expand, dense, shrink, packed)


def add_into(dst, srcs, rows):
    chunk = 16 if dst.shape[-1] > 1024 else 64

    def step(index, carry):
        at = pl.ds(pl.multiple_of(index * chunk, 16), chunk)
        total = srcs[0][at, :].astype(jnp.float32)
        for src in srcs[1:]:
            total = total + src[at, :].astype(jnp.float32)
        dst[at, :] = total.astype(dst.dtype)
        return carry

    lax.fori_loop(0, rows // chunk, step, 0)


TILE = 256


def turn_tables(length):
    freqs = np.exp(np.arange(ROT // 2) * (-2.0 * math.log(10000.0) / ROT))
    angles = np.arange(length)[:, None] * freqs[None, :]
    cos, sin = np.cos(angles), np.sin(angles)
    rest = np.zeros((length, 128 - ROT))
    return (
        jnp.asarray(np.concatenate([cos, cos, rest + 1.0], axis=1), jnp.float32),
        jnp.asarray(np.concatenate([-sin, sin, rest], axis=1), jnp.float32),
    )


def turn(head, cos, sin):
    front = head[:, :128]
    lane = lax.broadcasted_iota(jnp.int32, front.shape, 1)
    other = jnp.where(lane < ROT // 2, pltpu.roll(front, 128 - ROT // 2, 1), pltpu.roll(front, ROT // 2, 1))
    return jnp.concatenate([front * cos + other * sin, head[:, 128:]], axis=1)


def dot_nn(a, b):
    return lax.dot_general(a, b, (((1,), (0,)), ((), ())), preferred_element_type=jnp.float32)


def dot_nt(a, b):
    return lax.dot_general(a, b, (((1,), (1,)), ((), ())), preferred_element_type=jnp.float32)


def dot_tn(a, b):
    return lax.dot_general(a, b, (((0,), (0,)), ((), ())), preferred_element_type=jnp.float32)


def forward_kernel(
    tiles,
    levels,
    prefix,
    x,
    own_g,
    panels_in,
    out_w_in,
    gains,
    qkv_shift,
    expand_shift,
    cos,
    sin,
    hidden_attn,
    hidden_mlp,
    heads,
    probs,
    features,
    slopes,
    partial,
    g_all,
    first_out,
    panels,
    out_w,
    weight_sem,
    head_rows,
    acts,
    board,
    out_core,
    out_chain,
    core_send,
    core_recv,
    chain_send,
    chain_recv,
    store_sem,
    *g_sems,
):
    step = pl.program_id(0)
    micro = own_g.shape[0]
    d = lax.axis_index("dp")
    c = lax.axis_index("ctx")
    g_start, g_hop, g_finish = chain_gather(own_g, g_all, g_sems, d, c, levels)

    core = lax.rem(c, 2)
    span = board.shape[2]

    def own_block(level):
        return board.at[level, core]

    def core_copy(level):
        return remote(
            board.at[level, 1 - core],
            out_core.at[level],
            core_send.at[level],
            core_recv.at[level],
            d,
            c + 1 - 2 * core,
        )

    chain_open, chain_round, chain_end, chain_finish = chain_reduce(
        own_block, out_chain, (chain_send, chain_recv), d, c, levels
    )

    def out_store(level):
        return pltpu.make_async_copy(own_block(level), first_out, store_sem.at[0])

    panels_copy = pltpu.make_async_copy(panels_in, panels, weight_sem.at[0])
    out_w_copy = pltpu.make_async_copy(out_w_in, out_w, weight_sem.at[1])

    @pl.when(step == 0)
    def _():
        greet_line(d, c, levels)
        for m in range(micro):
            g_start(m)
        panels_copy.start()
        out_w_copy.start()
        panels_copy.wait()

    @pl.when(step == tiles)
    def _():
        out_w_copy.wait()

    for place, level in enumerate(outside_in(levels)):
        @pl.when(step == tiles + 1 + place)
        def _(level=level):
            core_copy(level).start()

        @pl.when(step == tiles + 2 + place)
        def _(level=level):
            core_copy(level).wait_recv()
            add_into(own_block(level), (own_block(level), out_core.at[level]), span)
            chain_open(level)

    @pl.when(step == 12)
    def _():
        chain_round(1)

    last = 4 * tiles - 1
    for at, hop, m in ((4, 0, 0), (7, 0, 1), (11, 1, 0), (14, 1, 1)):
        @pl.when(step == at)
        def _(hop=hop, m=m):
            g_hop(hop, m)

    seq = step // (2 * tiles)
    phase = lax.rem(step, 2 * tiles) // tiles
    tile = lax.rem(step, tiles)
    tile = jnp.where(phase == 0, tile, jnp.where(lax.rem(tile, 2) == 0, tiles - 1 - tile // 2, tile // 2))
    rows = pl.ds(pl.multiple_of(tile * TILE, TILE), TILE)
    n_expand = panels.shape[0] - 3
    scale = 1.0 / math.sqrt(HEAD)

    @pl.when(phase == 0)
    def _():
        values_in = x[...].astype(jnp.float32)
        centered = values_in - jnp.mean(values_in, axis=1, keepdims=True)
        normal = centered * lax.rsqrt(jnp.mean(centered * centered, axis=1, keepdims=True) + 1e-05)
        hidden_attn[...] = (normal * gains[0:1, :] + gains[1:2, :]).astype(jnp.bfloat16)
        hidden_mlp[...] = (normal * gains[2:3, :] + gains[3:4, :]).astype(jnp.bfloat16)
        wide = jnp.concatenate([panels[part] for part in range(3)], axis=1)
        all_joined = dot_nn(hidden_attn[...], wide) + qkv_shift[...]
        for part in range(3):
            joined = all_joined[:, part * HEAD : (part + 1) * HEAD]
            if part < 2:
                joined = turn(joined, cos[rows, :], sin[rows, :])
            joined = joined.astype(jnp.bfloat16)
            heads[part] = joined
            head_rows[part, rows, :] = joined
        for part in range(0, n_expand, 2):
            columns = slice(part * HEAD, (part + 2) * HEAD)
            wide = jnp.concatenate([panels[3 + part], panels[4 + part]], axis=1)
            expanded = dot_nn(hidden_mlp[...], wide) + expand_shift[:, columns]
            cdf = 0.5 * (1.0 + lax.erf(expanded * (1.0 / math.sqrt(2.0))))
            acts[rows, columns] = (expanded * cdf).astype(jnp.bfloat16)
            bell = jnp.exp(-0.5 * expanded * expanded) * (1.0 / math.sqrt(2.0 * math.pi))
            slopes[:, columns] = (cdf + expanded * bell).astype(jnp.bfloat16)

    @pl.when(phase == 1)
    def _():
        scores = dot_nt(head_rows[0, rows, :], head_rows[1]) * scale
        key_at = lax.broadcasted_iota(jnp.int32, scores.shape, 1)
        query_at = lax.broadcasted_iota(jnp.int32, scores.shape, 0) + tile * TILE
        allowed = jnp.logical_or(key_at <= query_at, key_at < prefix[seq])
        scores = jnp.where(allowed, scores, -1e30)
        expo = jnp.exp(scores - jnp.max(scores, axis=1, keepdims=True))
        low_probs = (expo * (1.0 / jnp.sum(expo, axis=1, keepdims=True))).astype(jnp.bfloat16)
        probs[0] = low_probs
        features[:, :HEAD] = dot_nn(low_probs, head_rows[2]).astype(jnp.bfloat16)
        features[:, HEAD:] = acts[rows, :]
        width = out_w.shape[1]
        for start in range(0, width, 1024):
            columns = slice(start, start + 1024)
            value = dot_nn(features[...], out_w[:, columns]).astype(jnp.bfloat16)

            @pl.when(seq == 0)
            def _(columns=columns, value=value):
                for parity in range(2):
                    board[tile, parity, :, columns] = value[parity * span : (parity + 1) * span]

            @pl.when(seq > 0)
            def _(columns=columns, value=value):
                partial[:, columns] = value

    @pl.when(step == last)
    def _():
        chain_round(2)
        for m in range(micro):
            for hop in range(2, levels - 1):
                g_hop(hop, m)
        chain_end(out_store)
        for m in range(micro):
            g_finish(m)
        for level in range(levels):
            core_copy(level).wait_send()
        chain_finish(out_store)


def whole_spec(array):
    zeros = (0,) * array.ndim
    return pl.BlockSpec(array.shape, lambda step: zeros, pipeline_mode=pl.Buffered(1))


def forward_call(levels, prefix, x, own_g, panels, out_w, gains, qkv_shift, expand_shift, cos, sin):
    tokens, width = x.shape
    length = cos.shape[0]
    tiles = length // TILE
    steps = 2 * tokens // TILE
    hidden = expand_shift.shape[1]
    span = own_g.shape[1]
    dma = pltpu.SemaphoreType.DMA

    def early(step):
        seq, at = step // (2 * tiles), lax.rem(step, 2 * tiles)
        return seq * tiles + jnp.minimum(at, tiles - 1)

    def late(step):
        seq, at = step // (2 * tiles), lax.rem(step, 2 * tiles)
        place = jnp.maximum(at - tiles, 0)
        return seq * tiles + jnp.where(lax.rem(place, 2) == 0, tiles - 1 - place // 2, place // 2)

    def last_only(step):
        return jnp.where(step < 2 * tiles, tiles - 1, late(step) - tiles)

    kind = jnp.bfloat16
    return pl.pallas_call(
        functools.partial(forward_kernel, tiles, levels),
        grid=(steps,),
        out_shape=(
            jax.ShapeDtypeStruct((tokens, width), kind),
            jax.ShapeDtypeStruct((tokens, width), kind),
            jax.ShapeDtypeStruct((3, tokens, HEAD), kind),
            jax.ShapeDtypeStruct((tokens // length, length, length), kind),
            jax.ShapeDtypeStruct((tokens, HEAD + hidden), kind),
            jax.ShapeDtypeStruct((tokens, hidden), kind),
            jax.ShapeDtypeStruct((length, width), kind),
            jax.ShapeDtypeStruct((tokens // length, length, width), kind),
            jax.ShapeDtypeStruct((span, width), kind),
        ),
        in_specs=[
            pl.BlockSpec(memory_space=pltpu.SMEM),
            pl.BlockSpec((TILE, width), lambda step: (early(step), 0)),
            pl.BlockSpec(memory_space=pl.ANY),
            pl.BlockSpec(memory_space=pl.ANY),
            pl.BlockSpec(memory_space=pl.ANY),
            whole_spec(gains),
            whole_spec(qkv_shift),
            whole_spec(expand_shift),
            whole_spec(cos),
            whole_spec(sin),
        ],
        out_specs=(
            pl.BlockSpec((TILE, width), lambda step: (early(step), 0)),
            pl.BlockSpec((TILE, width), lambda step: (early(step), 0)),
            pl.BlockSpec((3, TILE, HEAD), lambda step: (0, early(step), 0)),
            pl.BlockSpec((1, TILE, length), lambda step: (late(step) // tiles, lax.rem(late(step), tiles), 0)),
            pl.BlockSpec((TILE, HEAD + hidden), lambda step: (late(step), 0)),
            pl.BlockSpec((TILE, hidden), lambda step: (early(step), 0)),
            pl.BlockSpec((TILE, width), lambda step: (last_only(step), 0)),
            pl.BlockSpec(memory_space=pl.ANY),
            pl.BlockSpec(memory_space=pl.ANY),
        ),
        scratch_shapes=[
            pltpu.VMEM(panels.shape, kind),
            pltpu.VMEM(out_w.shape, kind),
            dma((2,)),
            pltpu.VMEM((3, length, HEAD), kind),
            pltpu.VMEM((length, hidden), kind),
            pltpu.VMEM((levels, 2, span, width), kind),
            pltpu.VMEM((levels, span, width), kind),
            pltpu.VMEM((2, levels - 1, span, width), kind),
            dma((levels,)),
            dma((levels,)),
            dma((2, levels)),
            dma((2, levels)),
            dma((1,)),
            *chain_scratch(levels, tokens // length),
        ],
        compiler_params=pltpu.CompilerParams(
            collective_id=3, has_side_effects=True, vmem_limit_bytes=60 * 1024 * 1024
        ),
        cost_estimate=pl.CostEstimate(
            flops=2 * tokens * width * (2 * hidden + 4 * HEAD) + 4 * tokens * length * HEAD,
            bytes_accessed=64 * 1024 * 1024,
            transcendentals=0,
        ),
        name="forward_part",
    )(prefix, x, own_g, panels, out_w, gains, qkv_shift, expand_shift, cos, sin)


def outside_in(levels):
    return [levels - 1 - place // 2 if place % 2 == 0 else place // 2 for place in range(levels)]


def chain_reduce(own, recv, sems, d, c, levels):
    chain_send, chain_recv = sems
    z = c // 2
    span = recv.shape[2]

    def copy(way, level):
        return remote(
            own(level),
            recv.at[way, level - 1 + way],
            chain_send.at[way, level],
            chain_recv.at[way, level],
            d,
            c + (2 if way == 0 else -2),
        )

    def sends(way, level):
        return z < level if way == 0 else z > level

    def hears(way, level):
        if way == 0:
            return jnp.logical_and(z >= 1, z <= level)
        return jnp.logical_and(z <= levels - 2, z >= level)

    def add(way, level):
        copy(way, level).wait_recv()
        add_into(own(level), (own(level), recv.at[way, level - 1 + way]), span)

    def open_level(level):
        for way, place in ((0, 0), (1, levels - 1)):
            if place != level:
                @pl.when(z == place)
                def _(way=way):
                    copy(way, level).start()

    def turn_round(index):
        for level in range(levels):
            for way in range(2):
                behind = levels - 1 - level if way == 0 else level
                place = index - behind if way == 0 else levels - 1 - (index - behind)
                if behind < index and (place < level if way == 0 else place > level):
                    @pl.when(z == place)
                    def _(way=way, level=level):
                        add(way, level)
                        copy(way, level).start()

    def end(store):
        for level in range(levels):
            for way in range(2):
                if 0 <= level - 1 + way < levels - 1:
                    @pl.when(jnp.logical_and(z == level, hears(way, level)))
                    def _(way=way, level=level):
                        add(way, level)

            @pl.when(z == level)
            def _(level=level):
                store(level).start()

    def finish(store):
        for level in range(levels):
            for way in range(2):
                if 0 <= level - 1 + way < levels - 1:
                    @pl.when(sends(way, level))
                    def _(way=way, level=level):
                        copy(way, level).wait_send()

        store(0).wait()

    return open_level, turn_round, end, finish


def square_sum(first, passing, recv, last, final, sems, d, c, count):
    first_send, first_recv, last_send, last_recv = sems
    x_mate = d + 1 - 2 * lax.rem(d, 2)
    y_mate = lax.rem(d + 2, 4)
    mates = ((x_mate, y_mate), (y_mate, x_mate))

    def first_copy(way, slot):
        return remote(
            first(way, slot), recv.at[way, slot], first_send.at[way, slot], first_recv.at[way, slot], mates[way][0], c
        )

    def last_copy(way):
        return remote(passing(way), last.at[way], last_send.at[way], last_recv.at[way], mates[way][1], c)

    def pass_on(way):
        first_copy(way, 1).wait_recv()
        add_into(passing(way), (passing(way), recv.at[way, 1]), count)
        last_copy(way).start()

    def arrive(way):
        first_copy(way, 0).wait_recv()
        last_copy(way).wait_recv()

    def add_final(way, start, rows):
        at = pl.ds(start, rows)
        own = final(way).at[at]
        add_into(own, (own, recv.at[way, 0, at], last.at[way, at]), rows)

    def finish():
        for way in range(2):
            first_copy(way, 0).wait_send()
            first_copy(way, 1).wait_send()
            last_copy(way).wait_send()

    return first_copy, pass_on, arrive, add_final, finish


def square_scratch():
    dma = pltpu.SemaphoreType.DMA
    return [dma((2, 2)), dma((2, 2)), dma((2,)), dma((2,))]


def backward_kernel(
    tiles,
    dp_size,
    ctx_size,
    g,
    x,
    panels_in,
    out_w_in,
    gains,
    cos,
    sin,
    heads,
    probs,
    slopes,
    features,
    grads,
    grad_expanded,
    grad_joined,
    combined,
    norm_sums,
    joined_sums,
    expand_sums,
    back_out,
    shrink_out,
    dense_out,
    panels,
    out_w,
    weight_sem,
    grad_queries,
    grad_keys,
    grad_values,
    board,
    back_core,
    back_chain,
    left,
    right,
    out_own,
    out_recv,
    out_last,
    dense_own,
    dense_recv,
    left_sem,
    right_sem,
    core_send,
    core_recv,
    chain_send,
    chain_recv,
    first_send,
    first_recv,
    last_send,
    last_recv,
    dense_send,
    dense_sem,
    store_sem,
):
    step = pl.program_id(0)
    seq = step // (2 * tiles)
    phase = lax.rem(step, 2 * tiles) // tiles
    tile = lax.rem(step, tiles)
    tile = jnp.where(phase == 0, tile, jnp.where(lax.rem(tile, 2) == 0, tiles - 1 - tile // 2, tile // 2))
    rows = pl.ds(pl.multiple_of(tile * TILE, TILE), TILE)
    n_expand = panels.shape[0] - 3
    width = out_w.shape[1]
    scale = 1.0 / math.sqrt(HEAD)

    d = lax.axis_index("dp")
    c = lax.axis_index("ctx")
    z = c // 2
    core = lax.rem(c, 2)
    sibling = c + 1 - 2 * core
    x_mate = d + 1 - 2 * lax.rem(d, 2)
    y_mate = lax.rem(d + 2, 4)
    diagonal = 3 - d
    levels = ctx_size // 2
    me = d * ctx_size + c
    span = board.shape[2]
    share = dense_out.shape[0]
    unit = (features.shape[1] - HEAD) // dp_size
    out_half = unit // 2
    head_half = HEAD // 2

    def left_copy(index):
        if index == 0:
            columns = pl.ds(0, HEAD)
        else:
            owner = (diagonal, x_mate, y_mate, d)[index - 1]
            columns = pl.ds(pl.multiple_of(HEAD + owner * unit, HEAD), unit)
        return pltpu.make_async_copy(features.at[:, columns], left.at[index % 2], left_sem.at[index % 2])

    right_copy = pltpu.make_async_copy(grads, right, right_sem.at[0])

    def compute(index):
        if index < dp_size:
            left_copy(index + 1).start()
        left_copy(index).wait()
        target = dense_own if index == 0 else out_own.at[index - 1]
        for start in range(0, width, 1024):
            columns = slice(start, start + 1024)
            target[:, columns] = dot_tn(left[index % 2], right[:, columns]).astype(jnp.bfloat16)

    def out_rows(index, way):
        return out_own.at[index, pl.ds(way * out_half, out_half)]

    first_copy, pass_on, arrive, add_final, square_finish = square_sum(
        lambda way, slot: out_rows(0 if slot == 1 else 1 + way, way),
        lambda way: out_rows(2 - way, way),
        out_recv,
        out_last,
        lambda way: out_rows(3, way),
        (first_send, first_recv, last_send, last_recv),
        d,
        c,
        out_half,
    )

    def out_store(way):
        return pltpu.make_async_copy(
            out_rows(3, way), shrink_out.at[pl.ds(way * out_half, out_half)], store_sem.at[way]
        )

    source = c // (ctx_size // dp_size)
    at_source = d == source
    from_x = x_mate == source
    from_y = y_mate == source
    across = diagonal == source
    per_head = HEAD // share

    def dense_half(way):
        return dense_own.at[pl.ds(way * head_half, head_half)]

    def dense_copy(way, mate):
        return remote(dense_half(way), dense_recv.at[way], dense_send.at[way], dense_sem.at[way], mate, c)

    def dense_add(way, mate):
        dense_copy(way, mate).wait_recv()
        add_into(dense_half(way), (dense_half(way), dense_recv.at[way]), head_half)

    def dense_open():
        @pl.when(from_y)
        def _():
            dense_copy(0, x_mate).start()

        @pl.when(from_x)
        def _():
            dense_copy(1, y_mate).start()

    def dense_second():
        @pl.when(across)
        def _():
            dense_add(0, y_mate)
            dense_copy(0, y_mate).start()
            dense_add(1, x_mate)
            dense_copy(1, x_mate).start()

    def dense_third():
        @pl.when(from_x)
        def _():
            dense_add(0, x_mate)
            dense_copy(0, x_mate).start()

        @pl.when(from_y)
        def _():
            dense_add(1, y_mate)
            dense_copy(1, y_mate).start()

    first_owner = lax.rem(c, ctx_size // per_head) * per_head

    def dense_chunk(piece):
        return dense_own.at[pl.ds(piece * share, share)]

    def dense_send_out(piece):
        return remote(
            dense_chunk(piece), dense_out, dense_send.at[2 + piece], dense_sem.at[2], d, first_owner + piece
        )

    def dense_store(piece):
        return pltpu.make_async_copy(dense_chunk(piece), dense_out, store_sem.at[2])

    def dense_fourth():
        @pl.when(at_source)
        def _():
            dense_add(0, x_mate)
            dense_add(1, y_mate)
            for piece in range(per_head):
                @pl.when(first_owner + piece == c)
                def _(piece=piece):
                    dense_store(piece).start()

                @pl.when(first_owner + piece != c)
                def _(piece=piece):
                    dense_send_out(piece).start()

    def dense_finish():
        @pl.when(jnp.logical_or(jnp.logical_or(from_y, across), from_x))
        def _():
            dense_copy(0, x_mate).wait_send()
            dense_copy(1, x_mate).wait_send()

        for piece in range(per_head):
            @pl.when(jnp.logical_and(at_source, first_owner + piece != c))
            def _(piece=piece):
                dense_send_out(piece).wait_send()

        stays = me // per_head == c

        @pl.when(stays)
        def _():
            dense_store(0).wait()

        @pl.when(jnp.logical_not(stays))
        def _():
            dense_send_out(0).wait_recv()

    def own_block(level):
        return board.at[level, core]

    def core_copy(level):
        return remote(
            board.at[level, 1 - core], back_core.at[level], core_send.at[level], core_recv.at[level], d, sibling
        )

    def core_add(level):
        core_copy(level).wait_recv()
        add_into(own_block(level), (own_block(level), back_core.at[level]), span)

    chain_open, chain_round, chain_end, chain_finish = chain_reduce(
        own_block, back_chain, (chain_send, chain_recv), d, c, levels
    )

    def back_store(level):
        return pltpu.make_async_copy(own_block(level), back_out, store_sem.at[3])

    def at(when):
        return pl.when(step == when)

    panels_copy = pltpu.make_async_copy(panels_in, panels, weight_sem.at[0])
    out_w_copy = pltpu.make_async_copy(out_w_in, out_w, weight_sem.at[1])

    @at(0)
    def _():
        out_w_copy.start()
        greet_all(d, c, dp_size, ctx_size)
        left_copy(0).start()
        right_copy.start()
        panels_copy.start()
        out_w_copy.wait()
        norm_sums[...] = jnp.zeros_like(norm_sums)
        joined_sums[...] = jnp.zeros_like(joined_sums)
        expand_sums[...] = jnp.zeros_like(expand_sums)

    @at(1)
    def _():
        right_copy.wait()
        compute(0)
        dense_open()

    @at(2)
    def _():
        compute(1)
        first_copy(0, 1).start()
        first_copy(1, 1).start()

    @at(3)
    def _():
        compute(2)
        first_copy(0, 0).start()
        compute(3)
        first_copy(1, 0).start()

    @at(4)
    def _():
        panels_copy.wait()
        compute(4)

    for place, level in enumerate(outside_in(levels)):
        @at(tiles + 1 + place)
        def _(level=level):
            core_copy(level).start()

        @at(tiles + 2 + place)
        def _(level=level):
            core_add(level)
            chain_open(level)

    @at(6)
    def _():
        dense_second()

    @at(7)
    def _():
        pass_on(0)
        pass_on(1)

    @at(10)
    def _():
        chain_round(1)
        dense_third()

    @at(13)
    def _():
        chain_round(2)
        for way in range(2):
            arrive(way)
            add_final(way, 0, out_half)
            out_store(way).start()

    @at(14)
    def _():
        dense_fourth()

    @pl.when(phase == 0)
    def _():
        low_probs = probs[0]
        own = dot_nt(g[...], out_w[:HEAD, :]).astype(jnp.bfloat16)
        grad_probs = dot_nt(own, heads[2])
        wide = low_probs.astype(jnp.float32)
        delta = jnp.sum(wide * grad_probs, axis=1, keepdims=True)
        grad_scores = (wide * (grad_probs - delta)).astype(jnp.bfloat16)
        grad_queries[rows, :] = dot_nn(grad_scores, heads[1]) * scale
        more_keys = dot_tn(grad_scores, heads[0, rows, :]) * scale
        more_values = dot_tn(low_probs, own)

        @pl.when(tile == 0)
        def _():
            grad_keys[...] = more_keys
            grad_values[...] = more_values

        @pl.when(tile > 0)
        def _():
            grad_keys[...] += more_keys
            grad_values[...] += more_values

    @pl.when(phase == 1)
    def _():
        grad = dot_nt(g[...], out_w[HEAD:, :])
        grad = (grad * slopes[...].astype(jnp.float32)).astype(jnp.bfloat16)
        grad_expanded[...] = grad
        expand_sums[...] += jnp.sum(grad.astype(jnp.float32), axis=0, keepdims=True)
        cos_rows, sin_rows = cos[rows, :], -sin[rows, :]
        parts = (
            turn(grad_queries[rows, :], cos_rows, sin_rows),
            turn(grad_keys[rows, :], cos_rows, sin_rows),
            grad_values[rows, :],
        )
        for part in range(3):
            columns = slice(part * HEAD, (part + 1) * HEAD)
            joined = parts[part].astype(jnp.bfloat16)
            grad_joined[:, columns] = joined
            joined_sums[:, columns] += jnp.sum(joined.astype(jnp.float32), axis=0, keepdims=True)
        values_in = x[...].astype(jnp.float32)
        mean = jnp.mean(values_in, axis=1, keepdims=True)
        centered = values_in - mean
        spread = lax.rsqrt(jnp.mean(centered * centered, axis=1, keepdims=True) + 1e-05)
        for start in range(0, width, 1024):
            columns = slice(start, start + 1024)
            normal = (x[:, columns].astype(jnp.float32) - mean) * spread
            wide = jnp.concatenate([panels[part, columns, :] for part in range(3)], axis=1)
            total = dot_nt(grad_joined[...], wide)
            wide = jnp.concatenate([panels[3 + part, columns, :] for part in range(n_expand)], axis=1)
            other = dot_nt(grad_expanded[...], wide)
            for row, value in ((0, total * normal), (1, total), (2, other * normal), (3, other)):
                norm_sums[row : row + 1, columns] += jnp.sum(value, axis=0, keepdims=True)
            value = (total * gains[0:1, columns] + other * gains[2:3, columns]).astype(jnp.bfloat16)

            @pl.when(seq == 0)
            def _(columns=columns, value=value):
                for parity in range(2):
                    board[tile, parity, :, columns] = value[parity * span : (parity + 1) * span]

            @pl.when(seq > 0)
            def _(columns=columns, value=value):
                combined[:, columns] = value

    @at(4 * tiles - 1)
    def _():
        chain_end(back_store)
        square_finish()
        for way in range(2):
            out_store(way).wait()
        dense_finish()
        for level in range(levels):
            core_copy(level).wait_send()
        chain_finish(back_store)


def backward_call(dp_size, ctx_size, g, x, panels, out_w, gains, cos, sin, heads, probs, slopes, features):
    tokens, width = x.shape
    length = cos.shape[0]
    tiles = length // TILE
    steps = 2 * tokens // TILE
    hidden = slopes.shape[1]
    levels = ctx_size // 2
    span = length // ctx_size
    unit = hidden // dp_size
    share = width // (dp_size * ctx_size)
    dma = pltpu.SemaphoreType.DMA
    vmem = pltpu.VMEM

    def first(step):
        seq, at = step // (2 * tiles), lax.rem(step, 2 * tiles)
        return seq * tiles + jnp.minimum(at, tiles - 1)

    def mixed_order(place):
        return jnp.where(lax.rem(place, 2) == 0, tiles - 1 - place // 2, place // 2)

    def second(step):
        seq, at = step // (2 * tiles), lax.rem(step, 2 * tiles)
        return seq * tiles + mixed_order(jnp.maximum(at - tiles, 0))

    def both(step):
        seq, at = step // (2 * tiles), lax.rem(step, 2 * tiles)
        return seq * tiles + jnp.where(at < tiles, at, mixed_order(at - tiles))

    def late(step):
        return jnp.where(step < 2 * tiles, mixed_order(0), second(step) - tiles)

    kind = jnp.bfloat16
    fixed = lambda step: (0, 0)
    anywhere = pl.BlockSpec(memory_space=pl.ANY)
    return pl.pallas_call(
        functools.partial(backward_kernel, tiles, dp_size, ctx_size),
        grid=(steps,),
        out_shape=(
            jax.ShapeDtypeStruct((tokens, hidden), kind),
            jax.ShapeDtypeStruct((tokens, 3 * HEAD), kind),
            jax.ShapeDtypeStruct((length, width), kind),
            jax.ShapeDtypeStruct((8, width), jnp.float32),
            jax.ShapeDtypeStruct((1, 3 * HEAD), jnp.float32),
            jax.ShapeDtypeStruct((1, hidden), jnp.float32),
            jax.ShapeDtypeStruct((span, width), kind),
            jax.ShapeDtypeStruct((unit, width), kind),
            jax.ShapeDtypeStruct((share, width), kind),
        ),
        in_specs=[
            pl.BlockSpec((TILE, width), lambda step: (both(step), 0)),
            pl.BlockSpec((TILE, width), lambda step: (second(step), 0)),
            pl.BlockSpec(memory_space=pl.ANY),
            pl.BlockSpec(memory_space=pl.ANY),
            whole_spec(gains),
            whole_spec(cos),
            whole_spec(sin),
            pl.BlockSpec((3, length, HEAD), lambda step: (0, step // (2 * tiles), 0)),
            pl.BlockSpec((1, TILE, length), lambda step: (first(step) // tiles, lax.rem(first(step), tiles), 0)),
            pl.BlockSpec((TILE, hidden), lambda step: (second(step), 0)),
            anywhere,
            anywhere,
        ],
        out_specs=(
            pl.BlockSpec((TILE, hidden), lambda step: (second(step), 0)),
            pl.BlockSpec((TILE, 3 * HEAD), lambda step: (second(step), 0)),
            pl.BlockSpec((TILE, width), lambda step: (late(step), 0)),
            pl.BlockSpec((8, width), fixed),
            pl.BlockSpec((1, 3 * HEAD), fixed),
            pl.BlockSpec((1, hidden), fixed),
            anywhere,
            anywhere,
            anywhere,
        ),
        scratch_shapes=[
            vmem(panels.shape, kind),
            vmem(out_w.shape, kind),
            dma((2,)),
            vmem((length, HEAD), jnp.float32),
            vmem((length, HEAD), jnp.float32),
            vmem((length, HEAD), jnp.float32),
            vmem((levels, 2, span, width), kind),
            vmem((levels, span, width), kind),
            vmem((2, levels - 1, span, width), kind),
            vmem((2, tokens, HEAD), kind),
            vmem((tokens, width), kind),
            vmem((dp_size, unit, width), kind),
            vmem((2, 2, unit // 2, width), kind),
            vmem((2, unit // 2, width), kind),
            vmem((HEAD, width), kind),
            vmem((2, HEAD // 2, width), kind),
            dma((2,)),
            dma((1,)),
            dma((levels,)),
            dma((levels,)),
            dma((2, levels)),
            dma((2, levels)),
            *square_scratch(),
            dma((2 + HEAD // share,)),
            dma((3,)),
            dma((4,)),
        ],
        compiler_params=pltpu.CompilerParams(
            collective_id=4, has_side_effects=True, vmem_limit_bytes=60 * 1024 * 1024
        ),
        name="backward_part",
    )(g, x, panels, out_w, gains, cos, sin, heads, probs, slopes, features, g)


def reduce_kernel(
    dp_size,
    ctx_size,
    back,
    hidden_attn,
    hidden_mlp,
    grad_joined,
    grad_expanded,
    board,
    back_out,
    attn_out,
    mlp_out,
    tail_out,
    back_own,
    back_core,
    back_chain,
    left,
    right_attn,
    right_mlp,
    attn_own,
    attn_recv,
    attn_last,
    mlp_own,
    mlp_recv,
    mlp_last,
    board_recv,
    load_sem,
    left_sem,
    right_sem,
    core_send,
    core_recv,
    chain_send,
    chain_recv,
    first_send_a,
    first_recv_a,
    last_send_a,
    last_recv_a,
    first_send_m,
    first_recv_m,
    last_send_m,
    last_recv_m,
    row_send,
    row_recv,
    board_sem,
    store_sem,
):
    d = lax.axis_index("dp")
    c = lax.axis_index("ctx")
    core = lax.rem(c, 2)
    sibling = c + 1 - 2 * core
    x_mate = d + 1 - 2 * lax.rem(d, 2)
    y_mate = lax.rem(d + 2, 4)
    diagonal = 3 - d
    span = back.shape[0] // ctx_size
    levels = ctx_size // 2
    devices = dp_size * ctx_size
    me = d * ctx_size + c
    group_rows = hidden_attn.shape[1] // dp_size
    half = group_rows // 2
    rows = group_rows // ctx_size

    greet_all(d, c, dp_size, ctx_size)

    def back_view(parity, level):
        start = (2 * level + parity) * span
        return back.at[pl.ds(pl.multiple_of(start, span), span)]

    def back_load(level):
        return pltpu.make_async_copy(back_view(core, level), back_own.at[level], load_sem.at[level])

    def core_copy(level):
        return remote(
            back_view(1 - core, level), back_core.at[level], core_send.at[level], core_recv.at[level], d, sibling
        )

    order = outside_in(levels)

    tile_of = []
    for owners in ((diagonal, diagonal), (x_mate, y_mate), (y_mate, x_mate), (d, d)):
        for way in range(2):
            tile_of.append((owners[way], way))
    sequence = [(0, index) for index in range(6)]
    sequence += [(1, index) for index in range(4)]
    sequence += [(0, index) for index in range(6, 8)]
    sequence += [(1, index) for index in range(4, 8)]

    def left_copy(place):
        kind, index = sequence[place]
        owner, way = tile_of[index]
        columns = pl.ds(pl.multiple_of(owner * group_rows + way * half, half), half)
        source = (hidden_attn, hidden_mlp)[kind]
        return pltpu.make_async_copy(source.at[:, columns], left.at[place % 2], left_sem.at[place % 2])

    right_copies = (
        pltpu.make_async_copy(grad_joined, right_attn, right_sem.at[0]),
        pltpu.make_async_copy(grad_expanded, right_mlp, right_sem.at[1]),
    )

    def compute(kind, index):
        place = sequence.index((kind, index))
        if place + 1 < len(sequence):
            left_copy(place + 1).start()
        left_copy(place).wait()
        if index == 0:
            right_copies[kind].wait()
        target, right = ((attn_own, right_attn), (mlp_own, right_mlp))[kind]
        target[index] = dot_tn(left[place % 2], right[...]).astype(jnp.bfloat16)

    def square(own, recv, last, sems):
        return square_sum(
            lambda way, slot: own.at[way + 2 * (1 - slot)],
            lambda way: own.at[4 + way],
            recv,
            last,
            lambda way: own.at[6 + way],
            sems,
            d,
            c,
            half,
        )

    squares = (
        square(attn_own, attn_recv, attn_last, (first_send_a, first_recv_a, last_send_a, last_recv_a)),
        square(mlp_own, mlp_recv, mlp_last, (first_send_m, first_recv_m, last_send_m, last_recv_m)),
    )

    per_half = half // rows

    def row_chunk(kind, way, piece):
        return (attn_own, mlp_own)[kind].at[6 + way, pl.ds(piece * rows, rows)]

    def row_copy(kind, way, piece):
        target = way * per_half + piece
        out = (attn_out, mlp_out)[kind]
        return remote(
            row_chunk(kind, way, piece), out.at[c], row_send.at[kind, target], row_recv.at[kind], d, target
        )

    def row_local(kind, way, piece):
        out = (attn_out, mlp_out)[kind]
        return pltpu.make_async_copy(row_chunk(kind, way, piece), out.at[c], store_sem.at[kind])

    def tile_end(kind):
        first_copy, pass_on, arrive, add_final, finish = squares[kind]
        for way in range(2):
            arrive(way)
            for piece in range(per_half):
                add_final(way, piece * rows, rows)
                target = way * per_half + piece

                @pl.when(c != target)
                def _(way=way, piece=piece):
                    row_copy(kind, way, piece).start()

                @pl.when(c == target)
                def _(way=way, piece=piece):
                    row_local(kind, way, piece).start()

    board_load = pltpu.make_async_copy(board.at[me], board_recv.at[me], load_sem.at[levels])

    def board_start():
        board_load.start()

        def push_board(step, carry):
            other = lax.rem(me + step, devices)
            remote(
                board.at[other],
                board_recv.at[me],
                board_sem.at[0],
                board_sem.at[1],
                other // ctx_size,
                lax.rem(other, ctx_size),
            ).start()
            return carry

        lax.fori_loop(1, devices, push_board, 0)

    def board_end():
        board_load.wait()
        rest = board_recv.at[pl.ds(0, devices - 1)]
        remote(rest, rest, board_sem.at[0], board_sem.at[1], d, sibling).wait()
        tail_out[...] = jnp.sum(board_recv[...], axis=0)

    chain_open, chain_round, chain_end, chain_finish = chain_reduce(
        lambda level: back_own.at[level], back_chain, (chain_send, chain_recv), d, c, levels
    )

    def back_store(level):
        return pltpu.make_async_copy(back_own.at[level], back_out, store_sem.at[2])

    right_copies[0].start()
    left_copy(0).start()
    for level in order:
        core_copy(level).start()
        back_load(level).start()
    right_copies[1].start()

    for way in range(2):
        compute(0, way)
        squares[0][0](way, 1).start()
    for way in range(2):
        compute(0, 2 + way)
        squares[0][0](way, 0).start()
    for level in order:
        back_load(level).wait()
        core_copy(level).wait_recv()
        own = back_own.at[level]
        add_into(own, (own, back_core.at[level]), span)
        chain_open(level)
    compute(0, 4)
    compute(0, 5)
    squares[0][1](0)
    squares[0][1](1)
    for way in range(2):
        compute(1, way)
        squares[1][0](way, 1).start()
    for way in range(2):
        compute(1, 2 + way)
        squares[1][0](way, 0).start()
    chain_round(1)
    board_start()
    compute(0, 6)
    compute(0, 7)
    compute(1, 4)
    compute(1, 5)
    tile_end(0)
    chain_round(2)
    compute(1, 6)
    compute(1, 7)
    squares[1][1](0)
    squares[1][1](1)
    chain_end(back_store)
    tile_end(1)
    board_end()

    for kind in range(2):
        squares[kind][4]()
        for way in range(2):
            for piece in range(per_half):
                target = way * per_half + piece

                @pl.when(c != target)
                def _(kind=kind, way=way, piece=piece):
                    row_copy(kind, way, piece).wait_send()

        out = (attn_out, mlp_out)[kind]
        rest = out.at[pl.ds(0, ctx_size - 1)]
        remote(rest, rest, row_send.at[kind, 0], row_recv.at[kind], d, sibling).wait_recv()
        row_local(kind, 0, 0).wait()
    for level in range(levels):
        core_copy(level).wait_send()
    chain_finish(back_store)


def reduce_call(dp_size, ctx_size, back, hidden_attn, hidden_mlp, grad_joined, grad_expanded, board):
    length, width = back.shape
    tokens = hidden_attn.shape[0]
    span = length // ctx_size
    group_rows = width // dp_size
    half = group_rows // 2
    rows = group_rows // ctx_size
    joined, hidden = grad_joined.shape[1], grad_expanded.shape[1]
    levels = ctx_size // 2
    devices = dp_size * ctx_size
    dma = pltpu.SemaphoreType.DMA
    kind = back.dtype
    vmem = pltpu.VMEM
    out_shape = (
        jax.ShapeDtypeStruct((span, width), kind),
        jax.ShapeDtypeStruct((ctx_size, rows, joined), kind),
        jax.ShapeDtypeStruct((ctx_size, rows, hidden), kind),
        jax.ShapeDtypeStruct(board.shape[1:], jnp.float32),
    )
    anywhere = pl.BlockSpec(memory_space=pl.ANY)
    return pl.pallas_call(
        functools.partial(reduce_kernel, dp_size, ctx_size),
        out_shape=out_shape,
        in_specs=[anywhere] * 6,
        out_specs=(anywhere,) * 3 + (pl.BlockSpec(memory_space=pltpu.VMEM),),
        scratch_shapes=[
            vmem((levels, span, width), kind),
            vmem((levels, span, width), kind),
            vmem((2, levels - 1, span, width), kind),
            vmem((2, tokens, HEAD), kind),
            vmem((tokens, joined), kind),
            vmem((tokens, hidden), kind),
            vmem((8, half, joined), kind),
            vmem((2, 2, half, joined), kind),
            vmem((2, half, joined), kind),
            vmem((8, half, hidden), kind),
            vmem((2, 2, half, hidden), kind),
            vmem((2, half, hidden), kind),
            vmem((devices,) + board.shape[1:], jnp.float32),
            dma((levels + 1,)),
            dma((2,)),
            dma((2,)),
            dma((levels,)),
            dma((levels,)),
            dma((2, levels)),
            dma((2, levels)),
            *square_scratch(),
            *square_scratch(),
            dma((2, ctx_size)),
            dma((2,)),
            dma((2,)),
            dma((3,)),
        ],
        compiler_params=pltpu.CompilerParams(
            collective_id=2, has_side_effects=True, vmem_limit_bytes=60 * 1024 * 1024
        ),
        name="reduce_all",
    )(back, hidden_attn, hidden_mlp, grad_joined, grad_expanded, board)


def finish_kernel(
    attn_rows,
    mlp_rows,
    shrink_rows,
    dense_rows,
    back_first,
    back_last,
    x,
    g,
    out_first,
    out_last,
    out_shift,
    tail,
    qkv_grad,
    expand_grad,
    shrink_grad,
    dense_grad,
    layer_output,
    input_grad,
    *small_grads,
):
    ctx_size = attn_rows.shape[0]
    at = 0
    for target in small_grads:
        size = target.shape[0] * target.shape[1]
        for row in range(target.shape[0]):
            start = at + row * target.shape[1]
            lane = start % 128
            target[row : row + 1, :] = tail[start // 128 : start // 128 + 1, lane : lane + target.shape[1]]
        at += size
    for rows, target in ((attn_rows, qkv_grad), (mlp_rows, expand_grad)):
        for member in range(ctx_size):
            for part in range(rows.shape[2] // HEAD):
                start = (part * ctx_size + member) * HEAD
                target[:, start : start + HEAD] = rows[member, :, part * HEAD : (part + 1) * HEAD].astype(jnp.float32)
    shrink_grad[...] = shrink_rows[...].astype(jnp.float32)
    dense_grad[...] = dense_rows[...].astype(jnp.float32)
    for m, (back, out) in enumerate(((back_first, out_first), (back_last, out_last))):
        own = x[m].astype(jnp.float32)
        layer_output[m] = (own + out[...].astype(jnp.float32) + out_shift[...]).astype(jnp.bfloat16)
        centered = own - jnp.mean(own, axis=1, keepdims=True)
        spread = lax.rsqrt(jnp.mean(centered * centered, axis=1, keepdims=True) + 1e-05)
        normal = centered * spread
        grad = back[...].astype(jnp.float32)
        share = spread * (
            grad
            - jnp.mean(grad, axis=1, keepdims=True)
            - normal * jnp.mean(grad * normal, axis=1, keepdims=True)
        )
        input_grad[m] = (g[m].astype(jnp.float32) + share).astype(jnp.bfloat16)


def finish_call(attn_rows, mlp_rows, shrink_rows, dense_rows, back_first, back_last, x, g, out_first, out_last, out_shift, tail, lengths):
    steps = 4
    arrays = (attn_rows, mlp_rows, shrink_rows, dense_rows, back_first, back_last, x, g, out_first, out_last)
    micro = x.shape[0]
    ctx_size, rows, joined = attn_rows.shape

    def spec(shape):
        block = shape[:-2] + (shape[-2] // steps, shape[-1])
        lead = (0,) * (len(shape) - 2)
        return pl.BlockSpec(block, lambda step: lead + (step, 0))

    outs = (
        jax.ShapeDtypeStruct((rows, joined * ctx_size), jnp.float32),
        jax.ShapeDtypeStruct((rows, mlp_rows.shape[2] * ctx_size), jnp.float32),
        jax.ShapeDtypeStruct(shrink_rows.shape, jnp.float32),
        jax.ShapeDtypeStruct(dense_rows.shape, jnp.float32),
        jax.ShapeDtypeStruct(x.shape, jnp.bfloat16),
        jax.ShapeDtypeStruct(x.shape, jnp.bfloat16),
    )
    smalls = tuple(
        jax.ShapeDtypeStruct((max(1, length // 128), min(length, 128)), jnp.float32) for length in lengths
    )
    return pl.pallas_call(
        finish_kernel,
        grid=(steps,),
        out_shape=outs + smalls,
        in_specs=[spec(array.shape) for array in arrays] + [whole_spec(out_shift), whole_spec(tail)],
        out_specs=tuple(spec(out.shape) for out in outs)
        + tuple(pl.BlockSpec(out.shape, lambda step: (0, 0)) for out in smalls),
        compiler_params=pltpu.CompilerParams(vmem_limit_bytes=60 * 1024 * 1024),
        name="finish_part",
    )(*arrays, out_shift, tail)


def tensor_shards(
    layer_input,
    out_grad,
    prefix_len,
    qkv_weight,
    qkv_bias,
    dense_weight,
    dense_bias,
    expand_weight,
    expand_bias,
    shrink_weight,
    shrink_bias,
    attn_gain,
    attn_shift,
    mlp_gain,
    mlp_shift,
):
    dp_size = lax.axis_size("dp")
    ctx_size = lax.axis_size("ctx")
    devices = dp_size * ctx_size
    me = lax.axis_index("ctx")
    group = lax.axis_index("dp")
    micro, seq_count, span, width = layer_input.shape
    sequences = micro * seq_count
    tokens = sequences * SEQ
    row_share = qkv_weight.shape[0]
    scale = 1.0 / math.sqrt(HEAD)
    ff = expand_weight.shape[1]
    unit = shrink_weight.shape[0]
    members = (attn_gain, attn_shift, mlp_gain, mlp_shift, qkv_bias, dense_bias, expand_bias, shrink_bias)
    columns = max(member.shape[0] for member in members)
    packed = sum(
        jnp.pad(member[None], ((row, 15 - row), (0, columns - member.shape[0])))
        for row, member in enumerate(members)
    )
    own_x = layer_input.reshape(sequences, span, width)
    own_g = out_grad.reshape(sequences, span, width)
    x_all, panels, out_part, small = gather_call(
        dp_size, ctx_size, own_x, qkv_weight, expand_weight, dense_weight, shrink_weight, packed
    )
    x_all = x_all.reshape(tokens, width)
    small = small.astype(jnp.float32)
    gains = jnp.transpose(small[:, :4, : attn_gain.shape[0]], (1, 0, 2)).reshape(4, width)
    qkv_shift = small[:, 4, : qkv_bias.shape[0]].reshape(3, ctx_size, HEAD)
    qkv_shift = lax.dynamic_slice_in_dim(qkv_shift, me, 1, 1).reshape(-1)
    expand_shift = small.reshape(dp_size, ctx_size, 16, columns)[:, :, 6, :unit]
    expand_shift = lax.dynamic_slice_in_dim(expand_shift, me, 1, 1).reshape(-1)
    out_shift = (small[:, 5, : dense_bias.shape[0]] + small[:, 7, : shrink_bias.shape[0]]).reshape(1, width)
    cos, sin = turn_tables(SEQ)
    hidden_attn, hidden_mlp, heads, probs, features, slopes, partial, g_all, out_first = forward_call(
        ctx_size // 2,
        prefix_len.reshape(sequences),
        x_all,
        own_g,
        panels,
        out_part,
        gains,
        qkv_shift[None],
        expand_shift[None],
        cos,
        sin,
    )
    g_all = g_all.reshape(tokens, width)
    out_last = lax.psum_scatter(partial, "ctx", scatter_dimension=0, tiled=True)

    (
        grad_expanded,
        grad_joined,
        combined,
        norm_sums,
        joined_sum,
        expand_sum,
        back_first,
        shrink_rows,
        dense_rows,
    ) = backward_call(
        dp_size, ctx_size, g_all, x_all, panels, out_part, gains, cos, sin, heads, probs, slopes, features
    )
    joined_sum, expand_sum = joined_sum[0], expand_sum[0]

    def place(values, parts):
        board = jnp.zeros((parts, ctx_size, values.shape[0] // parts), jnp.float32)
        board = lax.dynamic_update_slice(board, values.reshape(parts, 1, -1), (0, me, 0))
        return board.reshape(devices, -1)

    out_sum = jnp.sum(own_g.astype(jnp.float32), axis=(0, 1))
    board = jnp.concatenate(
        [
            place(joined_sum[: 2 * HEAD], 2),
            place(joined_sum[2 * HEAD :], 1),
            out_sum.reshape(devices, -1),
            place(expand_sum, dp_size),
            norm_sums[0].reshape(devices, -1),
            norm_sums[1].reshape(devices, -1),
            norm_sums[2].reshape(devices, -1),
            norm_sums[3].reshape(devices, -1),
        ],
        axis=1,
    )
    used = board.shape[1]
    board = jnp.pad(board, ((0, 0), (0, -used % 1024))).reshape(devices, -1, 128)
    back_last, attn_rows, mlp_rows, tail = reduce_call(
        dp_size, ctx_size, combined, hidden_attn, hidden_mlp, grad_joined, grad_expanded, board
    )
    share_len = width // devices
    small_lengths = (2 * share_len, share_len, share_len, ff // devices) + (share_len,) * 4
    qkv_grad, expand_grad, shrink_grad, dense_grad, layer_output, input_grad, *pieces = finish_call(
        attn_rows,
        mlp_rows,
        shrink_rows,
        dense_rows,
        back_first,
        back_last,
        own_x,
        own_g,
        out_first,
        out_last,
        out_shift,
        tail,
        small_lengths,
    )
    pieces = [piece.reshape(-1) for piece in pieces]
    layer_output = layer_output.reshape(layer_input.shape)
    input_grad = input_grad.reshape(layer_input.shape)
    return (
        layer_output,
        input_grad,
        qkv_grad,
        pieces[0],
        pieces[1],
        dense_grad,
        pieces[2],
        expand_grad,
        pieces[3],
        shrink_grad,
        pieces[2],
        pieces[4],
        pieces[5],
        pieces[6],
        pieces[7],
    )


def solution(mesh):
    placed = (
        P(None, "dp", "ctx", None),
        P(None, "dp", "ctx", None),
        P(None, "dp"),
        P(("dp", "ctx"), None),
        P(("dp", "ctx")),
        P(("dp", "ctx"), None),
        P(("dp", "ctx")),
        P(("dp", "ctx"), None),
        P(("dp", "ctx")),
        P(("dp", "ctx"), None),
        P(("dp", "ctx")),
        P(("dp", "ctx")),
        P(("dp", "ctx")),
        P(("dp", "ctx")),
        P(("dp", "ctx")),
    )
    return jax.shard_map(
        tensor_shards if (mesh.shape["dp"], mesh.shape["ctx"]) == (4, HEADS) else shards,
        mesh=mesh,
        in_specs=placed,
        out_specs=(
            P(None, "dp", "ctx", None),
            P(None, "dp", "ctx", None),
            P(("dp", "ctx"), None),
            P(("dp", "ctx")),
            P(("dp", "ctx")),
            P(("dp", "ctx"), None),
            P(("dp", "ctx")),
            P(("dp", "ctx"), None),
            P(("dp", "ctx")),
            P(("dp", "ctx"), None),
            P(("dp", "ctx")),
            P(("dp", "ctx")),
            P(("dp", "ctx")),
            P(("dp", "ctx")),
            P(("dp", "ctx")),
        ),
        check_vma=False,
    )
```

```python
import functools
import math

import jax
import jax.numpy as jnp
import numpy as np
from jax import lax
from jax.experimental import pallas as pl
from jax.experimental.pallas import tpu as pltpu
from jax.sharding import PartitionSpec as P

HEADS = 8
HEAD = 256
ROT = 64
SEQ = 1024


def norm_rows(inputs, norm_gain, norm_bias):
    row_mean = jnp.mean(inputs, axis=-1, keepdims=True)
    centered = inputs - row_mean
    variance = jnp.mean(centered * centered, axis=-1, keepdims=True)
    return centered * lax.rsqrt(variance + 1e-05) * norm_gain + norm_bias


def gelu_exact(values):
    return jax.nn.gelu(values, approximate=False)


def rope_tables(positions):
    freqs = jnp.exp(jnp.arange(ROT // 2, dtype=jnp.float32) * (-2.0 * math.log(10000.0) / ROT))
    angles = positions[:, None] * freqs[None, :]
    return (jnp.cos(angles), jnp.sin(angles))


def rotate(heads, cos_table, sin_table):
    half_rot = ROT // 2
    lower = heads[..., :half_rot]
    upper = heads[..., half_rot:ROT]
    cos_wide = cos_table[:, None, :]
    sin_wide = sin_table[:, None, :]
    return jnp.concatenate(
        [
            lower * cos_wide - upper * sin_wide,
            upper * cos_wide + lower * sin_wide,
            heads[..., ROT:],
        ],
        axis=-1,
    )


def unpack_small(packed, lengths, devices):
    table_rows = packed.reshape(devices, -1)
    members = []
    offset = 0
    for length in lengths:
        members.append(table_rows[:, offset : offset + length].reshape(-1).astype(jnp.float32))
        offset = offset + length
    return members


def contract_rows(left_mat, right_mat):
    return lax.dot_general(
        left_mat, right_mat, (((0,), (0,)), ((), ())), preferred_element_type=jnp.float32
    )


def contract_cols(left_mat, right_mat):
    return lax.dot_general(
        left_mat, right_mat, (((1,), (1,)), ((), ())), preferred_element_type=jnp.float32
    )


def shards(
    layer_input,
    out_grad,
    prefix_len,
    qkv_weight,
    qkv_bias,
    dense_weight,
    dense_bias,
    expand_weight,
    expand_bias,
    shrink_weight,
    shrink_bias,
    attn_gain,
    attn_shift,
    mlp_gain,
    mlp_shift,
):
    devices = lax.axis_size("dp") * lax.axis_size("ctx")
    ctx_index = lax.axis_index("ctx")
    micro, seq_count, span, width = layer_input.shape
    sequences = micro * seq_count
    rows = sequences * span
    heads_shape = (sequences, span, HEADS, HEAD)
    scale = 1.0 / math.sqrt(HEAD)
    attn_lengths = (attn_gain.shape[0], attn_shift.shape[0], qkv_bias.shape[0], dense_bias.shape[0])
    mlp_lengths = (
        mlp_gain.shape[0],
        mlp_shift.shape[0],
        expand_bias.shape[0],
        shrink_bias.shape[0],
    )
    attn_packed = jnp.concatenate([attn_gain, attn_shift, qkv_bias, dense_bias])
    mlp_packed = jnp.concatenate([mlp_gain, mlp_shift, expand_bias, shrink_bias])

    def fetch_attn():
        return (
            lax.all_gather(qkv_weight, ("dp", "ctx"), axis=0, tiled=True),
            lax.all_gather(dense_weight, ("dp", "ctx"), axis=0, tiled=True),
            lax.all_gather(attn_packed, ("dp", "ctx"), axis=0, tiled=True),
        )

    def fetch_mlp():
        return (
            lax.all_gather(expand_weight, ("dp", "ctx"), axis=0, tiled=True),
            lax.all_gather(shrink_weight, ("dp", "ctx"), axis=0, tiled=True),
            lax.all_gather(mlp_packed, ("dp", "ctx"), axis=0, tiled=True),
        )

    local_pos = ctx_index * span + jnp.arange(span, dtype=jnp.int32)
    cos_table, sin_table = rope_tables(local_pos.astype(jnp.float32))
    key_pos = jnp.arange(SEQ, dtype=jnp.int32)
    causal = key_pos[None, :] <= local_pos[:, None]
    inputs = layer_input.astype(jnp.float32).reshape(rows, width)
    cot_rows = out_grad.reshape(rows, width)
    cot_float = cot_rows.astype(jnp.float32)
    prefix = prefix_len.reshape(sequences)
    allowed = (causal[None] | (key_pos[None, None, :] < prefix[:, None, None]))[:, None]
    attn_set = fetch_attn()
    qkv_full, dense_full, attn_small = attn_set
    gain_attn, shift_attn, joined_shift, dense_shift = unpack_small(
        attn_small, attn_lengths, devices
    )
    hidden_attn = norm_rows(inputs, gain_attn, shift_attn).astype(jnp.bfloat16)
    joined = jnp.dot(hidden_attn, qkv_full, preferred_element_type=jnp.float32) + joined_shift
    queries = rotate(joined[:, :width].reshape(heads_shape), cos_table, sin_table).astype(
        jnp.bfloat16
    )
    key_rows = rotate(
        joined[:, width : 2 * width].reshape(heads_shape), cos_table, sin_table
    ).astype(jnp.bfloat16)
    value_rows = joined[:, 2 * width :].reshape(heads_shape).astype(jnp.bfloat16)
    all_keys, all_values = (
        lax.all_gather(key_rows, "ctx", axis=1, tiled=True),
        lax.all_gather(value_rows, "ctx", axis=1, tiled=True),
    )
    scores = (
        jnp.einsum("sqhe,skhe->shqk", queries, all_keys, preferred_element_type=jnp.float32) * scale
    )
    scores = jnp.where(allowed, scores, -1e30)
    row_max = jnp.max(scores, axis=-1, keepdims=True)
    expo = jnp.exp(scores - row_max)
    row_total = jnp.sum(expo, axis=-1, keepdims=True)
    log_total = row_max + jnp.log(row_total)
    probs_low = (expo / row_total).astype(jnp.bfloat16)
    mixed = jnp.einsum("shqk,skhe->sqhe", probs_low, all_values, preferred_element_type=jnp.float32)
    mixed = mixed.reshape(rows, width).astype(jnp.bfloat16)
    attn_out = jnp.dot(mixed, dense_full, preferred_element_type=jnp.float32) + dense_shift
    mlp_set = fetch_mlp()
    expand_full, shrink_full, mlp_small = mlp_set
    gain_mlp, shift_mlp, expand_shift, shrink_shift = unpack_small(mlp_small, mlp_lengths, devices)
    hidden_mlp = norm_rows(inputs, gain_mlp, shift_mlp).astype(jnp.bfloat16)
    expanded = jnp.dot(hidden_mlp, expand_full, preferred_element_type=jnp.float32) + expand_shift
    activated = gelu_exact(expanded).astype(jnp.bfloat16)
    mlp_out = jnp.dot(activated, shrink_full, preferred_element_type=jnp.float32) + shrink_shift
    layer_output = (
        (inputs + attn_out + mlp_out).astype(jnp.bfloat16).reshape(micro, seq_count, span, width)
    )
    attn_back_set = fetch_attn()
    qkv_back, dense_back, attn_small_back = attn_back_set
    gain_attn, shift_attn, joined_shift, dense_shift = unpack_small(
        attn_small_back, attn_lengths, devices
    )
    grad_out_shift = jnp.sum(cot_float, axis=0)
    grad_mixed = contract_cols(cot_rows, dense_back).astype(jnp.bfloat16).reshape(heads_shape)
    again = (
        jnp.einsum("sqhe,skhe->shqk", queries, all_keys, preferred_element_type=jnp.float32) * scale
    )
    again = jnp.where(allowed, again, -1e30)
    probs = jnp.exp(again - log_total)
    grad_probs = jnp.einsum(
        "sqhe,skhe->shqk", grad_mixed, all_values, preferred_element_type=jnp.float32
    )
    delta = jnp.sum(probs * grad_probs, axis=-1, keepdims=True)
    grad_scores = (probs * (grad_probs - delta)).astype(jnp.bfloat16)
    grad_queries = (
        jnp.einsum("shqk,skhe->sqhe", grad_scores, all_keys, preferred_element_type=jnp.float32)
        * scale
    )
    all_queries, all_grad_mixed = (
        lax.all_gather(queries, "ctx", axis=1, tiled=True),
        lax.all_gather(grad_mixed, "ctx", axis=1, tiled=True),
    )
    stat_lse = jnp.transpose(log_total[..., 0], (0, 2, 1))
    stat_delta = jnp.transpose(delta[..., 0], (0, 2, 1))
    lse_all, delta_all = (
        lax.all_gather(stat_lse, "ctx", axis=1, tiled=True),
        lax.all_gather(stat_delta, "ctx", axis=1, tiled=True),
    )
    lse_all = jnp.transpose(lse_all, (0, 2, 1))[..., None]
    delta_all = jnp.transpose(delta_all, (0, 2, 1))[..., None]
    key_allowed = (local_pos[None, :] <= key_pos[:, None])[None] | (
        local_pos[None, None, :] < prefix[:, None, None]
    )
    block_scores = (
        jnp.einsum("sqhe,skhe->shqk", all_queries, key_rows, preferred_element_type=jnp.float32)
        * scale
    )
    block_scores = jnp.where(key_allowed[:, None], block_scores, -1e30)
    block_probs = jnp.exp(block_scores - lse_all)
    block_grad_probs = jnp.einsum(
        "sqhe,skhe->shqk", all_grad_mixed, value_rows, preferred_element_type=jnp.float32
    )
    block_grad_scores = (block_probs * (block_grad_probs - delta_all)).astype(jnp.bfloat16)
    own_keys = (
        jnp.einsum(
            "shqk,sqhe->skhe", block_grad_scores, all_queries, preferred_element_type=jnp.float32
        )
        * scale
    )
    own_values = jnp.einsum(
        "shqk,sqhe->skhe",
        block_probs.astype(jnp.bfloat16),
        all_grad_mixed,
        preferred_element_type=jnp.float32,
    )
    grad_joined = jnp.concatenate(
        [
            rotate(grad_queries, cos_table, -sin_table).reshape(rows, width),
            rotate(own_keys, cos_table, -sin_table).reshape(rows, width),
            own_values.reshape(rows, width),
        ],
        axis=1,
    ).astype(jnp.bfloat16)
    grad_joined_shift = jnp.sum(grad_joined.astype(jnp.float32), axis=0)
    grad_hidden_attn = contract_cols(grad_joined, qkv_back)
    unused_attn, attn_back = jax.vjp(norm_rows, inputs, gain_attn, shift_attn)
    grad_in_attn, grad_gain_attn, grad_shift_attn = attn_back(grad_hidden_attn)
    attn_columns = jnp.concatenate(
        [
            grad_gain_attn[:, None],
            grad_shift_attn[:, None],
            grad_joined_shift[: 2 * width].reshape(width, 2),
            grad_joined_shift[2 * width :][:, None],
            grad_out_shift[:, None],
        ],
        axis=1,
    )
    hidden_part = hidden_attn
    small_part = attn_columns
    attn_grads = lax.psum_scatter(
        jnp.concatenate(
            [contract_rows(hidden_part, grad_joined), contract_rows(mixed, cot_rows), small_part],
            axis=1,
        ),
        ("dp", "ctx"),
        scatter_dimension=0,
        tiled=True,
    )
    qkv_grad = attn_grads[:, : 3 * width]
    dense_grad = attn_grads[:, 3 * width : 4 * width]
    attn_tail = attn_grads[:, 4 * width :]
    mlp_back_set = fetch_mlp()
    expand_back, shrink_back, mlp_small_back = mlp_back_set
    gain_mlp, shift_mlp, expand_shift, shrink_shift = unpack_small(
        mlp_small_back, mlp_lengths, devices
    )
    unused_gelu, gelu_back = jax.vjp(gelu_exact, expanded)
    grad_act = contract_cols(cot_rows, shrink_back)
    grad_expanded = gelu_back(grad_act)[0].astype(jnp.bfloat16)
    grad_expand_shift = jnp.sum(grad_expanded.astype(jnp.float32), axis=0)
    grad_hidden_mlp = contract_cols(grad_expanded, expand_back)
    unused_mlp, mlp_back = jax.vjp(norm_rows, inputs, gain_mlp, shift_mlp)
    grad_in_mlp, grad_gain_mlp, grad_shift_mlp = mlp_back(grad_hidden_mlp)
    ratio = expand_shift.shape[0] // width
    mlp_columns = jnp.concatenate(
        [
            grad_gain_mlp[:, None],
            grad_shift_mlp[:, None],
            grad_expand_shift.reshape(width, ratio),
            grad_out_shift[:, None],
        ],
        axis=1,
    )
    ff_width = expand_back.shape[1]
    hidden_part = hidden_mlp
    small_part = mlp_columns
    expand_grads = lax.psum_scatter(
        jnp.concatenate([contract_rows(hidden_part, grad_expanded), small_part], axis=1),
        ("dp", "ctx"),
        scatter_dimension=0,
        tiled=True,
    )
    shrink_grad = lax.psum_scatter(
        contract_rows(activated, cot_rows), ("dp", "ctx"), scatter_dimension=0, tiled=True
    )
    expand_grad = expand_grads[:, :ff_width]
    mlp_tail = expand_grads[:, ff_width:]
    input_grad = (
        (cot_float + grad_in_attn + grad_in_mlp)
        .astype(jnp.bfloat16)
        .reshape(micro, seq_count, span, width)
    )
    return (
        layer_output,
        input_grad,
        qkv_grad,
        attn_tail[:, 2:4].reshape(-1),
        attn_tail[:, 4],
        dense_grad,
        attn_tail[:, 5],
        expand_grad,
        mlp_tail[:, 2 : 2 + ratio].reshape(-1),
        shrink_grad,
        mlp_tail[:, 2 + ratio],
        attn_tail[:, 0],
        attn_tail[:, 1],
        mlp_tail[:, 0],
        mlp_tail[:, 1],
    )


def low(values):
    return values.astype(jnp.bfloat16)


MESH_ID = pl.DeviceIdType.MESH


def remote(src, dst, send_sem, recv_sem, dp, ctx):
    return pltpu.make_async_remote_copy(
        src_ref=src,
        dst_ref=dst,
        send_sem=send_sem,
        recv_sem=recv_sem,
        device_id=(dp, ctx),
        device_id_type=MESH_ID,
    )


def greet_all(dp, ctx, dp_size, ctx_size):
    barrier = pltpu.get_barrier_semaphore()
    devices = dp_size * ctx_size
    me = dp * ctx_size + ctx

    def greet(step, carry):
        other = lax.rem(me + step, devices)
        pl.semaphore_signal(
            barrier, inc=1, device_id=(other // ctx_size, lax.rem(other, ctx_size)), device_id_type=MESH_ID
        )
        return carry

    lax.fori_loop(1, devices, greet, 0)
    pl.semaphore_wait(barrier, devices - 1)


def chain_gather(src, dst, sems, d, c, levels):
    block_send, block_recv, core_send, core_recv, local = sems
    micro, span = src.shape[0], src.shape[1]
    z = c // 2
    sibling = c + 1 - 2 * lax.rem(c, 2)

    def block(origin, m):
        return dst.at[m, pl.ds(pl.multiple_of(origin * span, span), span)]

    def link(way, hop, m):
        step = 2 if way == 0 else -2
        origin = c - step * hop
        view = src.at[m] if hop == 0 else block(origin, m)
        return remote(view, block(origin, m), block_send.at[way, hop, m], block_recv.at[way, hop, m], d, c + step)

    def leaves(way, hop):
        if way == 0:
            return jnp.logical_and(z >= hop, z <= levels - 2)
        return jnp.logical_and(z + hop <= levels - 1, z >= 1)

    def arrives(way, hop):
        return z >= hop + 1 if way == 0 else z + hop + 1 <= levels - 1

    def slot_of(way, hop):
        return 1 + way * (levels - 1) + hop

    def core_copy(slot, origin, m):
        view = src.at[m] if slot == 0 else block(origin, m)
        return remote(view, block(origin, m), core_send.at[slot, m], core_recv.at[slot, m], d, sibling)

    def own_copy(m):
        return pltpu.make_async_copy(src.at[m], block(c, m), local.at[m])

    def start(m):
        for way in range(2):
            @pl.when(leaves(way, 0))
            def _(way=way):
                link(way, 0, m).start()

        core_copy(0, c, m).start()
        own_copy(m).start()

    def hop_step(hop, m):
        for way in range(2):
            step = 2 if way == 0 else -2

            @pl.when(arrives(way, hop))
            def _(way=way, step=step):
                link(way, hop, m).wait_recv()
                if hop + 1 <= levels - 2:
                    @pl.when(leaves(way, hop + 1))
                    def _():
                        link(way, hop + 1, m).start()

                core_copy(slot_of(way, hop), c - step * (hop + 1), m).start()

    def finish(m):
        own_copy(m).wait()
        core_copy(0, c, m).wait_send()
        core_copy(0, sibling, m).wait_recv()
        for way in range(2):
            step = 2 if way == 0 else -2
            for hop in range(levels - 1):
                @pl.when(leaves(way, hop))
                def _(way=way, hop=hop):
                    link(way, hop, m).wait_send()

                @pl.when(arrives(way, hop))
                def _(way=way, hop=hop, step=step):
                    slot = slot_of(way, hop)
                    core_copy(slot, c - step * (hop + 1), m).wait_send()
                    core_copy(slot, sibling - step * (hop + 1), m).wait_recv()

    return start, hop_step, finish


def chain_scratch(levels, micro):
    dma = pltpu.SemaphoreType.DMA
    return [
        dma((2, levels - 1, micro)),
        dma((2, levels - 1, micro)),
        dma((2 * levels - 1, micro)),
        dma((2 * levels - 1, micro)),
        dma((micro,)),
    ]


def greet_line(d, c, levels):
    barrier = pltpu.get_barrier_semaphore()
    z = c // 2
    sibling = c + 1 - 2 * lax.rem(c, 2)
    pl.semaphore_signal(barrier, inc=1, device_id=(d, sibling), device_id_type=MESH_ID)

    @pl.when(z >= 1)
    def _():
        pl.semaphore_signal(barrier, inc=1, device_id=(d, c - 2), device_id_type=MESH_ID)

    @pl.when(z <= levels - 2)
    def _():
        pl.semaphore_signal(barrier, inc=1, device_id=(d, c + 2), device_id_type=MESH_ID)

    peers = 1 + (z >= 1).astype(jnp.int32) + (z <= levels - 2).astype(jnp.int32)
    pl.semaphore_wait(barrier, peers)


def gather_kernel(
    dp_size,
    ctx_size,
    x,
    qkv,
    expand,
    dense,
    shrink,
    packed,
    x_all,
    panels,
    out_w,
    small,
    local_sem,
    small_sem,
    block_send,
    block_recv,
    core_send,
    core_recv,
    block_local,
    panel_send,
    panel_recv,
    share_send,
    share_recv,
    pass_send,
    pass_recv,
):
    d = lax.axis_index("dp")
    c = lax.axis_index("ctx")
    z = c // 2
    sibling = c + 1 - 2 * lax.rem(c, 2)
    x_mate = d + 1 - 2 * lax.rem(d, 2)
    y_mate = lax.rem(d + 2, 4)
    micro, span = x.shape[0], x.shape[1]
    devices = dp_size * ctx_size
    me = d * ctx_size + c
    rows = qkv.shape[0]
    unit = shrink.shape[0]
    levels = ctx_size // 2
    panel_rows = ctx_size * rows
    n_panels = 3 + dp_size

    greet_all(d, c, dp_size, ctx_size)

    def column_block(panel, target):
        if panel < 3:
            start = panel * (qkv.shape[1] // 3) + target * HEAD
            return qkv.at[:, pl.ds(pl.multiple_of(start, HEAD), HEAD)]
        start = (panel - 3) * ctx_size * unit + target * unit
        return expand.at[:, pl.ds(pl.multiple_of(start, HEAD), HEAD)]

    own_rows = pl.ds(pl.multiple_of((d * ctx_size + c) * rows, rows), rows)

    for panel in range(n_panels):
        pltpu.make_async_copy(
            column_block(panel, c), panels.at[panel, own_rows], local_sem.at[panel]
        ).start()

        def push(step, carry, panel=panel):
            target = lax.rem(c + step, ctx_size)
            remote(
                column_block(panel, target),
                panels.at[panel, own_rows],
                panel_send.at[panel],
                panel_recv.at[panel],
                d,
                target,
            ).start()
            return carry

        lax.fori_loop(1, ctx_size, push, 0)

    def shrink_rows(owner, offset, count):
        return out_w.at[pl.ds(pl.multiple_of(HEAD + owner * unit + offset, 16), count)]

    shrink_local = pltpu.make_async_copy(shrink, shrink_rows(d, 0, unit), local_sem.at[n_panels])
    shrink_local.start()
    for way, mate in ((0, x_mate), (1, y_mate)):
        remote(
            shrink, shrink_rows(d, 0, unit), share_send.at[n_panels, way], share_recv.at[n_panels, way], mate, c
        ).start()

    per_head = HEAD // rows
    head_of = (d * ctx_size + c) // per_head
    dense_rows = pl.ds(pl.multiple_of(lax.rem(c, per_head) * rows, rows), rows)
    dense_out = remote(dense, out_w.at[dense_rows], panel_send.at[n_panels], panel_recv.at[n_panels], d, head_of)
    dense_own = pltpu.make_async_copy(dense, out_w.at[dense_rows], local_sem.at[n_panels + 1])
    stays = head_of == c

    @pl.when(stays)
    def _():
        dense_own.start()

    @pl.when(jnp.logical_not(stays))
    def _():
        dense_out.start()

    x_start, x_hop, x_finish = chain_gather(
        x, x_all, (block_send, block_recv, core_send, core_recv, block_local), d, c, levels
    )
    for m in range(micro):
        x_start(m)

    small_copy = pltpu.make_async_copy(packed, small.at[me], local_sem.at[n_panels + 2])
    small_copy.start()

    def push_small(step, carry):
        other = lax.rem(me + step, devices)
        remote(
            packed,
            small.at[me],
            small_sem.at[0],
            small_sem.at[1],
            other // ctx_size,
            lax.rem(other, ctx_size),
        ).start()
        return carry

    lax.fori_loop(1, devices, push_small, 0)

    def group_rows(owner, offset, count):
        return pl.ds(pl.multiple_of(owner * panel_rows + offset, 16), count)

    def panel_share(panel, way, mate):
        view = panels.at[panel, group_rows(d, 0, panel_rows)]
        return remote(view, view, share_send.at[panel, way], share_recv.at[panel, way], mate, c)

    def panel_step(panel):
        pltpu.make_async_copy(column_block(panel, c), panels.at[panel, own_rows], local_sem.at[panel]).wait()
        whole = panels.at[panel, group_rows(d, 0, (ctx_size - 1) * rows)]
        remote(whole, whole, panel_send.at[panel], panel_recv.at[panel], d, sibling).wait_recv()
        panel_share(panel, 0, x_mate).start()
        panel_share(panel, 1, y_mate).start()

    half = panel_rows // 2

    def panel_pass(panel, way):
        owner, mate = ((x_mate, y_mate), (y_mate, x_mate))[way]
        view = panels.at[panel, group_rows(owner, way * half, half)]
        return remote(view, view, pass_send.at[panel, way], pass_recv.at[panel, way], mate, c)

    def panel_forward(panel):
        for way, owner in ((0, x_mate), (1, y_mate)):
            view = panels.at[panel, group_rows(owner, 0, panel_rows)]
            remote(view, view, share_send.at[panel, way], share_recv.at[panel, way], owner, c).wait_recv()
            panel_pass(panel, way).start()

    def shrink_share_wait(way, owner):
        view = shrink_rows(owner, 0, unit)
        remote(view, view, share_send.at[n_panels, way], share_recv.at[n_panels, way], owner, c).wait_recv()

    def shrink_pass(way):
        owner, mate = ((x_mate, y_mate), (y_mate, x_mate))[way]
        view = shrink_rows(owner, way * (unit // 2), unit // 2)
        return remote(view, view, pass_send.at[n_panels, way], pass_recv.at[n_panels, way], mate, c)

    source = c // (ctx_size // dp_size)
    at_source = d == source
    from_x = x_mate == source
    from_y = y_mate == source
    head_rows = out_w.at[pl.ds(0, HEAD)]
    half_head = HEAD // 2

    def dense_share(way, mate):
        view = out_w.at[pl.ds(way * half_head, half_head)]
        return remote(view, view, share_send.at[n_panels + 1, way], share_recv.at[n_panels + 1, way], mate, c)

    owns_share = jnp.logical_and(at_source, stays)

    def dense_gather_step():
        @pl.when(owns_share)
        def _():
            dense_own.wait()
            view = out_w.at[pl.ds(0, (per_head - 1) * rows)]
            remote(view, view, panel_send.at[n_panels], panel_recv.at[n_panels], d, sibling).wait_recv()

        @pl.when(jnp.logical_and(at_source, jnp.logical_not(stays)))
        def _():
            remote(head_rows, head_rows, panel_send.at[n_panels], panel_recv.at[n_panels], d, sibling).wait_recv()

        @pl.when(at_source)
        def _():
            dense_share(0, x_mate).start()
            dense_share(1, y_mate).start()

    def dense_forward_step():
        @pl.when(from_x)
        def _():
            dense_share(0, x_mate).wait_recv()
            dense_share(0, y_mate).start()

        @pl.when(from_y)
        def _():
            dense_share(1, y_mate).wait_recv()
            dense_share(1, x_mate).start()

    def dense_last_step():
        @pl.when(across)
        def _():
            dense_share(0, y_mate).wait_recv()
            dense_share(0, x_mate).start()
            dense_share(1, x_mate).wait_recv()
            dense_share(1, y_mate).start()

    across = jnp.logical_not(jnp.logical_or(at_source, jnp.logical_or(from_x, from_y)))

    for panel in range(3):
        panel_step(panel)
    shrink_share_wait(0, x_mate)
    shrink_pass(0).start()
    shrink_share_wait(1, y_mate)
    shrink_pass(1).start()
    for panel in range(3, n_panels):
        panel_step(panel)
    dense_gather_step()
    panel_forward(0)
    panel_forward(1)
    x_hop(0, 0)
    panel_forward(2)
    x_hop(0, 1)
    dense_forward_step()
    panel_forward(3)
    panel_forward(4)
    x_hop(1, 0)
    panel_forward(5)
    x_hop(1, 1)
    dense_last_step()
    panel_forward(6)
    for hop in range(2, levels - 1):
        for m in range(micro):
            x_hop(hop, m)

    for panel in range(n_panels):
        for way, mate in ((0, x_mate), (1, y_mate)):
            panel_share(panel, way, mate).wait_send()
            panel_pass(panel, way).wait_send()
        for way in range(2):
            diagonal = 3 - d
            view = panels.at[panel, group_rows(diagonal, way * half, half)]
            remote(view, view, pass_send.at[panel, way], pass_recv.at[panel, way], x_mate, c).wait_recv()
        whole = panels.at[panel, group_rows(d, 0, (ctx_size - 1) * rows)]
        remote(whole, whole, panel_send.at[panel], panel_recv.at[panel], x_mate, c).wait_send()
    shrink_local.wait()
    for way in range(2):
        mate = (x_mate, y_mate)[way]
        remote(
            shrink, shrink_rows(d, 0, unit), share_send.at[n_panels, way], share_recv.at[n_panels, way], mate, c
        ).wait_send()
        shrink_pass(way).wait_send()
        view = shrink_rows(3 - d, way * (unit // 2), unit // 2)
        remote(view, view, pass_send.at[n_panels, way], pass_recv.at[n_panels, way], mate, c).wait_recv()

    @pl.when(jnp.logical_not(stays))
    def _():
        dense_out.wait_send()

    @pl.when(at_source)
    def _():
        dense_share(0, x_mate).wait_send()
        dense_share(1, y_mate).wait_send()

    @pl.when(from_x)
    def _():
        dense_share(0, y_mate).wait_send()
        dense_share(1, y_mate).wait_recv()

    @pl.when(from_y)
    def _():
        dense_share(1, x_mate).wait_send()
        dense_share(0, x_mate).wait_recv()

    @pl.when(across)
    def _():
        dense_share(0, x_mate).wait_send()
        dense_share(1, y_mate).wait_send()

    for m in range(micro):
        x_finish(m)

    small_copy.wait()
    rest = small.at[pl.ds(0, devices - 1)]
    remote(rest, rest, small_sem.at[0], small_sem.at[1], d, sibling).wait()


def gather_call(dp_size, ctx_size, x, qkv, expand, dense, shrink, packed):
    micro, span, width = x.shape
    rows = qkv.shape[0]
    n_panels = 3 + dp_size
    levels = ctx_size // 2
    devices = dp_size * ctx_size
    dma = pltpu.SemaphoreType.DMA
    out_shape = (
        jax.ShapeDtypeStruct((micro, ctx_size * span, width), x.dtype),
        jax.ShapeDtypeStruct((n_panels, devices * rows, HEAD), x.dtype),
        jax.ShapeDtypeStruct((HEAD + dp_size * shrink.shape[0], width), x.dtype),
        jax.ShapeDtypeStruct((devices,) + packed.shape, x.dtype),
    )
    anywhere = pl.BlockSpec(memory_space=pl.ANY)
    return pl.pallas_call(
        functools.partial(gather_kernel, dp_size, ctx_size),
        out_shape=out_shape,
        in_specs=[anywhere] * 6,
        out_specs=(anywhere,) * 4,
        scratch_shapes=[
            dma((n_panels + 3,)),
            dma((2,)),
            *chain_scratch(levels, micro),
            dma((n_panels + 1,)),
            dma((n_panels + 1,)),
            dma((n_panels + 2, 2)),
            dma((n_panels + 2, 2)),
            dma((n_panels + 2, 2)),
            dma((n_panels + 2, 2)),
        ],
        compiler_params=pltpu.CompilerParams(collective_id=1, has_side_effects=True),
        name="gather_all",
    )(x, qkv, expand, dense, shrink, packed)


def add_into(dst, srcs, rows):
    chunk = 16 if dst.shape[-1] > 1024 else 64

    def step(index, carry):
        at = pl.ds(pl.multiple_of(index * chunk, 16), chunk)
        total = srcs[0][at, :].astype(jnp.float32)
        for src in srcs[1:]:
            total = total + src[at, :].astype(jnp.float32)
        dst[at, :] = total.astype(dst.dtype)
        return carry

    lax.fori_loop(0, rows // chunk, step, 0)


TILE = 256


def turn_tables(length):
    freqs = np.exp(np.arange(ROT // 2) * (-2.0 * math.log(10000.0) / ROT))
    angles = np.arange(length)[:, None] * freqs[None, :]
    cos, sin = np.cos(angles), np.sin(angles)
    rest = np.zeros((length, 128 - ROT))
    return (
        jnp.asarray(np.concatenate([cos, cos, rest + 1.0], axis=1), jnp.float32),
        jnp.asarray(np.concatenate([-sin, sin, rest], axis=1), jnp.float32),
    )


def turn(head, cos, sin):
    front = head[:, :128]
    lane = lax.broadcasted_iota(jnp.int32, front.shape, 1)
    other = jnp.where(lane < ROT // 2, pltpu.roll(front, 128 - ROT // 2, 1), pltpu.roll(front, ROT // 2, 1))
    return jnp.concatenate([front * cos + other * sin, head[:, 128:]], axis=1)


def dot_nn(a, b):
    return lax.dot_general(a, b, (((1,), (0,)), ((), ())), preferred_element_type=jnp.float32)


def dot_nt(a, b):
    return lax.dot_general(a, b, (((1,), (1,)), ((), ())), preferred_element_type=jnp.float32)


def dot_tn(a, b):
    return lax.dot_general(a, b, (((0,), (0,)), ((), ())), preferred_element_type=jnp.float32)


def forward_kernel(
    tiles,
    levels,
    prefix,
    x,
    own_g,
    panels_in,
    out_w_in,
    gains,
    qkv_shift,
    expand_shift,
    cos,
    sin,
    hidden_attn,
    hidden_mlp,
    heads,
    probs,
    features,
    slopes,
    partial,
    g_all,
    first_out,
    panels,
    out_w,
    weight_sem,
    head_rows,
    acts,
    board,
    out_core,
    out_chain,
    core_send,
    core_recv,
    chain_send,
    chain_recv,
    store_sem,
    *g_sems,
):
    step = pl.program_id(0)
    micro = own_g.shape[0]
    d = lax.axis_index("dp")
    c = lax.axis_index("ctx")
    g_start, g_hop, g_finish = chain_gather(own_g, g_all, g_sems, d, c, levels)

    core = lax.rem(c, 2)
    span = board.shape[2]

    def own_block(level):
        return board.at[level, core]

    def core_copy(level):
        return remote(
            board.at[level, 1 - core],
            out_core.at[level],
            core_send.at[level],
            core_recv.at[level],
            d,
            c + 1 - 2 * core,
        )

    chain_open, chain_round, chain_end, chain_finish = chain_reduce(
        own_block, out_chain, (chain_send, chain_recv), d, c, levels
    )

    def out_store(level):
        return pltpu.make_async_copy(own_block(level), first_out, store_sem.at[0])

    panels_copy = pltpu.make_async_copy(panels_in, panels, weight_sem.at[0])
    out_w_copy = pltpu.make_async_copy(out_w_in, out_w, weight_sem.at[1])

    @pl.when(step == 0)
    def _():
        greet_line(d, c, levels)
        for m in range(micro):
            g_start(m)
        panels_copy.start()
        out_w_copy.start()
        panels_copy.wait()

    @pl.when(step == tiles)
    def _():
        out_w_copy.wait()

    for place, level in enumerate(outside_in(levels)):
        @pl.when(step == tiles + 1 + place)
        def _(level=level):
            core_copy(level).start()

        @pl.when(step == tiles + 2 + place)
        def _(level=level):
            core_copy(level).wait_recv()
            add_into(own_block(level), (own_block(level), out_core.at[level]), span)
            chain_open(level)

    @pl.when(step == 12)
    def _():
        chain_round(1)

    last = 4 * tiles - 1
    for at, hop, m in ((4, 0, 0), (7, 0, 1), (11, 1, 0), (14, 1, 1)):
        @pl.when(step == at)
        def _(hop=hop, m=m):
            g_hop(hop, m)

    seq = step // (2 * tiles)
    phase = lax.rem(step, 2 * tiles) // tiles
    tile = lax.rem(step, tiles)
    tile = jnp.where(phase == 0, tile, jnp.where(lax.rem(tile, 2) == 0, tiles - 1 - tile // 2, tile // 2))
    rows = pl.ds(pl.multiple_of(tile * TILE, TILE), TILE)
    n_expand = panels.shape[0] - 3
    scale = 1.0 / math.sqrt(HEAD)

    @pl.when(phase == 0)
    def _():
        values_in = x[...].astype(jnp.float32)
        centered = values_in - jnp.mean(values_in, axis=1, keepdims=True)
        normal = centered * lax.rsqrt(jnp.mean(centered * centered, axis=1, keepdims=True) + 1e-05)
        hidden_attn[...] = (normal * gains[0:1, :] + gains[1:2, :]).astype(jnp.bfloat16)
        hidden_mlp[...] = (normal * gains[2:3, :] + gains[3:4, :]).astype(jnp.bfloat16)
        wide = jnp.concatenate([panels[part] for part in range(3)], axis=1)
        all_joined = dot_nn(hidden_attn[...], wide) + qkv_shift[...]
        for part in range(3):
            joined = all_joined[:, part * HEAD : (part + 1) * HEAD]
            if part < 2:
                joined = turn(joined, cos[rows, :], sin[rows, :])
            joined = joined.astype(jnp.bfloat16)
            heads[part] = joined
            head_rows[part, rows, :] = joined
        for part in range(0, n_expand, 2):
            columns = slice(part * HEAD, (part + 2) * HEAD)
            wide = jnp.concatenate([panels[3 + part], panels[4 + part]], axis=1)
            expanded = dot_nn(hidden_mlp[...], wide) + expand_shift[:, columns]
            cdf = 0.5 * (1.0 + lax.erf(expanded * (1.0 / math.sqrt(2.0))))
            acts[rows, columns] = (expanded * cdf).astype(jnp.bfloat16)
            bell = jnp.exp(-0.5 * expanded * expanded) * (1.0 / math.sqrt(2.0 * math.pi))
            slopes[:, columns] = (cdf + expanded * bell).astype(jnp.bfloat16)

    @pl.when(phase == 1)
    def _():
        scores = dot_nt(head_rows[0, rows, :], head_rows[1]) * scale
        key_at = lax.broadcasted_iota(jnp.int32, scores.shape, 1)
        query_at = lax.broadcasted_iota(jnp.int32, scores.shape, 0) + tile * TILE
        allowed = jnp.logical_or(key_at <= query_at, key_at < prefix[seq])
        scores = jnp.where(allowed, scores, -1e30)
        expo = jnp.exp(scores - jnp.max(scores, axis=1, keepdims=True))
        low_probs = (expo * (1.0 / jnp.sum(expo, axis=1, keepdims=True))).astype(jnp.bfloat16)
        probs[0] = low_probs
        features[:, :HEAD] = dot_nn(low_probs, head_rows[2]).astype(jnp.bfloat16)
        features[:, HEAD:] = acts[rows, :]
        width = out_w.shape[1]
        for start in range(0, width, 1024):
            columns = slice(start, start + 1024)
            value = dot_nn(features[...], out_w[:, columns]).astype(jnp.bfloat16)

            @pl.when(seq == 0)
            def _(columns=columns, value=value):
                for parity in range(2):
                    board[tile, parity, :, columns] = value[parity * span : (parity + 1) * span]

            @pl.when(seq > 0)
            def _(columns=columns, value=value):
                partial[:, columns] = value

    @pl.when(step == last)
    def _():
        chain_round(2)
        for m in range(micro):
            for hop in range(2, levels - 1):
                g_hop(hop, m)
        chain_end(out_store)
        for m in range(micro):
            g_finish(m)
        for level in range(levels):
            core_copy(level).wait_send()
        chain_finish(out_store)


def whole_spec(array):
    zeros = (0,) * array.ndim
    return pl.BlockSpec(array.shape, lambda step: zeros, pipeline_mode=pl.Buffered(1))


def forward_call(levels, prefix, x, own_g, panels, out_w, gains, qkv_shift, expand_shift, cos, sin):
    tokens, width = x.shape
    length = cos.shape[0]
    tiles = length // TILE
    steps = 2 * tokens // TILE
    hidden = expand_shift.shape[1]
    span = own_g.shape[1]
    dma = pltpu.SemaphoreType.DMA

    def early(step):
        seq, at = step // (2 * tiles), lax.rem(step, 2 * tiles)
        return seq * tiles + jnp.minimum(at, tiles - 1)

    def late(step):
        seq, at = step // (2 * tiles), lax.rem(step, 2 * tiles)
        place = jnp.maximum(at - tiles, 0)
        return seq * tiles + jnp.where(lax.rem(place, 2) == 0, tiles - 1 - place // 2, place // 2)

    def last_only(step):
        return jnp.where(step < 2 * tiles, tiles - 1, late(step) - tiles)

    kind = jnp.bfloat16
    return pl.pallas_call(
        functools.partial(forward_kernel, tiles, levels),
        grid=(steps,),
        out_shape=(
            jax.ShapeDtypeStruct((tokens, width), kind),
            jax.ShapeDtypeStruct((tokens, width), kind),
            jax.ShapeDtypeStruct((3, tokens, HEAD), kind),
            jax.ShapeDtypeStruct((tokens // length, length, length), kind),
            jax.ShapeDtypeStruct((tokens, HEAD + hidden), kind),
            jax.ShapeDtypeStruct((tokens, hidden), kind),
            jax.ShapeDtypeStruct((length, width), kind),
            jax.ShapeDtypeStruct((tokens // length, length, width), kind),
            jax.ShapeDtypeStruct((span, width), kind),
        ),
        in_specs=[
            pl.BlockSpec(memory_space=pltpu.SMEM),
            pl.BlockSpec((TILE, width), lambda step: (early(step), 0)),
            pl.BlockSpec(memory_space=pl.ANY),
            pl.BlockSpec(memory_space=pl.ANY),
            pl.BlockSpec(memory_space=pl.ANY),
            whole_spec(gains),
            whole_spec(qkv_shift),
            whole_spec(expand_shift),
            whole_spec(cos),
            whole_spec(sin),
        ],
        out_specs=(
            pl.BlockSpec((TILE, width), lambda step: (early(step), 0)),
            pl.BlockSpec((TILE, width), lambda step: (early(step), 0)),
            pl.BlockSpec((3, TILE, HEAD), lambda step: (0, early(step), 0)),
            pl.BlockSpec((1, TILE, length), lambda step: (late(step) // tiles, lax.rem(late(step), tiles), 0)),
            pl.BlockSpec((TILE, HEAD + hidden), lambda step: (late(step), 0)),
            pl.BlockSpec((TILE, hidden), lambda step: (early(step), 0)),
            pl.BlockSpec((TILE, width), lambda step: (last_only(step), 0)),
            pl.BlockSpec(memory_space=pl.ANY),
            pl.BlockSpec(memory_space=pl.ANY),
        ),
        scratch_shapes=[
            pltpu.VMEM(panels.shape, kind),
            pltpu.VMEM(out_w.shape, kind),
            dma((2,)),
            pltpu.VMEM((3, length, HEAD), kind),
            pltpu.VMEM((length, hidden), kind),
            pltpu.VMEM((levels, 2, span, width), kind),
            pltpu.VMEM((levels, span, width), kind),
            pltpu.VMEM((2, levels - 1, span, width), kind),
            dma((levels,)),
            dma((levels,)),
            dma((2, levels)),
            dma((2, levels)),
            dma((1,)),
            *chain_scratch(levels, tokens // length),
        ],
        compiler_params=pltpu.CompilerParams(
            collective_id=3, has_side_effects=True, vmem_limit_bytes=60 * 1024 * 1024
        ),
        cost_estimate=pl.CostEstimate(
            flops=2 * tokens * width * (2 * hidden + 4 * HEAD) + 4 * tokens * length * HEAD,
            bytes_accessed=64 * 1024 * 1024,
            transcendentals=0,
        ),
        name="forward_part",
    )(prefix, x, own_g, panels, out_w, gains, qkv_shift, expand_shift, cos, sin)


def outside_in(levels):
    return [levels - 1 - place // 2 if place % 2 == 0 else place // 2 for place in range(levels)]


def chain_reduce(own, recv, sems, d, c, levels):
    chain_send, chain_recv = sems
    z = c // 2
    span = recv.shape[2]

    def copy(way, level):
        return remote(
            own(level),
            recv.at[way, level - 1 + way],
            chain_send.at[way, level],
            chain_recv.at[way, level],
            d,
            c + (2 if way == 0 else -2),
        )

    def sends(way, level):
        return z < level if way == 0 else z > level

    def hears(way, level):
        if way == 0:
            return jnp.logical_and(z >= 1, z <= level)
        return jnp.logical_and(z <= levels - 2, z >= level)

    def add(way, level):
        copy(way, level).wait_recv()
        add_into(own(level), (own(level), recv.at[way, level - 1 + way]), span)

    def open_level(level):
        for way, place in ((0, 0), (1, levels - 1)):
            if place != level:
                @pl.when(z == place)
                def _(way=way):
                    copy(way, level).start()

    def turn_round(index):
        for level in range(levels):
            for way in range(2):
                behind = levels - 1 - level if way == 0 else level
                place = index - behind if way == 0 else levels - 1 - (index - behind)
                if behind < index and (place < level if way == 0 else place > level):
                    @pl.when(z == place)
                    def _(way=way, level=level):
                        add(way, level)
                        copy(way, level).start()

    def end(store):
        for level in range(levels):
            for way in range(2):
                if 0 <= level - 1 + way < levels - 1:
                    @pl.when(jnp.logical_and(z == level, hears(way, level)))
                    def _(way=way, level=level):
                        add(way, level)

            @pl.when(z == level)
            def _(level=level):
                store(level).start()

    def finish(store):
        for level in range(levels):
            for way in range(2):
                if 0 <= level - 1 + way < levels - 1:
                    @pl.when(sends(way, level))
                    def _(way=way, level=level):
                        copy(way, level).wait_send()

        store(0).wait()

    return open_level, turn_round, end, finish


def square_sum(first, passing, recv, last, final, sems, d, c, count):
    first_send, first_recv, last_send, last_recv = sems
    x_mate = d + 1 - 2 * lax.rem(d, 2)
    y_mate = lax.rem(d + 2, 4)
    mates = ((x_mate, y_mate), (y_mate, x_mate))

    def first_copy(way, slot):
        return remote(
            first(way, slot), recv.at[way, slot], first_send.at[way, slot], first_recv.at[way, slot], mates[way][0], c
        )

    def last_copy(way):
        return remote(passing(way), last.at[way], last_send.at[way], last_recv.at[way], mates[way][1], c)

    def pass_on(way):
        first_copy(way, 1).wait_recv()
        add_into(passing(way), (passing(way), recv.at[way, 1]), count)
        last_copy(way).start()

    def arrive(way):
        first_copy(way, 0).wait_recv()
        last_copy(way).wait_recv()

    def add_final(way, start, rows):
        at = pl.ds(start, rows)
        own = final(way).at[at]
        add_into(own, (own, recv.at[way, 0, at], last.at[way, at]), rows)

    def finish():
        for way in range(2):
            first_copy(way, 0).wait_send()
            first_copy(way, 1).wait_send()
            last_copy(way).wait_send()

    return first_copy, pass_on, arrive, add_final, finish


def square_scratch():
    dma = pltpu.SemaphoreType.DMA
    return [dma((2, 2)), dma((2, 2)), dma((2,)), dma((2,))]


def backward_kernel(
    tiles,
    dp_size,
    ctx_size,
    g,
    x,
    panels_in,
    out_w_in,
    gains,
    cos,
    sin,
    heads,
    probs,
    slopes,
    features,
    grads,
    grad_expanded,
    grad_joined,
    combined,
    norm_sums,
    joined_sums,
    expand_sums,
    back_out,
    shrink_out,
    dense_out,
    panels,
    out_w,
    weight_sem,
    grad_queries,
    grad_keys,
    grad_values,
    board,
    back_core,
    back_chain,
    left,
    right,
    out_own,
    out_recv,
    out_last,
    dense_own,
    dense_recv,
    left_sem,
    right_sem,
    core_send,
    core_recv,
    chain_send,
    chain_recv,
    first_send,
    first_recv,
    last_send,
    last_recv,
    dense_send,
    dense_sem,
    store_sem,
):
    step = pl.program_id(0)
    seq = step // (2 * tiles)
    phase = lax.rem(step, 2 * tiles) // tiles
    tile = lax.rem(step, tiles)
    tile = jnp.where(phase == 0, tile, jnp.where(lax.rem(tile, 2) == 0, tiles - 1 - tile // 2, tile // 2))
    rows = pl.ds(pl.multiple_of(tile * TILE, TILE), TILE)
    n_expand = panels.shape[0] - 3
    width = out_w.shape[1]
    scale = 1.0 / math.sqrt(HEAD)

    d = lax.axis_index("dp")
    c = lax.axis_index("ctx")
    z = c // 2
    core = lax.rem(c, 2)
    sibling = c + 1 - 2 * core
    x_mate = d + 1 - 2 * lax.rem(d, 2)
    y_mate = lax.rem(d + 2, 4)
    diagonal = 3 - d
    levels = ctx_size // 2
    me = d * ctx_size + c
    span = board.shape[2]
    share = dense_out.shape[0]
    unit = (features.shape[1] - HEAD) // dp_size
    out_half = unit // 2
    head_half = HEAD // 2

    def left_copy(index):
        if index == 0:
            columns = pl.ds(0, HEAD)
        else:
            owner = (diagonal, x_mate, y_mate, d)[index - 1]
            columns = pl.ds(pl.multiple_of(HEAD + owner * unit, HEAD), unit)
        return pltpu.make_async_copy(features.at[:, columns], left.at[index % 2], left_sem.at[index % 2])

    right_copy = pltpu.make_async_copy(grads, right, right_sem.at[0])

    def compute(index):
        if index < dp_size:
            left_copy(index + 1).start()
        left_copy(index).wait()
        target = dense_own if index == 0 else out_own.at[index - 1]
        for start in range(0, width, 1024):
            columns = slice(start, start + 1024)
            target[:, columns] = dot_tn(left[index % 2], right[:, columns]).astype(jnp.bfloat16)

    def out_rows(index, way):
        return out_own.at[index, pl.ds(way * out_half, out_half)]

    first_copy, pass_on, arrive, add_final, square_finish = square_sum(
        lambda way, slot: out_rows(0 if slot == 1 else 1 + way, way),
        lambda way: out_rows(2 - way, way),
        out_recv,
        out_last,
        lambda way: out_rows(3, way),
        (first_send, first_recv, last_send, last_recv),
        d,
        c,
        out_half,
    )

    def out_store(way):
        return pltpu.make_async_copy(
            out_rows(3, way), shrink_out.at[pl.ds(way * out_half, out_half)], store_sem.at[way]
        )

    source = c // (ctx_size // dp_size)
    at_source = d == source
    from_x = x_mate == source
    from_y = y_mate == source
    across = diagonal == source
    per_head = HEAD // share

    def dense_half(way):
        return dense_own.at[pl.ds(way * head_half, head_half)]

    def dense_copy(way, mate):
        return remote(dense_half(way), dense_recv.at[way], dense_send.at[way], dense_sem.at[way], mate, c)

    def dense_add(way, mate):
        dense_copy(way, mate).wait_recv()
        add_into(dense_half(way), (dense_half(way), dense_recv.at[way]), head_half)

    def dense_open():
        @pl.when(from_y)
        def _():
            dense_copy(0, x_mate).start()

        @pl.when(from_x)
        def _():
            dense_copy(1, y_mate).start()

    def dense_second():
        @pl.when(across)
        def _():
            dense_add(0, y_mate)
            dense_copy(0, y_mate).start()
            dense_add(1, x_mate)
            dense_copy(1, x_mate).start()

    def dense_third():
        @pl.when(from_x)
        def _():
            dense_add(0, x_mate)
            dense_copy(0, x_mate).start()

        @pl.when(from_y)
        def _():
            dense_add(1, y_mate)
            dense_copy(1, y_mate).start()

    first_owner = lax.rem(c, ctx_size // per_head) * per_head

    def dense_chunk(piece):
        return dense_own.at[pl.ds(piece * share, share)]

    def dense_send_out(piece):
        return remote(
            dense_chunk(piece), dense_out, dense_send.at[2 + piece], dense_sem.at[2], d, first_owner + piece
        )

    def dense_store(piece):
        return pltpu.make_async_copy(dense_chunk(piece), dense_out, store_sem.at[2])

    def dense_fourth():
        @pl.when(at_source)
        def _():
            dense_add(0, x_mate)
            dense_add(1, y_mate)
            for piece in range(per_head):
                @pl.when(first_owner + piece == c)
                def _(piece=piece):
                    dense_store(piece).start()

                @pl.when(first_owner + piece != c)
                def _(piece=piece):
                    dense_send_out(piece).start()

    def dense_finish():
        @pl.when(jnp.logical_or(jnp.logical_or(from_y, across), from_x))
        def _():
            dense_copy(0, x_mate).wait_send()
            dense_copy(1, x_mate).wait_send()

        for piece in range(per_head):
            @pl.when(jnp.logical_and(at_source, first_owner + piece != c))
            def _(piece=piece):
                dense_send_out(piece).wait_send()

        stays = me // per_head == c

        @pl.when(stays)
        def _():
            dense_store(0).wait()

        @pl.when(jnp.logical_not(stays))
        def _():
            dense_send_out(0).wait_recv()

    def own_block(level):
        return board.at[level, core]

    def core_copy(level):
        return remote(
            board.at[level, 1 - core], back_core.at[level], core_send.at[level], core_recv.at[level], d, sibling
        )

    def core_add(level):
        core_copy(level).wait_recv()
        add_into(own_block(level), (own_block(level), back_core.at[level]), span)

    chain_open, chain_round, chain_end, chain_finish = chain_reduce(
        own_block, back_chain, (chain_send, chain_recv), d, c, levels
    )

    def back_store(level):
        return pltpu.make_async_copy(own_block(level), back_out, store_sem.at[3])

    def at(when):
        return pl.when(step == when)

    panels_copy = pltpu.make_async_copy(panels_in, panels, weight_sem.at[0])
    out_w_copy = pltpu.make_async_copy(out_w_in, out_w, weight_sem.at[1])

    @at(0)
    def _():
        out_w_copy.start()
        greet_all(d, c, dp_size, ctx_size)
        left_copy(0).start()
        right_copy.start()
        panels_copy.start()
        out_w_copy.wait()
        norm_sums[...] = jnp.zeros_like(norm_sums)
        joined_sums[...] = jnp.zeros_like(joined_sums)
        expand_sums[...] = jnp.zeros_like(expand_sums)

    @at(1)
    def _():
        right_copy.wait()
        compute(0)
        dense_open()

    @at(2)
    def _():
        compute(1)
        first_copy(0, 1).start()
        first_copy(1, 1).start()

    @at(3)
    def _():
        compute(2)
        first_copy(0, 0).start()
        compute(3)
        first_copy(1, 0).start()

    @at(4)
    def _():
        panels_copy.wait()
        compute(4)

    for place, level in enumerate(outside_in(levels)):
        @at(tiles + 1 + place)
        def _(level=level):
            core_copy(level).start()

        @at(tiles + 2 + place)
        def _(level=level):
            core_add(level)
            chain_open(level)

    @at(6)
    def _():
        dense_second()

    @at(7)
    def _():
        pass_on(0)
        pass_on(1)

    @at(10)
    def _():
        chain_round(1)
        dense_third()

    @at(13)
    def _():
        chain_round(2)
        for way in range(2):
            arrive(way)
            add_final(way, 0, out_half)
            out_store(way).start()

    @at(14)
    def _():
        dense_fourth()

    @pl.when(phase == 0)
    def _():
        low_probs = probs[0]
        own = dot_nt(g[...], out_w[:HEAD, :]).astype(jnp.bfloat16)
        grad_probs = dot_nt(own, heads[2])
        wide = low_probs.astype(jnp.float32)
        delta = jnp.sum(wide * grad_probs, axis=1, keepdims=True)
        grad_scores = (wide * (grad_probs - delta)).astype(jnp.bfloat16)
        grad_queries[rows, :] = dot_nn(grad_scores, heads[1]) * scale
        more_keys = dot_tn(grad_scores, heads[0, rows, :]) * scale
        more_values = dot_tn(low_probs, own)

        @pl.when(tile == 0)
        def _():
            grad_keys[...] = more_keys
            grad_values[...] = more_values

        @pl.when(tile > 0)
        def _():
            grad_keys[...] += more_keys
            grad_values[...] += more_values

    @pl.when(phase == 1)
    def _():
        grad = dot_nt(g[...], out_w[HEAD:, :])
        grad = (grad * slopes[...].astype(jnp.float32)).astype(jnp.bfloat16)
        grad_expanded[...] = grad
        expand_sums[...] += jnp.sum(grad.astype(jnp.float32), axis=0, keepdims=True)
        cos_rows, sin_rows = cos[rows, :], -sin[rows, :]
        parts = (
            turn(grad_queries[rows, :], cos_rows, sin_rows),
            turn(grad_keys[rows, :], cos_rows, sin_rows),
            grad_values[rows, :],
        )
        for part in range(3):
            columns = slice(part * HEAD, (part + 1) * HEAD)
            joined = parts[part].astype(jnp.bfloat16)
            grad_joined[:, columns] = joined
            joined_sums[:, columns] += jnp.sum(joined.astype(jnp.float32), axis=0, keepdims=True)
        values_in = x[...].astype(jnp.float32)
        mean = jnp.mean(values_in, axis=1, keepdims=True)
        centered = values_in - mean
        spread = lax.rsqrt(jnp.mean(centered * centered, axis=1, keepdims=True) + 1e-05)
        for start in range(0, width, 1024):
            columns = slice(start, start + 1024)
            normal = (x[:, columns].astype(jnp.float32) - mean) * spread
            wide = jnp.concatenate([panels[part, columns, :] for part in range(3)], axis=1)
            total = dot_nt(grad_joined[...], wide)
            wide = jnp.concatenate([panels[3 + part, columns, :] for part in range(n_expand)], axis=1)
            other = dot_nt(grad_expanded[...], wide)
            for row, value in ((0, total * normal), (1, total), (2, other * normal), (3, other)):
                norm_sums[row : row + 1, columns] += jnp.sum(value, axis=0, keepdims=True)
            value = (total * gains[0:1, columns] + other * gains[2:3, columns]).astype(jnp.bfloat16)

            @pl.when(seq == 0)
            def _(columns=columns, value=value):
                for parity in range(2):
                    board[tile, parity, :, columns] = value[parity * span : (parity + 1) * span]

            @pl.when(seq > 0)
            def _(columns=columns, value=value):
                combined[:, columns] = value

    @at(4 * tiles - 1)
    def _():
        chain_end(back_store)
        square_finish()
        for way in range(2):
            out_store(way).wait()
        dense_finish()
        for level in range(levels):
            core_copy(level).wait_send()
        chain_finish(back_store)


def backward_call(dp_size, ctx_size, g, x, panels, out_w, gains, cos, sin, heads, probs, slopes, features):
    tokens, width = x.shape
    length = cos.shape[0]
    tiles = length // TILE
    steps = 2 * tokens // TILE
    hidden = slopes.shape[1]
    levels = ctx_size // 2
    span = length // ctx_size
    unit = hidden // dp_size
    share = width // (dp_size * ctx_size)
    dma = pltpu.SemaphoreType.DMA
    vmem = pltpu.VMEM

    def first(step):
        seq, at = step // (2 * tiles), lax.rem(step, 2 * tiles)
        return seq * tiles + jnp.minimum(at, tiles - 1)

    def mixed_order(place):
        return jnp.where(lax.rem(place, 2) == 0, tiles - 1 - place // 2, place // 2)

    def second(step):
        seq, at = step // (2 * tiles), lax.rem(step, 2 * tiles)
        return seq * tiles + mixed_order(jnp.maximum(at - tiles, 0))

    def both(step):
        seq, at = step // (2 * tiles), lax.rem(step, 2 * tiles)
        return seq * tiles + jnp.where(at < tiles, at, mixed_order(at - tiles))

    def late(step):
        return jnp.where(step < 2 * tiles, mixed_order(0), second(step) - tiles)

    kind = jnp.bfloat16
    fixed = lambda step: (0, 0)
    anywhere = pl.BlockSpec(memory_space=pl.ANY)
    return pl.pallas_call(
        functools.partial(backward_kernel, tiles, dp_size, ctx_size),
        grid=(steps,),
        out_shape=(
            jax.ShapeDtypeStruct((tokens, hidden), kind),
            jax.ShapeDtypeStruct((tokens, 3 * HEAD), kind),
            jax.ShapeDtypeStruct((length, width), kind),
            jax.ShapeDtypeStruct((8, width), jnp.float32),
            jax.ShapeDtypeStruct((1, 3 * HEAD), jnp.float32),
            jax.ShapeDtypeStruct((1, hidden), jnp.float32),
            jax.ShapeDtypeStruct((span, width), kind),
            jax.ShapeDtypeStruct((unit, width), kind),
            jax.ShapeDtypeStruct((share, width), kind),
        ),
        in_specs=[
            pl.BlockSpec((TILE, width), lambda step: (both(step), 0)),
            pl.BlockSpec((TILE, width), lambda step: (second(step), 0)),
            pl.BlockSpec(memory_space=pl.ANY),
            pl.BlockSpec(memory_space=pl.ANY),
            whole_spec(gains),
            whole_spec(cos),
            whole_spec(sin),
            pl.BlockSpec((3, length, HEAD), lambda step: (0, step // (2 * tiles), 0)),
            pl.BlockSpec((1, TILE, length), lambda step: (first(step) // tiles, lax.rem(first(step), tiles), 0)),
            pl.BlockSpec((TILE, hidden), lambda step: (second(step), 0)),
            anywhere,
            anywhere,
        ],
        out_specs=(
            pl.BlockSpec((TILE, hidden), lambda step: (second(step), 0)),
            pl.BlockSpec((TILE, 3 * HEAD), lambda step: (second(step), 0)),
            pl.BlockSpec((TILE, width), lambda step: (late(step), 0)),
            pl.BlockSpec((8, width), fixed),
            pl.BlockSpec((1, 3 * HEAD), fixed),
            pl.BlockSpec((1, hidden), fixed),
            anywhere,
            anywhere,
            anywhere,
        ),
        scratch_shapes=[
            vmem(panels.shape, kind),
            vmem(out_w.shape, kind),
            dma((2,)),
            vmem((length, HEAD), jnp.float32),
            vmem((length, HEAD), jnp.float32),
            vmem((length, HEAD), jnp.float32),
            vmem((levels, 2, span, width), kind),
            vmem((levels, span, width), kind),
            vmem((2, levels - 1, span, width), kind),
            vmem((2, tokens, HEAD), kind),
            vmem((tokens, width), kind),
            vmem((dp_size, unit, width), kind),
            vmem((2, 2, unit // 2, width), kind),
            vmem((2, unit // 2, width), kind),
            vmem((HEAD, width), kind),
            vmem((2, HEAD // 2, width), kind),
            dma((2,)),
            dma((1,)),
            dma((levels,)),
            dma((levels,)),
            dma((2, levels)),
            dma((2, levels)),
            *square_scratch(),
            dma((2 + HEAD // share,)),
            dma((3,)),
            dma((4,)),
        ],
        compiler_params=pltpu.CompilerParams(
            collective_id=4, has_side_effects=True, vmem_limit_bytes=60 * 1024 * 1024
        ),
        name="backward_part",
    )(g, x, panels, out_w, gains, cos, sin, heads, probs, slopes, features, g)


def reduce_kernel(
    dp_size,
    ctx_size,
    back,
    hidden_attn,
    hidden_mlp,
    grad_joined,
    grad_expanded,
    board,
    back_out,
    attn_out,
    mlp_out,
    tail_out,
    back_own,
    back_core,
    back_chain,
    left,
    right_attn,
    right_mlp,
    attn_own,
    attn_recv,
    attn_last,
    mlp_own,
    mlp_recv,
    mlp_last,
    board_recv,
    load_sem,
    left_sem,
    right_sem,
    core_send,
    core_recv,
    chain_send,
    chain_recv,
    first_send_a,
    first_recv_a,
    last_send_a,
    last_recv_a,
    first_send_m,
    first_recv_m,
    last_send_m,
    last_recv_m,
    row_send,
    row_recv,
    board_sem,
    store_sem,
):
    d = lax.axis_index("dp")
    c = lax.axis_index("ctx")
    core = lax.rem(c, 2)
    sibling = c + 1 - 2 * core
    x_mate = d + 1 - 2 * lax.rem(d, 2)
    y_mate = lax.rem(d + 2, 4)
    diagonal = 3 - d
    span = back.shape[0] // ctx_size
    levels = ctx_size // 2
    devices = dp_size * ctx_size
    me = d * ctx_size + c
    group_rows = hidden_attn.shape[1] // dp_size
    half = group_rows // 2
    rows = group_rows // ctx_size

    greet_all(d, c, dp_size, ctx_size)

    def back_view(parity, level):
        start = (2 * level + parity) * span
        return back.at[pl.ds(pl.multiple_of(start, span), span)]

    def back_load(level):
        return pltpu.make_async_copy(back_view(core, level), back_own.at[level], load_sem.at[level])

    def core_copy(level):
        return remote(
            back_view(1 - core, level), back_core.at[level], core_send.at[level], core_recv.at[level], d, sibling
        )

    order = outside_in(levels)

    tile_of = []
    for owners in ((diagonal, diagonal), (x_mate, y_mate), (y_mate, x_mate), (d, d)):
        for way in range(2):
            tile_of.append((owners[way], way))
    sequence = [(0, index) for index in range(6)]
    sequence += [(1, index) for index in range(4)]
    sequence += [(0, index) for index in range(6, 8)]
    sequence += [(1, index) for index in range(4, 8)]

    def left_copy(place):
        kind, index = sequence[place]
        owner, way = tile_of[index]
        columns = pl.ds(pl.multiple_of(owner * group_rows + way * half, half), half)
        source = (hidden_attn, hidden_mlp)[kind]
        return pltpu.make_async_copy(source.at[:, columns], left.at[place % 4], left_sem.at[place % 4])

    right_copies = (
        pltpu.make_async_copy(grad_joined, right_attn, right_sem.at[0]),
        pltpu.make_async_copy(grad_expanded, right_mlp, right_sem.at[1]),
    )

    def compute(kind, index):
        place = sequence.index((kind, index))
        if place + 3 < len(sequence):
            left_copy(place + 3).start()
        left_copy(place).wait()
        if index == 0:
            right_copies[kind].wait()
        target, right = ((attn_own, right_attn), (mlp_own, right_mlp))[kind]
        target[index] = dot_tn(left[place % 4], right[...]).astype(jnp.bfloat16)

    def square(own, recv, last, sems):
        return square_sum(
            lambda way, slot: own.at[way + 2 * (1 - slot)],
            lambda way: own.at[4 + way],
            recv,
            last,
            lambda way: own.at[6 + way],
            sems,
            d,
            c,
            half,
        )

    squares = (
        square(attn_own, attn_recv, attn_last, (first_send_a, first_recv_a, last_send_a, last_recv_a)),
        square(mlp_own, mlp_recv, mlp_last, (first_send_m, first_recv_m, last_send_m, last_recv_m)),
    )

    per_half = half // rows

    def row_chunk(kind, way, piece):
        return (attn_own, mlp_own)[kind].at[6 + way, pl.ds(piece * rows, rows)]

    def row_copy(kind, way, piece):
        target = way * per_half + piece
        out = (attn_out, mlp_out)[kind]
        return remote(
            row_chunk(kind, way, piece), out.at[c], row_send.at[kind, target], row_recv.at[kind], d, target
        )

    def row_local(kind, way, piece):
        out = (attn_out, mlp_out)[kind]
        return pltpu.make_async_copy(row_chunk(kind, way, piece), out.at[c], store_sem.at[kind])

    def tile_end(kind):
        first_copy, pass_on, arrive, add_final, finish = squares[kind]
        for way in range(2):
            arrive(way)
            for piece in range(per_half):
                add_final(way, piece * rows, rows)
                target = way * per_half + piece

                @pl.when(c != target)
                def _(way=way, piece=piece):
                    row_copy(kind, way, piece).start()

                @pl.when(c == target)
                def _(way=way, piece=piece):
                    row_local(kind, way, piece).start()

    board_load = pltpu.make_async_copy(board.at[me], board_recv.at[me], load_sem.at[levels])

    def board_start():
        board_load.start()

        def push_board(step, carry):
            other = lax.rem(me + step, devices)
            remote(
                board.at[other],
                board_recv.at[me],
                board_sem.at[0],
                board_sem.at[1],
                other // ctx_size,
                lax.rem(other, ctx_size),
            ).start()
            return carry

        lax.fori_loop(1, devices, push_board, 0)

    def board_end():
        board_load.wait()
        rest = board_recv.at[pl.ds(0, devices - 1)]
        remote(rest, rest, board_sem.at[0], board_sem.at[1], d, sibling).wait()
        tail_out[...] = jnp.sum(board_recv[...], axis=0)

    chain_open, chain_round, chain_end, chain_finish = chain_reduce(
        lambda level: back_own.at[level], back_chain, (chain_send, chain_recv), d, c, levels
    )

    def back_store(level):
        return pltpu.make_async_copy(back_own.at[level], back_out, store_sem.at[2])

    right_copies[0].start()
    for place in range(3):
        left_copy(place).start()
    for level in order:
        core_copy(level).start()
        back_load(level).start()
    right_copies[1].start()

    for way in range(2):
        compute(0, way)
        squares[0][0](way, 1).start()
    for way in range(2):
        compute(0, 2 + way)
        squares[0][0](way, 0).start()
    for level in order:
        back_load(level).wait()
        core_copy(level).wait_recv()
        own = back_own.at[level]
        add_into(own, (own, back_core.at[level]), span)
        chain_open(level)
    compute(0, 4)
    compute(0, 5)
    squares[0][1](0)
    squares[0][1](1)
    for way in range(2):
        compute(1, way)
        squares[1][0](way, 1).start()
    for way in range(2):
        compute(1, 2 + way)
        squares[1][0](way, 0).start()
    chain_round(1)
    board_start()
    compute(0, 6)
    compute(0, 7)
    compute(1, 4)
    compute(1, 5)
    tile_end(0)
    chain_round(2)
    compute(1, 6)
    compute(1, 7)
    squares[1][1](0)
    squares[1][1](1)
    chain_end(back_store)
    tile_end(1)
    board_end()

    for kind in range(2):
        squares[kind][4]()
        for way in range(2):
            for piece in range(per_half):
                target = way * per_half + piece

                @pl.when(c != target)
                def _(kind=kind, way=way, piece=piece):
                    row_copy(kind, way, piece).wait_send()

        out = (attn_out, mlp_out)[kind]
        rest = out.at[pl.ds(0, ctx_size - 1)]
        remote(rest, rest, row_send.at[kind, 0], row_recv.at[kind], d, sibling).wait_recv()
        row_local(kind, 0, 0).wait()
    for level in range(levels):
        core_copy(level).wait_send()
    chain_finish(back_store)


def reduce_call(dp_size, ctx_size, back, hidden_attn, hidden_mlp, grad_joined, grad_expanded, board):
    length, width = back.shape
    tokens = hidden_attn.shape[0]
    span = length // ctx_size
    group_rows = width // dp_size
    half = group_rows // 2
    rows = group_rows // ctx_size
    joined, hidden = grad_joined.shape[1], grad_expanded.shape[1]
    levels = ctx_size // 2
    devices = dp_size * ctx_size
    dma = pltpu.SemaphoreType.DMA
    kind = back.dtype
    vmem = pltpu.VMEM
    out_shape = (
        jax.ShapeDtypeStruct((span, width), kind),
        jax.ShapeDtypeStruct((ctx_size, rows, joined), kind),
        jax.ShapeDtypeStruct((ctx_size, rows, hidden), kind),
        jax.ShapeDtypeStruct(board.shape[1:], jnp.float32),
    )
    anywhere = pl.BlockSpec(memory_space=pl.ANY)
    return pl.pallas_call(
        functools.partial(reduce_kernel, dp_size, ctx_size),
        out_shape=out_shape,
        in_specs=[anywhere] * 6,
        out_specs=(anywhere,) * 3 + (pl.BlockSpec(memory_space=pltpu.VMEM),),
        scratch_shapes=[
            vmem((levels, span, width), kind),
            vmem((levels, span, width), kind),
            vmem((2, levels - 1, span, width), kind),
            vmem((4, tokens, HEAD), kind),
            vmem((tokens, joined), kind),
            vmem((tokens, hidden), kind),
            vmem((8, half, joined), kind),
            vmem((2, 2, half, joined), kind),
            vmem((2, half, joined), kind),
            vmem((8, half, hidden), kind),
            vmem((2, 2, half, hidden), kind),
            vmem((2, half, hidden), kind),
            vmem((devices,) + board.shape[1:], jnp.float32),
            dma((levels + 1,)),
            dma((4,)),
            dma((2,)),
            dma((levels,)),
            dma((levels,)),
            dma((2, levels)),
            dma((2, levels)),
            *square_scratch(),
            *square_scratch(),
            dma((2, ctx_size)),
            dma((2,)),
            dma((2,)),
            dma((3,)),
        ],
        compiler_params=pltpu.CompilerParams(
            collective_id=2, has_side_effects=True, vmem_limit_bytes=60 * 1024 * 1024
        ),
        name="reduce_all",
    )(back, hidden_attn, hidden_mlp, grad_joined, grad_expanded, board)


def finish_kernel(
    attn_rows,
    mlp_rows,
    shrink_rows,
    dense_rows,
    back_first,
    back_last,
    x,
    g,
    out_first,
    out_last,
    out_shift,
    tail,
    qkv_grad,
    expand_grad,
    shrink_grad,
    dense_grad,
    layer_output,
    input_grad,
    *small_grads,
):
    ctx_size = attn_rows.shape[0]
    at = 0
    for target in small_grads:
        size = target.shape[0] * target.shape[1]
        for row in range(target.shape[0]):
            start = at + row * target.shape[1]
            lane = start % 128
            target[row : row + 1, :] = tail[start // 128 : start // 128 + 1, lane : lane + target.shape[1]]
        at += size
    for rows, target in ((attn_rows, qkv_grad), (mlp_rows, expand_grad)):
        for member in range(ctx_size):
            for part in range(rows.shape[2] // HEAD):
                start = (part * ctx_size + member) * HEAD
                target[:, start : start + HEAD] = rows[member, :, part * HEAD : (part + 1) * HEAD].astype(jnp.float32)
    shrink_grad[...] = shrink_rows[...].astype(jnp.float32)
    dense_grad[...] = dense_rows[...].astype(jnp.float32)
    for m, (back, out) in enumerate(((back_first, out_first), (back_last, out_last))):
        own = x[m].astype(jnp.float32)
        layer_output[m] = (own + out[...].astype(jnp.float32) + out_shift[...]).astype(jnp.bfloat16)
        centered = own - jnp.mean(own, axis=1, keepdims=True)
        spread = lax.rsqrt(jnp.mean(centered * centered, axis=1, keepdims=True) + 1e-05)
        normal = centered * spread
        grad = back[...].astype(jnp.float32)
        share = spread * (
            grad
            - jnp.mean(grad, axis=1, keepdims=True)
            - normal * jnp.mean(grad * normal, axis=1, keepdims=True)
        )
        input_grad[m] = (g[m].astype(jnp.float32) + share).astype(jnp.bfloat16)


def finish_call(attn_rows, mlp_rows, shrink_rows, dense_rows, back_first, back_last, x, g, out_first, out_last, out_shift, tail, lengths):
    steps = 4
    arrays = (attn_rows, mlp_rows, shrink_rows, dense_rows, back_first, back_last, x, g, out_first, out_last)
    micro = x.shape[0]
    ctx_size, rows, joined = attn_rows.shape

    def spec(shape):
        block = shape[:-2] + (shape[-2] // steps, shape[-1])
        lead = (0,) * (len(shape) - 2)
        return pl.BlockSpec(block, lambda step: lead + (step, 0))

    outs = (
        jax.ShapeDtypeStruct((rows, joined * ctx_size), jnp.float32),
        jax.ShapeDtypeStruct((rows, mlp_rows.shape[2] * ctx_size), jnp.float32),
        jax.ShapeDtypeStruct(shrink_rows.shape, jnp.float32),
        jax.ShapeDtypeStruct(dense_rows.shape, jnp.float32),
        jax.ShapeDtypeStruct(x.shape, jnp.bfloat16),
        jax.ShapeDtypeStruct(x.shape, jnp.bfloat16),
    )
    smalls = tuple(
        jax.ShapeDtypeStruct((max(1, length // 128), min(length, 128)), jnp.float32) for length in lengths
    )
    return pl.pallas_call(
        finish_kernel,
        grid=(steps,),
        out_shape=outs + smalls,
        in_specs=[spec(array.shape) for array in arrays] + [whole_spec(out_shift), whole_spec(tail)],
        out_specs=tuple(spec(out.shape) for out in outs)
        + tuple(pl.BlockSpec(out.shape, lambda step: (0, 0)) for out in smalls),
        compiler_params=pltpu.CompilerParams(vmem_limit_bytes=60 * 1024 * 1024),
        name="finish_part",
    )(*arrays, out_shift, tail)


def tensor_shards(
    layer_input,
    out_grad,
    prefix_len,
    qkv_weight,
    qkv_bias,
    dense_weight,
    dense_bias,
    expand_weight,
    expand_bias,
    shrink_weight,
    shrink_bias,
    attn_gain,
    attn_shift,
    mlp_gain,
    mlp_shift,
):
    dp_size = lax.axis_size("dp")
    ctx_size = lax.axis_size("ctx")
    devices = dp_size * ctx_size
    me = lax.axis_index("ctx")
    group = lax.axis_index("dp")
    micro, seq_count, span, width = layer_input.shape
    sequences = micro * seq_count
    tokens = sequences * SEQ
    row_share = qkv_weight.shape[0]
    scale = 1.0 / math.sqrt(HEAD)
    ff = expand_weight.shape[1]
    unit = shrink_weight.shape[0]
    members = (attn_gain, attn_shift, mlp_gain, mlp_shift, qkv_bias, dense_bias, expand_bias, shrink_bias)
    columns = max(member.shape[0] for member in members)
    packed = sum(
        jnp.pad(member[None], ((row, 15 - row), (0, columns - member.shape[0])))
        for row, member in enumerate(members)
    )
    own_x = layer_input.reshape(sequences, span, width)
    own_g = out_grad.reshape(sequences, span, width)
    x_all, panels, out_part, small = gather_call(
        dp_size, ctx_size, own_x, qkv_weight, expand_weight, dense_weight, shrink_weight, packed
    )
    x_all = x_all.reshape(tokens, width)
    small = small.astype(jnp.float32)
    gains = jnp.transpose(small[:, :4, : attn_gain.shape[0]], (1, 0, 2)).reshape(4, width)
    qkv_shift = small[:, 4, : qkv_bias.shape[0]].reshape(3, ctx_size, HEAD)
    qkv_shift = lax.dynamic_slice_in_dim(qkv_shift, me, 1, 1).reshape(-1)
    expand_shift = small.reshape(dp_size, ctx_size, 16, columns)[:, :, 6, :unit]
    expand_shift = lax.dynamic_slice_in_dim(expand_shift, me, 1, 1).reshape(-1)
    out_shift = (small[:, 5, : dense_bias.shape[0]] + small[:, 7, : shrink_bias.shape[0]]).reshape(1, width)
    cos, sin = turn_tables(SEQ)
    hidden_attn, hidden_mlp, heads, probs, features, slopes, partial, g_all, out_first = forward_call(
        ctx_size // 2,
        prefix_len.reshape(sequences),
        x_all,
        own_g,
        panels,
        out_part,
        gains,
        qkv_shift[None],
        expand_shift[None],
        cos,
        sin,
    )
    g_all = g_all.reshape(tokens, width)
    out_last = lax.psum_scatter(partial, "ctx", scatter_dimension=0, tiled=True)

    (
        grad_expanded,
        grad_joined,
        combined,
        norm_sums,
        joined_sum,
        expand_sum,
        back_first,
        shrink_rows,
        dense_rows,
    ) = backward_call(
        dp_size, ctx_size, g_all, x_all, panels, out_part, gains, cos, sin, heads, probs, slopes, features
    )
    joined_sum, expand_sum = joined_sum[0], expand_sum[0]

    def place(values, parts):
        board = jnp.zeros((parts, ctx_size, values.shape[0] // parts), jnp.float32)
        board = lax.dynamic_update_slice(board, values.reshape(parts, 1, -1), (0, me, 0))
        return board.reshape(devices, -1)

    out_sum = jnp.sum(own_g.astype(jnp.float32), axis=(0, 1))
    board = jnp.concatenate(
        [
            place(joined_sum[: 2 * HEAD], 2),
            place(joined_sum[2 * HEAD :], 1),
            out_sum.reshape(devices, -1),
            place(expand_sum, dp_size),
            norm_sums[0].reshape(devices, -1),
            norm_sums[1].reshape(devices, -1),
            norm_sums[2].reshape(devices, -1),
            norm_sums[3].reshape(devices, -1),
        ],
        axis=1,
    )
    used = board.shape[1]
    board = jnp.pad(board, ((0, 0), (0, -used % 1024))).reshape(devices, -1, 128)
    back_last, attn_rows, mlp_rows, tail = reduce_call(
        dp_size, ctx_size, combined, hidden_attn, hidden_mlp, grad_joined, grad_expanded, board
    )
    share_len = width // devices
    small_lengths = (2 * share_len, share_len, share_len, ff // devices) + (share_len,) * 4
    qkv_grad, expand_grad, shrink_grad, dense_grad, layer_output, input_grad, *pieces = finish_call(
        attn_rows,
        mlp_rows,
        shrink_rows,
        dense_rows,
        back_first,
        back_last,
        own_x,
        own_g,
        out_first,
        out_last,
        out_shift,
        tail,
        small_lengths,
    )
    pieces = [piece.reshape(-1) for piece in pieces]
    layer_output = layer_output.reshape(layer_input.shape)
    input_grad = input_grad.reshape(layer_input.shape)
    return (
        layer_output,
        input_grad,
        qkv_grad,
        pieces[0],
        pieces[1],
        dense_grad,
        pieces[2],
        expand_grad,
        pieces[3],
        shrink_grad,
        pieces[2],
        pieces[4],
        pieces[5],
        pieces[6],
        pieces[7],
    )


def solution(mesh):
    placed = (
        P(None, "dp", "ctx", None),
        P(None, "dp", "ctx", None),
        P(None, "dp"),
        P(("dp", "ctx"), None),
        P(("dp", "ctx")),
        P(("dp", "ctx"), None),
        P(("dp", "ctx")),
        P(("dp", "ctx"), None),
        P(("dp", "ctx")),
        P(("dp", "ctx"), None),
        P(("dp", "ctx")),
        P(("dp", "ctx")),
        P(("dp", "ctx")),
        P(("dp", "ctx")),
        P(("dp", "ctx")),
    )
    return jax.shard_map(
        tensor_shards if (mesh.shape["dp"], mesh.shape["ctx"]) == (4, HEADS) else shards,
        mesh=mesh,
        in_specs=placed,
        out_specs=(
            P(None, "dp", "ctx", None),
            P(None, "dp", "ctx", None),
            P(("dp", "ctx"), None),
            P(("dp", "ctx")),
            P(("dp", "ctx")),
            P(("dp", "ctx"), None),
            P(("dp", "ctx")),
            P(("dp", "ctx"), None),
            P(("dp", "ctx")),
            P(("dp", "ctx"), None),
            P(("dp", "ctx")),
            P(("dp", "ctx")),
            P(("dp", "ctx")),
            P(("dp", "ctx")),
            P(("dp", "ctx")),
        ),
        check_vma=False,
    )
```
